32 devices in a mesh: section: 2 (over core), seq: 16 (over z, y, x).
Axes of the slice: x: 2, y: 2, z: 4, core: 2. Of those that a mesh axis runs over, the one named last changes fastest.
Arguments:
- io_pair: bfloat16 [2, 2, 2048, 512], P('section', None, 'seq'), may hold values from -6 to 6
- lengths: int32 [2], replicated, may hold values from 1024 to 2048, as said below
- filters: bfloat16 [2048, 24], P('seq'), may hold values from -0.125 to 0.125
- stu_maps: bfloat16 [26112, 512], P(('section', 'seq')), may hold values from -0.0390625 to 0.0390625
- attn_proj: bfloat16 [1536, 512], P(('section', 'seq')), may hold values from -0.25 to 0.25
- attn_out: bfloat16 [512, 512], P(('section', 'seq')), may hold values from -2 to 2
- norm_gains: bfloat16 [2, 2, 512], P('section', None, 'seq'), may hold values from 0.5 to 1.5
- mlp_gate: bfloat16 [2, 512, 2048], P('section', 'seq'), may hold values from -0.25 to 0.25
- mlp_up: bfloat16 [2, 512, 2048], P('section', 'seq'), may hold values from -0.25 to 0.25
- mlp_down: bfloat16 [2, 2048, 512], P('section', 'seq'), may hold values from -0.125 to 0.125
Outputs:
- result_pair: bfloat16 [2, 2, 2048, 512], P('section', None, 'seq')
- stu_maps_grad: float32 [26112, 512], P(('section', 'seq'))
- attn_proj_grad: float32 [1536, 512], P(('section', 'seq'))
- attn_out_grad: float32 [512, 512], P(('section', 'seq'))
- norm_gains_grad: float32 [2, 2, 512], P('section', None, 'seq')
- mlp_gate_grad: float32 [2, 512, 2048], P('section', 'seq')
- mlp_up_grad: float32 [2, 512, 2048], P('section', 'seq')
- mlp_down_grad: float32 [2, 2048, 512], P('section', 'seq')
The draws below stay inside these ranges and needn't reach their ends.
Inputs may be any that keep to these rules, and one draw needn't show every extreme that they name: `lengths`: valid length of each micro-batch's sequence; at least one equals 2048.
All inputs are finite; a program needn't handle non-finite values.
Results may differ from the reference program's by a relative error of at most 0.035.
Values may be sent and summed in bfloat16 or wider, within the bound.
A program may use at most 384 MiB of HBM per device.

```python
from functools import partial
import jax
import jax.numpy as jnp
from jax import lax

D = 512
FF = 2048
K = 24
ORDER = 3
HEAD_DIM = 64
WINDOW = 512
MB = 2
HEADS = 8
SLOTS = 2048
N_FREQ = 4096


def draw_lengths(key, part):
    key = jax.random.fold_in(key, 11)
    pick_key, value_key = jax.random.split(key)
    drawn = jax.random.randint(value_key, (MB,), SLOTS // 2, SLOTS + 1)
    chosen = jax.random.randint(pick_key, (), 0, MB)
    return jnp.where(jnp.arange(MB) == chosen, SLOTS, drawn).astype(jnp.int32)


def block_scale(stream_key, extent, shards, smallest, top_value):
    def one(axis_at, parts):
        draws = jax.random.uniform(jax.random.fold_in(jax.random.fold_in(stream_key, 6), axis_at), (parts,), jnp.float32, smallest / len(shards), top_value / len(shards))
        return jnp.repeat(jnp.exp(draws), extent[axis_at] // parts).reshape((-1,) + (1,) * (len(extent) - axis_at - 1))

    loudness = one(*shards[0])
    for cut in shards[1:]:
        loudness = loudness * one(*cut)
    return loudness


def bell_draw(key, extent, deviation, most, shards=(), kind=jnp.bfloat16):
    values = deviation * jax.random.normal(key, extent, jnp.float32)
    if shards:
        values = values * block_scale(key, extent, shards, -0.22, 0.18)
    return jnp.clip(values, -most, most).astype(kind)


def setup_inputs(seed: int = 0) -> dict:
    arg_keys = jax.random.split(jax.random.key(seed), 11)
    return {
        "io_pair": bell_draw(arg_keys[0], (2, MB, SLOTS, D), 1.0, 6.0, ((0, 2), (2, 16))),
        "lengths": draw_lengths(jax.random.fold_in(arg_keys[10], 71), 0),
        "filters": bell_draw(arg_keys[2], (SLOTS, K), SLOTS ** -0.5, 0.125, ((0, 16),)),
        "stu_maps": bell_draw(arg_keys[3], ((2 * K + ORDER) * D, D), ((2 * K + ORDER) * D) ** -0.5, 0.0390625, ((0, 32),)),
        "attn_proj": bell_draw(arg_keys[4], (3 * D, D), D ** -0.5, 0.25, ((0, 32),)),
        "attn_out": bell_draw(arg_keys[5], (D, D), (D // 64) ** -0.5, 2.0, ((0, 32),)),
        "norm_gains": jnp.clip(1.0 + 0.1 * jax.random.normal(arg_keys[6], (2, 2, D), jnp.float32), 0.5, 1.5).astype(jnp.bfloat16),
        "mlp_gate": bell_draw(arg_keys[7], (2, D, FF), D ** -0.5, 0.25, ((0, 2), (1, 16))),
        "mlp_up": bell_draw(arg_keys[8], (2, D, FF), D ** -0.5, 0.25, ((0, 2), (1, 16))),
        "mlp_down": bell_draw(arg_keys[9], (2, FF, D), FF ** -0.5, 0.125, ((0, 2), (1, 16))),
    }


EPSILON = 1e-05
BIG_NEGATIVE = -1e+30

@jax.custom_vjp
def low(v):
    return lax.optimization_barrier(v.astype(jnp.bfloat16)).astype(jnp.float32)

@jax.custom_vjp
def low_back(v):
    return v

def low_keep(v):
    return (low(v), None)

def low_pass(kept, grad):
    return (grad,)

def back_keep(v):
    return (v, None)

def back_low(kept, grad):
    return (low(grad),)
low.defvjp(low_keep, low_pass)
low_back.defvjp(back_keep, back_low)

def exact(left, right):
    return jnp.dot(left, right, precision=lax.Precision.HIGHEST, preferred_element_type=jnp.float32)

def rms_norm(values, weights):
    return values * lax.rsqrt(lax.optimization_barrier(jnp.mean(values * values, axis=-1, keepdims=True)) + EPSILON) * weights

def feed_forward(middle, gain, w_gate, w_up, w_down):
    inputs = low(rms_norm(middle, gain))
    gate_rows = low_back(exact(inputs, w_gate))
    up_rows = low_back(exact(inputs, w_up))
    active = low(jax.nn.silu(gate_rows) * up_rows)
    return low_back(exact(active, w_down))

def spectral_layer(hidden, stu_weights, spectra_real, spectra_imag, gains, w_gate, w_up, w_down, valid_rows):
    signal = low(rms_norm(hidden, gains[0]))
    spectrum = jnp.fft.fft(signal, n=N_FREQ, axis=0)
    block_rows = min(1024, N_FREQ)
    block_count = N_FREQ // block_rows
    filter_count = spectra_real.shape[1]

    def one_block(pieces):
        u_real, u_imag, f_real, f_imag = pieces
        a_real = f_real[:, :, None] * u_real[:, None, :] - f_imag[:, :, None] * u_imag[:, None, :]
        a_imag = f_real[:, :, None] * u_imag[:, None, :] + f_imag[:, :, None] * u_real[:, None, :]
        a_real = low(a_real.reshape(block_rows, filter_count * D))
        a_imag = low(a_imag.reshape(block_rows, filter_count * D))
        return (low_back(exact(a_real, stu_weights)), low_back(exact(a_imag, stu_weights)))
    pieces = (jnp.real(spectrum).reshape(block_count, block_rows, D), jnp.imag(spectrum).reshape(block_count, block_rows, D), spectra_real.reshape(block_count, block_rows, filter_count), spectra_imag.reshape(block_count, block_rows, filter_count))
    out_real, out_imag = lax.map(jax.checkpoint(one_block), pieces)
    joined = out_real.reshape(N_FREQ, D) + 1j * out_imag.reshape(N_FREQ, D)
    convolved = jnp.real(jnp.fft.ifft(joined, axis=0))[:SLOTS]
    middle = hidden + convolved
    return valid_rows * (middle + feed_forward(middle, gains[1], w_gate, w_up, w_down))

def window_layer(passed, proj_weights, out_weights, gains, w_gate, w_up, w_down, valid_rows):
    inputs = low(rms_norm(passed, gains[0]))
    triple = proj_weights.reshape(3, D, D)
    query_rows = low_back(low(exact(inputs, triple[0])))
    key_rows = low_back(low(exact(inputs, triple[1])))
    value_rows = low_back(low(exact(inputs, triple[2])))
    padding = jnp.zeros((WINDOW, D), jnp.float32)
    key_padded = jnp.concatenate([padding, key_rows], 0)
    value_padded = jnp.concatenate([padding, value_rows], 0)
    score_scale = HEAD_DIM ** (-0.5)

    def one_block(block_number):
        first_row = block_number * WINDOW
        queries = lax.dynamic_slice_in_dim(query_rows, first_row, WINDOW, 0).reshape(WINDOW, HEADS, HEAD_DIM)
        key_block = lax.dynamic_slice_in_dim(key_padded, first_row, 2 * WINDOW, 0).reshape(2 * WINDOW, HEADS, HEAD_DIM)
        value_block = lax.dynamic_slice_in_dim(value_padded, first_row, 2 * WINDOW, 0).reshape(2 * WINDOW, HEADS, HEAD_DIM)
        scores = low_back(jnp.einsum('qhe,khe->hqk', queries, key_block, precision=lax.Precision.HIGHEST) * score_scale)
        query_place = first_row + jnp.arange(WINDOW, dtype=jnp.int32)
        key_place = first_row - WINDOW + jnp.arange(2 * WINDOW, dtype=jnp.int32)
        distance = query_place[:, None] - key_place[None, :]
        allowed = (key_place[None, :] >= 0) & (distance >= 0) & (distance < WINDOW)
        scores = jnp.where(allowed[None], scores, BIG_NEGATIVE)
        highest = lax.optimization_barrier(jnp.max(scores, axis=-1, keepdims=True))
        weights = jnp.exp(scores - highest)
        weights = weights / lax.optimization_barrier(jnp.sum(weights, axis=-1, keepdims=True))
        attended = jnp.einsum('hqk,khe->qhe', low(weights), value_block, precision=lax.Precision.HIGHEST)
        return low_back(low(attended.reshape(WINDOW, D)))
    attended = lax.map(jax.checkpoint(one_block), jnp.arange(SLOTS // WINDOW, dtype=jnp.int32)).reshape(SLOTS, D)
    middle = passed + low_back(exact(attended, out_weights))
    return valid_rows * (middle + feed_forward(middle, gains[1], w_gate, w_up, w_down))

def two_layers(inputs, stu_weights, proj_weights, out_weights, gain_weights, gate_weights, up_weights, down_weights, valid_rows, spectra_real, spectra_imag):
    hidden = valid_rows * inputs
    first_out = spectral_layer(hidden, stu_weights, spectra_real, spectra_imag, gain_weights[0], gate_weights[0], up_weights[0], down_weights[0], valid_rows)
    passed = low_back(low(first_out))
    return window_layer(passed, proj_weights, out_weights, gain_weights[1], gate_weights[1], up_weights[1], down_weights[1], valid_rows)

def reference(io_pair, lengths, filters, stu_maps, attn_proj, attn_out, norm_gains, mlp_gate, mlp_up, mlp_down):
    positions = jnp.arange(SLOTS, dtype=jnp.int32)
    filter_rows = filters.astype(jnp.float32)
    alternate = (1 - 2 * (positions % 2)).astype(jnp.float32)
    impulses = (positions[:, None] == jnp.arange(ORDER, dtype=jnp.int32)[None, :]).astype(jnp.float32)
    every_filter = jnp.concatenate([filter_rows, filter_rows * alternate[:, None], impulses], 1)
    spectra = jnp.fft.fft(every_filter, n=N_FREQ, axis=0)
    spectra_real = jnp.real(spectra)
    spectra_imag = jnp.imag(spectra)
    params = (stu_maps.astype(jnp.float32), attn_proj.astype(jnp.float32), attn_out.astype(jnp.float32), norm_gains.astype(jnp.float32), mlp_gate.astype(jnp.float32), mlp_up.astype(jnp.float32), mlp_down.astype(jnp.float32))
    totals = [jnp.zeros_like(weight_item) for weight_item in params]
    input_grads = []
    outputs = []
    for batch_index in range(MB):
        valid_rows = (positions < lengths[batch_index]).astype(jnp.float32)[:, None]
        forward = partial(two_layers, valid_rows=valid_rows, spectra_real=spectra_real, spectra_imag=spectra_imag)
        result, pullback = jax.vjp(forward, io_pair[0, batch_index].astype(jnp.float32), *params)
        gradients = pullback(io_pair[1, batch_index].astype(jnp.float32))
        input_grads.append(gradients[0].astype(jnp.bfloat16))
        outputs.append(result.astype(jnp.bfloat16))
        totals = [running + fresh for running, fresh in zip(totals, gradients[1:])]
    result_pair = jnp.stack([jnp.stack(input_grads), jnp.stack(outputs)])
    return (result_pair, totals[0], totals[1], totals[2], totals[3], totals[4], totals[5], totals[6])
```

```python
import functools
import math

import jax
import jax.numpy as jnp
from jax import lax
from jax.experimental import pallas as pl
from jax.experimental.pallas import tpu as pltpu
from jax.sharding import PartitionSpec as P

ORDER = 3
HEAD_DIM = 64
WINDOW = 512
EPSILON = 1e-05
BIG_NEGATIVE = -1e30
MESH = pl.DeviceIdType.MESH
BF = jnp.bfloat16
F32 = jnp.float32
LANES = 128
BLOCK = 256
PIECE = 16
VMEM_LIMIT = 60 * 1024 * 1024


class Plan:
    def __init__(self, chips, tok_rows, width, filter_count, map_rows):
        self.chips = chips
        self.rows = tok_rows
        self.half = tok_rows // 2
        self.width = width
        self.filters = filter_count
        self.cols_in = 4
        self.cols_out = max(1, math.isqrt(chips // 4))
        self.groups = chips // (self.cols_in * self.cols_out)
        self.local = filter_count // self.groups
        self.length = chips * self.half
        self.blocks = self.length // BLOCK
        self.jb = width // self.cols_in
        self.ia = width // self.cols_out
        self.map_rows = map_rows
        self.routed = map_rows % PIECE == 0
        self.pieces = map_rows // PIECE
        self.f_rows = -(-self.local // 16) * 16


def spot():
    return lax.axis_index("section"), lax.axis_index("seq")


def greet_everyone(chips):
    section, chip = spot()
    me = section * chips + chip
    barrier = pltpu.get_barrier_semaphore()

    def one(step, carry):
        peer = lax.rem(me + step, 2 * chips)
        pl.semaphore_signal(
            barrier, inc=1, device_id=(peer // chips, lax.rem(peer, chips)), device_id_type=MESH
        )
        return carry

    lax.fori_loop(1, 2 * chips, one, 0)
    pl.semaphore_wait(barrier, 2 * chips - 1)


def push(src, dst, send, recv, target):
    return pltpu.make_async_remote_copy(
        src_ref=src,
        dst_ref=dst,
        send_sem=send,
        recv_sem=recv,
        device_id=target,
        device_id_type=MESH,
    )


def bytes_of(ref, sem):
    pltpu.make_async_copy(ref, ref, sem).wait()


def entry_kernel(chips, count, *refs):
    given = refs[:count]
    gains = refs[count]
    taken = refs[count + 1 : 2 * count + 1]
    gains_all = refs[2 * count + 1]
    send, recv, gain_send, gain_recv = refs[2 * count + 2 :]
    section, chip = spot()
    me = section * chips + chip
    greet_everyone(chips)
    copies = [
        push(given[i], taken[i], send.at[i], recv.at[i], (1 - section, chip)) for i in range(count)
    ]
    for copy in copies[:1]:
        copy.start()

    def one(step, carry):
        peer = lax.rem(me + step, 2 * chips)
        push(
            gains,
            gains_all.at[section, chip],
            gain_send,
            gain_recv,
            (peer // chips, lax.rem(peer, chips)),
        ).start()
        return carry

    lax.fori_loop(1, 2 * chips, one, 0)
    pltpu.make_async_copy(gains, gains_all.at[section, chip], gain_recv).start()
    for copy in copies[1:]:
        copy.start()
    bytes_of(gains_all, gain_recv)

    def drain(step, carry):
        push(gains, gains_all.at[section, chip], gain_send, gain_recv, (section, chip)).wait_send()
        return carry

    lax.fori_loop(1, 2 * chips, drain, 0)
    for copy in copies:
        copy.wait()


def entry_call(chips, arrays, gains):
    count = len(arrays)
    any_spec = pl.BlockSpec(memory_space=pl.ANY)
    return pl.pallas_call(
        functools.partial(entry_kernel, chips, count),
        out_shape=[jax.ShapeDtypeStruct(a.shape, a.dtype) for a in arrays]
        + [jax.ShapeDtypeStruct((2, chips) + gains.shape, gains.dtype)],
        in_specs=[any_spec] * (count + 1),
        out_specs=[any_spec] * (count + 1),
        scratch_shapes=[
            pltpu.SemaphoreType.DMA((count,)),
            pltpu.SemaphoreType.DMA((count,)),
            pltpu.SemaphoreType.DMA,
            pltpu.SemaphoreType.DMA,
        ],
        compiler_params=pltpu.CompilerParams(collective_id=1, has_side_effects=True),
        name="entry",
    )(*arrays, gains)


def exit_kernel(chips, give, tiles, take, land, send, recv, gain_send, gain_recv):
    section, chip = spot()
    me = section * chips + chip
    greet_everyone(chips)
    swap = push(give, take, send, recv, (1 - section, chip))
    swap.start()

    def one(step, carry):
        peer = lax.rem(me + step, 2 * chips)
        push(
            tiles.at[peer],
            land.at[me],
            gain_send,
            gain_recv,
            (peer // chips, lax.rem(peer, chips)),
        ).start()
        return carry

    lax.fori_loop(1, 2 * chips, one, 0)
    pltpu.make_async_copy(tiles.at[me], land.at[me], gain_recv).start()
    bytes_of(land, gain_recv)
    bytes_of(land.at[pl.ds(0, 2 * chips - 1)], gain_send)
    swap.wait()


def exit_call(chips, give, tiles):
    any_spec = pl.BlockSpec(memory_space=pl.ANY)
    return pl.pallas_call(
        functools.partial(exit_kernel, chips),
        out_shape=[
            jax.ShapeDtypeStruct(give.shape, give.dtype),
            jax.ShapeDtypeStruct(tiles.shape, tiles.dtype),
        ],
        in_specs=[any_spec] * 2,
        out_specs=[any_spec] * 2,
        scratch_shapes=[
            pltpu.SemaphoreType.DMA,
            pltpu.SemaphoreType.DMA,
            pltpu.SemaphoreType.DMA,
            pltpu.SemaphoreType.DMA,
        ],
        compiler_params=pltpu.CompilerParams(collective_id=4, has_side_effects=True),
        name="leave",
    )(give, tiles)


def filter_rows(plan, land, table, first_row, backward):
    lane = lax.broadcasted_iota(jnp.int32, (plan.f_rows, LANES), 1)
    low = lane < plan.half
    total = plan.length // LANES
    for m in range(total):
        if backward:
            one, two = 2 * m, 2 * m + 1
        else:
            one, two = plan.chips - 1 - 2 * m, plan.chips - 2 - 2 * m
        left = land[one, first_row : first_row + plan.f_rows, :].astype(F32)
        right = land[two, first_row : first_row + plan.f_rows, :].astype(F32)
        even = jnp.where(low, left, pltpu.roll(right, plan.half, 1))
        odd = jnp.where(low, pltpu.roll(left, plan.half, 1), right)
        at = LANES * m + (BLOCK if backward else 0)
        table[0, :, at : at + LANES] = even
        table[1, :, at : at + LANES] = odd
    blank = jnp.zeros((plan.f_rows, BLOCK), F32)
    at = 0 if backward else plan.length
    for parity in range(2):
        table[parity, :, at : at + BLOCK] = blank


def build_strips(plan, table, strip, backward):
    span = plan.length + BLOCK
    shift = span - LANES if backward else span - (LANES - 1)
    part = 32

    def one(k, carry):
        for parity in range(2):
            row = table[parity, pl.ds(k, 1), :]
            for start in range(0, LANES, part):
                spread = jnp.broadcast_to(row, (part, span))
                rolled = pltpu.roll(
                    spread, (shift + start) % span, 1, stride=1, stride_axis=0
                ).astype(BF)
                strip[2 * k + parity, LANES + start : LANES + start + part, :] = rolled[
                    :, : plan.length
                ]
                strip[2 * k + parity, start : start + part, :] = rolled[
                    :, LANES : LANES + plan.length
                ]
        return carry

    lax.fori_loop(0, plan.local, one, 0)


def owner_pieces(plan, act):
    section, chip = spot()
    dev = section * plan.chips + chip
    per_map = plan.width // PIECE
    per_block = plan.jb // PIECE

    def unit(m, carry):
        g = plan.pieces * dev + m
        which = g // per_map
        inside = lax.rem(g, per_map)
        b = inside // per_block
        sub = lax.rem(inside, per_block)
        sign = which // plan.filters
        full = lax.rem(which, plan.filters)
        group = full // plan.local
        k = lax.rem(full, plan.local)

        @pl.when(sign < 2)
        def _():
            for a in range(plan.cols_out):
                target = a + plan.cols_out * (b + plan.cols_in * group)
                act(m, False, k, sub, a, sign, target)

        @pl.when(sign >= 2)
        def _():
            for a in range(plan.cols_out):
                for core in range(2):
                    act(m, True, full, sub, a, core, a + plan.cols_out * b)

        return carry

    lax.fori_loop(0, plan.pieces, unit, 0)


def forward_kernel(plan, *refs):
    if plan.routed:
        u_ref, f_ref, maps_ref = refs[:3]
        rest = refs[3:]
    else:
        u_ref, f_ref, mine_ref, other_ref, taps_ref = refs[:5]
        rest = refs[5:]
    (
        conv_ref,
        v_ref,
        pq_ref,
        tapw_ref,
        x_ref,
        xs_ref,
        filt_ref,
        x_buf,
        xo_buf,
        xs_buf,
        xf_buf,
        f_land,
        table,
        strip,
        mine,
        other,
        taps,
        pq,
        acc,
        y_buf,
        land,
        stage,
        u_send,
        x_recv,
        f_send,
        f_recv,
        m_send,
        m_recv,
        t_recv,
        o_send,
        o_recv,
        c_send,
        c_recv,
        v_sem,
        out_sem,
    ) = rest
    chips, half, jb, ia = plan.chips, plan.half, plan.jb, plan.ia
    section, chip = spot()
    dev = section * chips + chip
    my_group = chip // (plan.cols_out * plan.cols_in)
    greet_everyone(chips)

    def send_u(step, carry):
        peer = lax.rem(chip + step, chips)
        b = lax.rem(peer // plan.cols_out, plan.cols_in)
        group = peer // (plan.cols_out * plan.cols_in)
        push(
            u_ref.at[b],
            x_buf.at[pl.ds(half * chip, half), :],
            u_send,
            x_recv,
            (section, peer),
        ).start()
        push(f_ref.at[group], f_land.at[chip], f_send, f_recv, (section, peer)).start()
        return carry

    lax.fori_loop(1, chips, send_u, 0)
    pltpu.make_async_copy(
        u_ref.at[lax.rem(chip // plan.cols_out, plan.cols_in)],
        x_buf.at[pl.ds(half * chip, half), :],
        x_recv,
    ).start()
    pltpu.make_async_copy(f_ref.at[my_group], f_land.at[chip], f_recv).start()

    if plan.routed:

        def places(m, tap, k, sub, a):
            src = maps_ref.at[pl.ds(PIECE * m, PIECE), pl.ds(a * ia, ia)]
            if tap:
                return src, taps.at[pl.ds(jb * k + PIECE * sub, PIECE), :], t_recv
            return src, mine.at[k, pl.ds(PIECE * sub, PIECE), :], m_recv

        def start_piece(m, tap, k, sub, a, to_section, to_chip):
            src, dst, sem = places(m, tap, k, sub, a)
            here = to_section * chips + to_chip == dev

            @pl.when(here)
            def _():
                pltpu.make_async_copy(src, dst, sem).start()

            @pl.when(jnp.logical_not(here))
            def _():
                push(src, dst, m_send, sem, (to_section, to_chip)).start()

        def drain_piece(m, tap, k, sub, a, to_section, to_chip):
            src, dst, sem = places(m, tap, k, sub, a)

            @pl.when(to_section * chips + to_chip != dev)
            def _():
                push(src, dst, m_send, sem, (to_section, to_chip)).wait_send()

        owner_pieces(plan, start_piece)

    bytes_of(f_land, f_recv)
    filter_rows(plan, f_land, table, 0, False)
    build_strips(plan, table, strip, False)
    filt_out = pltpu.make_async_copy(f_land, filt_ref, out_sem.at[0])
    filt_out.start()

    if plan.routed:
        bytes_of(mine, m_recv)
        swap = push(mine, other, o_send, o_recv, (1 - section, chip))
        swap.start()

        @pl.when(my_group == 0)
        def _():
            bytes_of(taps, t_recv)

        @pl.when(my_group != 0)
        def _():
            taps[...] = jnp.zeros_like(taps)
    else:
        for src, dst in ((mine_ref, mine), (other_ref, other), (taps_ref, taps)):
            pltpu.sync_copy(src, dst)

    bytes_of(x_buf, x_recv)
    x_out = pltpu.make_async_copy(x_buf, x_ref, out_sem.at[1])
    x_out.start()
    xf_buf[0:8, :] = jnp.zeros((8, 2 * jb), F32)
    for i in range(plan.blocks):
        rows = slice(BLOCK * i, BLOCK * (i + 1))
        xf_buf[8 + BLOCK * i : 8 + BLOCK * (i + 1), :] = x_buf[rows, :].astype(F32)
    for i in range(plan.blocks):
        rows = slice(BLOCK * i, BLOCK * (i + 1))
        moved = xf_buf[7 + BLOCK * i : 7 + BLOCK * (i + 1), :].astype(BF)
        xs_buf[rows, :] = moved
        xo_buf[rows, :jb] = x_buf[rows, :jb]
        xo_buf[rows, jb:] = moved[:, jb:]
    xs_out = pltpu.make_async_copy(xs_buf, xs_ref, out_sem.at[2])
    xs_out.start()

    if plan.routed:
        swap.wait()
    turn = (1 - 2 * section).astype(F32)

    def mix(k, carry):
        first = mine[k].astype(F32)
        second = other[k].astype(F32)
        pq[k, :jb, :] = (first + second).astype(BF)
        pq[k, jb:, :] = ((first - second) * turn).astype(BF)
        return carry

    lax.fori_loop(0, plan.local, mix, 0)
    pq_out = pltpu.make_async_copy(pq, pq_ref, out_sem.at[3])
    pq_out.start()
    taps_out = pltpu.make_async_copy(taps, tapw_ref, out_sem.at[4])
    taps_out.start()

    for i in range(plan.blocks):
        rows = slice(BLOCK * i, BLOCK * (i + 1))
        depth = BLOCK * (i + 1)
        offset = plan.length - depth
        x_now = x_buf[rows, :]
        s_now = xs_buf[rows, :]
        acc[0] = jnp.dot(
            jnp.concatenate([x_now[:, :jb], s_now[:, jb:]], 1),
            taps[: 2 * jb, :],
            preferred_element_type=F32,
        ) + jnp.dot(s_now[:, :jb], taps[2 * jb :, :], preferred_element_type=F32)
        acc[1] = jnp.dot(
            jnp.concatenate([x_now[:, jb:], x_now[:, :jb]], 1),
            taps[: 2 * jb, :],
            preferred_element_type=F32,
        ) + jnp.dot(s_now[:, jb:], taps[2 * jb :, :], preferred_element_type=F32)

        def step(k, carry, i=i, depth=depth, offset=offset):
            slot = lax.rem(k, 2)
            v_copy = pltpu.make_async_copy(
                stage.at[slot], v_ref.at[k, :, pl.ds(BLOCK * i, BLOCK), :], v_sem.at[slot]
            )
            even = jnp.dot(
                strip[2 * k, :, offset:], x_buf[:depth, :], preferred_element_type=F32
            ).astype(BF)
            odd = jnp.dot(
                strip[2 * k + 1, :, offset:], xo_buf[:depth, :], preferred_element_type=F32
            ).astype(BF)
            first = jnp.concatenate([even[:, :jb], odd[:, jb:]], 1)
            second = jnp.concatenate([even[:, jb:], odd[:, :jb]], 1)
            if i == 0:
                pl.when(k >= 2)(v_copy.wait)
            else:
                v_copy.wait()
            stage[slot, 0] = first
            stage[slot, 1] = second
            v_copy.start()
            acc[0] += jnp.dot(first, pq[k], preferred_element_type=F32)
            acc[1] += jnp.dot(second, pq[k], preferred_element_type=F32)
            return carry

        lax.fori_loop(0, plan.local, step, 0)
        y_buf[0, rows, :] = acc[0].astype(BF)
        y_buf[1, rows, :] = acc[1].astype(BF)

        def give(r, carry, i=i):
            peer = BLOCK // half * i + r
            src = y_buf.at[:, pl.ds(half * peer, half), :]

            @pl.when(peer == chip)
            def _():
                pltpu.make_async_copy(src, land.at[chip], c_recv).start()

            @pl.when(peer != chip)
            def _():
                push(src, land.at[chip], c_send, c_recv, (section, peer)).start()

            return carry

        lax.fori_loop(0, BLOCK // half, give, 0)

    for slot in range(2):
        pltpu.make_async_copy(
            stage.at[slot], v_ref.at[slot, :, pl.ds(0, BLOCK), :], v_sem.at[slot]
        ).wait()
    bytes_of(x_buf.at[pl.ds(0, half * (chips - 1)), :], u_send)
    bytes_of(f_land.at[pl.ds(0, chips - 1)], f_send)
    if plan.routed:
        owner_pieces(plan, drain_piece)
    for copy in (filt_out, x_out, xs_out, pq_out, taps_out):
        copy.wait()
    bytes_of(land, c_recv)
    for a in range(plan.cols_out):
        total = None
        for other_part in range(plan.cols_in * plan.groups):
            term = land[a + plan.cols_out * other_part].astype(F32)
            total = term if total is None else total + term
        conv_ref[:, :, a * ia : (a + 1) * ia] = total
    bytes_of(land.at[pl.ds(0, chips - 1)], c_send)


def forward_call(plan, u, packed, maps):
    chips, half, jb, ia = plan.chips, plan.half, plan.jb, plan.ia
    any_spec = pl.BlockSpec(memory_space=pl.ANY)
    vmem_spec = pl.BlockSpec(memory_space=pltpu.VMEM)
    dma = pltpu.SemaphoreType.DMA
    shapes = [
        ((2, half, plan.width), F32),
        ((plan.local, 2, plan.length, 2 * jb), BF),
        ((plan.local, 2 * jb, ia), BF),
        ((ORDER * jb, ia), BF),
        ((plan.length, 2 * jb), BF),
        ((plan.length, 2 * jb), BF),
        ((chips, 2 * plan.f_rows, LANES), BF),
    ]
    return pl.pallas_call(
        functools.partial(forward_kernel, plan),
        out_shape=[jax.ShapeDtypeStruct(s, d) for s, d in shapes],
        in_specs=[vmem_spec] * 2 + [any_spec] * len(maps),
        out_specs=[vmem_spec] + [any_spec] * 6,
        scratch_shapes=[
            pltpu.VMEM((plan.length, 2 * jb), BF),
            pltpu.VMEM((plan.length, 2 * jb), BF),
            pltpu.VMEM((plan.length, 2 * jb), BF),
            pltpu.VMEM((plan.length + 8, 2 * jb), F32),
            pltpu.VMEM((chips, 2 * plan.f_rows, LANES), BF),
            pltpu.VMEM((2, plan.f_rows, plan.length + BLOCK), F32),
            pltpu.VMEM((2 * plan.local, BLOCK, plan.length), BF),
            pltpu.VMEM((plan.local, jb, ia), BF),
            pltpu.VMEM((plan.local, jb, ia), BF),
            pltpu.VMEM((ORDER * jb, ia), BF),
            pltpu.VMEM((plan.local, 2 * jb, ia), BF),
            pltpu.VMEM((2, BLOCK, ia), F32),
            pltpu.VMEM((2, plan.length, ia), BF),
            pltpu.VMEM((chips, 2, half, ia), BF),
            pltpu.VMEM((2, 2, BLOCK, 2 * jb), BF),
        ]
        + [dma] * 11
        + [dma((2,)), dma((5,))],
        compiler_params=pltpu.CompilerParams(
            collective_id=2, has_side_effects=True, vmem_limit_bytes=VMEM_LIMIT
        ),
        name="spectral_forward",
    )(u, packed, *maps)


def backward_kernel(plan, *refs):
    g_ref, filt_ref, v_ref, pq, tapw, x_buf, xs_buf, du_ref = refs[:8]
    if plan.routed:
        dmaps_ref = refs[8]
        rest = refs[9:]
    else:
        dmap_ref, dtap_ref = refs[8:10]
        rest = refs[10:]
    (
        g_buf,
        gt_buf,
        table,
        strip,
        v_buf,
        z_even,
        z_odd,
        acc_even,
        acc_odd,
        kept,
        give_m,
        take_m,
        total_m,
        kept_t,
        give_t,
        take_t,
        total_t,
        du_buf,
        land,
        g_send,
        g_recv,
        v_sem,
        m_send,
        m_recv,
        t_send,
        t_recv,
        w_send,
        w_recv,
        d_send,
        d_recv,
    ) = rest
    chips, half, jb, ia = plan.chips, plan.half, plan.jb, plan.ia
    section, chip = spot()
    dev = section * chips + chip
    my_a = lax.rem(chip, plan.cols_out)
    my_b = lax.rem(chip // plan.cols_out, plan.cols_in)
    my_group = chip // (plan.cols_out * plan.cols_in)
    greet_everyone(chips)

    def send_g(step, carry):
        peer = lax.rem(chip + step, chips)
        a = lax.rem(peer, plan.cols_out)
        push(
            g_ref.at[:, :, pl.ds(pl.multiple_of(a * ia, ia), ia)],
            g_buf.at[:, pl.ds(half * chip, half), :],
            g_send,
            g_recv,
            (section, peer),
        ).start()
        return carry

    lax.fori_loop(1, chips, send_g, 0)
    pltpu.make_async_copy(
        g_ref.at[:, :, pl.ds(pl.multiple_of(my_a * ia, ia), ia)],
        g_buf.at[:, pl.ds(half * chip, half), :],
        g_recv,
    ).start()
    v_copy = [pltpu.make_async_copy(v_ref.at[k], v_buf.at[k], v_sem.at[k]) for k in range(2)]
    for copy in v_copy:
        copy.start()
    filter_rows(plan, filt_ref, table, plan.f_rows, True)
    build_strips(plan, table, strip, True)
    acc_even[...] = jnp.zeros_like(acc_even)
    acc_odd[...] = jnp.zeros_like(acc_odd)
    bytes_of(g_buf, g_recv)
    for phase in range(2):
        for i in range(plan.blocks):
            rows = slice(BLOCK * i, BLOCK * (i + 1))
            gt_buf[phase, :, rows] = g_buf[phase, rows, :].astype(F32).T.astype(BF)
    turn = (1 - 2 * section).astype(F32)
    half_ways = (((1,), (1,)), ((), ()))

    def piece_of(k, tap, sub):
        per_map = plan.width // PIECE
        which = 2 * plan.filters + k if tap else section * plan.filters + my_group * plan.local + k
        g = which * per_map + my_b * (plan.jb // PIECE) + sub
        return g // plan.pieces, lax.rem(g, plan.pieces)

    def piece_copies(k, tap, begin):
        def one(sub, carry):
            owner, row = piece_of(k, tap, sub)
            src = (
                total_t.at[pl.ds(jb * k + PIECE * sub, PIECE), :]
                if tap
                else total_m.at[k, pl.ds(PIECE * sub, PIECE), :]
            )
            dst = dmaps_ref.at[
                pl.ds(PIECE * row, PIECE), pl.ds(pl.multiple_of(my_a * ia, ia), ia)
            ]
            if begin:

                @pl.when(owner == dev)
                def _():
                    pltpu.make_async_copy(src, dst, w_recv).start()

            @pl.when(owner != dev)
            def _():
                copy = push(src, dst, w_send, w_recv, (owner // chips, lax.rem(owner, chips)))
                if begin:
                    copy.start()
                else:
                    copy.wait_send()

            return carry

        lax.fori_loop(0, plan.jb // PIECE, one, 0)

    def exchange(k):
        return push(give_m.at[k], take_m.at[k], m_send.at[k], m_recv.at[k], (1 - section, chip))

    def finish(k):
        exchange(k).wait()
        total_m[k] = (kept[k] + take_m[k].astype(F32)).astype(BF)
        if plan.routed:
            piece_copies(k, False, True)

    x_even, x_odd = x_buf[:, :jb], x_buf[:, jb:]
    s_even, s_odd = xs_buf[:, :jb], xs_buf[:, jb:]
    for tap, (on_even, on_odd) in enumerate(((x_even, x_odd), (s_odd, x_even), (s_even, s_odd))):
        tap_grad = jnp.dot(gt_buf[0], on_even, preferred_element_type=F32) + jnp.dot(
            gt_buf[1], on_odd, preferred_element_type=F32
        )
        tap_grad = tap_grad.T
        kept_t[tap * jb : (tap + 1) * jb, :] = tap_grad
        give_t[tap * jb : (tap + 1) * jb, :] = tap_grad.astype(BF)
    tap_swap = push(give_t, take_t, t_send, t_recv, (1 - section, chip))
    tap_swap.start()
    for i in range(plan.blocks):
        rows = slice(BLOCK * i, BLOCK * (i + 1))
        from_even = lax.dot_general(
            g_buf[0, rows, :], tapw[...], half_ways, preferred_element_type=F32
        )
        from_odd = lax.dot_general(
            g_buf[1, rows, :], tapw[...], half_ways, preferred_element_type=F32
        )
        acc_even[rows, :jb] = from_even[:, :jb] + from_odd[:, jb : 2 * jb]
        acc_even[rows, jb : 2 * jb] = from_odd[:, :jb]
        acc_odd[rows, :jb] = from_even[:, 2 * jb :]
        acc_odd[rows, jb : 2 * jb] = from_even[:, jb : 2 * jb] + from_odd[:, 2 * jb :]

    def step(k, carry):
        slot = lax.rem(k, 2)
        for i in range(plan.blocks):
            rows = slice(BLOCK * i, BLOCK * (i + 1))
            from_even = lax.dot_general(
                g_buf[0, rows, :], pq[k], half_ways, preferred_element_type=F32
            ).astype(BF)
            from_odd = lax.dot_general(
                g_buf[1, rows, :], pq[k], half_ways, preferred_element_type=F32
            ).astype(BF)
            z_even[rows, :jb] = from_even[:, :jb]
            z_even[rows, jb:] = from_odd[:, :jb]
            z_odd[rows, :jb] = from_odd[:, jb:]
            z_odd[rows, jb:] = from_even[:, jb:]
        pltpu.make_async_copy(v_ref.at[k], v_buf.at[slot], v_sem.at[slot]).wait()
        grad = jnp.dot(gt_buf[0], v_buf[slot, 0], preferred_element_type=F32) + jnp.dot(
            gt_buf[1], v_buf[slot, 1], preferred_element_type=F32
        )
        grad = grad.T
        plus, minus = grad[:jb, :], grad[jb:, :] * turn
        kept[k] = plus + minus
        give_m[k] = (plus - minus).astype(BF)
        exchange(k).start()

        @pl.when(k + 2 < plan.local)
        def _():
            pltpu.make_async_copy(v_ref.at[k + 2], v_buf.at[slot], v_sem.at[slot]).start()

        for j in range(plan.blocks):
            rows = slice(BLOCK * j, BLOCK * (j + 1))
            depth = plan.length - BLOCK * j
            acc_even[rows, :] += jnp.dot(
                strip[2 * k, :, :depth], z_even[BLOCK * j :, :], preferred_element_type=F32
            )
            out = jnp.dot(
                strip[2 * k + 1, :, :depth], z_odd[BLOCK * j :, :], preferred_element_type=F32
            )
            acc_even[rows, :jb] += out[:, :jb]
            acc_odd[rows, jb:] += out[:, jb:]

        @pl.when(k >= 1)
        def _():
            finish(k - 1)

        return carry

    lax.fori_loop(0, plan.local, step, 0)
    for i in range(plan.blocks):
        rows = slice(BLOCK * i, BLOCK * (i + 1))
        moved = acc_odd[BLOCK * i + 1 : BLOCK * (i + 1) + 1, :]
        both = (acc_even[rows, :] + moved).astype(BF)
        du_buf[0, rows, :] = both[:, :jb]
        du_buf[1, rows, :] = both[:, jb:]

        def give(r, carry, i=i):
            peer = BLOCK // half * i + r
            src = du_buf.at[:, pl.ds(half * peer, half), :]

            @pl.when(peer == chip)
            def _():
                pltpu.make_async_copy(src, land.at[chip], d_recv).start()

            @pl.when(peer != chip)
            def _():
                push(src, land.at[chip], d_send, d_recv, (section, peer)).start()

            return carry

        lax.fori_loop(0, BLOCK // half, give, 0)
    finish(plan.local - 1)
    tap_swap.wait()
    total_t[...] = (kept_t[...] + take_t[...].astype(F32)).astype(BF)
    if plan.routed:

        @pl.when(jnp.logical_and(section == 0, my_group == 0))
        def _():
            for tap in range(ORDER):
                piece_copies(tap, True, True)
    else:
        pltpu.sync_copy(total_m, dmap_ref)
        pltpu.sync_copy(total_t, dtap_ref)
    bytes_of(g_buf.at[0, pl.ds(0, 2 * half * (chips - 1) // 2), :], g_send)
    bytes_of(g_buf.at[1, pl.ds(0, 2 * half * (chips - 1) // 2), :], g_send)
    bytes_of(land, d_recv)
    for b in range(plan.cols_in):
        total = None
        for c in range(plan.groups):
            for a in range(plan.cols_out):
                term = land[a + plan.cols_out * (b + plan.cols_in * c)].astype(F32)
                total = term if total is None else total + term
        du_ref[:, :, b * jb : (b + 1) * jb] = total
    bytes_of(land.at[pl.ds(0, chips - 1)], d_send)
    if plan.routed:

        def drain(k, carry):
            piece_copies(k, False, False)
            return carry

        lax.fori_loop(0, plan.local, drain, 0)

        @pl.when(jnp.logical_and(section == 0, my_group == 0))
        def _():
            for tap in range(ORDER):
                piece_copies(tap, True, False)

        bytes_of(dmaps_ref, w_recv)


def backward_call(plan, g, filt, v, pq, tapw, x, xs):
    chips, half, jb, ia = plan.chips, plan.half, plan.jb, plan.ia
    any_spec = pl.BlockSpec(memory_space=pl.ANY)
    vmem_spec = pl.BlockSpec(memory_space=pltpu.VMEM)
    dma = pltpu.SemaphoreType.DMA
    out_shape = [jax.ShapeDtypeStruct((2, half, plan.width), F32)]
    if plan.routed:
        out_shape.append(jax.ShapeDtypeStruct((plan.map_rows, plan.width), BF))
    else:
        out_shape.append(jax.ShapeDtypeStruct((plan.local, jb, ia), BF))
        out_shape.append(jax.ShapeDtypeStruct((ORDER * jb, ia), BF))
    return pl.pallas_call(
        functools.partial(backward_kernel, plan),
        out_shape=out_shape,
        in_specs=[vmem_spec, vmem_spec, any_spec] + [vmem_spec] * 4,
        out_specs=[vmem_spec] + [any_spec] * (len(out_shape) - 1),
        scratch_shapes=[
            pltpu.VMEM((2, plan.length, ia), BF),
            pltpu.VMEM((2, ia, plan.length), BF),
            pltpu.VMEM((2, plan.f_rows, plan.length + BLOCK), F32),
            pltpu.VMEM((2 * plan.local, BLOCK, plan.length), BF),
            pltpu.VMEM((2, 2, plan.length, 2 * jb), BF),
            pltpu.VMEM((plan.length, 2 * jb), BF),
            pltpu.VMEM((plan.length, 2 * jb), BF),
            pltpu.VMEM((plan.length, 2 * jb), F32),
            pltpu.VMEM((plan.length + 8, 2 * jb), F32),
            pltpu.VMEM((plan.local, jb, ia), F32),
            pltpu.VMEM((plan.local, jb, ia), BF),
            pltpu.VMEM((plan.local, jb, ia), BF),
            pltpu.VMEM((plan.local, jb, ia), BF),
            pltpu.VMEM((ORDER * jb, ia), F32),
            pltpu.VMEM((ORDER * jb, ia), BF),
            pltpu.VMEM((ORDER * jb, ia), BF),
            pltpu.VMEM((ORDER * jb, ia), BF),
            pltpu.VMEM((2, plan.length, jb), BF),
            pltpu.VMEM((chips, 2, half, jb), BF),
            dma,
            dma,
            dma((2,)),
            dma((plan.local,)),
            dma((plan.local,)),
            dma,
            dma,
            dma,
            dma,
            dma,
            dma,
        ],
        compiler_params=pltpu.CompilerParams(
            collective_id=3, has_side_effects=True, vmem_limit_bytes=VMEM_LIMIT
        ),
        name="spectral_backward",
    )(g, filt, v, pq, tapw, x, xs)


def swapped(block):
    return lax.ppermute(block, "section", [(0, 1), (1, 0)])


def shifted(block, axis, distance):
    devices = range(lax.axis_size(axis))
    route = [(i - distance, i) for i in devices if i - distance in devices]
    return lax.ppermute(block, axis, route)


def dot(formula, left, right):
    return jnp.einsum(formula, left, right, preferred_element_type=F32)


def norm_forward(values, weights):
    factor = lax.rsqrt(jnp.mean(values * values, axis=-1, keepdims=True) + EPSILON)
    return (values * factor * weights, factor)


def norm_backward(values, factor, weights, upstream):
    weighted = upstream * weights
    gain_grad = jnp.sum(upstream * values * factor, axis=0)
    correction = jnp.mean(weighted * values, axis=-1, keepdims=True)
    return (factor * weighted - values * factor * factor * factor * correction, gain_grad)


def mlp_forward(middle, gain, weights):
    w_gate, w_up, w_down = weights
    rows = middle.shape[0]
    normed, factor = norm_forward(middle, gain)
    own = normed.astype(BF)
    inputs = jnp.concatenate([own, swapped(own)], 0)
    gate_rows = dot("td,df->tf", inputs, w_gate)
    up_rows = dot("td,df->tf", inputs, w_up)
    active = (jax.nn.silu(gate_rows) * up_rows).astype(BF)
    part = dot("tf,fd->td", active, w_down)
    branch = part[:rows] + swapped(part[rows:].astype(BF)).astype(F32)
    return branch, (factor, inputs, gate_rows, up_rows, active)


def mlp_backward(middle, gain, weights, saved, upstream, branch_grad):
    w_gate, w_up, w_down = weights
    rows = middle.shape[0]
    factor, inputs, gate_rows, up_rows, active = saved
    down_grad = dot("tf,td->fd", active, branch_grad)
    active_grad = dot("td,fd->tf", branch_grad, w_down)
    sigmoid = jax.nn.sigmoid(gate_rows)
    slope = sigmoid * (1.0 + gate_rows * (1.0 - sigmoid))
    gate_grad = (active_grad * up_rows * slope).astype(BF)
    up_grad = (active_grad * gate_rows * sigmoid).astype(BF)
    gate_w_grad = dot("td,tf->df", inputs, gate_grad)
    up_w_grad = dot("td,tf->df", inputs, up_grad)
    part = dot("tf,df->td", gate_grad, w_gate) + dot("tf,df->td", up_grad, w_up)
    normed_grad = part[:rows] + swapped(part[rows:].astype(BF)).astype(F32)
    middle_grad, gain_grad = norm_backward(middle, factor, gain, normed_grad)
    return upstream + middle_grad, gain_grad, (gate_w_grad, up_w_grad, down_grad)


def body(
    io_pair, lengths, filters, stu_maps, attn_proj, attn_out, norm_gains, mlp_gate, mlp_up, mlp_down
):
    chips = lax.axis_size("seq")
    section, chip = spot()
    core_zero = section == 0
    tok_rows = io_pair.shape[2]
    width = io_pair.shape[3]
    half = tok_rows // 2
    heads = width // HEAD_DIM
    reach = WINDOW // tok_rows
    score_scale = HEAD_DIM ** (-0.5)
    plan = Plan(chips, tok_rows, width, filters.shape[1], stu_maps.shape[0])

    sib_io, sib_gate, sib_up, sib_down, sib_proj, sib_out, gains_all = entry_call(
        chips,
        [io_pair[0], mlp_gate[0], mlp_up[0], mlp_down[0], attn_proj, attn_out],
        norm_gains[0],
    )
    gains = jnp.transpose(gains_all, (0, 2, 1, 3)).reshape(2, 2, width).astype(F32)

    def split_phases(rows):
        return (
            rows.reshape(rows.shape[:-2] + (half, 2, width))
            .swapaxes(-3, -2)
            .reshape(rows.shape)
        )

    def join_phases(rows):
        return rows.reshape(2, half, width).swapaxes(0, 1).reshape(rows.shape)

    local = jnp.arange(tok_rows, dtype=jnp.int32)
    order = 2 * (local % half) + local // half
    places = chip * tok_rows + order
    own_length = jnp.where(core_zero, lengths[0], lengths[1])
    other_length = jnp.where(core_zero, lengths[1], lengths[0])
    mask_rows = (places < own_length).astype(F32)[:, None]
    other_mask = (places < other_length).astype(F32)[:, None]
    x = split_phases(jnp.where(core_zero, io_pair[0, 0], sib_io[1]))
    cot_pair = jnp.where(core_zero, sib_io, io_pair[0])
    cot = split_phases(jnp.where(core_zero, cot_pair[0], cot_pair[1]))
    cot_other = split_phases(jnp.where(core_zero, cot_pair[1], cot_pair[0]))
    hidden = x.astype(F32) * mask_rows
    normed, spectral_factor = norm_forward(hidden, gains[0, 0])
    u = normed.astype(BF)
    u_parts = jnp.transpose(
        u.reshape(2, half, plan.cols_in, plan.jb), (2, 1, 0, 3)
    ).reshape(plan.cols_in, half, 2 * plan.jb)

    lags = jnp.transpose(filters.reshape(half, 2, plan.filters), (2, 1, 0))
    lags = jnp.stack([lags[:, :, ::-1], lags], 0).reshape(
        2, plan.groups, plan.local, 2 * half
    )
    lags = jnp.pad(lags, ((0, 0), (0, 0), (0, plan.f_rows - plan.local), (0, LANES - 2 * half)))
    packed = jnp.transpose(lags, (1, 0, 2, 3)).reshape(plan.groups, 2 * plan.f_rows, LANES)

    my_a = chip % plan.cols_out
    my_b = (chip // plan.cols_out) % plan.cols_in
    my_group = chip // (plan.cols_out * plan.cols_in)
    if plan.routed:
        maps = [stu_maps]
    else:
        whole = lax.all_gather(stu_maps, ("section", "seq"), axis=0, tiled=True)
        whole = lax.dynamic_slice(
            whole.reshape(-1, width, width),
            (0, my_b * plan.jb, my_a * plan.ia),
            (whole.shape[0] // width, plan.jb, plan.ia),
        )
        pair = whole[: 2 * plan.filters].reshape(2, plan.filters, plan.jb, plan.ia)
        pair = lax.dynamic_slice_in_dim(pair, my_group * plan.local, plan.local, 1)
        taps = jnp.where(my_group == 0, whole[2 * plan.filters :], 0).astype(BF)
        maps = [
            jnp.where(core_zero, pair[0], pair[1]),
            jnp.where(core_zero, pair[1], pair[0]),
            taps.reshape(-1, plan.ia),
        ]
    conv, v, pq, tapw, x_all, xs_all, filt = forward_call(plan, u_parts, packed, maps)

    ff = mlp_gate.shape[2]
    ff_rows = mlp_down.shape[1]
    ff_half = ff_rows // 2

    def my_half(layer, gate, up, down):
        del layer
        def pick(w):
            w = w.reshape(w.shape[0], chips, 2, ff_half)
            return jnp.where(core_zero, w[:, :, 0], w[:, :, 1]).reshape(w.shape[0], -1)

        return (
            pick(gate),
            pick(up),
            jnp.where(core_zero, down[:ff_half], down[ff_half:]),
        )

    own_raw = (mlp_gate[0], mlp_up[0], mlp_down[0])
    sib_raw = (sib_gate, sib_up, sib_down)
    layers = []
    for layer in range(2):
        raw = tuple(
            jnp.where(core_zero == (layer == 0), mine, theirs)
            for mine, theirs in zip(own_raw, sib_raw)
        )
        shares = my_half(layer, *raw)
        layers.append(
            tuple(lax.all_gather(w, "seq", axis=0, tiled=True) for w in shares)
        )
    proj_rows = attn_proj.shape[0]
    out_rows = attn_out.shape[0]
    both_rows = jnp.concatenate(
        [
            jnp.where(core_zero, attn_proj, sib_proj),
            jnp.where(core_zero, sib_proj, attn_proj),
            jnp.where(core_zero, attn_out, sib_out),
            jnp.where(core_zero, sib_out, attn_out),
        ],
        0,
    )
    attn_all = lax.all_gather(both_rows, "seq", axis=0, tiled=False)
    w_proj = jnp.swapaxes(
        attn_all[:, : 2 * proj_rows].reshape(chips, 2, proj_rows, width), 0, 1
    ).reshape(3, width, width)
    w_out = jnp.swapaxes(
        attn_all[:, 2 * proj_rows :].reshape(chips, 2, out_rows, width), 0, 1
    ).reshape(width, width)

    middle0 = hidden + conv.reshape(tok_rows, width)
    branch0, saved0 = mlp_forward(middle0, gains[0, 1], layers[0])
    passed = (mask_rows * (middle0 + branch0)).astype(BF)

    window_hidden = passed.astype(F32)
    window_normed, window_factor = norm_forward(window_hidden, gains[1, 0])
    inputs = window_normed.astype(BF)
    triple = dot("td,wde->wte", inputs, w_proj).astype(BF)
    key_value = triple[1:]
    parts = [shifted(key_value, "seq", distance) for distance in range(reach, 0, -1)]
    windows = jnp.concatenate(parts + [key_value], 1)
    key_window = windows[0].reshape(-1, heads, HEAD_DIM)
    value_window = windows[1].reshape(-1, heads, HEAD_DIM)
    queries = triple[0].reshape(tok_rows, heads, HEAD_DIM)
    scores = dot("qhe,khe->hqk", queries, key_window) * score_scale
    key_place = (
        (chip - reach + jnp.arange(reach + 1, dtype=jnp.int32))[:, None] * tok_rows + order[None, :]
    ).reshape(-1)
    distance_rows = places[:, None] - key_place[None, :]
    allowed = (key_place[None, :] >= 0) & (distance_rows >= 0) & (distance_rows < WINDOW)
    scores = jnp.where(allowed[None], scores, BIG_NEGATIVE)
    highest = jnp.max(scores, axis=-1, keepdims=True)
    weights = jnp.exp(scores - highest)
    weights = weights / jnp.sum(weights, axis=-1, keepdims=True)
    weights_low = weights.astype(BF)
    attended = dot("hqk,khe->qhe", weights_low, value_window)
    attended = attended.reshape(tok_rows, width).astype(BF)
    middle1 = window_hidden + dot("td,de->te", attended, w_out)
    branch1, saved1 = mlp_forward(middle1, gains[1, 1], layers[1])
    block_out = (mask_rows * (middle1 + branch1)).astype(BF)

    upstream1 = cot.astype(F32) * mask_rows
    other_upstream = cot_other.astype(F32) * other_mask
    grad_pair = jnp.concatenate([upstream1, other_upstream], 0).astype(BF)
    middle1_grad, gain11, mlp1_grads = mlp_backward(
        middle1, gains[1, 1], layers[1], saved1, upstream1, grad_pair
    )
    output_input = middle1_grad.astype(BF)
    output_grad = dot("td,te->de", attended, output_input)
    attended_grad = dot("te,de->td", output_input, w_out)
    attended_grad = attended_grad.astype(BF).reshape(tok_rows, heads, HEAD_DIM)
    value_grad = dot("hqk,qhe->khe", weights_low, attended_grad)
    weight_grad = dot("qhe,khe->hqk", attended_grad, value_window)
    row_total = jnp.sum(weights * weight_grad, axis=-1, keepdims=True)
    score_grad = (weights * (weight_grad - row_total)).astype(BF)
    query_grad = dot("hqk,khe->qhe", score_grad, key_window) * score_scale
    key_grad = dot("hqk,qhe->khe", score_grad, queries) * score_scale
    pair_grad = jnp.stack([key_grad.reshape(-1, width), value_grad.reshape(-1, width)])
    own_pair = pair_grad[:, reach * tok_rows :]
    for distance in range(reach, 0, -1):
        offset = (reach - distance) * tok_rows
        back = shifted(pair_grad[:, offset : offset + tok_rows].astype(BF), "seq", -distance)
        own_pair = own_pair + back.astype(F32)
    triple_grad = jnp.concatenate([query_grad.reshape(1, tok_rows, width), own_pair], 0).astype(BF)
    proj_grad = dot("td,wte->wde", inputs, triple_grad).reshape(3 * width, width)
    normed_grad = dot("wte,wde->td", triple_grad, w_proj)
    hidden1_grad, gain10 = norm_backward(window_hidden, window_factor, gains[1, 0], normed_grad)
    passed_grad = (middle1_grad + hidden1_grad).astype(BF)

    upstream0 = passed_grad.astype(F32) * mask_rows
    own_branch = upstream0.astype(BF)
    branch_pair = jnp.concatenate([own_branch, swapped(own_branch)], 0)
    middle0_grad, gain01, mlp0_grads = mlp_backward(
        middle0, gains[0, 1], layers[0], saved0, upstream0, branch_pair
    )
    g = middle0_grad.astype(BF).reshape(2, half, width)
    results = backward_call(plan, g, filt, v, pq, tapw, x_all, xs_all)
    signal_grad = results[0].reshape(tok_rows, width)
    if plan.routed:
        maps_grad = results[1].astype(F32)
    else:
        piece, tap_piece = (r.astype(F32) for r in results[1:])
        full = jnp.zeros((2, plan.filters, width, width), F32)
        full = lax.dynamic_update_slice(
            full,
            piece[None],
            (section, my_group * plan.local, my_b * plan.jb, my_a * plan.ia),
        )
        tap_piece = jnp.where(core_zero & (my_group == 0), tap_piece, 0.0)
        tap_full = lax.dynamic_update_slice(
            jnp.zeros((ORDER, width, width), F32),
            tap_piece.reshape(ORDER, plan.jb, plan.ia),
            (0, my_b * plan.jb, my_a * plan.ia),
        )
        full = jnp.concatenate([full.reshape(-1, width), tap_full.reshape(-1, width)], 0)
        maps_grad = lax.psum_scatter(full, ("section", "seq"), scatter_dimension=0, tiled=True)
    hidden_grad, gain00 = norm_backward(hidden, spectral_factor, gains[0, 0], signal_grad)
    inputs_grad = (mask_rows * (middle0_grad + hidden_grad)).astype(BF)

    def scattered(grads):
        return [
            lax.psum_scatter(w.astype(BF), "seq", scatter_dimension=0, tiled=True) for w in grads
        ]

    halves = [scattered(mlp0_grads), scattered(mlp1_grads)]
    outs = []
    for index in range(3):
        keep = jnp.where(core_zero, halves[0][index], halves[1][index])
        give = jnp.where(core_zero, halves[1][index], halves[0][index])
        take = swapped(give)
        low = jnp.where(core_zero, keep, take).astype(F32)
        high = jnp.where(core_zero, take, keep).astype(F32)
        if index < 2:
            rows = low.shape[0]
            joined = jnp.stack(
                [low.reshape(rows, chips, ff_half), high.reshape(rows, chips, ff_half)], 2
            ).reshape(rows, ff)
        else:
            joined = jnp.concatenate([low, high], 0)
        outs.append(joined[None])
    proj_out = lax.psum_scatter(
        proj_grad.astype(BF), ("section", "seq"), scatter_dimension=0, tiled=True
    ).astype(F32)
    out_out = lax.psum_scatter(
        output_grad.astype(BF), ("section", "seq"), scatter_dimension=0, tiled=True
    ).astype(F32)

    gain_parts = jnp.stack([jnp.stack([gain00, gain01]), jnp.stack([gain10, gain11])])
    gain_cols = width // chips
    tiles = jnp.transpose(gain_parts.reshape(2, 2, chips, gain_cols), (0, 2, 1, 3))
    tiles = jnp.pad(
        tiles.reshape(2 * chips, 2, gain_cols), ((0, 0), (0, 6), (0, LANES - gain_cols))
    )
    done_in, done_out = join_phases(inputs_grad), join_phases(block_out)
    taken, landed = exit_call(chips, jnp.where(core_zero, done_out, done_in), tiles)
    first = jnp.where(core_zero, done_in, taken)
    second = jnp.where(core_zero, taken, done_out)
    result_pair = jnp.stack([first, second])[None]
    gain_out = jnp.sum(landed, axis=0)[None, :2, :gain_cols]
    return (result_pair, maps_grad, proj_out, out_out, gain_out, outs[0], outs[1], outs[2])


def solution(mesh):
    placed = (
        P("section", None, "seq", None),
        P(),
        P("seq", None),
        P(("section", "seq"), None),
        P(("section", "seq"), None),
        P(("section", "seq"), None),
        P("section", None, "seq"),
        P("section", "seq", None),
        P("section", "seq", None),
        P("section", "seq", None),
    )
    return jax.shard_map(
        body,
        mesh=mesh,
        in_specs=placed,
        out_specs=(
            P("section", None, "seq", None),
            P(("section", "seq"), None),
            P(("section", "seq"), None),
            P(("section", "seq"), None),
            P("section", None, "seq"),
            P("section", "seq", None),
            P("section", "seq", None),
            P("section", "seq", None),
        ),
        check_vma=False,
    )
```

```python
import functools
import math

import jax
import jax.numpy as jnp
from jax import lax
from jax.experimental import pallas as pl
from jax.experimental.pallas import tpu as pltpu
from jax.sharding import PartitionSpec as P

ORDER = 3
HEAD_DIM = 64
WINDOW = 512
EPSILON = 1e-05
BIG_NEGATIVE = -1e30
MESH = pl.DeviceIdType.MESH
BF = jnp.bfloat16
F32 = jnp.float32
LANES = 128
BLOCK = 256
PIECE = 16
VMEM_LIMIT = 63 * 1024 * 1024


class Plan:
    def __init__(self, chips, tok_rows, width, filter_count, map_rows):
        self.chips = chips
        self.rows = tok_rows
        self.half = tok_rows // 2
        self.width = width
        self.filters = filter_count
        self.cols_in = 4
        self.cols_out = max(1, math.isqrt(chips // 4))
        self.groups = chips // (self.cols_in * self.cols_out)
        self.local = filter_count // self.groups
        self.length = chips * self.half
        self.blocks = self.length // BLOCK
        self.jb = width // self.cols_in
        self.ia = width // self.cols_out
        self.map_rows = map_rows
        self.routed = map_rows % PIECE == 0
        self.pieces = map_rows // PIECE
        self.f_rows = -(-self.local // 16) * 16
        self.side = max(1, math.isqrt(chips // 4))
        self.depth = chips // (self.side * self.side)

    def place(self, chip):
        return (
            chip // (self.side * self.side),
            lax.rem(chip // self.side, self.side),
            lax.rem(chip, self.side),
        )

    def chip_at(self, z, y, x):
        return (z * self.side + y) * self.side + x

    def routes(self, rows):
        if rows % (2 * PIECE) == 0:
            return [(0, rows // 2, True), (rows // 2, rows // 2, False)]
        return [(0, rows, True)]


def spot():
    return lax.axis_index("section"), lax.axis_index("seq")


def greet_everyone(chips):
    section, chip = spot()
    me = section * chips + chip
    barrier = pltpu.get_barrier_semaphore()

    def one(step, carry):
        peer = lax.rem(me + step, 2 * chips)
        pl.semaphore_signal(
            barrier, inc=1, device_id=(peer // chips, lax.rem(peer, chips)), device_id_type=MESH
        )
        return carry

    lax.fori_loop(1, 2 * chips, one, 0)
    pl.semaphore_wait(barrier, 2 * chips - 1)


def push(src, dst, send, recv, target):
    return pltpu.make_async_remote_copy(
        src_ref=src,
        dst_ref=dst,
        send_sem=send,
        recv_sem=recv,
        device_id=target,
        device_id_type=MESH,
    )


def bytes_of(ref, sem):
    pltpu.make_async_copy(ref, ref, sem).wait()


class Gather:
    def __init__(self, plan, shards, outs, send, recv):
        self.plan, self.shards, self.outs = plan, shards, outs
        self.send, self.recv = send, recv
        self.section, chip = spot()
        self.z, self.y, self.x = plan.place(chip)

    def to(self, z, y, x):
        return self.section, self.plan.chip_at(z, y, x)

    def parts(self, i):
        for number, (start, rows, x_first) in enumerate(self.plan.routes(self.shards[i].shape[0])):
            out = self.outs[i]
            sl = pl.ds(start, rows)
            yield number, x_first, out, sl

    def begin(self):
        plan = self.plan
        for i, shard in enumerate(self.shards):
            spot_ref = self.outs[i].at[self.z, self.y, self.x]
            for step in range(1, plan.depth):
                z = lax.rem(self.z + step, plan.depth)
                push(
                    shard, spot_ref, self.send.at[i, 0], self.recv.at[i, 0], self.to(z, self.y, self.x)
                ).start()
            pltpu.make_async_copy(shard, spot_ref, self.recv.at[i, 0]).start()

    def second(self):
        side = self.plan.side
        for i in range(len(self.shards)):
            bytes_of(self.outs[i].at[:, self.y, self.x], self.recv.at[i, 0])
            for number, x_first, out, sl in self.parts(i):
                src = out.at[:, self.y, self.x, sl]
                for step in range(1, side):
                    if x_first:
                        peer = self.to(self.z, self.y, lax.rem(self.x + step, side))
                    else:
                        peer = self.to(self.z, lax.rem(self.y + step, side), self.x)
                    push(
                        src, src, self.send.at[i, 1 + number], self.recv.at[i, 1 + number], peer
                    ).start()

    def third(self):
        side = self.plan.side
        for i in range(len(self.shards)):
            for number, x_first, out, sl in self.parts(i):
                sem = self.recv.at[i, 1 + number]
                if x_first:
                    bytes_of(out.at[:, self.y, pl.ds(0, side - 1), sl], sem)
                    src = out.at[:, self.y, :, sl]
                else:
                    bytes_of(out.at[:, pl.ds(0, side - 1), self.x, sl], sem)
                    src = out.at[:, :, self.x, sl]
                for step in range(1, side):
                    if x_first:
                        peer = self.to(self.z, lax.rem(self.y + step, side), self.x)
                    else:
                        peer = self.to(self.z, self.y, lax.rem(self.x + step, side))
                    push(
                        src, src, self.send.at[i, 3 + number], self.recv.at[i, 3 + number], peer
                    ).start()

    def end(self):
        plan = self.plan
        side = plan.side
        for i in range(len(self.shards)):
            bytes_of(self.outs[i].at[pl.ds(0, plan.depth - 1), 0, 0], self.send.at[i, 0])
            for number, x_first, out, sl in self.parts(i):
                bytes_of(out.at[:, 0, pl.ds(0, side - 1), sl], self.send.at[i, 1 + number])
                last = out.at[:, :, pl.ds(0, side - 1), sl]
                bytes_of(last, self.recv.at[i, 3 + number])
                bytes_of(last, self.send.at[i, 3 + number])


class Scatter:
    @staticmethod
    def scratch(plan, shapes):
        refs = []
        for rows, cols in shapes:
            for _, part, _ in plan.routes(rows):
                for lead in (
                    (plan.side - 1, plan.depth, plan.side),
                    (plan.depth, plan.side),
                    (plan.side - 1, plan.depth),
                    (plan.depth,),
                    (plan.depth - 1,),
                ):
                    refs.append(pltpu.VMEM(lead + (part, cols), BF))
        return refs

    def __init__(self, plan, grads, outs, buffers, send, recv):
        self.plan, self.grads, self.outs = plan, grads, outs
        self.send, self.recv = send, recv
        self.section, chip = spot()
        self.z, self.y, self.x = plan.place(chip)
        self.work = []
        buffers = list(buffers)
        for i, grad in enumerate(grads):
            for number, (start, rows, x_first) in enumerate(plan.routes(grad.shape[3])):
                self.work.append((i, number, start, rows, x_first, buffers[:5]))
                buffers = buffers[5:]

    def to(self, z, y, x):
        return self.section, self.plan.chip_at(z, y, x)

    def begin(self):
        side = self.plan.side
        for i, number, start, rows, x_first, (land, *_) in self.work:
            grad, sl = self.grads[i], pl.ds(start, rows)
            for step in range(1, side):
                if x_first:
                    y = lax.rem(self.y + step, side)
                    src, peer = grad.at[:, y, :, sl], self.to(self.z, y, self.x)
                else:
                    x = lax.rem(self.x + step, side)
                    src, peer = grad.at[:, :, x, sl], self.to(self.z, self.y, x)
                push(
                    src, land.at[step - 1], self.send.at[i, number], self.recv.at[i, number], peer
                ).start()

    def second(self):
        plan, side = self.plan, self.plan.side
        for i, number, start, rows, x_first, (land, part, land2, *_) in self.work:
            grad = self.grads[i]
            bytes_of(land, self.recv.at[i, number])

            def one(index, carry, grad=grad, land=land, part=part, start=start, rows=rows, x_first=x_first):
                z, j = index // side, lax.rem(index, side)
                y, x = (self.y, j) if x_first else (j, self.x)
                total = grad[z, y, x, start : start + rows, :].astype(F32)
                for step in range(side - 1):
                    total = total + land[step, z, j].astype(F32)
                part[z, j] = total.astype(BF)
                return carry

            lax.fori_loop(0, plan.depth * side, one, 0)
            for step in range(1, side):
                if x_first:
                    j = lax.rem(self.x + step, side)
                    peer = self.to(self.z, self.y, j)
                else:
                    j = lax.rem(self.y + step, side)
                    peer = self.to(self.z, j, self.x)
                push(
                    part.at[:, j],
                    land2.at[step - 1],
                    self.send.at[i, 2 + number],
                    self.recv.at[i, 2 + number],
                    peer,
                ).start()

    def third(self):
        plan, side = self.plan, self.plan.side
        for i, number, start, rows, x_first, (_, part, land2, line, land3) in self.work:
            bytes_of(land2, self.recv.at[i, 2 + number])
            mine = self.x if x_first else self.y

            def one(z, carry, part=part, land2=land2, line=line, mine=mine):
                total = part[z, mine].astype(F32)
                for step in range(side - 1):
                    total = total + land2[step, z].astype(F32)
                line[z] = total.astype(BF)
                return carry

            lax.fori_loop(0, plan.depth, one, 0)
            for step in range(1, plan.depth):
                z = lax.rem(self.z + step, plan.depth)
                push(
                    line.at[z],
                    land3.at[step - 1],
                    self.send.at[i, 4 + number],
                    self.recv.at[i, 4 + number],
                    self.to(z, self.y, self.x),
                ).start()

    def end(self):
        for i, number, start, rows, x_first, (land, part, land2, line, land3) in self.work:
            bytes_of(land3, self.recv.at[i, 4 + number])
            total = line[self.z].astype(F32)
            for step in range(self.plan.depth - 1):
                total = total + land3[step].astype(F32)
            self.outs[i][start : start + rows, :] = total
            bytes_of(land, self.send.at[i, number])
            bytes_of(land2, self.send.at[i, 2 + number])
            bytes_of(land3, self.send.at[i, 4 + number])


def entry_kernel(chips, count, *refs):
    given = refs[:count]
    gains = refs[count]
    taken = refs[count + 1 : 2 * count + 1]
    gains_all = refs[2 * count + 1]
    send, recv, gain_send, gain_recv = refs[2 * count + 2 :]
    section, chip = spot()
    me = section * chips + chip
    greet_everyone(chips)
    copies = [
        push(given[i], taken[i], send.at[i], recv.at[i], (1 - section, chip)) for i in range(count)
    ]
    for copy in copies[:1]:
        copy.start()

    def one(step, carry):
        peer = lax.rem(me + step, 2 * chips)
        push(
            gains,
            gains_all.at[section, chip],
            gain_send,
            gain_recv,
            (peer // chips, lax.rem(peer, chips)),
        ).start()
        return carry

    lax.fori_loop(1, 2 * chips, one, 0)
    pltpu.make_async_copy(gains, gains_all.at[section, chip], gain_recv).start()
    for copy in copies[1:]:
        copy.start()
    bytes_of(gains_all, gain_recv)

    def drain(step, carry):
        push(gains, gains_all.at[section, chip], gain_send, gain_recv, (section, chip)).wait_send()
        return carry

    lax.fori_loop(1, 2 * chips, drain, 0)
    for copy in copies:
        copy.wait()


def entry_call(chips, arrays, gains):
    count = len(arrays)
    any_spec = pl.BlockSpec(memory_space=pl.ANY)
    return pl.pallas_call(
        functools.partial(entry_kernel, chips, count),
        out_shape=[jax.ShapeDtypeStruct(a.shape, a.dtype) for a in arrays]
        + [jax.ShapeDtypeStruct((2, chips) + gains.shape, gains.dtype)],
        in_specs=[any_spec] * (count + 1),
        out_specs=[any_spec] * (count + 1),
        scratch_shapes=[
            pltpu.SemaphoreType.DMA((count,)),
            pltpu.SemaphoreType.DMA((count,)),
            pltpu.SemaphoreType.DMA,
            pltpu.SemaphoreType.DMA,
        ],
        compiler_params=pltpu.CompilerParams(collective_id=1, has_side_effects=True),
        name="entry",
    )(*arrays, gains)


def exit_kernel(chips, give, tiles, take, land, send, recv, gain_send, gain_recv):
    section, chip = spot()
    me = section * chips + chip
    greet_everyone(chips)
    swap = push(give, take, send, recv, (1 - section, chip))
    swap.start()

    def one(step, carry):
        peer = lax.rem(me + step, 2 * chips)
        push(
            tiles.at[peer],
            land.at[me],
            gain_send,
            gain_recv,
            (peer // chips, lax.rem(peer, chips)),
        ).start()
        return carry

    lax.fori_loop(1, 2 * chips, one, 0)
    pltpu.make_async_copy(tiles.at[me], land.at[me], gain_recv).start()
    bytes_of(land, gain_recv)
    bytes_of(land.at[pl.ds(0, 2 * chips - 1)], gain_send)
    swap.wait()


def exit_call(chips, give, tiles):
    any_spec = pl.BlockSpec(memory_space=pl.ANY)
    return pl.pallas_call(
        functools.partial(exit_kernel, chips),
        out_shape=[
            jax.ShapeDtypeStruct(give.shape, give.dtype),
            jax.ShapeDtypeStruct(tiles.shape, tiles.dtype),
        ],
        in_specs=[any_spec] * 2,
        out_specs=[any_spec] * 2,
        scratch_shapes=[
            pltpu.SemaphoreType.DMA,
            pltpu.SemaphoreType.DMA,
            pltpu.SemaphoreType.DMA,
            pltpu.SemaphoreType.DMA,
        ],
        compiler_params=pltpu.CompilerParams(collective_id=4, has_side_effects=True),
        name="leave",
    )(give, tiles)


def filter_rows(plan, land, table, first_row, backward):
    lane = lax.broadcasted_iota(jnp.int32, (plan.f_rows, LANES), 1)
    low = lane < plan.half
    total = plan.length // LANES
    for m in range(total):
        if backward:
            one, two = 2 * m, 2 * m + 1
        else:
            one, two = plan.chips - 1 - 2 * m, plan.chips - 2 - 2 * m
        left = land[one, first_row : first_row + plan.f_rows, :].astype(F32)
        right = land[two, first_row : first_row + plan.f_rows, :].astype(F32)
        even = jnp.where(low, left, pltpu.roll(right, plan.half, 1))
        odd = jnp.where(low, pltpu.roll(left, plan.half, 1), right)
        at = LANES * m + (BLOCK if backward else 0)
        table[0, :, at : at + LANES] = even
        table[1, :, at : at + LANES] = odd
    blank = jnp.zeros((plan.f_rows, BLOCK), F32)
    at = 0 if backward else plan.length
    for parity in range(2):
        table[parity, :, at : at + BLOCK] = blank


def build_strips(plan, table, strip, backward):
    span = plan.length + BLOCK
    shift = span - LANES if backward else span - (LANES - 1)
    part = 32

    def one(k, carry):
        for parity in range(2):
            row = table[parity, pl.ds(k, 1), :]
            for start in range(0, LANES, part):
                spread = jnp.broadcast_to(row, (part, span))
                rolled = pltpu.roll(
                    spread, (shift + start) % span, 1, stride=1, stride_axis=0
                ).astype(BF)
                strip[2 * k + parity, LANES + start : LANES + start + part, :] = rolled[
                    :, : plan.length
                ]
                strip[2 * k + parity, start : start + part, :] = rolled[
                    :, LANES : LANES + plan.length
                ]
        return carry

    lax.fori_loop(0, plan.local, one, 0)


def owner_pieces(plan, act):
    section, chip = spot()
    dev = section * plan.chips + chip
    per_map = plan.width // PIECE
    per_block = plan.jb // PIECE

    def unit(m, carry):
        g = plan.pieces * dev + m
        which = g // per_map
        inside = lax.rem(g, per_map)
        b = inside // per_block
        sub = lax.rem(inside, per_block)
        sign = which // plan.filters
        full = lax.rem(which, plan.filters)
        group = full // plan.local
        k = lax.rem(full, plan.local)

        @pl.when(sign < 2)
        def _():
            for a in range(plan.cols_out):
                target = a + plan.cols_out * (b + plan.cols_in * group)
                act(m, False, k, sub, a, sign, target)

        @pl.when(sign >= 2)
        def _():
            for a in range(plan.cols_out):
                for core in range(2):
                    act(m, True, full, sub, a, core, a + plan.cols_out * b)

        return carry

    lax.fori_loop(0, plan.pieces, unit, 0)


def forward_kernel(plan, *refs):
    u_ref, f_ref, *shards = refs[:5]
    if plan.routed:
        maps_ref = refs[5]
        rest = refs[6:]
    else:
        mine_ref, other_ref, taps_ref = refs[5:8]
        rest = refs[8:]
    full_weights, rest = rest[:3], rest[3:]
    (
        conv_ref,
        v_ref,
        pq_ref,
        tapw_ref,
        x_ref,
        xs_ref,
        filt_ref,
        x_buf,
        xo_buf,
        xs_buf,
        xf_buf,
        f_land,
        table,
        strip,
        mine,
        other,
        taps,
        pq,
        acc,
        y_buf,
        land,
        stage,
        u_send,
        x_recv,
        f_send,
        f_recv,
        m_send,
        m_recv,
        t_recv,
        o_send,
        o_recv,
        c_send,
        c_recv,
        v_sem,
        out_sem,
        w_send,
        w_recv,
    ) = rest
    chips, half, jb, ia = plan.chips, plan.half, plan.jb, plan.ia
    section, chip = spot()
    dev = section * chips + chip
    my_group = chip // (plan.cols_out * plan.cols_in)
    greet_everyone(chips)

    def send_u(step, carry):
        peer = lax.rem(chip + step, chips)
        b = lax.rem(peer // plan.cols_out, plan.cols_in)
        group = peer // (plan.cols_out * plan.cols_in)
        push(
            u_ref.at[b],
            x_buf.at[pl.ds(half * chip, half), :],
            u_send,
            x_recv,
            (section, peer),
        ).start()
        push(f_ref.at[group], f_land.at[chip], f_send, f_recv, (section, peer)).start()
        return carry

    lax.fori_loop(1, chips, send_u, 0)
    pltpu.make_async_copy(
        u_ref.at[lax.rem(chip // plan.cols_out, plan.cols_in)],
        x_buf.at[pl.ds(half * chip, half), :],
        x_recv,
    ).start()
    pltpu.make_async_copy(f_ref.at[my_group], f_land.at[chip], f_recv).start()

    if plan.routed:

        def places(m, tap, k, sub, a):
            src = maps_ref.at[pl.ds(PIECE * m, PIECE), pl.ds(a * ia, ia)]
            if tap:
                return src, taps.at[pl.ds(jb * k + PIECE * sub, PIECE), :], t_recv
            return src, mine.at[k, pl.ds(PIECE * sub, PIECE), :], m_recv

        def start_piece(m, tap, k, sub, a, to_section, to_chip):
            src, dst, sem = places(m, tap, k, sub, a)
            here = to_section * chips + to_chip == dev

            @pl.when(here)
            def _():
                pltpu.make_async_copy(src, dst, sem).start()

            @pl.when(jnp.logical_not(here))
            def _():
                push(src, dst, m_send, sem, (to_section, to_chip)).start()

        def drain_piece(m, tap, k, sub, a, to_section, to_chip):
            src, dst, sem = places(m, tap, k, sub, a)

            @pl.when(to_section * chips + to_chip != dev)
            def _():
                push(src, dst, m_send, sem, (to_section, to_chip)).wait_send()

        owner_pieces(plan, start_piece)

    gather = Gather(plan, shards, full_weights, w_send, w_recv)
    gather.begin()
    bytes_of(f_land, f_recv)
    filter_rows(plan, f_land, table, 0, False)
    build_strips(plan, table, strip, False)
    filt_out = pltpu.make_async_copy(f_land, filt_ref, out_sem.at[0])
    filt_out.start()

    if plan.routed:
        bytes_of(mine, m_recv)
        swap = push(mine, other, o_send, o_recv, (1 - section, chip))
        swap.start()

        @pl.when(my_group == 0)
        def _():
            bytes_of(taps, t_recv)

        @pl.when(my_group != 0)
        def _():
            taps[...] = jnp.zeros_like(taps)
    else:
        for src, dst in ((mine_ref, mine), (other_ref, other), (taps_ref, taps)):
            pltpu.sync_copy(src, dst)

    bytes_of(x_buf, x_recv)
    x_out = pltpu.make_async_copy(x_buf, x_ref, out_sem.at[1])
    x_out.start()
    xf_buf[0:8, :] = jnp.zeros((8, 2 * jb), F32)
    for i in range(plan.blocks):
        rows = slice(BLOCK * i, BLOCK * (i + 1))
        xf_buf[8 + BLOCK * i : 8 + BLOCK * (i + 1), :] = x_buf[rows, :].astype(F32)
    for i in range(plan.blocks):
        rows = slice(BLOCK * i, BLOCK * (i + 1))
        moved = xf_buf[7 + BLOCK * i : 7 + BLOCK * (i + 1), :].astype(BF)
        xs_buf[rows, :] = moved
        xo_buf[rows, :jb] = x_buf[rows, :jb]
        xo_buf[rows, jb:] = moved[:, jb:]
    xs_out = pltpu.make_async_copy(xs_buf, xs_ref, out_sem.at[2])
    xs_out.start()

    if plan.routed:
        swap.wait()
    turn = (1 - 2 * section).astype(F32)

    def mix(k, carry):
        first = mine[k].astype(F32)
        second = other[k].astype(F32)
        pq[k, :jb, :] = (first + second).astype(BF)
        pq[k, jb:, :] = ((first - second) * turn).astype(BF)
        return carry

    lax.fori_loop(0, plan.local, mix, 0)
    pq_out = pltpu.make_async_copy(pq, pq_ref, out_sem.at[3])
    pq_out.start()
    taps_out = pltpu.make_async_copy(taps, tapw_ref, out_sem.at[4])
    taps_out.start()

    gather.second()
    for i in range(plan.blocks):
        if i == plan.blocks // 2:
            gather.third()
        rows = slice(BLOCK * i, BLOCK * (i + 1))
        depth = BLOCK * (i + 1)
        offset = plan.length - depth
        x_now = x_buf[rows, :]
        s_now = xs_buf[rows, :]
        acc[0] = jnp.dot(
            jnp.concatenate([x_now[:, :jb], s_now[:, jb:]], 1),
            taps[: 2 * jb, :],
            preferred_element_type=F32,
        ) + jnp.dot(s_now[:, :jb], taps[2 * jb :, :], preferred_element_type=F32)
        acc[1] = jnp.dot(
            jnp.concatenate([x_now[:, jb:], x_now[:, :jb]], 1),
            taps[: 2 * jb, :],
            preferred_element_type=F32,
        ) + jnp.dot(s_now[:, jb:], taps[2 * jb :, :], preferred_element_type=F32)

        def step(k, carry, i=i, depth=depth, offset=offset):
            slot = lax.rem(k, 2)
            v_copy = pltpu.make_async_copy(
                stage.at[slot], v_ref.at[k, :, pl.ds(BLOCK * i, BLOCK), :], v_sem.at[slot]
            )
            even = jnp.dot(
                strip[2 * k, :, offset:], x_buf[:depth, :], preferred_element_type=F32
            ).astype(BF)
            odd = jnp.dot(
                strip[2 * k + 1, :, offset:], xo_buf[:depth, :], preferred_element_type=F32
            ).astype(BF)
            first = jnp.concatenate([even[:, :jb], odd[:, jb:]], 1)
            second = jnp.concatenate([even[:, jb:], odd[:, :jb]], 1)
            if i == 0:
                pl.when(k >= 2)(v_copy.wait)
            else:
                v_copy.wait()
            stage[slot, 0] = first
            stage[slot, 1] = second
            v_copy.start()
            acc[0] += jnp.dot(first, pq[k], preferred_element_type=F32)
            acc[1] += jnp.dot(second, pq[k], preferred_element_type=F32)
            return carry

        lax.fori_loop(0, plan.local, step, 0)
        y_buf[0, rows, :] = acc[0].astype(BF)
        y_buf[1, rows, :] = acc[1].astype(BF)

        def give(r, carry, i=i):
            peer = BLOCK // half * i + r
            src = y_buf.at[:, pl.ds(half * peer, half), :]

            @pl.when(peer == chip)
            def _():
                pltpu.make_async_copy(src, land.at[chip], c_recv).start()

            @pl.when(peer != chip)
            def _():
                push(src, land.at[chip], c_send, c_recv, (section, peer)).start()

            return carry

        lax.fori_loop(0, BLOCK // half, give, 0)

    for slot in range(2):
        pltpu.make_async_copy(
            stage.at[slot], v_ref.at[slot, :, pl.ds(0, BLOCK), :], v_sem.at[slot]
        ).wait()
    bytes_of(x_buf.at[pl.ds(0, half * (chips - 1)), :], u_send)
    bytes_of(f_land.at[pl.ds(0, chips - 1)], f_send)
    if plan.routed:
        owner_pieces(plan, drain_piece)
    for copy in (filt_out, x_out, xs_out, pq_out, taps_out):
        copy.wait()
    bytes_of(land, c_recv)
    for a in range(plan.cols_out):
        total = None
        for other_part in range(plan.cols_in * plan.groups):
            term = land[a + plan.cols_out * other_part].astype(F32)
            total = term if total is None else total + term
        conv_ref[:, :, a * ia : (a + 1) * ia] = total
    bytes_of(land.at[pl.ds(0, chips - 1)], c_send)
    gather.end()


def forward_call(plan, u, packed, shards, maps):
    chips, half, jb, ia = plan.chips, plan.half, plan.jb, plan.ia
    any_spec = pl.BlockSpec(memory_space=pl.ANY)
    vmem_spec = pl.BlockSpec(memory_space=pltpu.VMEM)
    dma = pltpu.SemaphoreType.DMA
    grid = (plan.depth, plan.side, plan.side)
    shapes = [(grid + w.shape, BF) for w in shards] + [
        ((2, half, plan.width), F32),
        ((plan.local, 2, plan.length, 2 * jb), BF),
        ((plan.local, 2 * jb, ia), BF),
        ((ORDER * jb, ia), BF),
        ((plan.length, 2 * jb), BF),
        ((plan.length, 2 * jb), BF),
        ((chips, 2 * plan.f_rows, LANES), BF),
    ]
    return pl.pallas_call(
        functools.partial(forward_kernel, plan),
        out_shape=[jax.ShapeDtypeStruct(s, d) for s, d in shapes],
        in_specs=[vmem_spec] * 2 + [any_spec] * (3 + len(maps)),
        out_specs=[any_spec] * 3 + [vmem_spec] + [any_spec] * 6,
        scratch_shapes=[
            pltpu.VMEM((plan.length, 2 * jb), BF),
            pltpu.VMEM((plan.length, 2 * jb), BF),
            pltpu.VMEM((plan.length, 2 * jb), BF),
            pltpu.VMEM((plan.length + 8, 2 * jb), F32),
            pltpu.VMEM((chips, 2 * plan.f_rows, LANES), BF),
            pltpu.VMEM((2, plan.f_rows, plan.length + BLOCK), F32),
            pltpu.VMEM((2 * plan.local, BLOCK, plan.length), BF),
            pltpu.VMEM((plan.local, jb, ia), BF),
            pltpu.VMEM((plan.local, jb, ia), BF),
            pltpu.VMEM((ORDER * jb, ia), BF),
            pltpu.VMEM((plan.local, 2 * jb, ia), BF),
            pltpu.VMEM((2, BLOCK, ia), F32),
            pltpu.VMEM((2, plan.length, ia), BF),
            pltpu.VMEM((chips, 2, half, ia), BF),
            pltpu.VMEM((2, 2, BLOCK, 2 * jb), BF),
        ]
        + [dma] * 11
        + [dma((2,)), dma((5,)), dma((3, 5)), dma((3, 5))],
        compiler_params=pltpu.CompilerParams(
            collective_id=2, has_side_effects=True, vmem_limit_bytes=VMEM_LIMIT
        ),
        name="spectral_forward",
    )(u, packed, *shards, *maps)


def backward_kernel(plan, *refs):
    g_ref, filt_ref, v_ref, pq, tapw, x_ref, xs_ref = refs[:7]
    grads = refs[7:10]
    sums = refs[10:13]
    du_ref = refs[13]
    if plan.routed:
        dmaps_ref = refs[14]
        rest = refs[15:]
    else:
        dmap_ref, dtap_ref = refs[14:16]
        rest = refs[16:]
    count = 5 * sum(len(plan.routes(grad.shape[3])) for grad in grads)
    scatter = Scatter(plan, grads, sums, rest[:count], *rest[count : count + 2])
    rest = rest[count + 2 :]
    (
        g_buf,
        gt_buf,
        table,
        strip,
        v_buf,
        z_even,
        z_odd,
        acc_even,
        acc_odd,
        kept,
        give_m,
        take_m,
        total_m,
        kept_t,
        give_t,
        take_t,
        total_t,
        du_buf,
        land,
        g_send,
        g_recv,
        v_sem,
        m_send,
        m_recv,
        t_send,
        t_recv,
        w_send,
        w_recv,
        d_send,
        d_recv,
        x_sem,
    ) = rest
    chips, half, jb, ia = plan.chips, plan.half, plan.jb, plan.ia
    section, chip = spot()
    dev = section * chips + chip
    my_a = lax.rem(chip, plan.cols_out)
    my_b = lax.rem(chip // plan.cols_out, plan.cols_in)
    my_group = chip // (plan.cols_out * plan.cols_in)
    greet_everyone(chips)

    def send_g(step, carry):
        peer = lax.rem(chip + step, chips)
        a = lax.rem(peer, plan.cols_out)
        push(
            g_ref.at[:, :, pl.ds(pl.multiple_of(a * ia, ia), ia)],
            g_buf.at[:, pl.ds(half * chip, half), :],
            g_send,
            g_recv,
            (section, peer),
        ).start()
        return carry

    lax.fori_loop(1, chips, send_g, 0)
    pltpu.make_async_copy(
        g_ref.at[:, :, pl.ds(pl.multiple_of(my_a * ia, ia), ia)],
        g_buf.at[:, pl.ds(half * chip, half), :],
        g_recv,
    ).start()
    v_copy = [pltpu.make_async_copy(v_ref.at[k], v_buf.at[k], v_sem.at[k]) for k in range(2)]
    for copy in v_copy:
        copy.start()
    x_copy = [
        pltpu.make_async_copy(src, dst, x_sem.at[i])
        for i, (src, dst) in enumerate(((x_ref, z_even), (xs_ref, z_odd)))
    ]
    for copy in x_copy:
        copy.start()
    scatter.begin()
    filter_rows(plan, filt_ref, table, plan.f_rows, True)
    build_strips(plan, table, strip, True)
    acc_even[...] = jnp.zeros_like(acc_even)
    acc_odd[...] = jnp.zeros_like(acc_odd)
    bytes_of(g_buf, g_recv)
    for phase in range(2):
        for i in range(plan.blocks):
            rows = slice(BLOCK * i, BLOCK * (i + 1))
            gt_buf[phase, :, rows] = g_buf[phase, rows, :].astype(F32).T.astype(BF)
    turn = (1 - 2 * section).astype(F32)
    half_ways = (((1,), (1,)), ((), ()))

    def piece_of(k, tap, sub):
        per_map = plan.width // PIECE
        which = 2 * plan.filters + k if tap else section * plan.filters + my_group * plan.local + k
        g = which * per_map + my_b * (plan.jb // PIECE) + sub
        return g // plan.pieces, lax.rem(g, plan.pieces)

    def piece_copies(k, tap, begin):
        def one(sub, carry):
            owner, row = piece_of(k, tap, sub)
            src = (
                total_t.at[pl.ds(jb * k + PIECE * sub, PIECE), :]
                if tap
                else total_m.at[k, pl.ds(PIECE * sub, PIECE), :]
            )
            dst = dmaps_ref.at[
                pl.ds(PIECE * row, PIECE), pl.ds(pl.multiple_of(my_a * ia, ia), ia)
            ]
            if begin:

                @pl.when(owner == dev)
                def _():
                    pltpu.make_async_copy(src, dst, w_recv).start()

            @pl.when(owner != dev)
            def _():
                copy = push(src, dst, w_send, w_recv, (owner // chips, lax.rem(owner, chips)))
                if begin:
                    copy.start()
                else:
                    copy.wait_send()

            return carry

        lax.fori_loop(0, plan.jb // PIECE, one, 0)

    def exchange(k):
        return push(give_m.at[k], take_m.at[k], m_send.at[k], m_recv.at[k], (1 - section, chip))

    def finish(k):
        exchange(k).wait()
        total_m[k] = (kept[k] + take_m[k].astype(F32)).astype(BF)
        if plan.routed:
            piece_copies(k, False, True)

    for copy in x_copy:
        copy.wait()
    x_even, x_odd = z_even[:, :jb], z_even[:, jb:]
    s_even, s_odd = z_odd[:, :jb], z_odd[:, jb:]
    for tap, (on_even, on_odd) in enumerate(((x_even, x_odd), (s_odd, x_even), (s_even, s_odd))):
        tap_grad = jnp.dot(gt_buf[0], on_even, preferred_element_type=F32) + jnp.dot(
            gt_buf[1], on_odd, preferred_element_type=F32
        )
        tap_grad = tap_grad.T
        kept_t[tap * jb : (tap + 1) * jb, :] = tap_grad
        give_t[tap * jb : (tap + 1) * jb, :] = tap_grad.astype(BF)
    tap_swap = push(give_t, take_t, t_send, t_recv, (1 - section, chip))
    tap_swap.start()
    for i in range(plan.blocks):
        rows = slice(BLOCK * i, BLOCK * (i + 1))
        from_even = lax.dot_general(
            g_buf[0, rows, :], tapw[...], half_ways, preferred_element_type=F32
        )
        from_odd = lax.dot_general(
            g_buf[1, rows, :], tapw[...], half_ways, preferred_element_type=F32
        )
        acc_even[rows, :jb] = from_even[:, :jb] + from_odd[:, jb : 2 * jb]
        acc_even[rows, jb : 2 * jb] = from_odd[:, :jb]
        acc_odd[rows, :jb] = from_even[:, 2 * jb :]
        acc_odd[rows, jb : 2 * jb] = from_even[:, jb : 2 * jb] + from_odd[:, 2 * jb :]

    def step(k, carry):
        slot = lax.rem(k, 2)
        for i in range(plan.blocks):
            rows = slice(BLOCK * i, BLOCK * (i + 1))
            from_even = lax.dot_general(
                g_buf[0, rows, :], pq[k], half_ways, preferred_element_type=F32
            ).astype(BF)
            from_odd = lax.dot_general(
                g_buf[1, rows, :], pq[k], half_ways, preferred_element_type=F32
            ).astype(BF)
            z_even[rows, :jb] = from_even[:, :jb]
            z_even[rows, jb:] = from_odd[:, :jb]
            z_odd[rows, :jb] = from_odd[:, jb:]
            z_odd[rows, jb:] = from_even[:, jb:]
        pltpu.make_async_copy(v_ref.at[k], v_buf.at[slot], v_sem.at[slot]).wait()
        grad = jnp.dot(gt_buf[0], v_buf[slot, 0], preferred_element_type=F32) + jnp.dot(
            gt_buf[1], v_buf[slot, 1], preferred_element_type=F32
        )
        grad = grad.T
        plus, minus = grad[:jb, :], grad[jb:, :] * turn
        kept[k] = plus + minus
        give_m[k] = (plus - minus).astype(BF)
        exchange(k).start()

        @pl.when(k + 2 < plan.local)
        def _():
            pltpu.make_async_copy(v_ref.at[k + 2], v_buf.at[slot], v_sem.at[slot]).start()

        for j in range(plan.blocks):
            rows = slice(BLOCK * j, BLOCK * (j + 1))
            depth = plan.length - BLOCK * j
            acc_even[rows, :] += jnp.dot(
                strip[2 * k, :, :depth], z_even[BLOCK * j :, :], preferred_element_type=F32
            )
            out = jnp.dot(
                strip[2 * k + 1, :, :depth], z_odd[BLOCK * j :, :], preferred_element_type=F32
            )
            acc_even[rows, :jb] += out[:, :jb]
            acc_odd[rows, jb:] += out[:, jb:]

        @pl.when(k >= 1)
        def _():
            finish(k - 1)

        pl.when(k == plan.local // 4)(scatter.second)
        pl.when(k == plan.local // 2 + 1)(scatter.third)
        return carry

    lax.fori_loop(0, plan.local, step, 0)
    for i in range(plan.blocks):
        rows = slice(BLOCK * i, BLOCK * (i + 1))
        moved = acc_odd[BLOCK * i + 1 : BLOCK * (i + 1) + 1, :]
        both = (acc_even[rows, :] + moved).astype(BF)
        du_buf[0, rows, :] = both[:, :jb]
        du_buf[1, rows, :] = both[:, jb:]

        def give(r, carry, i=i):
            peer = BLOCK // half * i + r
            src = du_buf.at[:, pl.ds(half * peer, half), :]

            @pl.when(peer == chip)
            def _():
                pltpu.make_async_copy(src, land.at[chip], d_recv).start()

            @pl.when(peer != chip)
            def _():
                push(src, land.at[chip], d_send, d_recv, (section, peer)).start()

            return carry

        lax.fori_loop(0, BLOCK // half, give, 0)
    finish(plan.local - 1)
    tap_swap.wait()
    total_t[...] = (kept_t[...] + take_t[...].astype(F32)).astype(BF)
    if plan.routed:

        @pl.when(jnp.logical_and(section == 0, my_group == 0))
        def _():
            for tap in range(ORDER):
                piece_copies(tap, True, True)
    else:
        pltpu.sync_copy(total_m, dmap_ref)
        pltpu.sync_copy(total_t, dtap_ref)
    bytes_of(g_buf.at[0, pl.ds(0, 2 * half * (chips - 1) // 2), :], g_send)
    bytes_of(g_buf.at[1, pl.ds(0, 2 * half * (chips - 1) // 2), :], g_send)
    bytes_of(land, d_recv)
    for b in range(plan.cols_in):
        total = None
        for c in range(plan.groups):
            for a in range(plan.cols_out):
                term = land[a + plan.cols_out * (b + plan.cols_in * c)].astype(F32)
                total = term if total is None else total + term
        du_ref[:, :, b * jb : (b + 1) * jb] = total
    bytes_of(land.at[pl.ds(0, chips - 1)], d_send)
    scatter.end()
    if plan.routed:

        def drain(k, carry):
            piece_copies(k, False, False)
            return carry

        lax.fori_loop(0, plan.local, drain, 0)

        @pl.when(jnp.logical_and(section == 0, my_group == 0))
        def _():
            for tap in range(ORDER):
                piece_copies(tap, True, False)

        bytes_of(dmaps_ref, w_recv)


def backward_call(plan, g, filt, v, pq, tapw, x, xs, grads):
    chips, half, jb, ia = plan.chips, plan.half, plan.jb, plan.ia
    any_spec = pl.BlockSpec(memory_space=pl.ANY)
    vmem_spec = pl.BlockSpec(memory_space=pltpu.VMEM)
    dma = pltpu.SemaphoreType.DMA
    shapes = [g_part.shape[3:] for g_part in grads]
    out_shape = [jax.ShapeDtypeStruct(shape, F32) for shape in shapes]
    out_shape.append(jax.ShapeDtypeStruct((2, half, plan.width), F32))
    if plan.routed:
        out_shape.append(jax.ShapeDtypeStruct((plan.map_rows, plan.width), BF))
    else:
        out_shape.append(jax.ShapeDtypeStruct((plan.local, jb, ia), BF))
        out_shape.append(jax.ShapeDtypeStruct((ORDER * jb, ia), BF))
    return pl.pallas_call(
        functools.partial(backward_kernel, plan),
        out_shape=out_shape,
        in_specs=[vmem_spec, vmem_spec, any_spec, vmem_spec, vmem_spec, any_spec, any_spec]
        + [vmem_spec] * 3,
        out_specs=[vmem_spec] * 4 + [any_spec] * (len(out_shape) - 4),
        scratch_shapes=Scatter.scratch(plan, shapes)
        + [dma((3, 6)), dma((3, 6))]
        + [
            pltpu.VMEM((2, plan.length, ia), BF),
            pltpu.VMEM((2, ia, plan.length), BF),
            pltpu.VMEM((2, plan.f_rows, plan.length + BLOCK), F32),
            pltpu.VMEM((2 * plan.local, BLOCK, plan.length), BF),
            pltpu.VMEM((2, 2, plan.length, 2 * jb), BF),
            pltpu.VMEM((plan.length, 2 * jb), BF),
            pltpu.VMEM((plan.length, 2 * jb), BF),
            pltpu.VMEM((plan.length, 2 * jb), F32),
            pltpu.VMEM((plan.length + 8, 2 * jb), F32),
            pltpu.VMEM((plan.local, jb, ia), F32),
            pltpu.VMEM((plan.local, jb, ia), BF),
            pltpu.VMEM((plan.local, jb, ia), BF),
            pltpu.VMEM((plan.local, jb, ia), BF),
            pltpu.VMEM((ORDER * jb, ia), F32),
            pltpu.VMEM((ORDER * jb, ia), BF),
            pltpu.VMEM((ORDER * jb, ia), BF),
            pltpu.VMEM((ORDER * jb, ia), BF),
            pltpu.VMEM((2, plan.length, jb), BF),
            pltpu.VMEM((chips, 2, half, jb), BF),
            dma,
            dma,
            dma((2,)),
            dma((plan.local,)),
            dma((plan.local,)),
            dma,
            dma,
            dma,
            dma,
            dma,
            dma,
            dma((2,)),
        ],
        compiler_params=pltpu.CompilerParams(
            collective_id=3, has_side_effects=True, vmem_limit_bytes=VMEM_LIMIT
        ),
        name="spectral_backward",
    )(g, filt, v, pq, tapw, x, xs, *grads)


def swapped(block):
    return lax.ppermute(block, "section", [(0, 1), (1, 0)])


def shifted(block, axis, distance):
    devices = range(lax.axis_size(axis))
    route = [(i - distance, i) for i in devices if i - distance in devices]
    return lax.ppermute(block, axis, route)


def dot(formula, left, right):
    return jnp.einsum(formula, left, right, preferred_element_type=F32)


def norm_forward(values, weights):
    factor = lax.rsqrt(jnp.mean(values * values, axis=-1, keepdims=True) + EPSILON)
    return (values * factor * weights, factor)


def norm_backward(values, factor, weights, upstream):
    weighted = upstream * weights
    gain_grad = jnp.sum(upstream * values * factor, axis=0)
    correction = jnp.mean(weighted * values, axis=-1, keepdims=True)
    return (factor * weighted - values * factor * factor * factor * correction, gain_grad)


def mlp_forward(middle, gain, weights):
    w_gate, w_up, w_down = weights
    rows = middle.shape[0]
    normed, factor = norm_forward(middle, gain)
    own = normed.astype(BF)
    inputs = jnp.concatenate([own, swapped(own)], 0)
    gate_rows = dot("td,df->tf", inputs, w_gate)
    up_rows = dot("td,df->tf", inputs, w_up)
    active = (jax.nn.silu(gate_rows) * up_rows).astype(BF)
    part = dot("tf,fd->td", active, w_down)
    branch = part[:rows] + swapped(part[rows:].astype(BF)).astype(F32)
    return branch, (factor, inputs, gate_rows, up_rows, active)


def mlp_backward(middle, gain, weights, saved, upstream, branch_grad):
    w_gate, w_up, w_down = weights
    rows = middle.shape[0]
    factor, inputs, gate_rows, up_rows, active = saved
    down_grad = dot("tf,td->fd", active, branch_grad)
    active_grad = dot("td,fd->tf", branch_grad, w_down)
    sigmoid = jax.nn.sigmoid(gate_rows)
    slope = sigmoid * (1.0 + gate_rows * (1.0 - sigmoid))
    gate_grad = (active_grad * up_rows * slope).astype(BF)
    up_grad = (active_grad * gate_rows * sigmoid).astype(BF)
    gate_w_grad = dot("td,tf->df", inputs, gate_grad)
    up_w_grad = dot("td,tf->df", inputs, up_grad)
    part = dot("tf,df->td", gate_grad, w_gate) + dot("tf,df->td", up_grad, w_up)
    normed_grad = part[:rows] + swapped(part[rows:].astype(BF)).astype(F32)
    middle_grad, gain_grad = norm_backward(middle, factor, gain, normed_grad)
    return upstream + middle_grad, gain_grad, (gate_w_grad, up_w_grad, down_grad)


def body(
    io_pair, lengths, filters, stu_maps, attn_proj, attn_out, norm_gains, mlp_gate, mlp_up, mlp_down
):
    chips = lax.axis_size("seq")
    section, chip = spot()
    core_zero = section == 0
    tok_rows = io_pair.shape[2]
    width = io_pair.shape[3]
    half = tok_rows // 2
    heads = width // HEAD_DIM
    reach = WINDOW // tok_rows
    score_scale = HEAD_DIM ** (-0.5)
    plan = Plan(chips, tok_rows, width, filters.shape[1], stu_maps.shape[0])

    sib_io, sib_gate, sib_up, sib_down, sib_proj, sib_out, gains_all = entry_call(
        chips,
        [io_pair[0], mlp_gate[0], mlp_up[0], mlp_down[0], attn_proj, attn_out],
        norm_gains[0],
    )
    gains = jnp.transpose(gains_all, (0, 2, 1, 3)).reshape(2, 2, width).astype(F32)

    def split_phases(rows):
        return (
            rows.reshape(rows.shape[:-2] + (half, 2, width))
            .swapaxes(-3, -2)
            .reshape(rows.shape)
        )

    def join_phases(rows):
        return rows.reshape(2, half, width).swapaxes(0, 1).reshape(rows.shape)

    local = jnp.arange(tok_rows, dtype=jnp.int32)
    order = 2 * (local % half) + local // half
    places = chip * tok_rows + order
    own_length = jnp.where(core_zero, lengths[0], lengths[1])
    other_length = jnp.where(core_zero, lengths[1], lengths[0])
    mask_rows = (places < own_length).astype(F32)[:, None]
    other_mask = (places < other_length).astype(F32)[:, None]
    x = split_phases(jnp.where(core_zero, io_pair[0, 0], sib_io[1]))
    cot_pair = jnp.where(core_zero, sib_io, io_pair[0])
    cot = split_phases(jnp.where(core_zero, cot_pair[0], cot_pair[1]))
    cot_other = split_phases(jnp.where(core_zero, cot_pair[1], cot_pair[0]))
    hidden = x.astype(F32) * mask_rows
    normed, spectral_factor = norm_forward(hidden, gains[0, 0])
    u = normed.astype(BF)
    u_parts = jnp.transpose(
        u.reshape(2, half, plan.cols_in, plan.jb), (2, 1, 0, 3)
    ).reshape(plan.cols_in, half, 2 * plan.jb)

    lags = jnp.transpose(filters.reshape(half, 2, plan.filters), (2, 1, 0))
    lags = jnp.stack([lags[:, :, ::-1], lags], 0).reshape(
        2, plan.groups, plan.local, 2 * half
    )
    lags = jnp.pad(lags, ((0, 0), (0, 0), (0, plan.f_rows - plan.local), (0, LANES - 2 * half)))
    packed = jnp.transpose(lags, (1, 0, 2, 3)).reshape(plan.groups, 2 * plan.f_rows, LANES)

    my_a = chip % plan.cols_out
    my_b = (chip // plan.cols_out) % plan.cols_in
    my_group = chip // (plan.cols_out * plan.cols_in)
    if plan.routed:
        maps = [stu_maps]
    else:
        whole = lax.all_gather(stu_maps, ("section", "seq"), axis=0, tiled=True)
        whole = lax.dynamic_slice(
            whole.reshape(-1, width, width),
            (0, my_b * plan.jb, my_a * plan.ia),
            (whole.shape[0] // width, plan.jb, plan.ia),
        )
        pair = whole[: 2 * plan.filters].reshape(2, plan.filters, plan.jb, plan.ia)
        pair = lax.dynamic_slice_in_dim(pair, my_group * plan.local, plan.local, 1)
        taps = jnp.where(my_group == 0, whole[2 * plan.filters :], 0).astype(BF)
        maps = [
            jnp.where(core_zero, pair[0], pair[1]),
            jnp.where(core_zero, pair[1], pair[0]),
            taps.reshape(-1, plan.ia),
        ]

    ff = mlp_gate.shape[2]
    ff_rows = mlp_down.shape[1]
    ff_half = ff_rows // 2

    def my_half(layer):
        mine = core_zero == (layer == 0)
        gate, up, down = (
            jnp.where(mine, own, theirs)
            for own, theirs in (
                (mlp_gate[0], sib_gate),
                (mlp_up[0], sib_up),
                (mlp_down[0], sib_down),
            )
        )

        def pick(w):
            w = w.reshape(w.shape[0], chips, 2, ff_half)
            return jnp.where(core_zero, w[:, :, 0], w[:, :, 1]).reshape(w.shape[0], -1)

        return pick(gate), pick(up), jnp.where(core_zero, down[:ff_half], down[ff_half:])

    results = forward_call(plan, u_parts, packed, my_half(0), maps)
    layer0 = tuple(w.reshape(-1, w.shape[-1]) for w in results[:3])
    conv, v, pq, tapw, x_all, xs_all, filt = results[3:]
    gate1, up1, down1 = my_half(1)
    proj_rows = attn_proj.shape[0]
    out_rows = attn_out.shape[0]
    both_rows = jnp.concatenate(
        [
            jnp.where(core_zero, attn_proj, sib_proj),
            jnp.where(core_zero, sib_proj, attn_proj),
            jnp.where(core_zero, attn_out, sib_out),
            jnp.where(core_zero, sib_out, attn_out),
            down1,
        ],
        0,
    )
    gate_rows = gate1.shape[0]
    pieces = [both_rows]
    for w in (gate1, up1):
        pieces += [w[:, :width], w[:, width:]]
    attn_all = lax.all_gather(jnp.concatenate(pieces, 0), "seq", axis=0, tiled=False)
    at = both_rows.shape[0]
    columns = [attn_all[:, at + gate_rows * i : at + gate_rows * (i + 1)] for i in range(4)]
    columns = [c.reshape(-1, width) for c in columns]
    layer1 = (
        jnp.concatenate(columns[:2], 1),
        jnp.concatenate(columns[2:], 1),
        attn_all[:, at - ff_half : at].reshape(-1, width),
    )
    w_proj = jnp.swapaxes(
        attn_all[:, : 2 * proj_rows].reshape(chips, 2, proj_rows, width), 0, 1
    ).reshape(3, width, width)
    w_out = jnp.swapaxes(
        attn_all[:, 2 * proj_rows : 2 * (proj_rows + out_rows)].reshape(chips, 2, out_rows, width), 0, 1
    ).reshape(width, width)

    middle0 = hidden + conv.reshape(tok_rows, width)
    branch0, saved0 = mlp_forward(middle0, gains[0, 1], layer0)
    passed = (mask_rows * (middle0 + branch0)).astype(BF)

    window_hidden = passed.astype(F32)
    window_normed, window_factor = norm_forward(window_hidden, gains[1, 0])
    inputs = window_normed.astype(BF)
    triple = dot("td,wde->wte", inputs, w_proj).astype(BF)
    key_value = triple[1:]
    parts = [shifted(key_value, "seq", distance) for distance in range(reach, 0, -1)]
    windows = jnp.concatenate(parts + [key_value], 1)
    key_window = windows[0].reshape(-1, heads, HEAD_DIM)
    value_window = windows[1].reshape(-1, heads, HEAD_DIM)
    queries = triple[0].reshape(tok_rows, heads, HEAD_DIM)
    scores = dot("qhe,khe->hqk", queries, key_window) * score_scale
    key_place = (
        (chip - reach + jnp.arange(reach + 1, dtype=jnp.int32))[:, None] * tok_rows + order[None, :]
    ).reshape(-1)
    distance_rows = places[:, None] - key_place[None, :]
    allowed = (key_place[None, :] >= 0) & (distance_rows >= 0) & (distance_rows < WINDOW)
    scores = jnp.where(allowed[None], scores, BIG_NEGATIVE)
    highest = jnp.max(scores, axis=-1, keepdims=True)
    weights = jnp.exp(scores - highest)
    weights = weights / jnp.sum(weights, axis=-1, keepdims=True)
    weights_low = weights.astype(BF)
    attended = dot("hqk,khe->qhe", weights_low, value_window)
    attended = attended.reshape(tok_rows, width).astype(BF)
    middle1 = window_hidden + dot("td,de->te", attended, w_out)
    branch1, saved1 = mlp_forward(middle1, gains[1, 1], layer1)
    block_out = (mask_rows * (middle1 + branch1)).astype(BF)

    upstream1 = cot.astype(F32) * mask_rows
    other_upstream = cot_other.astype(F32) * other_mask
    grad_pair = jnp.concatenate([upstream1, other_upstream], 0).astype(BF)
    middle1_grad, gain11, mlp1_grads = mlp_backward(
        middle1, gains[1, 1], layer1, saved1, upstream1, grad_pair
    )
    output_input = middle1_grad.astype(BF)
    output_grad = dot("td,te->de", attended, output_input)
    attended_grad = dot("te,de->td", output_input, w_out)
    attended_grad = attended_grad.astype(BF).reshape(tok_rows, heads, HEAD_DIM)
    value_grad = dot("hqk,qhe->khe", weights_low, attended_grad)
    weight_grad = dot("qhe,khe->hqk", attended_grad, value_window)
    row_total = jnp.sum(weights * weight_grad, axis=-1, keepdims=True)
    score_grad = (weights * (weight_grad - row_total)).astype(BF)
    query_grad = dot("hqk,khe->qhe", score_grad, key_window) * score_scale
    key_grad = dot("hqk,qhe->khe", score_grad, queries) * score_scale
    pair_grad = jnp.stack([key_grad.reshape(-1, width), value_grad.reshape(-1, width)])
    own_pair = pair_grad[:, reach * tok_rows :]
    for distance in range(reach, 0, -1):
        offset = (reach - distance) * tok_rows
        back = shifted(pair_grad[:, offset : offset + tok_rows].astype(BF), "seq", -distance)
        own_pair = own_pair + back.astype(F32)
    triple_grad = jnp.concatenate([query_grad.reshape(1, tok_rows, width), own_pair], 0).astype(BF)
    proj_grad = dot("td,wte->wde", inputs, triple_grad).reshape(3 * width, width)
    normed_grad = dot("wte,wde->td", triple_grad, w_proj)
    hidden1_grad, gain10 = norm_backward(window_hidden, window_factor, gains[1, 0], normed_grad)
    passed_grad = (middle1_grad + hidden1_grad).astype(BF)

    upstream0 = passed_grad.astype(F32) * mask_rows
    own_branch = upstream0.astype(BF)
    branch_pair = jnp.concatenate([own_branch, swapped(own_branch)], 0)
    middle0_grad, gain01, mlp0_grads = mlp_backward(
        middle0, gains[0, 1], layer0, saved0, upstream0, branch_pair
    )
    g = middle0_grad.astype(BF).reshape(2, half, width)
    grid = (plan.depth, plan.side, plan.side)
    blocks0 = [
        w.astype(BF).reshape(grid + (w.shape[0] // chips, w.shape[1])) for w in mlp0_grads
    ]
    results = backward_call(plan, g, filt, v, pq, tapw, x_all, xs_all, blocks0)
    half0, results = results[:3], results[3:]
    signal_grad = results[0].reshape(tok_rows, width)
    if plan.routed:
        maps_grad = results[1].astype(F32)
    else:
        piece, tap_piece = (r.astype(F32) for r in results[1:])
        full = jnp.zeros((2, plan.filters, width, width), F32)
        full = lax.dynamic_update_slice(
            full,
            piece[None],
            (section, my_group * plan.local, my_b * plan.jb, my_a * plan.ia),
        )
        tap_piece = jnp.where(core_zero & (my_group == 0), tap_piece, 0.0)
        tap_full = lax.dynamic_update_slice(
            jnp.zeros((ORDER, width, width), F32),
            tap_piece.reshape(ORDER, plan.jb, plan.ia),
            (0, my_b * plan.jb, my_a * plan.ia),
        )
        full = jnp.concatenate([full.reshape(-1, width), tap_full.reshape(-1, width)], 0)
        maps_grad = lax.psum_scatter(full, ("section", "seq"), scatter_dimension=0, tiled=True)
    hidden_grad, gain00 = norm_backward(hidden, spectral_factor, gains[0, 0], signal_grad)
    inputs_grad = (mask_rows * (middle0_grad + hidden_grad)).astype(BF)

    proj_blocks = jnp.swapaxes(proj_grad.reshape(2, chips, proj_rows, width), 0, 1)
    out_blocks = jnp.swapaxes(output_grad.reshape(2, chips, out_rows, width), 0, 1)
    pieces = [
        proj_blocks.reshape(chips, 2 * proj_rows, width),
        out_blocks.reshape(chips, 2 * out_rows, width),
        mlp1_grads[2].reshape(chips, ff_half, width),
    ]
    for w in mlp1_grads[:2]:
        w = w.reshape(chips, gate_rows, 2 * width)
        pieces += [w[:, :, :width], w[:, :, width:]]
    packed_grads = jnp.concatenate([p.astype(BF) for p in pieces], 1)
    summed = lax.psum_scatter(packed_grads, "seq", scatter_dimension=0, tiled=False)
    columns = [summed[at + gate_rows * i : at + gate_rows * (i + 1)] for i in range(4)]
    half1 = [
        jnp.concatenate(columns[:2], 1),
        jnp.concatenate(columns[2:], 1),
        summed[at - ff_half : at],
    ]
    attn_parts = summed[: 2 * (proj_rows + out_rows)]
    low_part = jnp.concatenate(
        [attn_parts[:proj_rows], attn_parts[2 * proj_rows : 2 * proj_rows + out_rows]], 0
    )
    high_part = jnp.concatenate(
        [attn_parts[proj_rows : 2 * proj_rows], attn_parts[2 * proj_rows + out_rows :]], 0
    )
    attn_keep = jnp.where(core_zero, low_part, high_part).astype(F32)
    attn_take = swapped(jnp.where(core_zero, high_part, low_part)).astype(F32)
    attn_sum = attn_keep + attn_take
    proj_out, out_out = attn_sum[:proj_rows], attn_sum[proj_rows:]
    outs = []
    for index in range(3):
        zero, one = half0[index].astype(BF), half1[index]
        keep = jnp.where(core_zero, zero, one)
        take = swapped(jnp.where(core_zero, one, zero))
        low = jnp.where(core_zero, keep, take).astype(F32)
        high = jnp.where(core_zero, take, keep).astype(F32)
        if index < 2:
            rows = low.shape[0]
            joined = jnp.stack(
                [low.reshape(rows, chips, ff_half), high.reshape(rows, chips, ff_half)], 2
            ).reshape(rows, ff)
        else:
            joined = jnp.concatenate([low, high], 0)
        outs.append(joined[None])

    gain_parts = jnp.stack([jnp.stack([gain00, gain01]), jnp.stack([gain10, gain11])])
    gain_cols = width // chips
    tiles = jnp.transpose(gain_parts.reshape(2, 2, chips, gain_cols), (0, 2, 1, 3))
    tiles = jnp.pad(
        tiles.reshape(2 * chips, 2, gain_cols), ((0, 0), (0, 6), (0, LANES - gain_cols))
    )
    done_in, done_out = join_phases(inputs_grad), join_phases(block_out)
    taken, landed = exit_call(chips, jnp.where(core_zero, done_out, done_in), tiles)
    first = jnp.where(core_zero, done_in, taken)
    second = jnp.where(core_zero, taken, done_out)
    result_pair = jnp.stack([first, second])[None]
    gain_out = jnp.sum(landed, axis=0)[None, :2, :gain_cols]
    return (result_pair, maps_grad, proj_out, out_out, gain_out, outs[0], outs[1], outs[2])


def solution(mesh):
    placed = (
        P("section", None, "seq", None),
        P(),
        P("seq", None),
        P(("section", "seq"), None),
        P(("section", "seq"), None),
        P(("section", "seq"), None),
        P("section", None, "seq"),
        P("section", "seq", None),
        P("section", "seq", None),
        P("section", "seq", None),
    )
    return jax.shard_map(
        body,
        mesh=mesh,
        in_specs=placed,
        out_specs=(
            P("section", None, "seq", None),
            P(("section", "seq"), None),
            P(("section", "seq"), None),
            P(("section", "seq"), None),
            P("section", None, "seq"),
            P("section", "seq", None),
            P("section", "seq", None),
            P("section", "seq", None),
        ),
        check_vma=False,
    )
```

```python
import functools
import math

import jax
import jax.numpy as jnp
from jax import lax
from jax.experimental import pallas as pl
from jax.experimental.pallas import tpu as pltpu
from jax.sharding import PartitionSpec as P

ORDER = 3
HEAD_DIM = 64
WINDOW = 512
EPSILON = 1e-05
BIG_NEGATIVE = -1e30
MESH = pl.DeviceIdType.MESH
BF = jnp.bfloat16
F32 = jnp.float32
LANES = 128
BLOCK = 256
PIECE = 16
VMEM_LIMIT = 63 * 1024 * 1024


class Plan:
    def __init__(self, chips, tok_rows, width, filter_count, map_rows, ff):
        self.chips = chips
        self.rows = tok_rows
        self.half = tok_rows // 2
        self.width = width
        self.filters = filter_count
        self.cols_in = 4
        self.cols_out = max(1, math.isqrt(chips // 4))
        self.groups = chips // (self.cols_in * self.cols_out)
        self.local = filter_count // self.groups
        self.length = chips * self.half
        self.blocks = self.length // BLOCK
        self.jb = width // self.cols_in
        self.ia = width // self.cols_out
        self.map_rows = map_rows
        self.routed = map_rows % PIECE == 0
        self.pieces = map_rows // PIECE
        self.f_rows = -(-self.local // 16) * 16
        self.ff = ff
        self.pick_here = ff // chips == LANES
        self.side = max(1, math.isqrt(chips // 4))
        self.depth = chips // (self.side * self.side)

    def place(self, chip):
        return (
            chip // (self.side * self.side),
            lax.rem(chip // self.side, self.side),
            lax.rem(chip, self.side),
        )

    def chip_at(self, z, y, x):
        return (z * self.side + y) * self.side + x

    def routes(self, rows, index=0):
        if rows % (2 * PIECE) == 0:
            return [(0, rows // 2, True), (rows // 2, rows // 2, False)]
        return [(0, rows, index % 2 == 0)]


def spot():
    return lax.axis_index("section"), lax.axis_index("seq")


def greet_everyone(chips):
    section, chip = spot()
    me = section * chips + chip
    barrier = pltpu.get_barrier_semaphore()

    def one(step, carry):
        peer = lax.rem(me + step, 2 * chips)
        pl.semaphore_signal(
            barrier, inc=1, device_id=(peer // chips, lax.rem(peer, chips)), device_id_type=MESH
        )
        return carry

    lax.fori_loop(1, 2 * chips, one, 0)

    def wait():
        pl.semaphore_wait(barrier, 2 * chips - 1)

    return wait


def push(src, dst, send, recv, target):
    return pltpu.make_async_remote_copy(
        src_ref=src,
        dst_ref=dst,
        send_sem=send,
        recv_sem=recv,
        device_id=target,
        device_id_type=MESH,
    )


def bytes_of(ref, sem):
    pltpu.make_async_copy(ref, ref, sem).wait()


def rows_dot(left, right):
    return lax.dot_general(left, right, (((1,), (1,)), ((), ())), preferred_element_type=F32)


def cols_dot(left, right):
    return lax.dot_general(left, right, (((0,), (0,)), ((), ())), preferred_element_type=F32)


def flat_dot(left, right):
    return jnp.dot(left, right, preferred_element_type=F32)


class Gather:
    def __init__(self, plan, shards, outs, send, recv):
        self.plan, self.shards, self.outs = plan, shards, outs
        self.send, self.recv = send, recv
        self.section, chip = spot()
        self.z, self.y, self.x = plan.place(chip)

    def to(self, z, y, x):
        return self.section, self.plan.chip_at(z, y, x)

    def parts(self, i):
        for number, (start, rows, x_first) in enumerate(self.plan.routes(self.shards[i].shape[0], i)):
            out = self.outs[i]
            sl = pl.ds(start, rows)
            yield number, x_first, out, sl

    def begin(self):
        plan = self.plan
        for i, shard in enumerate(self.shards):
            spot_ref = self.outs[i].at[self.z, self.y, self.x]
            for step in range(1, plan.depth):
                z = lax.rem(self.z + step, plan.depth)
                push(
                    shard, spot_ref, self.send.at[i, 0], self.recv.at[i, 0], self.to(z, self.y, self.x)
                ).start()
            pltpu.make_async_copy(shard, spot_ref, self.recv.at[i, 0]).start()

    def second(self):
        side = self.plan.side
        for i in range(len(self.shards)):
            bytes_of(self.outs[i].at[:, self.y, self.x], self.recv.at[i, 0])
            for number, x_first, out, sl in self.parts(i):
                src = out.at[:, self.y, self.x, sl]
                for step in range(1, side):
                    if x_first:
                        peer = self.to(self.z, self.y, lax.rem(self.x + step, side))
                    else:
                        peer = self.to(self.z, lax.rem(self.y + step, side), self.x)
                    push(
                        src, src, self.send.at[i, 1 + number], self.recv.at[i, 1 + number], peer
                    ).start()

    def third(self):
        side = self.plan.side
        for i in range(len(self.shards)):
            for number, x_first, out, sl in self.parts(i):
                sem = self.recv.at[i, 1 + number]
                if x_first:
                    bytes_of(out.at[:, self.y, pl.ds(0, side - 1), sl], sem)
                    src = out.at[:, self.y, :, sl]
                else:
                    bytes_of(out.at[:, pl.ds(0, side - 1), self.x, sl], sem)
                    src = out.at[:, :, self.x, sl]
                for step in range(1, side):
                    if x_first:
                        peer = self.to(self.z, lax.rem(self.y + step, side), self.x)
                    else:
                        peer = self.to(self.z, self.y, lax.rem(self.x + step, side))
                    push(
                        src, src, self.send.at[i, 3 + number], self.recv.at[i, 3 + number], peer
                    ).start()

    def end(self):
        plan = self.plan
        side = plan.side
        for i in range(len(self.shards)):
            bytes_of(self.outs[i].at[pl.ds(0, plan.depth - 1), 0, 0], self.send.at[i, 0])
            for number, x_first, out, sl in self.parts(i):
                bytes_of(out.at[:, 0, pl.ds(0, side - 1), sl], self.send.at[i, 1 + number])
                last = out.at[:, :, pl.ds(0, side - 1), sl]
                bytes_of(last, self.recv.at[i, 3 + number])
                bytes_of(last, self.send.at[i, 3 + number])


class Scatter:
    @staticmethod
    def scratch(plan, shapes):
        refs = []
        for index, (rows, cols) in enumerate(shapes):
            for _, part, _ in plan.routes(rows, index):
                for lead in (
                    (plan.side - 1, plan.depth, plan.side),
                    (plan.depth, plan.side),
                    (plan.side - 1, plan.depth),
                    (plan.depth,),
                    (plan.depth - 1,),
                ):
                    refs.append(pltpu.VMEM(lead + (part, cols), BF))
        return refs

    def __init__(self, plan, grads, outs, buffers, send, recv):
        self.plan, self.grads, self.outs = plan, grads, outs
        self.send, self.recv = send, recv
        self.section, chip = spot()
        self.z, self.y, self.x = plan.place(chip)
        self.work = []
        buffers = list(buffers)
        for i, grad in enumerate(grads):
            for number, (start, rows, x_first) in enumerate(plan.routes(grad.shape[3], i)):
                self.work.append((i, number, start, rows, x_first, buffers[:5]))
                buffers = buffers[5:]

    def to(self, z, y, x):
        return self.section, self.plan.chip_at(z, y, x)

    def begin(self):
        side = self.plan.side
        for i, number, start, rows, x_first, (land, *_) in self.work:
            grad, sl = self.grads[i], pl.ds(start, rows)
            for step in range(1, side):
                if x_first:
                    y = lax.rem(self.y + step, side)
                    src, peer = grad.at[:, y, :, sl], self.to(self.z, y, self.x)
                else:
                    x = lax.rem(self.x + step, side)
                    src, peer = grad.at[:, :, x, sl], self.to(self.z, self.y, x)
                push(
                    src, land.at[step - 1], self.send.at[i, number], self.recv.at[i, number], peer
                ).start()

    def second(self):
        plan, side = self.plan, self.plan.side
        for i, number, start, rows, x_first, (land, part, land2, *_) in self.work:
            grad = self.grads[i]
            bytes_of(land, self.recv.at[i, number])

            def one(index, carry, grad=grad, land=land, part=part, start=start, rows=rows, x_first=x_first):
                z, j = index // side, lax.rem(index, side)
                y, x = (self.y, j) if x_first else (j, self.x)
                total = grad[z, y, x, start : start + rows, :].astype(F32)
                for step in range(side - 1):
                    total = total + land[step, z, j].astype(F32)
                part[z, j] = total.astype(BF)
                return carry

            lax.fori_loop(0, plan.depth * side, one, 0)
            for step in range(1, side):
                if x_first:
                    j = lax.rem(self.x + step, side)
                    peer = self.to(self.z, self.y, j)
                else:
                    j = lax.rem(self.y + step, side)
                    peer = self.to(self.z, j, self.x)
                push(
                    part.at[:, j],
                    land2.at[step - 1],
                    self.send.at[i, 2 + number],
                    self.recv.at[i, 2 + number],
                    peer,
                ).start()

    def third(self):
        plan, side = self.plan, self.plan.side
        for i, number, start, rows, x_first, (_, part, land2, line, land3) in self.work:
            bytes_of(land2, self.recv.at[i, 2 + number])
            mine = self.x if x_first else self.y

            def one(z, carry, part=part, land2=land2, line=line, mine=mine):
                total = part[z, mine].astype(F32)
                for step in range(side - 1):
                    total = total + land2[step, z].astype(F32)
                line[z] = total.astype(BF)
                return carry

            lax.fori_loop(0, plan.depth, one, 0)
            for step in range(1, plan.depth):
                z = lax.rem(self.z + step, plan.depth)
                push(
                    line.at[z],
                    land3.at[step - 1],
                    self.send.at[i, 4 + number],
                    self.recv.at[i, 4 + number],
                    self.to(z, self.y, self.x),
                ).start()

    def end(self):
        for i, number, start, rows, x_first, (land, part, land2, line, land3) in self.work:
            bytes_of(land3, self.recv.at[i, 4 + number])
            total = line[self.z].astype(F32)
            for step in range(self.plan.depth - 1):
                total = total + land3[step].astype(F32)
            self.outs[i][start : start + rows, :] = total
            bytes_of(land, self.send.at[i, number])
            bytes_of(land2, self.send.at[i, 2 + number])
            bytes_of(land3, self.send.at[i, 4 + number])


def exit_kernel(chips, give, tiles, take, land, send, recv, gain_send, gain_recv):
    section, chip = spot()
    me = section * chips + chip
    greet_everyone(chips)()
    swap = push(give, take, send, recv, (1 - section, chip))
    swap.start()

    def one(step, carry):
        peer = lax.rem(me + step, 2 * chips)
        push(
            tiles.at[peer],
            land.at[me],
            gain_send,
            gain_recv,
            (peer // chips, lax.rem(peer, chips)),
        ).start()
        return carry

    lax.fori_loop(1, 2 * chips, one, 0)
    pltpu.make_async_copy(tiles.at[me], land.at[me], gain_recv).start()
    bytes_of(land, gain_recv)
    bytes_of(land.at[pl.ds(0, 2 * chips - 1)], gain_send)
    swap.wait()


def exit_call(chips, give, tiles):
    any_spec = pl.BlockSpec(memory_space=pl.ANY)
    return pl.pallas_call(
        functools.partial(exit_kernel, chips),
        out_shape=[
            jax.ShapeDtypeStruct(give.shape, give.dtype),
            jax.ShapeDtypeStruct(tiles.shape, tiles.dtype),
        ],
        in_specs=[any_spec] * 2,
        out_specs=[any_spec] * 2,
        scratch_shapes=[
            pltpu.SemaphoreType.DMA,
            pltpu.SemaphoreType.DMA,
            pltpu.SemaphoreType.DMA,
            pltpu.SemaphoreType.DMA,
        ],
        compiler_params=pltpu.CompilerParams(collective_id=4, has_side_effects=True),
        name="leave",
    )(give, tiles)


def filter_rows(plan, land, table, first_row, backward):
    lane = lax.broadcasted_iota(jnp.int32, (plan.f_rows, LANES), 1)
    low = lane < plan.half
    total = plan.length // LANES
    for m in range(total):
        if backward:
            one, two = 2 * m, 2 * m + 1
        else:
            one, two = plan.chips - 1 - 2 * m, plan.chips - 2 - 2 * m
        left = land[one, first_row : first_row + plan.f_rows, :].astype(F32)
        right = land[two, first_row : first_row + plan.f_rows, :].astype(F32)
        even = jnp.where(low, left, pltpu.roll(right, plan.half, 1))
        odd = jnp.where(low, pltpu.roll(left, plan.half, 1), right)
        at = LANES * m + (BLOCK if backward else 0)
        table[0, :, at : at + LANES] = even
        table[1, :, at : at + LANES] = odd
    blank = jnp.zeros((plan.f_rows, BLOCK), F32)
    at = 0 if backward else plan.length
    for parity in range(2):
        table[parity, :, at : at + BLOCK] = blank


def build_strips(plan, table, strip, backward):
    span = plan.length + BLOCK
    shift = span - LANES if backward else span - (LANES - 1)
    part = 32

    def one(k, carry):
        for parity in range(2):
            row = table[parity, pl.ds(k, 1), :]
            for start in range(0, LANES, part):
                spread = jnp.broadcast_to(row, (part, span))
                rolled = pltpu.roll(
                    spread, (shift + start) % span, 1, stride=1, stride_axis=0
                ).astype(BF)
                strip[2 * k + parity, LANES + start : LANES + start + part, :] = rolled[
                    :, : plan.length
                ]
                strip[2 * k + parity, start : start + part, :] = rolled[
                    :, LANES : LANES + plan.length
                ]
        return carry

    lax.fori_loop(0, plan.local, one, 0)


def owner_pieces(plan, act, first=0, last=None):
    section, chip = spot()
    dev = section * plan.chips + chip
    per_map = plan.width // PIECE
    per_block = plan.jb // PIECE

    def unit(m, carry):
        g = plan.pieces * dev + m
        which = g // per_map
        inside = lax.rem(g, per_map)
        b = inside // per_block
        sub = lax.rem(inside, per_block)
        sign = which // plan.filters
        full = lax.rem(which, plan.filters)
        group = full // plan.local
        k = lax.rem(full, plan.local)

        @pl.when(sign < 2)
        def _():
            for a in range(plan.cols_out):
                target = a + plan.cols_out * (b + plan.cols_in * group)
                act(m, False, k, sub, a, sign, target)

        @pl.when(sign >= 2)
        def _():
            for a in range(plan.cols_out):
                for core in range(2):
                    act(m, True, full, sub, a, core, a + plan.cols_out * b)

        return carry

    lax.fori_loop(first, plan.pieces if last is None else last, unit, 0)


def forward_kernel(plan, *refs):
    io_ref, gain_ref, filters_ref, lengths_ref = refs[:4]
    gate_raw, up_raw, down_raw, proj_raw, attn_raw = refs[4:9]
    if plan.routed:
        maps_ref = refs[9]
        rest = refs[10:]
    else:
        mine_ref, other_ref, taps_ref = refs[9:12]
        rest = refs[12:]
    full_weights, rest = rest[:10], rest[10:]
    (
        conv_ref,
        hidden_ref,
        upstream_ref,
        pair_ref,
        gains_ref,
        mask_ref,
        v_ref,
        pq_ref,
        tapw_ref,
        x_ref,
        xs_ref,
        filt_ref,
        io_own,
        io_sib,
        gain_tile,
        gain_land,
        gate_half,
        gate_shard,
        up_half,
        up_shard,
        down_shard,
        proj_shard,
        attn_shard,
        u_ref,
        f_ref,
        x_buf,
        xo_buf,
        xs_buf,
        xf_buf,
        f_land,
        table,
        strip,
        mine,
        other,
        taps,
        pq,
        acc,
        y_buf,
        land,
        stage,
        io_sem,
        gain_send,
        gain_recv,
        s_send,
        s_recv,
        u_send,
        x_recv,
        f_send,
        f_recv,
        m_send,
        m_recv,
        t_recv,
        o_send,
        o_recv,
        c_send,
        c_recv,
        v_sem,
        out_sem,
        w_send,
        w_recv,
    ) = rest
    chips, half, jb, ia, rows_here = plan.chips, plan.half, plan.jb, plan.ia, plan.rows
    section, chip = spot()
    dev = section * chips + chip
    sibling = (1 - section, chip)
    my_group = chip // (plan.cols_out * plan.cols_in)
    greeted = greet_everyone(chips)

    row = lax.broadcasted_iota(jnp.int32, (rows_here, rows_here), 0)
    col = lax.broadcasted_iota(jnp.int32, (rows_here, rows_here), 1)
    order = jnp.where(col == 2 * lax.rem(row, half) + row // half, 1.0, 0.0).astype(BF)
    for i in range(2):
        io_own[i] = flat_dot(order, io_ref[i]).astype(BF)
    cols = gain_ref.shape[1]
    gain_tile[...] = jnp.zeros_like(gain_tile)
    gain_tile[0:2, 0:cols] = gain_ref[...].astype(F32)
    if plan.pick_here:
        lane = lax.broadcasted_iota(jnp.int32, (gate_raw.shape[0], LANES), 1)
        low = lane < half
        for raw, halves, shard in ((gate_raw, gate_half, gate_shard), (up_raw, up_half, up_shard)):
            for j in range(raw.shape[1] // (2 * LANES)):
                one = raw[:, 2 * LANES * j : 2 * LANES * j + LANES].astype(F32)
                two = raw[:, 2 * LANES * j + LANES : 2 * LANES * (j + 1)].astype(F32)
                zero_half = jnp.where(low, one, pltpu.roll(two, half, 1)).astype(BF)
                one_half = jnp.where(low, pltpu.roll(one, half, 1), two).astype(BF)
                at = slice(LANES * j, LANES * (j + 1))
                shard[section, :, at] = jnp.where(section == 0, zero_half, one_half)
                halves[:, at] = jnp.where(section == 0, one_half, zero_half)
    else:
        for raw, halves, shard in ((gate_raw, gate_half, gate_shard), (up_raw, up_half, up_shard)):
            shard[section] = raw[section]
            halves[...] = raw[1 - section]
    part = down_shard.shape[1]
    down_shard[section] = down_raw[pl.ds(pl.multiple_of(part * section, 16), part), :]
    proj_shard[section] = proj_raw[...]
    attn_shard[section] = attn_raw[...]
    greeted()
    io_swap = push(io_own, io_sib, io_sem.at[0], io_sem.at[1], sibling)
    io_swap.start()

    def send_gain(step, carry):
        peer = lax.rem(dev + step, 2 * chips)
        push(
            gain_tile,
            gain_land.at[section, chip],
            gain_send,
            gain_recv,
            (peer // chips, lax.rem(peer, chips)),
        ).start()
        return carry

    lax.fori_loop(1, 2 * chips, send_gain, 0)
    pltpu.make_async_copy(gain_tile, gain_land.at[section, chip], gain_recv).start()
    shares = [
        push(src, dst, s_send.at[i], s_recv.at[i], sibling)
        for i, (src, dst) in enumerate(
            (
                (gate_half, gate_shard.at[section]),
                (up_half, up_shard.at[section]),
                (
                    down_raw.at[pl.ds(pl.multiple_of(part * (1 - section), 16), part), :],
                    down_shard.at[section],
                ),
                (proj_shard.at[section], proj_shard.at[section]),
                (attn_shard.at[section], attn_shard.at[section]),
            )
        )
    ]
    for share in shares:
        share.start()

    if plan.routed:

        def places(m, tap, k, sub, a):
            src = maps_ref.at[pl.ds(PIECE * m, PIECE), pl.ds(a * ia, ia)]
            if tap:
                return src, taps.at[pl.ds(jb * k + PIECE * sub, PIECE), :], t_recv
            return src, mine.at[k, pl.ds(PIECE * sub, PIECE), :], m_recv

        def start_piece(m, tap, k, sub, a, to_section, to_chip):
            src, dst, sem = places(m, tap, k, sub, a)
            here = to_section * chips + to_chip == dev

            @pl.when(here)
            def _():
                pltpu.make_async_copy(src, dst, sem).start()

            @pl.when(jnp.logical_not(here))
            def _():
                push(src, dst, m_send, sem, (to_section, to_chip)).start()

        def drain_piece(m, tap, k, sub, a, to_section, to_chip):
            src, dst, sem = places(m, tap, k, sub, a)

            @pl.when(to_section * chips + to_chip != dev)
            def _():
                push(src, dst, m_send, sem, (to_section, to_chip)).wait_send()

        owner_pieces(plan, start_piece, 0, plan.pieces // 3)

    lag = lax.broadcasted_iota(jnp.int32, (rows_here, LANES), 0)
    lane = lax.broadcasted_iota(jnp.int32, (rows_here, LANES), 1)
    stretch = lax.rem(lane, half)
    backwards = jnp.where(lag == 2 * (half - 1 - stretch) + lane // half, 1.0, 0.0).astype(BF)
    plain = jnp.where(lag == 2 * stretch + lane // half, 1.0, 0.0).astype(BF)
    for group in range(plan.groups):
        source = lax.broadcasted_iota(jnp.int32, (plan.filters, plan.f_rows), 0)
        target = lax.broadcasted_iota(jnp.int32, (plan.filters, plan.f_rows), 1)
        chosen = jnp.where(
            (source == group * plan.local + target) & (target < plan.local), 1.0, 0.0
        ).astype(BF)
        some = flat_dot(filters_ref[...], chosen).astype(BF)
        f_ref[group, : plan.f_rows, :] = cols_dot(some, backwards).astype(BF)
        f_ref[group, plan.f_rows :, :] = cols_dot(some, plain).astype(BF)

    bytes_of(gain_land, gain_recv)
    pick_row = lax.broadcasted_iota(jnp.int32, (LANES, plan.width), 0)
    pick_col = lax.broadcasted_iota(jnp.int32, (LANES, plan.width), 1)
    repeat = jnp.where(pick_row == lax.rem(pick_col, cols), 1.0, 0.0).astype(BF)
    tile_row = lax.broadcasted_iota(jnp.int32, (chips * 8, plan.width), 0)
    tile_col = lax.broadcasted_iota(jnp.int32, (chips * 8, plan.width), 1)
    for layer in range(2):
        spread = flat_dot(gain_land[layer].reshape(chips * 8, LANES).astype(BF), repeat)
        for number in range(2):
            here = (tile_row // 8 == tile_col // cols) & (lax.rem(tile_row, 8) == number)
            gains_ref[2 * layer + number : 2 * layer + number + 1, :] = jnp.sum(
                jnp.where(here, spread, 0.0), axis=0, keepdims=True
            )
    position = lax.broadcasted_iota(jnp.int32, (rows_here, 1), 0)
    position = chip * rows_here + 2 * lax.rem(position, half) + position // half
    length_own = jnp.where(section == 0, lengths_ref[0], lengths_ref[1])
    length_other = jnp.where(section == 0, lengths_ref[1], lengths_ref[0])
    mask = jnp.where(position < length_own, 1.0, 0.0)
    mask_other = jnp.where(position < length_other, 1.0, 0.0)
    mask_ref[...] = mask
    io_swap.wait()
    core_zero = section == 0
    hidden = jnp.where(core_zero, io_own[0], io_sib[1]).astype(F32) * mask
    hidden_ref[...] = hidden
    factor = lax.rsqrt(jnp.mean(hidden * hidden, axis=-1, keepdims=True) + EPSILON)
    u = (hidden * factor * gains_ref[0:1, :]).astype(BF)
    for b in range(plan.cols_in):
        u_ref[b, :, :jb] = u[:half, b * jb : (b + 1) * jb]
        u_ref[b, :, jb:] = u[half:, b * jb : (b + 1) * jb]

    def send_u(step, carry):
        peer = lax.rem(chip + step, chips)
        b = lax.rem(peer // plan.cols_out, plan.cols_in)
        group = peer // (plan.cols_out * plan.cols_in)
        push(
            u_ref.at[b],
            x_buf.at[pl.ds(half * chip, half), :],
            u_send,
            x_recv,
            (section, peer),
        ).start()
        push(f_ref.at[group], f_land.at[chip], f_send, f_recv, (section, peer)).start()
        return carry

    lax.fori_loop(1, chips, send_u, 0)
    pltpu.make_async_copy(
        u_ref.at[lax.rem(chip // plan.cols_out, plan.cols_in)],
        x_buf.at[pl.ds(half * chip, half), :],
        x_recv,
    ).start()
    pltpu.make_async_copy(f_ref.at[my_group], f_land.at[chip], f_recv).start()
    if plan.routed:
        owner_pieces(plan, start_piece, plan.pieces // 3)

    for share in shares:
        share.wait_recv()
    groups = []
    for first, arrays in (
        (0, (gate_shard.at[0], up_shard.at[0], down_shard.at[0])),
        (3, (proj_shard.at[0], proj_shard.at[1], attn_shard.at[0], attn_shard.at[1])),
        (7, (gate_shard.at[1], up_shard.at[1], down_shard.at[1])),
    ):
        last = first + len(arrays)
        groups.append(
            Gather(
                plan,
                arrays,
                full_weights[first:last],
                w_send.at[pl.ds(first, len(arrays))],
                w_recv.at[pl.ds(first, len(arrays))],
            )
        )
    layer0, attention, layer1 = groups
    for group in groups:
        group.begin()
    cot_own = jnp.where(core_zero, io_sib[0], io_own[1]).astype(F32) * mask
    cot_other = jnp.where(core_zero, io_sib[1], io_own[0]).astype(F32) * mask_other
    upstream_ref[...] = cot_own
    pair_ref[:rows_here, :] = cot_own.astype(BF)
    pair_ref[rows_here:, :] = cot_other.astype(BF)
    bytes_of(f_land, f_recv)
    filter_rows(plan, f_land, table, 0, False)
    build_strips(plan, table, strip, False)
    filt_out = pltpu.make_async_copy(f_land, filt_ref, out_sem.at[0])
    filt_out.start()

    if plan.routed:
        bytes_of(mine, m_recv)
        swap = push(mine, other, o_send, o_recv, (1 - section, chip))
        swap.start()

        @pl.when(my_group == 0)
        def _():
            bytes_of(taps, t_recv)

        @pl.when(my_group != 0)
        def _():
            taps[...] = jnp.zeros_like(taps)
    else:
        for src, dst in ((mine_ref, mine), (other_ref, other), (taps_ref, taps)):
            pltpu.sync_copy(src, dst)

    bytes_of(x_buf, x_recv)
    x_out = pltpu.make_async_copy(x_buf, x_ref, out_sem.at[1])
    x_out.start()
    xf_buf[0:8, :] = jnp.zeros((8, 2 * jb), F32)
    for i in range(plan.blocks):
        rows = slice(BLOCK * i, BLOCK * (i + 1))
        xf_buf[8 + BLOCK * i : 8 + BLOCK * (i + 1), :] = x_buf[rows, :].astype(F32)
    for i in range(plan.blocks):
        rows = slice(BLOCK * i, BLOCK * (i + 1))
        moved = xf_buf[7 + BLOCK * i : 7 + BLOCK * (i + 1), :].astype(BF)
        xs_buf[rows, :] = moved
        xo_buf[rows, :jb] = x_buf[rows, :jb]
        xo_buf[rows, jb:] = moved[:, jb:]
    xs_out = pltpu.make_async_copy(xs_buf, xs_ref, out_sem.at[2])
    xs_out.start()

    if plan.routed:
        swap.wait()
    turn = (1 - 2 * section).astype(F32)

    def mix(k, carry):
        first = mine[k].astype(F32)
        second = other[k].astype(F32)
        pq[k, :jb, :] = (first + second).astype(BF)
        pq[k, jb:, :] = ((first - second) * turn).astype(BF)
        return carry

    lax.fori_loop(0, plan.local, mix, 0)
    pq_out = pltpu.make_async_copy(pq, pq_ref, out_sem.at[3])
    pq_out.start()
    taps_out = pltpu.make_async_copy(taps, tapw_ref, out_sem.at[4])
    taps_out.start()

    layer0.second()
    for i in range(plan.blocks):
        if i == 1:
            attention.second()
        if i == plan.blocks // 2:
            layer0.third()
        if i == plan.blocks - 1:
            layer1.second()
            attention.third()
        rows = slice(BLOCK * i, BLOCK * (i + 1))
        depth = BLOCK * (i + 1)
        offset = plan.length - depth
        x_now = x_buf[rows, :]
        s_now = xs_buf[rows, :]
        acc[0] = jnp.dot(
            jnp.concatenate([x_now[:, :jb], s_now[:, jb:]], 1),
            taps[: 2 * jb, :],
            preferred_element_type=F32,
        ) + jnp.dot(s_now[:, :jb], taps[2 * jb :, :], preferred_element_type=F32)
        acc[1] = jnp.dot(
            jnp.concatenate([x_now[:, jb:], x_now[:, :jb]], 1),
            taps[: 2 * jb, :],
            preferred_element_type=F32,
        ) + jnp.dot(s_now[:, jb:], taps[2 * jb :, :], preferred_element_type=F32)

        def step(k, carry, i=i, depth=depth, offset=offset):
            slot = lax.rem(k, 2)
            v_copy = pltpu.make_async_copy(
                stage.at[slot], v_ref.at[k, :, pl.ds(BLOCK * i, BLOCK), :], v_sem.at[slot]
            )
            even = jnp.dot(
                strip[2 * k, :, offset:], x_buf[:depth, :], preferred_element_type=F32
            ).astype(BF)
            odd = jnp.dot(
                strip[2 * k + 1, :, offset:], xo_buf[:depth, :], preferred_element_type=F32
            ).astype(BF)
            first = jnp.concatenate([even[:, :jb], odd[:, jb:]], 1)
            second = jnp.concatenate([even[:, jb:], odd[:, :jb]], 1)
            if i == 0:
                pl.when(k >= 2)(v_copy.wait)
            else:
                v_copy.wait()
            stage[slot, 0] = first
            stage[slot, 1] = second
            v_copy.start()
            acc[0] += jnp.dot(first, pq[k], preferred_element_type=F32)
            acc[1] += jnp.dot(second, pq[k], preferred_element_type=F32)
            return carry

        lax.fori_loop(0, plan.local, step, 0)
        y_buf[0, rows, :] = acc[0].astype(BF)
        y_buf[1, rows, :] = acc[1].astype(BF)

        def give(r, carry, i=i):
            peer = BLOCK // half * i + r
            src = y_buf.at[:, pl.ds(half * peer, half), :]

            @pl.when(peer == chip)
            def _():
                pltpu.make_async_copy(src, land.at[chip], c_recv).start()

            @pl.when(peer != chip)
            def _():
                push(src, land.at[chip], c_send, c_recv, (section, peer)).start()

            return carry

        lax.fori_loop(0, BLOCK // half, give, 0)

    layer1.third()
    for slot in range(2):
        pltpu.make_async_copy(
            stage.at[slot], v_ref.at[slot, :, pl.ds(0, BLOCK), :], v_sem.at[slot]
        ).wait()
    bytes_of(x_buf.at[pl.ds(0, half * (chips - 1)), :], u_send)
    bytes_of(f_land.at[pl.ds(0, chips - 1)], f_send)
    if plan.routed:
        owner_pieces(plan, drain_piece)
    for copy in (filt_out, x_out, xs_out, pq_out, taps_out):
        copy.wait()
    bytes_of(land, c_recv)
    for a in range(plan.cols_out):
        total = None
        for other_part in range(plan.cols_in * plan.groups):
            term = land[a + plan.cols_out * other_part].astype(F32)
            total = term if total is None else total + term
        conv_ref[:, :, a * ia : (a + 1) * ia] = total
    bytes_of(land.at[pl.ds(0, chips - 1)], c_send)
    for group in groups:
        group.end()
    def drain_gain(step, carry):
        push(
            gain_tile, gain_land.at[section, chip], gain_send, gain_recv, sibling
        ).wait_send()
        return carry

    lax.fori_loop(1, 2 * chips, drain_gain, 0)
    for share in shares:
        share.wait_send()


def forward_call(plan, io, gain, filters, lengths, raw, maps):
    chips, half, jb, ia, rows = plan.chips, plan.half, plan.jb, plan.ia, plan.rows
    width = plan.width
    any_spec = pl.BlockSpec(memory_space=pl.ANY)
    vmem_spec = pl.BlockSpec(memory_space=pltpu.VMEM)
    smem_spec = pl.BlockSpec(memory_space=pltpu.SMEM)
    dma = pltpu.SemaphoreType.DMA
    down, proj, attn = raw[2].shape, raw[3].shape, raw[4].shape
    share = (raw[0].shape[-2], plan.ff // 2)
    down_share = (down[0] // 2, width)
    grid = (plan.depth, plan.side, plan.side)
    layer = [share, share, down_share]
    gathered = layer + [proj, proj, attn, attn] + layer
    shapes = [(grid + w, BF) for w in gathered] + [
        ((2, half, width), F32),
        ((rows, width), F32),
        ((rows, width), F32),
        ((2 * rows, width), BF),
        ((8, width), F32),
        ((rows, 1), F32),
        ((plan.local, 2, plan.length, 2 * jb), BF),
        ((plan.local, 2 * jb, ia), BF),
        ((ORDER * jb, ia), BF),
        ((plan.length, 2 * jb), BF),
        ((plan.length, 2 * jb), BF),
        ((chips, 2 * plan.f_rows, LANES), BF),
    ]
    return pl.pallas_call(
        functools.partial(forward_kernel, plan),
        out_shape=[jax.ShapeDtypeStruct(s, d) for s, d in shapes],
        in_specs=[vmem_spec] * 3
        + [smem_spec]
        + [vmem_spec] * 5
        + [any_spec] * len(maps),
        out_specs=[any_spec] * 10 + [vmem_spec] * 6 + [any_spec] * 6,
        scratch_shapes=[
            pltpu.VMEM((2, rows, width), BF),
            pltpu.VMEM((2, rows, width), BF),
            pltpu.VMEM((8, LANES), F32),
            pltpu.VMEM((2, chips, 8, LANES), F32),
            pltpu.VMEM(share, BF),
            pltpu.VMEM((2,) + share, BF),
            pltpu.VMEM(share, BF),
            pltpu.VMEM((2,) + share, BF),
            pltpu.VMEM((2,) + down_share, BF),
            pltpu.VMEM((2,) + proj, BF),
            pltpu.VMEM((2,) + attn, BF),
            pltpu.VMEM((plan.cols_in, half, 2 * jb), BF),
            pltpu.VMEM((plan.groups, 2 * plan.f_rows, LANES), BF),
            pltpu.VMEM((plan.length, 2 * jb), BF),
            pltpu.VMEM((plan.length, 2 * jb), BF),
            pltpu.VMEM((plan.length, 2 * jb), BF),
            pltpu.VMEM((plan.length + 8, 2 * jb), F32),
            pltpu.VMEM((chips, 2 * plan.f_rows, LANES), BF),
            pltpu.VMEM((2, plan.f_rows, plan.length + BLOCK), F32),
            pltpu.VMEM((2 * plan.local, BLOCK, plan.length), BF),
            pltpu.VMEM((plan.local, jb, ia), BF),
            pltpu.VMEM((plan.local, jb, ia), BF),
            pltpu.VMEM((ORDER * jb, ia), BF),
            pltpu.VMEM((plan.local, 2 * jb, ia), BF),
            pltpu.VMEM((2, BLOCK, ia), F32),
            pltpu.VMEM((2, plan.length, ia), BF),
            pltpu.VMEM((chips, 2, half, ia), BF),
            pltpu.VMEM((2, 2, BLOCK, 2 * jb), BF),
            dma((2,)),
            dma,
            dma,
            dma((5,)),
            dma((5,)),
        ]
        + [dma] * 11
        + [dma((2,)), dma((5,)), dma((10, 5)), dma((10, 5))],
        compiler_params=pltpu.CompilerParams(
            collective_id=2, has_side_effects=True, vmem_limit_bytes=VMEM_LIMIT
        ),
        name="spectral_forward",
    )(io, gain, filters, lengths, *raw, *maps)


def backward_kernel(plan, number, *refs):
    g_ref, filt_ref, v_ref, pq, tapw, x_ref, xs_ref = refs[:7]
    grads, rest = refs[7 : 7 + number], refs[7 + number :]
    sums, rest = rest[:number], rest[number:]
    du_ref = rest[0]
    if plan.routed:
        dmaps_ref = rest[1]
        rest = rest[2:]
    else:
        dmap_ref, dtap_ref = rest[1:3]
        rest = rest[3:]
    count = 5 * sum(len(plan.routes(grad.shape[3])) for grad in grads)
    scatter = Scatter(plan, grads, sums, rest[:count], *rest[count : count + 2])
    rest = rest[count + 2 :]
    (
        g_buf,
        gt_buf,
        table,
        strip,
        v_buf,
        z_even,
        z_odd,
        acc_even,
        acc_odd,
        kept,
        give_m,
        take_m,
        total_m,
        kept_t,
        give_t,
        take_t,
        total_t,
        du_buf,
        land,
        g_send,
        g_recv,
        v_sem,
        m_send,
        m_recv,
        t_send,
        t_recv,
        w_send,
        w_recv,
        d_send,
        d_recv,
        x_sem,
    ) = rest
    chips, half, jb, ia = plan.chips, plan.half, plan.jb, plan.ia
    section, chip = spot()
    dev = section * chips + chip
    my_a = lax.rem(chip, plan.cols_out)
    my_b = lax.rem(chip // plan.cols_out, plan.cols_in)
    my_group = chip // (plan.cols_out * plan.cols_in)
    greet_everyone(chips)()

    def send_g(step, carry):
        peer = lax.rem(chip + step, chips)
        a = lax.rem(peer, plan.cols_out)
        push(
            g_ref.at[:, :, pl.ds(pl.multiple_of(a * ia, ia), ia)],
            g_buf.at[:, pl.ds(half * chip, half), :],
            g_send,
            g_recv,
            (section, peer),
        ).start()
        return carry

    lax.fori_loop(1, chips, send_g, 0)
    pltpu.make_async_copy(
        g_ref.at[:, :, pl.ds(pl.multiple_of(my_a * ia, ia), ia)],
        g_buf.at[:, pl.ds(half * chip, half), :],
        g_recv,
    ).start()
    v_copy = [pltpu.make_async_copy(v_ref.at[k], v_buf.at[k], v_sem.at[k]) for k in range(2)]
    for copy in v_copy:
        copy.start()
    x_copy = [
        pltpu.make_async_copy(src, dst, x_sem.at[i])
        for i, (src, dst) in enumerate(((x_ref, z_even), (xs_ref, z_odd)))
    ]
    for copy in x_copy:
        copy.start()
    scatter.begin()
    filter_rows(plan, filt_ref, table, plan.f_rows, True)
    build_strips(plan, table, strip, True)
    acc_even[...] = jnp.zeros_like(acc_even)
    acc_odd[...] = jnp.zeros_like(acc_odd)
    bytes_of(g_buf, g_recv)
    for phase in range(2):
        for i in range(plan.blocks):
            rows = slice(BLOCK * i, BLOCK * (i + 1))
            gt_buf[phase, :, rows] = g_buf[phase, rows, :].astype(F32).T.astype(BF)
    turn = (1 - 2 * section).astype(F32)
    half_ways = (((1,), (1,)), ((), ()))

    def piece_of(k, tap, sub):
        per_map = plan.width // PIECE
        which = 2 * plan.filters + k if tap else section * plan.filters + my_group * plan.local + k
        g = which * per_map + my_b * (plan.jb // PIECE) + sub
        return g // plan.pieces, lax.rem(g, plan.pieces)

    def piece_copies(k, tap, begin):
        def one(sub, carry):
            owner, row = piece_of(k, tap, sub)
            src = (
                total_t.at[pl.ds(jb * k + PIECE * sub, PIECE), :]
                if tap
                else total_m.at[k, pl.ds(PIECE * sub, PIECE), :]
            )
            dst = dmaps_ref.at[
                pl.ds(PIECE * row, PIECE), pl.ds(pl.multiple_of(my_a * ia, ia), ia)
            ]
            if begin:

                @pl.when(owner == dev)
                def _():
                    pltpu.make_async_copy(src, dst, w_recv).start()

            @pl.when(owner != dev)
            def _():
                copy = push(src, dst, w_send, w_recv, (owner // chips, lax.rem(owner, chips)))
                if begin:
                    copy.start()
                else:
                    copy.wait_send()

            return carry

        lax.fori_loop(0, plan.jb // PIECE, one, 0)

    def exchange(k):
        return push(give_m.at[k], take_m.at[k], m_send.at[k], m_recv.at[k], (1 - section, chip))

    def finish(k):
        exchange(k).wait()
        total_m[k] = (kept[k] + take_m[k].astype(F32)).astype(BF)
        if plan.routed:
            piece_copies(k, False, True)

    for copy in x_copy:
        copy.wait()
    x_even, x_odd = z_even[:, :jb], z_even[:, jb:]
    s_even, s_odd = z_odd[:, :jb], z_odd[:, jb:]
    for tap, (on_even, on_odd) in enumerate(((x_even, x_odd), (s_odd, x_even), (s_even, s_odd))):
        tap_grad = jnp.dot(gt_buf[0], on_even, preferred_element_type=F32) + jnp.dot(
            gt_buf[1], on_odd, preferred_element_type=F32
        )
        tap_grad = tap_grad.T
        kept_t[tap * jb : (tap + 1) * jb, :] = tap_grad
        give_t[tap * jb : (tap + 1) * jb, :] = tap_grad.astype(BF)
    tap_swap = push(give_t, take_t, t_send, t_recv, (1 - section, chip))
    tap_swap.start()
    for i in range(plan.blocks):
        rows = slice(BLOCK * i, BLOCK * (i + 1))
        from_even = lax.dot_general(
            g_buf[0, rows, :], tapw[...], half_ways, preferred_element_type=F32
        )
        from_odd = lax.dot_general(
            g_buf[1, rows, :], tapw[...], half_ways, preferred_element_type=F32
        )
        acc_even[rows, :jb] = from_even[:, :jb] + from_odd[:, jb : 2 * jb]
        acc_even[rows, jb : 2 * jb] = from_odd[:, :jb]
        acc_odd[rows, :jb] = from_even[:, 2 * jb :]
        acc_odd[rows, jb : 2 * jb] = from_even[:, jb : 2 * jb] + from_odd[:, 2 * jb :]

    def step(k, carry):
        slot = lax.rem(k, 2)
        for i in range(plan.blocks):
            rows = slice(BLOCK * i, BLOCK * (i + 1))
            from_even = lax.dot_general(
                g_buf[0, rows, :], pq[k], half_ways, preferred_element_type=F32
            ).astype(BF)
            from_odd = lax.dot_general(
                g_buf[1, rows, :], pq[k], half_ways, preferred_element_type=F32
            ).astype(BF)
            z_even[rows, :jb] = from_even[:, :jb]
            z_even[rows, jb:] = from_odd[:, :jb]
            z_odd[rows, :jb] = from_odd[:, jb:]
            z_odd[rows, jb:] = from_even[:, jb:]
        pltpu.make_async_copy(v_ref.at[k], v_buf.at[slot], v_sem.at[slot]).wait()
        grad = jnp.dot(gt_buf[0], v_buf[slot, 0], preferred_element_type=F32) + jnp.dot(
            gt_buf[1], v_buf[slot, 1], preferred_element_type=F32
        )
        grad = grad.T
        plus, minus = grad[:jb, :], grad[jb:, :] * turn
        kept[k] = plus + minus
        give_m[k] = (plus - minus).astype(BF)
        exchange(k).start()

        @pl.when(k + 2 < plan.local)
        def _():
            pltpu.make_async_copy(v_ref.at[k + 2], v_buf.at[slot], v_sem.at[slot]).start()

        for j in range(plan.blocks):
            rows = slice(BLOCK * j, BLOCK * (j + 1))
            depth = plan.length - BLOCK * j
            acc_even[rows, :] += jnp.dot(
                strip[2 * k, :, :depth], z_even[BLOCK * j :, :], preferred_element_type=F32
            )
            out = jnp.dot(
                strip[2 * k + 1, :, :depth], z_odd[BLOCK * j :, :], preferred_element_type=F32
            )
            acc_even[rows, :jb] += out[:, :jb]
            acc_odd[rows, jb:] += out[:, jb:]

        @pl.when(k >= 1)
        def _():
            finish(k - 1)

        pl.when(k == plan.local // 4)(scatter.second)
        pl.when(k == plan.local // 2 + 1)(scatter.third)
        return carry

    lax.fori_loop(0, plan.local, step, 0)
    for i in range(plan.blocks):
        rows = slice(BLOCK * i, BLOCK * (i + 1))
        moved = acc_odd[BLOCK * i + 1 : BLOCK * (i + 1) + 1, :]
        both = (acc_even[rows, :] + moved).astype(BF)
        du_buf[0, rows, :] = both[:, :jb]
        du_buf[1, rows, :] = both[:, jb:]

        def give(r, carry, i=i):
            peer = BLOCK // half * i + r
            src = du_buf.at[:, pl.ds(half * peer, half), :]

            @pl.when(peer == chip)
            def _():
                pltpu.make_async_copy(src, land.at[chip], d_recv).start()

            @pl.when(peer != chip)
            def _():
                push(src, land.at[chip], d_send, d_recv, (section, peer)).start()

            return carry

        lax.fori_loop(0, BLOCK // half, give, 0)
    finish(plan.local - 1)
    tap_swap.wait()
    total_t[...] = (kept_t[...] + take_t[...].astype(F32)).astype(BF)
    if plan.routed:

        @pl.when(jnp.logical_and(section == 0, my_group == 0))
        def _():
            for tap in range(ORDER):
                piece_copies(tap, True, True)
    else:
        pltpu.sync_copy(total_m, dmap_ref)
        pltpu.sync_copy(total_t, dtap_ref)
    bytes_of(g_buf.at[0, pl.ds(0, 2 * half * (chips - 1) // 2), :], g_send)
    bytes_of(g_buf.at[1, pl.ds(0, 2 * half * (chips - 1) // 2), :], g_send)
    bytes_of(land, d_recv)
    for b in range(plan.cols_in):
        total = None
        for c in range(plan.groups):
            for a in range(plan.cols_out):
                term = land[a + plan.cols_out * (b + plan.cols_in * c)].astype(F32)
                total = term if total is None else total + term
        du_ref[:, :, b * jb : (b + 1) * jb] = total
    bytes_of(land.at[pl.ds(0, chips - 1)], d_send)
    scatter.end()
    if plan.routed:

        def drain(k, carry):
            piece_copies(k, False, False)
            return carry

        lax.fori_loop(0, plan.local, drain, 0)

        @pl.when(jnp.logical_and(section == 0, my_group == 0))
        def _():
            for tap in range(ORDER):
                piece_copies(tap, True, False)

        bytes_of(dmaps_ref, w_recv)


def backward_call(plan, g, filt, v, pq, tapw, x, xs, grads):
    chips, half, jb, ia = plan.chips, plan.half, plan.jb, plan.ia
    any_spec = pl.BlockSpec(memory_space=pl.ANY)
    vmem_spec = pl.BlockSpec(memory_space=pltpu.VMEM)
    dma = pltpu.SemaphoreType.DMA
    shapes = [g_part.shape[3:] for g_part in grads]
    out_shape = [jax.ShapeDtypeStruct(shape, F32) for shape in shapes]
    out_shape.append(jax.ShapeDtypeStruct((2, half, plan.width), F32))
    if plan.routed:
        out_shape.append(jax.ShapeDtypeStruct((plan.map_rows, plan.width), BF))
    else:
        out_shape.append(jax.ShapeDtypeStruct((plan.local, jb, ia), BF))
        out_shape.append(jax.ShapeDtypeStruct((ORDER * jb, ia), BF))
    return pl.pallas_call(
        functools.partial(backward_kernel, plan, len(grads)),
        out_shape=out_shape,
        in_specs=[vmem_spec, vmem_spec, any_spec, vmem_spec, vmem_spec, any_spec, any_spec]
        + [vmem_spec] * len(grads),
        out_specs=[vmem_spec] * (len(grads) + 1) + [any_spec] * (len(out_shape) - len(grads) - 1),
        scratch_shapes=Scatter.scratch(plan, shapes)
        + [dma((len(grads), 6)), dma((len(grads), 6))]
        + [
            pltpu.VMEM((2, plan.length, ia), BF),
            pltpu.VMEM((2, ia, plan.length), BF),
            pltpu.VMEM((2, plan.f_rows, plan.length + BLOCK), F32),
            pltpu.VMEM((2 * plan.local, BLOCK, plan.length), BF),
            pltpu.VMEM((2, 2, plan.length, 2 * jb), BF),
            pltpu.VMEM((plan.length, 2 * jb), BF),
            pltpu.VMEM((plan.length, 2 * jb), BF),
            pltpu.VMEM((plan.length, 2 * jb), F32),
            pltpu.VMEM((plan.length + 8, 2 * jb), F32),
            pltpu.VMEM((plan.local, jb, ia), F32),
            pltpu.VMEM((plan.local, jb, ia), BF),
            pltpu.VMEM((plan.local, jb, ia), BF),
            pltpu.VMEM((plan.local, jb, ia), BF),
            pltpu.VMEM((ORDER * jb, ia), F32),
            pltpu.VMEM((ORDER * jb, ia), BF),
            pltpu.VMEM((ORDER * jb, ia), BF),
            pltpu.VMEM((ORDER * jb, ia), BF),
            pltpu.VMEM((2, plan.length, jb), BF),
            pltpu.VMEM((chips, 2, half, jb), BF),
            dma,
            dma,
            dma((2,)),
            dma((plan.local,)),
            dma((plan.local,)),
            dma,
            dma,
            dma,
            dma,
            dma,
            dma,
            dma((2,)),
        ],
        compiler_params=pltpu.CompilerParams(
            collective_id=3, has_side_effects=True, vmem_limit_bytes=VMEM_LIMIT
        ),
        name="spectral_backward",
    )(g, filt, v, pq, tapw, x, xs, *grads)

SWAPS = 7


def middle_kernel(plan, *refs):
    (
        conv_ref,
        hidden_ref,
        gains_ref,
        mask_ref,
        up_ref,
        up_pair,
        *stored,
    ) = refs[:16]
    (
        out_ref,
        g_ref,
        dmid_ref,
        gain_ref,
        gate0_g,
        up0_g,
        down0_g,
        gate1_g,
        up1_g,
        down1_g,
        proj_g,
        attn_g,
    ) = refs[16:28]
    held = refs[28:36]
    (
        pair0,
        pair1,
        give,
        take,
        gates,
        ups,
        acts,
        dgate,
        dup,
        kv,
        q_buf,
        probs,
        dkv,
        back,
        back_land,
        att,
        dq_buf,
        load_sem,
        send,
        recv,
        kv_send,
        kv_recv,
        bk_send,
        bk_recv,
    ) = refs[36:]
    chips, rows, width = plan.chips, plan.rows, plan.width
    section, chip = spot()
    sibling = (1 - section, chip)
    reach = WINDOW // rows
    span = (reach + 1) * rows
    layer0, (w_proj, w_out), layer1 = held[:3], held[3:5], held[5:]
    split = 3 * plan.width // 2
    homes = [
        *layer0,
        w_proj.at[:split],
        w_proj.at[split:],
        w_out.at[: plan.width // 2],
        w_out.at[plan.width // 2 :],
        *layer1,
    ]
    loads = [
        pltpu.make_async_copy(a, b, load_sem.at[i]) for i, (a, b) in enumerate(zip(stored, homes))
    ]
    for load in loads:
        load.start()
    greet_everyone(chips)()
    ff = layer0[0].shape[1]
    own = slice(0, rows)
    second = slice(rows, 2 * rows)
    mask = mask_ref[...]

    def swap(number, src, dst):
        copy = push(src, dst, send.at[number], recv.at[number], sibling)
        copy.start()
        copy.wait()

    def norm(values, gain):
        factor = lax.rsqrt(jnp.mean(values * values, axis=-1, keepdims=True) + EPSILON)
        return values * factor * gain, factor

    def norm_back(values, factor, gain, upstream):
        weighted = upstream * gain
        gain_grad = jnp.sum(upstream * values * factor, axis=0, keepdims=True)
        correction = jnp.mean(weighted * values, axis=-1, keepdims=True)
        return factor * weighted - values * factor * factor * factor * correction, gain_grad

    def feed(layer, pair, weights, number):
        w_gate, w_up, w_down = weights
        swap(number, pair.at[own], pair.at[second])
        for start in range(0, ff, BLOCK):
            cols = slice(start, start + BLOCK)
            gate_rows = flat_dot(pair[...], w_gate[:, cols])
            up_rows = flat_dot(pair[...], w_up[:, cols])
            gates[layer, :, cols] = gate_rows
            ups[layer, :, cols] = up_rows
            acts[layer, :, cols] = (gate_rows * jax.nn.sigmoid(gate_rows) * up_rows).astype(BF)
        part = flat_dot(acts[layer], w_down[...])
        give[number] = part[second].astype(BF)
        swap(number + 1, give.at[number], take.at[number])
        return part[own] + take[number].astype(F32)

    def feed_back(layer, pair, weights, grads, upstream_pair, number):
        w_gate, w_up, w_down = weights
        gate_g, up_g, down_g = grads
        turned = pair[...].astype(F32).T.astype(BF)
        for start in range(0, ff, BLOCK):
            cols = slice(start, start + BLOCK)
            active_grad = rows_dot(upstream_pair, w_down[cols, :])
            gate_rows, up_rows = gates[layer, :, cols], ups[layer, :, cols]
            sigmoid = jax.nn.sigmoid(gate_rows)
            slope = sigmoid * (1.0 + gate_rows * (1.0 - sigmoid))
            gate_grad = (active_grad * up_rows * slope).astype(BF)
            up_grad = (active_grad * gate_rows * sigmoid).astype(BF)
            dgate[:, cols] = gate_grad
            dup[:, cols] = up_grad
        for start in range(0, width, BLOCK):
            cols = slice(start, start + BLOCK)
            part = rows_dot(dgate[...], w_gate[cols, :]) + rows_dot(dup[...], w_up[cols, :])
            give[number, :, cols] = part[second].astype(BF)
            att[:, cols] = part[own]
        copy = push(
            give.at[number], take.at[number], send.at[number], recv.at[number], sibling
        )
        copy.start()
        for start in range(0, ff, BLOCK):
            cols = slice(start, start + BLOCK)
            gate_g[:, cols] = flat_dot(turned, dgate[:, cols]).astype(BF)
            up_g[:, cols] = flat_dot(turned, dup[:, cols]).astype(BF)
            down_g[cols, :] = flat_dot(
                acts[layer, :, cols].astype(F32).T.astype(BF), upstream_pair
            ).astype(BF)
        copy.wait()
        return att[...] + take[number].astype(F32)

    middle0 = hidden_ref[...] + conv_ref[...]
    normed, factor0 = norm(middle0, gains_ref[1:2, :])
    pair0[own] = normed.astype(BF)
    dmid_ref[...] = middle0
    for load in loads[:3]:
        load.wait()
    branch = feed(0, pair0, layer0, 0)
    passed = (mask * (dmid_ref[...] + branch)).astype(BF).astype(F32)

    normed, factor10 = norm(passed, gains_ref[2:3, :])
    inputs = normed.astype(BF)
    for load in loads[3:7]:
        load.wait()
    mine = slice(reach * rows, span)
    q_buf[...] = flat_dot(inputs, w_proj[:width]).astype(BF)
    kv[mine, :width] = flat_dot(inputs, w_proj[width : 2 * width]).astype(BF)
    kv[mine, width:] = flat_dot(inputs, w_proj[2 * width :]).astype(BF)

    def ahead(distance):
        return push(
            kv.at[mine],
            kv.at[pl.ds((reach - distance) * rows, rows)],
            kv_send.at[distance - 1],
            kv_recv.at[distance - 1],
            (section, chip + distance),
        )

    for distance in range(1, reach + 1):

        @pl.when(chip + distance < chips)
        def _():
            ahead(distance).start()

        @pl.when(chip < distance)
        def _():
            kv[(reach - distance) * rows : (reach - distance + 1) * rows, :] = jnp.zeros(
                (rows, 2 * width), BF
            )

    half = plan.half
    row = lax.broadcasted_iota(jnp.int32, (rows, span), 0)
    col = lax.broadcasted_iota(jnp.int32, (rows, span), 1)
    inner = lax.rem(col, rows)
    q_place = 2 * lax.rem(row, half) + row // half
    k_place = (col // rows - reach) * rows + 2 * lax.rem(inner, half) + inner // half
    distance_rows = q_place - k_place
    allowed = (
        (k_place + chip * rows >= 0) & (distance_rows >= 0) & (distance_rows < WINDOW)
    )
    lane = lax.broadcasted_iota(jnp.int32, (rows, LANES), 1)
    low = lane < HEAD_DIM
    scale = HEAD_DIM ** (-0.5)
    zero = jnp.zeros((rows, LANES), BF)
    for distance in range(1, reach + 1):

        @pl.when(chip >= distance)
        def _():
            push(
                kv.at[mine],
                kv.at[pl.ds((reach - distance) * rows, rows)],
                kv_send.at[distance - 1],
                kv_recv.at[distance - 1],
                sibling,
            ).wait_recv()

    for pair in range(width // LANES):
        lanes = slice(LANES * pair, LANES * (pair + 1))
        keys, values = kv[:, lanes], kv[:, width + LANES * pair : width + LANES * (pair + 1)]
        parts = []
        for side in range(2):
            here = low if side == 0 else jnp.logical_not(low)
            queries = jnp.where(here, q_buf[:, lanes], zero)
            scores = rows_dot(queries, keys) * scale
            scores = jnp.where(allowed, scores, BIG_NEGATIVE)
            weights = jnp.exp(scores - jnp.max(scores, axis=-1, keepdims=True))
            weights = weights / jnp.sum(weights, axis=-1, keepdims=True)
            probs[2 * pair + side] = weights
            parts.append(flat_dot(weights.astype(BF), values))
        att[:, lanes] = jnp.where(low, parts[0], parts[1])
    attended = att[...].astype(BF)
    middle1 = passed + flat_dot(attended, w_out[...])

    for load in loads[7:]:
        load.wait()
    normed, factor11 = norm(middle1, gains_ref[3:4, :])
    pair1[own] = normed.astype(BF)
    branch = feed(1, pair1, layer1, 2)
    out_ref[...] = (mask * (middle1 + branch)).astype(BF)
    dnormed = feed_back(1, pair1, layer1, (gate1_g, up1_g, down1_g), up_pair[...], 4)
    dmiddle, gain11 = norm_back(middle1, factor11, gains_ref[3:4, :], dnormed)
    dmiddle = up_ref[...] + dmiddle
    gain_ref[3:4, :] = gain11

    dy = dmiddle.astype(BF)
    attn_g[...] = flat_dot(attended.astype(F32).T.astype(BF), dy).astype(BF)
    datt = rows_dot(dy, w_out[...]).astype(BF)
    for pair in range(width // LANES):
        lanes = slice(LANES * pair, LANES * (pair + 1))
        value_lanes = slice(width + LANES * pair, width + LANES * (pair + 1))
        keys, values = kv[:, lanes], kv[:, value_lanes]
        dq_parts, key_grad, value_grad = [], None, None
        for side in range(2):
            here = low if side == 0 else jnp.logical_not(low)
            queries = jnp.where(here, q_buf[:, lanes], zero)
            upstream = jnp.where(here, datt[:, lanes], zero)
            weights = probs[2 * pair + side]
            grad = rows_dot(upstream, values)
            total = jnp.sum(weights * grad, axis=-1, keepdims=True)
            dscores = weights * (grad - total)
            dq_parts.append(flat_dot(dscores.astype(BF), keys))
            one = flat_dot(dscores.T.astype(BF), queries)
            two = flat_dot(weights.T.astype(BF), upstream)
            key_grad = one if key_grad is None else key_grad + one
            value_grad = two if value_grad is None else value_grad + two
        dq_buf[0, :, lanes] = (jnp.where(low, dq_parts[0], dq_parts[1]) * scale).astype(BF)
        key_grad = key_grad * scale
        back[:, lanes] = key_grad[: reach * rows].astype(BF)
        back[:, value_lanes] = value_grad[: reach * rows].astype(BF)
        dkv[:, lanes] = key_grad[reach * rows :]
        dkv[:, value_lanes] = value_grad[reach * rows :]

    def behind(distance, peer):
        return push(
            back.at[pl.ds((reach - distance) * rows, rows)],
            back_land.at[distance - 1],
            bk_send.at[distance - 1],
            bk_recv.at[distance - 1],
            (section, peer),
        )

    for distance in range(1, reach + 1):

        @pl.when(chip >= distance)
        def _():
            behind(distance, chip - distance).start()

    for distance in range(1, reach + 1):

        @pl.when(chip + distance < chips)
        def _():
            behind(distance, chip).wait_recv()
            dkv[...] += back_land[distance - 1].astype(F32)

    dq_buf[1] = dkv[:, :width].astype(BF)
    dq_buf[2] = dkv[:, width:].astype(BF)
    turned = inputs.astype(F32).T.astype(BF)
    dnormed = None
    for part in range(3):
        term = rows_dot(dq_buf[part], w_proj[part * width : (part + 1) * width])
        dnormed = term if dnormed is None else dnormed + term
    dpassed, gain10 = norm_back(passed, factor10, gains_ref[2:3, :], dnormed)
    gain_ref[2:3, :] = gain10
    dpassed = (dmiddle + dpassed).astype(BF).astype(F32)

    upstream0 = mask * dpassed
    give[5] = upstream0.astype(BF)
    copy = push(give.at[5], take.at[5], send.at[5], recv.at[5], sibling)
    copy.start()
    for part in range(3):
        proj_g[part * width : (part + 1) * width, :] = flat_dot(turned, dq_buf[part]).astype(BF)
    copy.wait()
    both = jnp.concatenate([give[5], take[5]], 0)
    dnormed = feed_back(0, pair0, layer0, (gate0_g, up0_g, down0_g), both, 6)
    middle0 = dmid_ref[...]
    dmiddle, gain01 = norm_back(middle0, factor0, gains_ref[1:2, :], dnormed)
    gain_ref[1:2, :] = gain01
    dmiddle = upstream0 + dmiddle
    dmid_ref[...] = dmiddle
    g_ref[...] = dmiddle.astype(BF)

    for distance in range(1, reach + 1):

        @pl.when(chip + distance < chips)
        def _():
            ahead(distance).wait_send()

        @pl.when(chip >= distance)
        def _():
            behind(distance, chip).wait_send()


def middle_call(plan, conv, hidden, gains, mask, upstream, pair, stored):
    rows, width = plan.rows, plan.width
    reach = WINDOW // rows
    ff = plan.ff // 2
    any_spec = pl.BlockSpec(memory_space=pl.ANY)
    vmem_spec = pl.BlockSpec(memory_space=pltpu.VMEM)
    dma = pltpu.SemaphoreType.DMA
    layer = [(width, ff), (width, ff), (ff, width)]
    held = layer + [(3 * width, width), (width, width)] + layer
    shapes = [
        ((rows, width), BF),
        ((rows, width), BF),
        ((rows, width), F32),
        ((8, width), F32),
        ((width, ff), BF),
        ((width, ff), BF),
        ((ff, width), BF),
        ((width, ff), BF),
        ((width, ff), BF),
        ((ff, width), BF),
        ((3 * width, width), BF),
        ((width, width), BF),
    ]
    return pl.pallas_call(
        functools.partial(middle_kernel, plan),
        out_shape=[jax.ShapeDtypeStruct(s, d) for s, d in shapes],
        in_specs=[vmem_spec] * 6 + [any_spec] * 10,
        out_specs=[vmem_spec] * len(shapes),
        scratch_shapes=[pltpu.VMEM(w, BF) for w in held]
        + [
            pltpu.VMEM((2 * rows, width), BF),
            pltpu.VMEM((2 * rows, width), BF),
            pltpu.VMEM((SWAPS, rows, width), BF),
            pltpu.VMEM((SWAPS, rows, width), BF),
            pltpu.VMEM((2, 2 * rows, ff), F32),
            pltpu.VMEM((2, 2 * rows, ff), F32),
            pltpu.VMEM((2, 2 * rows, ff), BF),
            pltpu.VMEM((2 * rows, ff), BF),
            pltpu.VMEM((2 * rows, ff), BF),
            pltpu.VMEM(((reach + 1) * rows, 2 * width), BF),
            pltpu.VMEM((rows, width), BF),
            pltpu.VMEM((width // HEAD_DIM, rows, (reach + 1) * rows), F32),
            pltpu.VMEM((rows, 2 * width), F32),
            pltpu.VMEM((reach * rows, 2 * width), BF),
            pltpu.VMEM((reach, rows, 2 * width), BF),
            pltpu.VMEM((rows, width), F32),
            pltpu.VMEM((3, rows, width), BF),
            dma((10,)),
            dma((SWAPS,)),
            dma((SWAPS,)),
            dma((reach,)),
            dma((reach,)),
            dma((reach,)),
            dma((reach,)),
        ],
        compiler_params=pltpu.CompilerParams(
            collective_id=5, has_side_effects=True, vmem_limit_bytes=VMEM_LIMIT
        ),
        name="middle",
    )(conv, hidden, gains, mask, upstream, pair, *stored)


def swapped(block):
    return lax.ppermute(block, "section", [(0, 1), (1, 0)])


def norm_backward(values, factor, weights, upstream):
    weighted = upstream * weights
    gain_grad = jnp.sum(upstream * values * factor, axis=0)
    correction = jnp.mean(weighted * values, axis=-1, keepdims=True)
    return (factor * weighted - values * factor * factor * factor * correction, gain_grad)


def body(
    io_pair, lengths, filters, stu_maps, attn_proj, attn_out, norm_gains, mlp_gate, mlp_up, mlp_down
):
    chips = lax.axis_size("seq")
    section, chip = spot()
    core_zero = section == 0
    tok_rows = io_pair.shape[2]
    width = io_pair.shape[3]
    half = tok_rows // 2
    ff = mlp_gate.shape[2]
    ff_half = mlp_down.shape[1] // 2
    plan = Plan(chips, tok_rows, width, filters.shape[1], stu_maps.shape[0], ff)

    def join_phases(rows):
        return rows.reshape(2, half, width).swapaxes(0, 1).reshape(rows.shape)

    my_a = chip % plan.cols_out
    my_b = (chip // plan.cols_out) % plan.cols_in
    my_group = chip // (plan.cols_out * plan.cols_in)
    if plan.routed:
        maps = [stu_maps]
    else:
        whole = lax.all_gather(stu_maps, ("section", "seq"), axis=0, tiled=True)
        whole = lax.dynamic_slice(
            whole.reshape(-1, width, width),
            (0, my_b * plan.jb, my_a * plan.ia),
            (whole.shape[0] // width, plan.jb, plan.ia),
        )
        pair = whole[: 2 * plan.filters].reshape(2, plan.filters, plan.jb, plan.ia)
        pair = lax.dynamic_slice_in_dim(pair, my_group * plan.local, plan.local, 1)
        taps = jnp.where(my_group == 0, whole[2 * plan.filters :], 0).astype(BF)
        maps = [
            jnp.where(core_zero, pair[0], pair[1]),
            jnp.where(core_zero, pair[1], pair[0]),
            taps.reshape(-1, plan.ia),
        ]

    gate, up = mlp_gate[0], mlp_up[0]
    if not plan.pick_here:
        gate, up = (
            jnp.transpose(w.reshape(w.shape[0], chips, 2, ff_half), (2, 0, 1, 3)).reshape(
                2, w.shape[0], ff // 2
            )
            for w in (gate, up)
        )
    results = forward_call(
        plan,
        io_pair[0],
        norm_gains[0],
        filters,
        lengths,
        [gate, up, mlp_down[0], attn_proj, attn_out],
        maps,
    )
    weights = [w.reshape(-1, w.shape[-1]) for w in results[:10]]
    conv, hidden, upstream1, grad_pair, gains, mask_rows = results[10:16]
    v, pq, tapw, x_all, xs_all, filt = results[16:]
    proj_rows = attn_proj.shape[0]
    block_out, g, middle0_grad, gain_sums, *grads = middle_call(
        plan,
        conv.reshape(tok_rows, width),
        hidden,
        gains,
        mask_rows,
        upstream1,
        grad_pair,
        weights,
    )
    mlp0_grads, mlp1_grads = tuple(grads[:3]), tuple(grads[3:6])
    proj_grad, output_grad = grads[6:]
    gain01, gain10, gain11 = gain_sums[1], gain_sums[2], gain_sums[3]
    g = g.reshape(2, half, width)
    grid = (plan.depth, plan.side, plan.side)
    half_width = width // 2
    blocks0 = [
        w.astype(BF).reshape(grid + (w.shape[0] // chips, w.shape[1])) for w in mlp0_grads
    ]
    blocks1 = [
        w.astype(BF).reshape(grid + (w.shape[0] // chips, w.shape[1]))
        for w in mlp1_grads
        + (
            proj_grad[: width + half_width],
            proj_grad[width + half_width :],
            output_grad[:half_width],
            output_grad[half_width:],
        )
    ]
    if plan.routed:
        results = backward_call(plan, g, filt, v, pq, tapw, x_all, xs_all, blocks0 + blocks1)
        half0, half1, attn_sums, results = results[:3], results[3:6], results[6:10], results[10:]
    else:
        results = backward_call(plan, g, filt, v, pq, tapw, x_all, xs_all, blocks0)
        half0, results = results[:3], results[3:]
        summed = [
            lax.psum_scatter(
                w.reshape((chips,) + w.shape[3:]), "seq", scatter_dimension=0, tiled=False
            )
            for w in blocks1
        ]
        half1, attn_sums = summed[:3], summed[3:]
    signal_grad = results[0].reshape(tok_rows, width)
    if plan.routed:
        maps_grad = results[1].astype(F32)
    else:
        piece, tap_piece = (r.astype(F32) for r in results[1:])
        full = jnp.zeros((2, plan.filters, width, width), F32)
        full = lax.dynamic_update_slice(
            full,
            piece[None],
            (section, my_group * plan.local, my_b * plan.jb, my_a * plan.ia),
        )
        tap_piece = jnp.where(core_zero & (my_group == 0), tap_piece, 0.0)
        tap_full = lax.dynamic_update_slice(
            jnp.zeros((ORDER, width, width), F32),
            tap_piece.reshape(ORDER, plan.jb, plan.ia),
            (0, my_b * plan.jb, my_a * plan.ia),
        )
        full = jnp.concatenate([full.reshape(-1, width), tap_full.reshape(-1, width)], 0)
        maps_grad = lax.psum_scatter(full, ("section", "seq"), scatter_dimension=0, tiled=True)
    spectral_factor = lax.rsqrt(jnp.mean(hidden * hidden, axis=-1, keepdims=True) + EPSILON)
    hidden_grad, gain00 = norm_backward(hidden, spectral_factor, gains[0], signal_grad)
    inputs_grad = (mask_rows * (middle0_grad + hidden_grad)).astype(BF)

    low_part = jnp.concatenate([attn_sums[0], attn_sums[2]], 0)
    high_part = jnp.concatenate([attn_sums[1], attn_sums[3]], 0)
    attn_keep = jnp.where(core_zero, low_part, high_part).astype(F32)
    attn_take = swapped(jnp.where(core_zero, high_part, low_part).astype(BF)).astype(F32)
    attn_sum = attn_keep + attn_take
    proj_out, out_out = attn_sum[:proj_rows], attn_sum[proj_rows:]
    outs = []
    for index in range(3):
        zero, one = half0[index].astype(BF), half1[index].astype(BF)
        keep = jnp.where(core_zero, zero, one)
        take = swapped(jnp.where(core_zero, one, zero))
        low = jnp.where(core_zero, keep, take).astype(F32)
        high = jnp.where(core_zero, take, keep).astype(F32)
        if index < 2:
            rows = low.shape[0]
            joined = jnp.stack(
                [low.reshape(rows, chips, ff_half), high.reshape(rows, chips, ff_half)], 2
            ).reshape(rows, ff)
        else:
            joined = jnp.concatenate([low, high], 0)
        outs.append(joined[None])

    gain_parts = jnp.stack([jnp.stack([gain00, gain01]), jnp.stack([gain10, gain11])])
    gain_cols = width // chips
    tiles = jnp.transpose(gain_parts.reshape(2, 2, chips, gain_cols), (0, 2, 1, 3))
    tiles = jnp.pad(
        tiles.reshape(2 * chips, 2, gain_cols), ((0, 0), (0, 6), (0, LANES - gain_cols))
    )
    done_in, done_out = join_phases(inputs_grad), join_phases(block_out)
    taken, landed = exit_call(chips, jnp.where(core_zero, done_out, done_in), tiles)
    first = jnp.where(core_zero, done_in, taken)
    second = jnp.where(core_zero, taken, done_out)
    result_pair = jnp.stack([first, second])[None]
    gain_out = jnp.sum(landed, axis=0)[None, :2, :gain_cols]
    return (result_pair, maps_grad, proj_out, out_out, gain_out, outs[0], outs[1], outs[2])


def solution(mesh):
    placed = (
        P("section", None, "seq", None),
        P(),
        P("seq", None),
        P(("section", "seq"), None),
        P(("section", "seq"), None),
        P(("section", "seq"), None),
        P("section", None, "seq"),
        P("section", "seq", None),
        P("section", "seq", None),
        P("section", "seq", None),
    )
    return jax.shard_map(
        body,
        mesh=mesh,
        in_specs=placed,
        out_specs=(
            P("section", None, "seq", None),
            P(("section", "seq"), None),
            P(("section", "seq"), None),
            P(("section", "seq"), None),
            P("section", None, "seq"),
            P("section", "seq", None),
            P("section", "seq", None),
            P("section", "seq", None),
        ),
        check_vma=False,
    )
```

```python
import functools
import math

import jax
import jax.numpy as jnp
from jax import lax
from jax.experimental import pallas as pl
from jax.experimental.pallas import tpu as pltpu
from jax.sharding import PartitionSpec as P

ORDER = 3
HEAD_DIM = 64
WINDOW = 512
EPSILON = 1e-05
BIG_NEGATIVE = -1e30
MESH = pl.DeviceIdType.MESH
BF = jnp.bfloat16
F32 = jnp.float32
LANES = 128
BLOCK = 256
PIECE = 16
VMEM_LIMIT = 63 * 1024 * 1024


class Plan:
    def __init__(self, chips, tok_rows, width, filter_count, map_rows, ff):
        self.chips = chips
        self.rows = tok_rows
        self.half = tok_rows // 2
        self.width = width
        self.filters = filter_count
        self.cols_in = 4
        self.cols_out = max(1, math.isqrt(chips // 4))
        self.groups = chips // (self.cols_in * self.cols_out)
        self.local = filter_count // self.groups
        self.length = chips * self.half
        self.blocks = self.length // BLOCK
        self.jb = width // self.cols_in
        self.ia = width // self.cols_out
        self.map_rows = map_rows
        self.routed = map_rows % PIECE == 0
        self.pieces = map_rows // PIECE
        self.f_rows = -(-self.local // 16) * 16
        self.batch = 4 if self.local % 4 == 0 else 2
        self.ff = ff
        self.pick_here = ff // chips == LANES
        self.late = self.pick_here and self.routed
        self.routed = self.late
        self.side = max(1, math.isqrt(chips // 4))
        self.depth = chips // (self.side * self.side)

    def place(self, chip):
        return (
            chip // (self.side * self.side),
            lax.rem(chip // self.side, self.side),
            lax.rem(chip, self.side),
        )

    def chip_at(self, z, y, x):
        return (z * self.side + y) * self.side + x

    def routes(self, rows, index=0):
        if rows % (2 * PIECE) == 0:
            return [(0, rows // 2, True), (rows // 2, rows // 2, False)]
        return [(0, rows, index % 2 == 0)]


def spot():
    return lax.axis_index("section"), lax.axis_index("seq")


def greet_everyone(chips):
    section, chip = spot()
    me = section * chips + chip
    barrier = pltpu.get_barrier_semaphore()

    def one(step, carry):
        peer = lax.rem(me + step, 2 * chips)
        pl.semaphore_signal(
            barrier, inc=1, device_id=(peer // chips, lax.rem(peer, chips)), device_id_type=MESH
        )
        return carry

    lax.fori_loop(1, 2 * chips, one, 0)

    def wait():
        pl.semaphore_wait(barrier, 2 * chips - 1)

    return wait


def push(src, dst, send, recv, target):
    return pltpu.make_async_remote_copy(
        src_ref=src,
        dst_ref=dst,
        send_sem=send,
        recv_sem=recv,
        device_id=target,
        device_id_type=MESH,
    )


def bytes_of(ref, sem):
    pltpu.make_async_copy(ref, ref, sem).wait()


def rows_dot(left, right):
    return lax.dot_general(left, right, (((1,), (1,)), ((), ())), preferred_element_type=F32)


def cols_dot(left, right):
    return lax.dot_general(left, right, (((0,), (0,)), ((), ())), preferred_element_type=F32)


def flat_dot(left, right):
    return jnp.dot(left, right, preferred_element_type=F32)


class Flat:
    def __init__(self, ref):
        self.ref = ref
        self.split = len(ref.shape) == 5
        if self.split:
            depth, side, _, rows, _ = ref.shape
            self.plane = side * side * rows

    def columns(self, start, count):
        sl = slice(start, start + count)
        if self.split:
            return self.ref[:, :, :, :, sl].reshape(-1, count)
        return self.ref[:, sl]

    def rows(self, start, count):
        if self.split:
            sl = slice(start // self.plane, (start + count) // self.plane)
            return self.ref[sl].reshape(count, self.ref.shape[4])
        return self.ref[start : start + count, :]

    def all(self):
        return self.ref[...].reshape(-1, self.ref.shape[-1])

    def put_columns(self, start, value):
        sl = slice(start, start + value.shape[1])
        if self.split:
            shape = self.ref.shape[:4] + (value.shape[1],)
            self.ref[:, :, :, :, sl] = value.reshape(shape)
        else:
            self.ref[:, sl] = value

    def put_rows(self, start, value):
        count = value.shape[0]
        if self.split:
            sl = slice(start // self.plane, (start + count) // self.plane)
            self.ref[sl] = value.reshape((count // self.plane,) + self.ref.shape[1:])
        else:
            self.ref[start : start + count, :] = value


class Gather:
    def __init__(self, plan, shards, outs, send, recv):
        self.plan, self.shards, self.outs = plan, shards, outs
        self.send, self.recv = send, recv
        self.section, chip = spot()
        self.z, self.y, self.x = plan.place(chip)

    @staticmethod
    def semaphores(plan, count):
        return [
            pltpu.SemaphoreType.DMA((count, 5)),
            pltpu.SemaphoreType.DMA((count, 5 * plan.depth)),
        ]

    def to(self, z, y, x):
        return self.section, self.plan.chip_at(z, y, x)

    def across(self, step, along_x):
        side = self.plan.side
        if along_x:
            return self.to(self.z, self.y, lax.rem(self.x + step, side))
        return self.to(self.z, lax.rem(self.y + step, side), self.x)

    def routes(self, i):
        for number, (start, rows, x_first) in enumerate(self.plan.routes(self.shards[i].shape[0], i)):
            yield number, x_first, self.outs[i], pl.ds(start, rows)

    def level(self, t):
        return lax.rem(self.z - t + self.plan.depth, self.plan.depth)

    def begin(self):
        plan = self.plan
        for i, shard in enumerate(self.shards):
            home = self.outs[i].at[self.z, self.y, self.x]
            for step in range(1, plan.depth):
                z = lax.rem(self.z + step, plan.depth)
                push(
                    shard, home, self.send.at[i, 0], self.recv.at[i, step], self.to(z, self.y, self.x)
                ).start()
            pltpu.make_async_copy(shard, home, self.recv.at[i, 0]).start()
        self.second(0)

    def second(self, t):
        plan = self.plan
        for i, shard in enumerate(self.shards):
            z = self.level(t)
            if t > 0:
                bytes_of(self.outs[i].at[z, self.y, self.x], self.recv.at[i, t])
            for number, x_first, out, sl in self.routes(i):
                dst = out.at[z, self.y, self.x, sl]
                src = shard.at[sl] if t == 0 else dst
                for step in range(1, plan.side):
                    push(
                        src,
                        dst,
                        self.send.at[i, 1 + number],
                        self.recv.at[i, (1 + number) * plan.depth + t],
                        self.across(step, x_first),
                    ).start()

    def third(self, t):
        plan, side = self.plan, self.plan.side
        for i, shard in enumerate(self.shards):
            z = self.level(t)
            if t == 0:
                pltpu.make_async_copy(
                    shard, self.outs[i].at[z, self.y, self.x], self.recv.at[i, 0]
                ).wait()
            for number, x_first, out, sl in self.routes(i):
                sem = self.recv.at[i, (1 + number) * plan.depth + t]
                if x_first:
                    bytes_of(out.at[z, self.y, pl.ds(0, side - 1), sl], sem)
                    src = out.at[z, self.y, :, sl]
                else:
                    bytes_of(out.at[z, pl.ds(0, side - 1), self.x, sl], sem)
                    src = out.at[z, :, self.x, sl]
                for step in range(1, side):
                    push(
                        src,
                        src,
                        self.send.at[i, 3 + number],
                        self.recv.at[i, (3 + number) * plan.depth + t],
                        self.across(step, not x_first),
                    ).start()

    def end(self):
        plan, side = self.plan, self.plan.side
        for i in range(len(self.shards)):
            bytes_of(self.outs[i].at[pl.ds(0, plan.depth - 1), 0, 0], self.send.at[i, 0])
            for number, x_first, out, sl in self.routes(i):
                bytes_of(out.at[:, 0, pl.ds(0, side - 1), sl], self.send.at[i, 1 + number])
                for t in range(plan.depth):
                    bytes_of(
                        out.at[0, :, pl.ds(0, side - 1), sl],
                        self.recv.at[i, (3 + number) * plan.depth + t],
                    )
                bytes_of(out.at[:, :, pl.ds(0, side - 1), sl], self.send.at[i, 3 + number])

    def stage(self, number):
        if number > 0:
            self.third(number - 1)
        if 0 <= number < self.plan.depth - 1:
            self.second(number + 1)


class Scatter:
    @staticmethod
    def scratch(plan, shapes):
        refs = []
        for index, (rows, cols) in enumerate(shapes):
            for _, part, _ in plan.routes(rows, index):
                for lead in (
                    (plan.depth, plan.side - 1, plan.side),
                    (plan.depth, plan.side),
                    (plan.depth, plan.side - 1),
                    (plan.depth,),
                    (plan.depth - 1,),
                ):
                    refs.append(pltpu.VMEM(lead + (part, cols), BF))
        return refs

    @staticmethod
    def semaphores(plan, count):
        return [
            pltpu.SemaphoreType.DMA((count, 6)),
            pltpu.SemaphoreType.DMA((count, 4 * plan.depth + 2)),
        ]

    def __init__(self, plan, grads, outs, buffers, send, recv):
        self.plan, self.grads, self.outs = plan, grads, outs
        self.send, self.recv = send, recv
        self.section, chip = spot()
        self.z, self.y, self.x = plan.place(chip)
        self.work = []
        buffers = list(buffers)
        for i, grad in enumerate(grads):
            for number, (start, rows, x_first) in enumerate(plan.routes(grad.shape[3], i)):
                self.work.append((i, number, start, rows, x_first, buffers[:5]))
                buffers = buffers[5:]

    def to(self, z, y, x):
        return self.section, self.plan.chip_at(z, y, x)

    def level(self, t):
        return lax.rem(self.z + 1 + t, self.plan.depth)

    def begin(self):
        plan, side = self.plan, self.plan.side
        for t in range(plan.depth):
            z = self.level(t)
            for i, number, start, rows, x_first, (land, *_) in self.work:
                grad, sl = self.grads[i], pl.ds(start, rows)
                for step in range(1, side):
                    if x_first:
                        y = lax.rem(self.y + step, side)
                        src, peer = grad.at[z, y, :, sl], self.to(self.z, y, self.x)
                    else:
                        x = lax.rem(self.x + step, side)
                        src, peer = grad.at[z, :, x, sl], self.to(self.z, self.y, x)
                    push(
                        src,
                        land.at[t, step - 1],
                        self.send.at[i, number],
                        self.recv.at[i, number * plan.depth + t],
                        peer,
                    ).start()

    def second(self, t):
        plan, side = self.plan, self.plan.side
        z = self.level(t)
        for i, number, start, rows, x_first, (land, part, land2, *_) in self.work:
            grad = self.grads[i]
            bytes_of(land.at[t], self.recv.at[i, number * plan.depth + t])
            for j in range(side):
                y, x = (self.y, j) if x_first else (j, self.x)
                total = grad[z, y, x, start : start + rows, :].astype(F32)
                for step in range(side - 1):
                    total = total + land[t, step, j].astype(F32)
                part[t, j] = total.astype(BF)
            for step in range(1, side):
                if x_first:
                    j = lax.rem(self.x + step, side)
                    peer = self.to(self.z, self.y, j)
                else:
                    j = lax.rem(self.y + step, side)
                    peer = self.to(self.z, j, self.x)
                push(
                    part.at[t, j],
                    land2.at[t, step - 1],
                    self.send.at[i, 2 + number],
                    self.recv.at[i, (2 + number) * plan.depth + t],
                    peer,
                ).start()

    def third(self, t):
        plan, side = self.plan, self.plan.side
        for i, number, start, rows, x_first, (_, part, land2, line, land3) in self.work:
            bytes_of(land2.at[t], self.recv.at[i, (2 + number) * plan.depth + t])
            mine = self.x if x_first else self.y
            total = part[t, mine].astype(F32)
            for step in range(side - 1):
                total = total + land2[t, step].astype(F32)
            line[t] = total.astype(BF)
            if t < plan.depth - 1:
                push(
                    line.at[t],
                    land3.at[t],
                    self.send.at[i, 4 + number],
                    self.recv.at[i, 4 * plan.depth + number],
                    self.to(self.level(t), self.y, self.x),
                ).start()

    def end(self):
        plan = self.plan
        for i, number, start, rows, x_first, (land, part, land2, line, land3) in self.work:
            bytes_of(land3, self.recv.at[i, 4 * plan.depth + number])
            total = line[plan.depth - 1].astype(F32)
            for step in range(plan.depth - 1):
                total = total + land3[step].astype(F32)
            self.outs[i][start : start + rows, :] = total
            bytes_of(land, self.send.at[i, number])
            bytes_of(land2, self.send.at[i, 2 + number])
            bytes_of(land3, self.send.at[i, 4 + number])

    def stage(self, number):
        if number < self.plan.depth:
            self.second(number)
        if number > 0:
            self.third(number - 1)


def exit_kernel(chips, give, tiles, take, land, send, recv, gain_send, gain_recv):
    section, chip = spot()
    me = section * chips + chip
    greet_everyone(chips)()
    swap = push(give, take, send, recv, (1 - section, chip))
    swap.start()

    def one(step, carry):
        peer = lax.rem(me + step, 2 * chips)
        push(
            tiles.at[peer],
            land.at[me],
            gain_send,
            gain_recv,
            (peer // chips, lax.rem(peer, chips)),
        ).start()
        return carry

    lax.fori_loop(1, 2 * chips, one, 0)
    pltpu.make_async_copy(tiles.at[me], land.at[me], gain_recv).start()
    bytes_of(land, gain_recv)
    bytes_of(land.at[pl.ds(0, 2 * chips - 1)], gain_send)
    swap.wait()


def exit_call(chips, give, tiles):
    any_spec = pl.BlockSpec(memory_space=pl.ANY)
    return pl.pallas_call(
        functools.partial(exit_kernel, chips),
        out_shape=[
            jax.ShapeDtypeStruct(give.shape, give.dtype),
            jax.ShapeDtypeStruct(tiles.shape, tiles.dtype),
        ],
        in_specs=[any_spec] * 2,
        out_specs=[any_spec] * 2,
        scratch_shapes=[
            pltpu.SemaphoreType.DMA,
            pltpu.SemaphoreType.DMA,
            pltpu.SemaphoreType.DMA,
            pltpu.SemaphoreType.DMA,
        ],
        compiler_params=pltpu.CompilerParams(collective_id=4, has_side_effects=True),
        name="leave",
    )(give, tiles)


def filter_rows(plan, land, table, first_row, backward):
    lane = lax.broadcasted_iota(jnp.int32, (plan.f_rows, LANES), 1)
    low = lane < plan.half
    total = plan.length // LANES
    for m in range(total):
        if backward:
            one, two = 2 * m, 2 * m + 1
        else:
            one, two = plan.chips - 1 - 2 * m, plan.chips - 2 - 2 * m
        left = land[one, first_row : first_row + plan.f_rows, :].astype(F32)
        right = land[two, first_row : first_row + plan.f_rows, :].astype(F32)
        even = jnp.where(low, left, pltpu.roll(right, plan.half, 1))
        odd = jnp.where(low, pltpu.roll(left, plan.half, 1), right)
        at = LANES * m + (BLOCK if backward else 0)
        table[0, :, at : at + LANES] = even
        table[1, :, at : at + LANES] = odd
    blank = jnp.zeros((plan.f_rows, BLOCK), F32)
    at = 0 if backward else plan.length
    for parity in range(2):
        table[parity, :, at : at + BLOCK] = blank


def build_strips(plan, table, strip, backward):
    span = plan.length + BLOCK
    shift = span - LANES if backward else span - (LANES - 1)
    part = 32

    def one(k, carry):
        for parity in range(2):
            row = table[parity, pl.ds(k, 1), :]
            for start in range(0, LANES, part):
                spread = jnp.broadcast_to(row, (part, span))
                rolled = pltpu.roll(
                    spread, (shift + start) % span, 1, stride=1, stride_axis=0
                ).astype(BF)
                strip[parity, k, LANES + start : LANES + start + part, :] = rolled[
                    :, : plan.length
                ]
                strip[parity, k, start : start + part, :] = rolled[
                    :, LANES : LANES + plan.length
                ]
        return carry

    lax.fori_loop(0, plan.local, one, 0)


def sizes(plan):
    size = plan.jb // PIECE
    while size:
        yield size
        size //= 2


def owner_pieces(plan, act):
    section, chip = spot()
    start = plan.pieces * (section * plan.chips + chip)
    per_block = plan.jb // PIECE

    def block(j, carry):
        number = start // per_block + j
        base = number * per_block
        low = jnp.maximum(start - base, 0)
        high = jnp.minimum(start + plan.pieces - base, per_block)
        count = jnp.maximum(high - low, 0)
        which = number // plan.cols_in
        b = lax.rem(number, plan.cols_in)
        sign = which // plan.filters
        full = lax.rem(which, plan.filters)
        group = full // plan.local
        k = lax.rem(full, plan.local)
        for size in sizes(plan):
            done = count // (2 * size) * (2 * size)
            here = lax.rem(count // size, 2) == 1
            source = base + low - start + done
            target = low + done

            @pl.when(jnp.logical_and(here, sign < 2))
            def _():
                for a in range(plan.cols_out):
                    to_chip = a + plan.cols_out * (b + plan.cols_in * group)
                    act(source, size, False, k, target, a, sign, to_chip)

            @pl.when(jnp.logical_and(here, sign >= 2))
            def _():
                for a in range(plan.cols_out):
                    for core in range(2):
                        to_chip = a + plan.cols_out * (b + plan.cols_in * (plan.groups - 1))
                        act(source, size, True, full, target, a, core, to_chip)

        return carry

    lax.fori_loop(0, plan.pieces // per_block + 2, block, 0)


def forward_kernel(plan, *refs):
    io_ref, gain_ref, filters_ref, lengths_ref = refs[:4]
    gate_raw, up_raw, down_raw, proj_raw, attn_raw = refs[4:9]
    if plan.routed:
        maps_ref = refs[9]
        rest = refs[10:]
    else:
        mine_ref, other_ref, taps_ref = refs[9:12]
        rest = refs[12:]
    full_weights, rest = rest[:8], rest[8:]
    (
        conv_ref,
        hidden_ref,
        upstream_ref,
        pair_ref,
        gains_ref,
        mask_ref,
        v_ref,
        pq_ref,
        tapw_ref,
        x_ref,
        xs_ref,
        filt_ref,
        io_own,
        io_sib,
        gain_tile,
        gate_half,
        gate_shard,
        up_half,
        up_shard,
        down_shard,
        u_ref,
        f_ref,
        x_buf,
        xo_buf,
        xs_buf,
        xf_buf,
        f_land,
        table,
        strip,
        mine,
        other,
        taps,
        pq,
        acc,
        joined,
        y_buf,
        land,
        stage,
        io_sem,
        gain_send,
        gain_recv,
        s_send,
        s_recv,
        u_send,
        x_recv,
        f_send,
        f_recv,
        m_send,
        m_recv,
        t_recv,
        o_send,
        o_recv,
        c_send,
        c_recv,
        v_sem,
        out_sem,
        w_send,
        w_recv,
    ) = rest
    chips, half, jb, ia, rows_here = plan.chips, plan.half, plan.jb, plan.ia, plan.rows
    section, chip = spot()
    dev = section * chips + chip
    sibling = (1 - section, chip)
    my_group = chip // (plan.cols_out * plan.cols_in)
    greeted = greet_everyone(chips)

    row = lax.broadcasted_iota(jnp.int32, (rows_here, rows_here), 0)
    col = lax.broadcasted_iota(jnp.int32, (rows_here, rows_here), 1)
    order = jnp.where(col == 2 * lax.rem(row, half) + row // half, 1.0, 0.0).astype(BF)
    for i in range(2):
        io_own[i] = flat_dot(order, io_ref[i]).astype(BF)
    cols = gain_ref.shape[1]
    gain_tile[0] = jnp.zeros((8, LANES), F32)
    gain_tile[0, 0:2, 0:cols] = gain_ref[...].astype(F32)
    if plan.pick_here:
        lane = lax.broadcasted_iota(jnp.int32, (gate_raw.shape[0], LANES), 1)
        low = lane < half
        for raw, halves, shard in ((gate_raw, gate_half, gate_shard), (up_raw, up_half, up_shard)):
            for j in range(raw.shape[1] // (2 * LANES)):
                one = raw[:, 2 * LANES * j : 2 * LANES * j + LANES].astype(F32)
                two = raw[:, 2 * LANES * j + LANES : 2 * LANES * (j + 1)].astype(F32)
                zero_half = jnp.where(low, one, pltpu.roll(two, half, 1)).astype(BF)
                one_half = jnp.where(low, pltpu.roll(one, half, 1), two).astype(BF)
                at = slice(LANES * j, LANES * (j + 1))
                shard[section, :, at] = jnp.where(section == 0, zero_half, one_half)
                halves[:, at] = jnp.where(section == 0, one_half, zero_half)
    else:
        for raw, halves, shard in ((gate_raw, gate_half, gate_shard), (up_raw, up_half, up_shard)):
            shard[section] = raw[section]
            halves[...] = raw[1 - section]
    part = down_shard.shape[1]
    down_shard[section] = down_raw[pl.ds(pl.multiple_of(part * section, 16), part), :]
    greeted()
    io_swap = push(io_own, io_sib, io_sem.at[0], io_sem.at[1], sibling)
    io_swap.start()

    gain_swap = push(gain_tile.at[0], gain_tile.at[1], gain_send, gain_recv, sibling)
    gain_swap.start()
    shares = [
        push(src, dst, s_send.at[i], s_recv.at[i], sibling)
        for i, (src, dst) in enumerate(
            (
                (gate_half, gate_shard.at[section]),
                (up_half, up_shard.at[section]),
                (
                    down_raw.at[pl.ds(pl.multiple_of(part * (1 - section), 16), part), :],
                    down_shard.at[section],
                ),
            )
        )
    ]
    for share in shares:
        share.start()

    if plan.routed:

        def places(source, size, tap, k, target, a):
            rows = size * PIECE
            src = maps_ref.at[pl.ds(PIECE * source, rows), pl.ds(a * ia, ia)]
            if tap:
                return src, taps.at[pl.ds(jb * k + PIECE * target, rows), :], t_recv
            return src, mine.at[k, pl.ds(PIECE * target, rows), :], m_recv

        def start_piece(source, size, tap, k, target, a, to_section, to_chip):
            src, dst, sem = places(source, size, tap, k, target, a)
            here = to_section * chips + to_chip == dev

            @pl.when(here)
            def _():
                pltpu.make_async_copy(src, dst, sem).start()

            @pl.when(jnp.logical_not(here))
            def _():
                push(src, dst, m_send, sem, (to_section, to_chip)).start()

        def drain_piece(source, size, tap, k, target, a, to_section, to_chip):
            src, dst, sem = places(source, size, tap, k, target, a)

            @pl.when(to_section * chips + to_chip != dev)
            def _():
                push(src, dst, m_send, sem, (to_section, to_chip)).wait_send()

        owner_pieces(plan, start_piece)

    lag = lax.broadcasted_iota(jnp.int32, (rows_here, LANES), 0)
    lane = lax.broadcasted_iota(jnp.int32, (rows_here, LANES), 1)
    stretch = lax.rem(lane, half)
    backwards = jnp.where(lag == 2 * (half - 1 - stretch) + lane // half, 1.0, 0.0).astype(BF)
    plain = jnp.where(lag == 2 * stretch + lane // half, 1.0, 0.0).astype(BF)
    gain_swap.wait_recv()
    core_zero = section == 0
    own_gain, sib_gain = gain_tile[0], gain_tile[1]
    gain_rows = jnp.concatenate(
        [jnp.where(core_zero, own_gain, sib_gain), jnp.where(core_zero, sib_gain, own_gain)], 0
    ).astype(BF)
    for group in range(plan.groups):
        source = lax.broadcasted_iota(jnp.int32, (plan.filters, plan.f_rows), 0)
        target = lax.broadcasted_iota(jnp.int32, (plan.filters, plan.f_rows), 1)
        chosen = jnp.where(
            (source == group * plan.local + target) & (target < plan.local), 1.0, 0.0
        ).astype(BF)
        some = flat_dot(filters_ref[...], chosen).astype(BF)
        f_ref[group, : plan.f_rows, :] = cols_dot(some, backwards).astype(BF)
        f_ref[group, plan.f_rows : 2 * plan.f_rows, :] = cols_dot(some, plain).astype(BF)
        f_ref[group, 2 * plan.f_rows :, :] = gain_rows

    def send_f(step, carry):
        peer = lax.rem(chip + step, chips)
        group = peer // (plan.cols_out * plan.cols_in)
        push(f_ref.at[group], f_land.at[chip], f_send, f_recv, (section, peer)).start()
        return carry

    lax.fori_loop(1, chips, send_f, 0)
    pltpu.make_async_copy(f_ref.at[my_group], f_land.at[chip], f_recv).start()
    for share in shares:
        share.wait_recv()
    second_layer = (gate_shard.at[1], up_shard.at[1], down_shard.at[1])
    parts = [
        (0, (gate_shard.at[0], up_shard.at[0], down_shard.at[0])),
        (3, (proj_raw, attn_raw)),
    ]
    if not plan.late:
        parts.append((5, second_layer))
    groups = []
    for first, arrays in parts:
        last = first + len(arrays)
        groups.append(
            Gather(
                plan,
                arrays,
                full_weights[first:last],
                w_send.at[pl.ds(first, len(arrays))],
                w_recv.at[pl.ds(first, len(arrays))],
            )
        )
    layer0, attention = groups[:2]
    layer0.begin()
    position = lax.broadcasted_iota(jnp.int32, (rows_here, 1), 0)
    position = chip * rows_here + 2 * lax.rem(position, half) + position // half
    length_own = jnp.where(section == 0, lengths_ref[0], lengths_ref[1])
    length_other = jnp.where(section == 0, lengths_ref[1], lengths_ref[0])
    mask = jnp.where(position < length_own, 1.0, 0.0)
    mask_other = jnp.where(position < length_other, 1.0, 0.0)
    mask_ref[...] = mask
    io_swap.wait()
    bytes_of(f_land, f_recv)
    pick_row = lax.broadcasted_iota(jnp.int32, (LANES, plan.width), 0)
    pick_col = lax.broadcasted_iota(jnp.int32, (LANES, plan.width), 1)
    repeat = jnp.where(pick_row == lax.rem(pick_col, cols), 1.0, 0.0).astype(BF)
    tile_row = lax.broadcasted_iota(jnp.int32, (chips * 16, plan.width), 0)
    tile_col = lax.broadcasted_iota(jnp.int32, (chips * 16, plan.width), 1)
    rows_all = f_land[:, 2 * plan.f_rows :, :].reshape(chips * 16, LANES)
    spread = jnp.where(
        tile_row // 16 == tile_col // cols, flat_dot(rows_all, repeat), 0.0
    ).astype(BF)
    gain_row = lax.broadcasted_iota(jnp.int32, (16, chips * 16), 0)
    gain_col = lax.broadcasted_iota(jnp.int32, (16, chips * 16), 1)
    gather_rows = jnp.where(lax.rem(gain_col, 16) == gain_row, 1.0, 0.0).astype(BF)
    gathered = flat_dot(gather_rows, spread)
    gains_ref[0:2, :] = gathered[0:2, :]
    gains_ref[2:4, :] = gathered[8:10, :]
    gains_ref[4:8, :] = jnp.zeros((4, plan.width), F32)
    hidden = jnp.where(core_zero, io_own[0], io_sib[1]).astype(F32) * mask
    hidden_ref[...] = hidden
    factor = lax.rsqrt(jnp.mean(hidden * hidden, axis=-1, keepdims=True) + EPSILON)
    u = (hidden * factor * gains_ref[0:1, :]).astype(BF)
    for b in range(plan.cols_in):
        u_ref[b, :, :jb] = u[:half, b * jb : (b + 1) * jb]
        u_ref[b, :, jb:] = u[half:, b * jb : (b + 1) * jb]

    def send_u(step, carry):
        peer = lax.rem(chip + step, chips)
        b = lax.rem(peer // plan.cols_out, plan.cols_in)
        push(
            u_ref.at[b],
            x_buf.at[pl.ds(half * chip, half), :],
            u_send,
            x_recv,
            (section, peer),
        ).start()
        return carry

    lax.fori_loop(1, chips, send_u, 0)
    pltpu.make_async_copy(
        u_ref.at[lax.rem(chip // plan.cols_out, plan.cols_in)],
        x_buf.at[pl.ds(half * chip, half), :],
        x_recv,
    ).start()
    for group in groups[1:]:
        group.begin()
    kept_copies = []
    if plan.late:
        for i, (src, dst) in enumerate(zip(second_layer, full_weights[5:])):
            kept_copies.append(pltpu.make_async_copy(src, dst, w_recv.at[5 + i, 0]))
            kept_copies[-1].start()
    cot_own = jnp.where(core_zero, io_sib[0], io_own[1]).astype(F32) * mask
    cot_other = jnp.where(core_zero, io_sib[1], io_own[0]).astype(F32) * mask_other
    upstream_ref[...] = cot_own
    pair_ref[:rows_here, :] = cot_own.astype(BF)
    pair_ref[rows_here:, :] = cot_other.astype(BF)
    layer0.stage(0)
    filter_rows(plan, f_land, table, 0, False)
    build_strips(plan, table, strip, False)
    filt_out = pltpu.make_async_copy(f_land, filt_ref, out_sem.at[0])
    filt_out.start()

    if plan.routed:
        bytes_of(mine, m_recv)
        swap = push(mine, other, o_send, o_recv, (1 - section, chip))
        swap.start()

        @pl.when(my_group == plan.groups - 1)
        def _():
            bytes_of(taps, t_recv)

        @pl.when(my_group != plan.groups - 1)
        def _():
            taps[...] = jnp.zeros_like(taps)
    else:
        for src, dst in ((mine_ref, mine), (other_ref, other), (taps_ref, taps)):
            pltpu.sync_copy(src, dst)

    layer0.stage(1)
    bytes_of(x_buf, x_recv)
    x_out = pltpu.make_async_copy(x_buf, x_ref, out_sem.at[1])
    x_out.start()
    xf_buf[0:8, :] = jnp.zeros((8, 2 * jb), F32)
    for i in range(plan.blocks):
        rows = slice(BLOCK * i, BLOCK * (i + 1))
        xf_buf[8 + BLOCK * i : 8 + BLOCK * (i + 1), :] = x_buf[rows, :].astype(F32)
    for i in range(plan.blocks):
        rows = slice(BLOCK * i, BLOCK * (i + 1))
        moved = xf_buf[7 + BLOCK * i : 7 + BLOCK * (i + 1), :].astype(BF)
        xs_buf[rows, :] = moved
        xo_buf[rows, :jb] = x_buf[rows, :jb]
        xo_buf[rows, jb:] = moved[:, jb:]
    xs_out = pltpu.make_async_copy(xs_buf, xs_ref, out_sem.at[2])
    xs_out.start()

    if plan.routed:
        swap.wait()
    turn = (1 - 2 * section).astype(F32)

    def mix(k, carry):
        first = mine[k].astype(F32)
        second = other[k].astype(F32)
        pq[k, :jb, :] = (first + second).astype(BF)
        pq[k, jb:, :] = ((first - second) * turn).astype(BF)
        return carry

    lax.fori_loop(0, plan.local, mix, 0)
    pq_out = pltpu.make_async_copy(pq, pq_ref, out_sem.at[3])
    pq_out.start()
    taps_out = pltpu.make_async_copy(taps, tapw_ref, out_sem.at[4])
    taps_out.start()

    layer0.stage(2)
    attention.stage(0)
    batch = plan.batch
    for i in range(plan.blocks):
        if i == 1:
            layer0.stage(3)
            attention.stage(1)
        if i == 2:
            layer0.stage(4)
            attention.stage(2)
        if i == 3:
            attention.stage(3)
            attention.stage(4)
        rows = slice(BLOCK * i, BLOCK * (i + 1))
        depth = BLOCK * (i + 1)
        offset = plan.length - depth
        x_now = x_buf[rows, :]
        s_now = xs_buf[rows, :]
        acc[:BLOCK] = flat_dot(
            jnp.concatenate([x_now[:, :jb], s_now[:, jb:]], 1), taps[: 2 * jb, :]
        ) + flat_dot(s_now[:, :jb], taps[2 * jb :, :])
        acc[BLOCK:] = flat_dot(
            jnp.concatenate([x_now[:, jb:], x_now[:, :jb]], 1), taps[: 2 * jb, :]
        ) + flat_dot(s_now[:, jb:], taps[2 * jb :, :])

        def step(t, carry, i=i, depth=depth, offset=offset):
            count = plan.local // batch * i + t
            slot = lax.rem(count, 2)
            some = pl.ds(batch * t, batch)
            v_copy = pltpu.make_async_copy(
                stage.at[slot], v_ref.at[some, :, pl.ds(BLOCK * i, BLOCK), :], v_sem.at[slot]
            )
            even = flat_dot(
                strip[0, some, :, offset:].reshape(batch * BLOCK, depth), x_buf[:depth, :]
            ).astype(BF)
            odd = flat_dot(
                strip[1, some, :, offset:].reshape(batch * BLOCK, depth), xo_buf[:depth, :]
            ).astype(BF)
            if i == 0:
                pl.when(t >= 2)(v_copy.wait)
            else:
                v_copy.wait()
            for k in range(batch):
                here = slice(BLOCK * k, BLOCK * (k + 1))
                first = jnp.concatenate([even[here, :jb], odd[here, jb:]], 1)
                second = jnp.concatenate([even[here, jb:], odd[here, :jb]], 1)
                stage[slot, k, 0] = first
                stage[slot, k, 1] = second
                lanes = slice(2 * jb * k, 2 * jb * (k + 1))
                joined[:BLOCK, lanes] = first
                joined[BLOCK:, lanes] = second
            v_copy.start()
            acc[...] += flat_dot(joined[...], pq[some].reshape(batch * 2 * jb, ia))
            return carry

        lax.fori_loop(0, plan.local // batch, step, 0)
        y_buf[0, rows, :] = acc[:BLOCK].astype(BF)
        y_buf[1, rows, :] = acc[BLOCK:].astype(BF)

        def give(r, carry, i=i):
            peer = BLOCK // half * i + r
            src = y_buf.at[:, pl.ds(half * peer, half), :]

            @pl.when(peer == chip)
            def _():
                pltpu.make_async_copy(src, land.at[chip], c_recv).start()

            @pl.when(peer != chip)
            def _():
                push(src, land.at[chip], c_send, c_recv, (section, peer)).start()

            return carry

        lax.fori_loop(0, BLOCK // half, give, 0)

    if not plan.late:
        for turn_number in range(plan.depth + 1):
            groups[2].stage(turn_number)
    for slot in range(2):
        pltpu.make_async_copy(
            stage.at[slot], v_ref.at[pl.ds(0, batch), :, pl.ds(0, BLOCK), :], v_sem.at[slot]
        ).wait()
    bytes_of(x_buf.at[pl.ds(0, half * (chips - 1)), :], u_send)
    bytes_of(f_land.at[pl.ds(0, chips - 1)], f_send)
    if plan.routed:
        owner_pieces(plan, drain_piece)
    for copy in (filt_out, x_out, xs_out, pq_out, taps_out):
        copy.wait()
    bytes_of(land, c_recv)
    for a in range(plan.cols_out):
        total = None
        for other_part in range(plan.cols_in * plan.groups):
            term = land[a + plan.cols_out * other_part].astype(F32)
            total = term if total is None else total + term
        conv_ref[:, :, a * ia : (a + 1) * ia] = total
    bytes_of(land.at[pl.ds(0, chips - 1)], c_send)
    for group in groups:
        group.end()
    for copy in kept_copies:
        copy.wait()
    gain_swap.wait_send()
    for share in shares:
        share.wait_send()


def forward_call(plan, io, gain, filters, lengths, raw, maps):
    chips, half, jb, ia, rows = plan.chips, plan.half, plan.jb, plan.ia, plan.rows
    width = plan.width
    any_spec = pl.BlockSpec(memory_space=pl.ANY)
    vmem_spec = pl.BlockSpec(memory_space=pltpu.VMEM)
    smem_spec = pl.BlockSpec(memory_space=pltpu.SMEM)
    dma = pltpu.SemaphoreType.DMA
    down, proj, attn = raw[2].shape, raw[3].shape, raw[4].shape
    share = (raw[0].shape[-2], plan.ff // 2)
    down_share = (down[0] // 2, width)
    grid = (plan.depth, plan.side, plan.side)
    layer = [share, share, down_share]
    gathered = [grid + w for w in layer + [proj, attn]]
    gathered += layer if plan.late else [grid + w for w in layer]
    shapes = [(w, BF) for w in gathered] + [
        ((2, half, width), F32),
        ((rows, width), F32),
        ((rows, width), F32),
        ((2 * rows, width), BF),
        ((8, width), F32),
        ((rows, 1), F32),
        ((plan.local, 2, plan.length, 2 * jb), BF),
        ((plan.local, 2 * jb, ia), BF),
        ((ORDER * jb, ia), BF),
        ((plan.length, 2 * jb), BF),
        ((plan.length, 2 * jb), BF),
        ((chips, 2 * plan.f_rows + 16, LANES), BF),
    ]
    return pl.pallas_call(
        functools.partial(forward_kernel, plan),
        out_shape=[jax.ShapeDtypeStruct(s, d) for s, d in shapes],
        in_specs=[vmem_spec] * 3
        + [smem_spec]
        + [vmem_spec] * 3
        + [any_spec] * 2
        + [vmem_spec if plan.routed else any_spec] * len(maps),
        out_specs=[any_spec] * 8 + [vmem_spec] * 6 + [any_spec] * 6,
        scratch_shapes=[
            pltpu.VMEM((2, rows, width), BF),
            pltpu.VMEM((2, rows, width), BF),
            pltpu.VMEM((2, 8, LANES), F32),
            pltpu.VMEM(share, BF),
            pltpu.VMEM((2,) + share, BF),
            pltpu.VMEM(share, BF),
            pltpu.VMEM((2,) + share, BF),
            pltpu.VMEM((2,) + down_share, BF),
            pltpu.VMEM((plan.cols_in, half, 2 * jb), BF),
            pltpu.VMEM((plan.groups, 2 * plan.f_rows + 16, LANES), BF),
            pltpu.VMEM((plan.length, 2 * jb), BF),
            pltpu.VMEM((plan.length, 2 * jb), BF),
            pltpu.VMEM((plan.length, 2 * jb), BF),
            pltpu.VMEM((plan.length + 8, 2 * jb), F32),
            pltpu.VMEM((chips, 2 * plan.f_rows + 16, LANES), BF),
            pltpu.VMEM((2, plan.f_rows, plan.length + BLOCK), F32),
            pltpu.VMEM((2, plan.local, BLOCK, plan.length), BF),
            pltpu.VMEM((plan.local, jb, ia), BF),
            pltpu.VMEM((plan.local, jb, ia), BF),
            pltpu.VMEM((ORDER * jb, ia), BF),
            pltpu.VMEM((plan.local, 2 * jb, ia), BF),
            pltpu.VMEM((2 * BLOCK, ia), F32),
            pltpu.VMEM((2 * BLOCK, plan.batch * 2 * jb), BF),
            pltpu.VMEM((2, plan.length, ia), BF),
            pltpu.VMEM((chips, 2, half, ia), BF),
            pltpu.VMEM((2, plan.batch, 2, BLOCK, 2 * jb), BF),
            dma((2,)),
            dma,
            dma,
            dma((3,)),
            dma((3,)),
        ]
        + [dma] * 11
        + [dma((2,)), dma((5,)), *Gather.semaphores(plan, 8)],
        compiler_params=pltpu.CompilerParams(
            collective_id=2, has_side_effects=True, vmem_limit_bytes=VMEM_LIMIT
        ),
        name="spectral_forward",
    )(io, gain, filters, lengths, *raw, *maps)


def backward_kernel(plan, number, *refs):
    g_ref, filt_ref, v_ref, pq, tapw, x_ref, xs_ref = refs[:7]
    grads, rest = refs[7 : 7 + number], refs[7 + number :]
    if plan.late:
        hidden_ref, gains_ref, mask_ref, dmid_ref, out_ref, gain_sums_ref, *half1 = rest[:9]
        res_ref, gate_ref, up_ref, down_ref, proj_ref, attn_ref, gain_out, dmaps_ref = rest[9:17]
        du_ref, gain_buf, gain_land, give_res, *half_parts = rest[17:30]
        half0, crossing, arrived = half_parts[:3], half_parts[3:6], half_parts[6:9]
        e_send, e_recv, n_send, n_recv = rest[30:34]
        rest = rest[34:]
        sums = [*half0, proj_ref, attn_ref]
    else:
        sums, rest = rest[:number], rest[number:]
        du_ref, dmap_ref, dtap_ref = rest[:3]
        rest = rest[3:]
    count = 5 * sum(len(plan.routes(grad.shape[3])) for grad in grads)
    scatter = Scatter(plan, grads, sums, rest[:count], *rest[count : count + 2])
    rest = rest[count + 2 :]
    (
        g_buf,
        gt_buf,
        table,
        strip,
        v_buf,
        z_even,
        z_odd,
        acc_even,
        acc_odd,
        kept,
        give_m,
        take_m,
        total_m,
        kept_t,
        give_t,
        take_t,
        total_t,
        du_buf,
        land,
        g_send,
        g_recv,
        v_sem,
        m_send,
        m_recv,
        t_send,
        t_recv,
        w_send,
        w_recv,
        d_send,
        d_recv,
        x_sem,
    ) = rest
    chips, half, jb, ia = plan.chips, plan.half, plan.jb, plan.ia
    section, chip = spot()
    dev = section * chips + chip
    my_a = lax.rem(chip, plan.cols_out)
    my_b = lax.rem(chip // plan.cols_out, plan.cols_in)
    my_group = chip // (plan.cols_out * plan.cols_in)
    sibling = (1 - section, chip)
    greet_everyone(chips)()

    def send_g(step, carry):
        peer = lax.rem(chip + step, chips)
        a = lax.rem(peer, plan.cols_out)
        push(
            g_ref.at[:, :, pl.ds(pl.multiple_of(a * ia, ia), ia)],
            g_buf.at[:, pl.ds(half * chip, half), :],
            g_send,
            g_recv,
            (section, peer),
        ).start()
        return carry

    lax.fori_loop(1, chips, send_g, 0)
    pltpu.make_async_copy(
        g_ref.at[:, :, pl.ds(pl.multiple_of(my_a * ia, ia), ia)],
        g_buf.at[:, pl.ds(half * chip, half), :],
        g_recv,
    ).start()
    v_copy = [pltpu.make_async_copy(v_ref.at[k], v_buf.at[k], v_sem.at[k]) for k in range(2)]
    for copy in v_copy:
        copy.start()
    x_copy = [
        pltpu.make_async_copy(src, dst, x_sem.at[i])
        for i, (src, dst) in enumerate(((x_ref, z_even), (xs_ref, z_odd)))
    ]
    for copy in x_copy:
        copy.start()
    scatter.begin()
    filter_rows(plan, filt_ref, table, plan.f_rows, True)
    build_strips(plan, table, strip, True)
    acc_even[...] = jnp.zeros_like(acc_even)
    acc_odd[...] = jnp.zeros_like(acc_odd)
    bytes_of(g_buf, g_recv)
    for phase in range(2):
        for i in range(plan.blocks):
            rows = slice(BLOCK * i, BLOCK * (i + 1))
            gt_buf[phase, :, rows] = g_buf[phase, rows, :].astype(F32).T.astype(BF)
    turn = (1 - 2 * section).astype(F32)
    half_ways = (((1,), (1,)), ((), ()))

    def piece_copies(k, tap, begin):
        per_block = jb // PIECE
        which = 2 * plan.filters + k if tap else section * plan.filters + my_group * plan.local + k
        start = (which * plan.cols_in + my_b) * per_block
        owner, row = start // plan.pieces, lax.rem(start, plan.pieces)
        first = jnp.minimum(plan.pieces - row, per_block)
        for to, at, base, count in ((owner, row, 0, first), (owner + 1, 0, first, per_block - first)):
            for size in sizes(plan):
                done = count // (2 * size) * (2 * size)
                rows = size * PIECE
                here = lax.rem(count // size, 2) == 1
                source = PIECE * (base + done)
                src = (
                    total_t.at[pl.ds(jb * k + source, rows), :]
                    if tap
                    else total_m.at[k, pl.ds(source, rows), :]
                )
                dst = dmaps_ref.at[
                    pl.ds(PIECE * (at + done), rows), pl.ds(pl.multiple_of(my_a * ia, ia), ia)
                ]
                if begin:

                    @pl.when(jnp.logical_and(here, to == dev))
                    def _():
                        pltpu.make_async_copy(src, dst, w_recv).start()

                @pl.when(jnp.logical_and(here, to != dev))
                def _():
                    copy = push(src, dst, w_send, w_recv, (to // chips, lax.rem(to, chips)))
                    if begin:
                        copy.start()
                    else:
                        copy.wait_send()

    def exchange(k):
        return push(give_m.at[k], take_m.at[k], m_send.at[k], m_recv.at[k], (1 - section, chip))

    def finish(k):
        exchange(k).wait()
        total_m[k] = (kept[k] + take_m[k].astype(F32)).astype(BF)
        if plan.routed:
            piece_copies(k, False, True)

    for copy in x_copy:
        copy.wait()
    x_even, x_odd = z_even[:, :jb], z_even[:, jb:]
    s_even, s_odd = z_odd[:, :jb], z_odd[:, jb:]
    for tap, (on_even, on_odd) in enumerate(((x_even, x_odd), (s_odd, x_even), (s_even, s_odd))):
        tap_grad = jnp.dot(gt_buf[0], on_even, preferred_element_type=F32) + jnp.dot(
            gt_buf[1], on_odd, preferred_element_type=F32
        )
        tap_grad = tap_grad.T
        kept_t[tap * jb : (tap + 1) * jb, :] = tap_grad
        give_t[tap * jb : (tap + 1) * jb, :] = tap_grad.astype(BF)
    tap_swap = push(give_t, take_t, t_send, t_recv, (1 - section, chip))
    tap_swap.start()
    for i in range(plan.blocks):
        rows = slice(BLOCK * i, BLOCK * (i + 1))
        from_even = lax.dot_general(
            g_buf[0, rows, :], tapw[...], half_ways, preferred_element_type=F32
        )
        from_odd = lax.dot_general(
            g_buf[1, rows, :], tapw[...], half_ways, preferred_element_type=F32
        )
        acc_even[rows, :jb] = from_even[:, :jb] + from_odd[:, jb : 2 * jb]
        acc_even[rows, jb : 2 * jb] = from_odd[:, :jb]
        acc_odd[rows, :jb] = from_even[:, 2 * jb :]
        acc_odd[rows, jb : 2 * jb] = from_even[:, jb : 2 * jb] + from_odd[:, 2 * jb :]

    def step(k, carry):
        slot = lax.rem(k, 2)
        from_even = rows_dot(g_buf[0], pq[k]).astype(BF)
        from_odd = rows_dot(g_buf[1], pq[k]).astype(BF)
        z_even[:, :jb] = from_even[:, :jb]
        z_even[:, jb:] = from_odd[:, :jb]
        z_odd[:, :jb] = from_odd[:, jb:]
        z_odd[:, jb:] = from_even[:, jb:]
        pltpu.make_async_copy(v_ref.at[k], v_buf.at[slot], v_sem.at[slot]).wait()
        grad = jnp.dot(gt_buf[0], v_buf[slot, 0], preferred_element_type=F32) + jnp.dot(
            gt_buf[1], v_buf[slot, 1], preferred_element_type=F32
        )
        grad = grad.T
        plus, minus = grad[:jb, :], grad[jb:, :] * turn
        kept[k] = plus + minus
        give_m[k] = (plus - minus).astype(BF)
        exchange(k).start()

        @pl.when(k + 2 < plan.local)
        def _():
            pltpu.make_async_copy(v_ref.at[k + 2], v_buf.at[slot], v_sem.at[slot]).start()

        for j in range(plan.blocks):
            rows = slice(BLOCK * j, BLOCK * (j + 1))
            depth = plan.length - BLOCK * j
            acc_even[rows, :] += jnp.dot(
                strip[0, k, :, :depth], z_even[BLOCK * j :, :], preferred_element_type=F32
            )
            out = jnp.dot(
                strip[1, k, :, :depth], z_odd[BLOCK * j :, :], preferred_element_type=F32
            )
            acc_even[rows, :jb] += out[:, :jb]
            acc_odd[rows, jb:] += out[:, jb:]

        @pl.when(k >= 1)
        def _():
            finish(k - 1)

        for turn_number in range(plan.depth + 1):
            at = 1 + (turn_number * (plan.local - 2)) // plan.depth
            pl.when(k == at)(functools.partial(scatter.stage, turn_number))
        return carry

    lax.fori_loop(0, plan.local, step, 0)
    for i in range(plan.blocks):
        rows = slice(BLOCK * i, BLOCK * (i + 1))
        moved = acc_odd[BLOCK * i + 1 : BLOCK * (i + 1) + 1, :]
        both = (acc_even[rows, :] + moved).astype(BF)
        du_buf[0, rows, :] = both[:, :jb]
        du_buf[1, rows, :] = both[:, jb:]

        def give(r, carry, i=i):
            peer = BLOCK // half * i + r
            src = du_buf.at[:, pl.ds(half * peer, half), :]

            @pl.when(peer == chip)
            def _():
                pltpu.make_async_copy(src, land.at[chip], d_recv).start()

            @pl.when(peer != chip)
            def _():
                push(src, land.at[chip], d_send, d_recv, (section, peer)).start()

            return carry

        lax.fori_loop(0, BLOCK // half, give, 0)
    finish(plan.local - 1)
    tap_swap.wait()
    total_t[...] = (kept_t[...] + take_t[...].astype(F32)).astype(BF)
    if plan.routed:

        @pl.when(jnp.logical_and(section == 0, my_group == plan.groups - 1))
        def _():
            for tap in range(ORDER):
                piece_copies(tap, True, True)
    else:
        pltpu.sync_copy(total_m, dmap_ref)
        pltpu.sync_copy(total_t, dtap_ref)
    bytes_of(g_buf.at[0, pl.ds(0, 2 * half * (chips - 1) // 2), :], g_send)
    bytes_of(g_buf.at[1, pl.ds(0, 2 * half * (chips - 1) // 2), :], g_send)
    bytes_of(land, d_recv)
    for b in range(plan.cols_in):
        total = None
        for c in range(plan.groups):
            for a in range(plan.cols_out):
                term = land[a + plan.cols_out * (b + plan.cols_in * c)].astype(F32)
                total = term if total is None else total + term
        du_ref[:, :, b * jb : (b + 1) * jb] = total
    bytes_of(land.at[pl.ds(0, chips - 1)], d_send)
    scatter.end()
    if plan.late:
        core_zero = section == 0
        for i in range(3):
            crossing[i][...] = jnp.where(core_zero, half1[i][...], half0[i][...])
            push(crossing[i], arrived[i], e_send.at[i], e_recv.at[i], sibling).start()
        hidden = hidden_ref[...]
        factor = lax.rsqrt(jnp.mean(hidden * hidden, axis=-1, keepdims=True) + EPSILON)
        signal_grad = du_ref[...].reshape(plan.rows, plan.width)
        weighted = signal_grad * gains_ref[0:1, :]
        correction = jnp.mean(weighted * hidden, axis=-1, keepdims=True)
        hidden_grad = factor * weighted - hidden * factor * factor * factor * correction
        gain_buf[...] = gain_sums_ref[...]
        gain_buf[0:1, :] = jnp.sum(signal_grad * hidden * factor, axis=0, keepdims=True)
        per_tile = LANES * chips // plan.width

        def send_gain(step, carry):
            peer = lax.rem(dev + step, 2 * chips)
            tile = lax.rem(peer, chips) // per_tile
            push(
                gain_buf.at[:, pl.ds(pl.multiple_of(LANES * tile, LANES), LANES)],
                gain_land.at[dev],
                n_send,
                n_recv,
                (peer // chips, lax.rem(peer, chips)),
            ).start()
            return carry

        lax.fori_loop(1, 2 * chips, send_gain, 0)
        pltpu.make_async_copy(
            gain_buf.at[:, pl.ds(pl.multiple_of(LANES * (chip // per_tile), LANES), LANES)],
            gain_land.at[dev],
            n_recv,
        ).start()
        done_in = (mask_ref[...] * (dmid_ref[...] + hidden_grad)).astype(BF)
        row = lax.broadcasted_iota(jnp.int32, (plan.rows, plan.rows), 0)
        col = lax.broadcasted_iota(jnp.int32, (plan.rows, plan.rows), 1)
        order = jnp.where(col == 2 * lax.rem(row, half) + row // half, 1.0, 0.0).astype(BF)
        done_in = cols_dot(order, done_in).astype(BF)
        done_out = cols_dot(order, out_ref[...]).astype(BF)
        give_res[...] = jnp.where(core_zero, done_out, done_in)
        swap_res = push(give_res, res_ref.at[section], e_send.at[3], e_recv.at[3], sibling)
        swap_res.start()
        res_ref[section] = jnp.where(core_zero, done_in, done_out)
        for i in range(3):
            push(crossing[i], arrived[i], e_send.at[i], e_recv.at[i], sibling).wait()
        lane = lax.broadcasted_iota(jnp.int32, (gate_ref.shape[0], LANES), 1)
        low = lane < half
        kept_half = [jnp.where(core_zero, half0[i][...], half1[i][...]) for i in range(3)]
        for i, out in ((0, gate_ref), (1, up_ref)):
            came = arrived[i][...]
            first = jnp.where(core_zero, kept_half[i], came)
            second = jnp.where(core_zero, came, kept_half[i])
            for j in range(out.shape[1] // (2 * LANES)):
                one, two = (w[:, LANES * j : LANES * (j + 1)] for w in (first, second))
                at = 2 * LANES * j
                out[:, at : at + LANES] = jnp.where(low, one, pltpu.roll(two, half, 1))
                out[:, at + LANES : at + 2 * LANES] = jnp.where(
                    low, pltpu.roll(one, half, 1), two
                )
        part = half0[2].shape[0]
        came = arrived[2][...]
        down_ref[:part, :] = jnp.where(core_zero, kept_half[2], came)
        down_ref[part:, :] = jnp.where(core_zero, came, kept_half[2])
        swap_res.wait()
        bytes_of(gain_land, n_recv)
        gain_out[...] = jnp.sum(gain_land[...], axis=0)
        bytes_of(gain_land.at[pl.ds(0, 2 * chips - 1)], n_send)
    if plan.routed:

        def drain(k, carry):
            piece_copies(k, False, False)
            return carry

        lax.fori_loop(0, plan.local, drain, 0)

        @pl.when(jnp.logical_and(section == 0, my_group == plan.groups - 1))
        def _():
            for tap in range(ORDER):
                piece_copies(tap, True, False)

        bytes_of(dmaps_ref, w_recv)


def backward_call(plan, g, filt, v, pq, tapw, x, xs, grads, rest=()):
    chips, half, jb, ia = plan.chips, plan.half, plan.jb, plan.ia
    any_spec = pl.BlockSpec(memory_space=pl.ANY)
    vmem_spec = pl.BlockSpec(memory_space=pltpu.VMEM)
    dma = pltpu.SemaphoreType.DMA
    shapes = [g_part.shape[3:] for g_part in grads]
    rows, width = plan.rows, plan.width
    finish = []
    if plan.late:
        out_shape = [jax.ShapeDtypeStruct((2, rows, width), BF)]
        out_shape += [
            jax.ShapeDtypeStruct(shape, F32)
            for shape in (
                (shapes[0][0], plan.ff),
                (shapes[1][0], plan.ff),
                (2 * shapes[2][0], width),
                *shapes[3:],
                (8, LANES),
            )
        ]
        in_vmem = len(out_shape)
        out_shape.append(jax.ShapeDtypeStruct((plan.map_rows, width), BF))
        finish = [
            pltpu.VMEM((2, half, width), F32),
            pltpu.VMEM((8, width), F32),
            pltpu.VMEM((2 * chips, 8, LANES), F32),
            pltpu.VMEM((rows, width), BF),
        ]
        finish += [pltpu.VMEM(shape, F32) for shape in shapes[:3]] * 3
        finish += [dma((4,)), dma((4,)), dma, dma]
    else:
        out_shape = [jax.ShapeDtypeStruct(shape, F32) for shape in shapes]
        out_shape.append(jax.ShapeDtypeStruct((2, half, width), F32))
        in_vmem = len(out_shape)
        out_shape.append(jax.ShapeDtypeStruct((plan.local, jb, ia), BF))
        out_shape.append(jax.ShapeDtypeStruct((ORDER * jb, ia), BF))
    return pl.pallas_call(
        functools.partial(backward_kernel, plan, len(grads)),
        out_shape=out_shape,
        in_specs=[vmem_spec, vmem_spec, any_spec, vmem_spec, vmem_spec, any_spec, any_spec]
        + [vmem_spec] * (len(grads) + len(rest)),
        out_specs=[vmem_spec] * in_vmem + [any_spec] * (len(out_shape) - in_vmem),
        scratch_shapes=finish
        + Scatter.scratch(plan, shapes)
        + Scatter.semaphores(plan, len(grads))
        + [
            pltpu.VMEM((2, plan.length, ia), BF),
            pltpu.VMEM((2, ia, plan.length), BF),
            pltpu.VMEM((2, plan.f_rows, plan.length + BLOCK), F32),
            pltpu.VMEM((2, plan.local, BLOCK, plan.length), BF),
            pltpu.VMEM((2, 2, plan.length, 2 * jb), BF),
            pltpu.VMEM((plan.length, 2 * jb), BF),
            pltpu.VMEM((plan.length, 2 * jb), BF),
            pltpu.VMEM((plan.length, 2 * jb), F32),
            pltpu.VMEM((plan.length + 8, 2 * jb), F32),
            pltpu.VMEM((plan.local, jb, ia), F32),
            pltpu.VMEM((plan.local, jb, ia), BF),
            pltpu.VMEM((plan.local, jb, ia), BF),
            pltpu.VMEM((plan.local, jb, ia), BF),
            pltpu.VMEM((ORDER * jb, ia), F32),
            pltpu.VMEM((ORDER * jb, ia), BF),
            pltpu.VMEM((ORDER * jb, ia), BF),
            pltpu.VMEM((ORDER * jb, ia), BF),
            pltpu.VMEM((2, plan.length, jb), BF),
            pltpu.VMEM((chips, 2, half, jb), BF),
            dma,
            dma,
            dma((2,)),
            dma((plan.local,)),
            dma((plan.local,)),
            dma,
            dma,
            dma,
            dma,
            dma,
            dma,
            dma((2,)),
        ],
        compiler_params=pltpu.CompilerParams(
            collective_id=3, has_side_effects=True, vmem_limit_bytes=VMEM_LIMIT
        ),
        name="spectral_backward",
    )(g, filt, v, pq, tapw, x, xs, *grads, *rest)

SWAPS = 7


def middle_kernel(plan, *refs):
    (
        conv_ref,
        hidden_ref,
        gains_ref,
        mask_ref,
        up_ref,
        up_pair,
        *stored,
    ) = refs[:14]
    (
        out_ref,
        g_ref,
        dmid_ref,
        gain_ref,
        gate0_g,
        up0_g,
        down0_g,
        gate1_g,
        up1_g,
        down1_g,
        proj_g,
        attn_g,
    ) = refs[14:26]
    held = refs[26:34]
    (
        pair0,
        pair1,
        give,
        take,
        gates,
        ups,
        acts,
        dgate,
        dup,
        kv,
        q_buf,
        probs,
        dkv,
        back,
        back_land,
        att,
        dq_buf,
        proj_all,
        attn_all,
        proj_take,
        attn_take,
        load_sem,
        a_send,
        a_recv,
        send,
        recv,
        kv_send,
        kv_recv,
        bk_send,
        bk_recv,
        *extra,
    ) = refs[34:]
    chips, rows, width = plan.chips, plan.rows, plan.width
    section, chip = spot()
    sibling = (1 - section, chip)
    reach = WINDOW // rows
    span = (reach + 1) * rows
    layer0, (w_proj, w_out), layer1 = held[:3], held[3:5], held[5:]
    split, cut = 3 * plan.width // 2, plan.width // 2
    own_rows = [
        w_proj.at[pl.ds(pl.multiple_of(split * section, 16), split), :],
        w_out.at[pl.ds(pl.multiple_of(cut * section, 16), cut), :],
    ]
    homes = list(layer0) + own_rows + ([] if plan.late else list(layer1))
    loads = [
        pltpu.make_async_copy(a, b, load_sem.at[i]) for i, (a, b) in enumerate(zip(stored, homes))
    ]
    for load in loads:
        load.start()
    greet_everyone(chips)()
    passes = [
        push(stored[3 + i], own_rows[i], a_send.at[i], a_recv.at[i], sibling) for i in range(2)
    ]
    for copy in passes:
        copy.start()
    if plan.late:
        grads1, gather_send, gather_recv, scatter_send, scatter_recv = extra[:3], *extra[3:7]
        gather = Gather(plan, stored[5:], layer1, gather_send, gather_recv)
        scatter = Scatter(
            plan, grads1, (gate1_g, up1_g, down1_g), extra[7:], scatter_send, scatter_recv
        )
        gather.begin()
    ff = plan.ff // 2
    own = slice(0, rows)
    second = slice(rows, 2 * rows)
    mask = mask_ref[...]

    def swap(number, src, dst):
        copy = push(src, dst, send.at[number], recv.at[number], sibling)
        copy.start()
        copy.wait()

    def norm(values, gain):
        factor = lax.rsqrt(jnp.mean(values * values, axis=-1, keepdims=True) + EPSILON)
        return values * factor * gain, factor

    def norm_back(values, factor, gain, upstream):
        weighted = upstream * gain
        gain_grad = jnp.sum(upstream * values * factor, axis=0, keepdims=True)
        correction = jnp.mean(weighted * values, axis=-1, keepdims=True)
        return factor * weighted - values * factor * factor * factor * correction, gain_grad

    def feed(layer, pair, weights, number):
        w_gate, w_up, w_down = (Flat(w) for w in weights)
        swap(number, pair.at[own], pair.at[second])
        for start in range(0, ff, BLOCK):
            cols = slice(start, start + BLOCK)
            gate_rows = flat_dot(pair[...], w_gate.columns(start, BLOCK))
            up_rows = flat_dot(pair[...], w_up.columns(start, BLOCK))
            gates[layer, :, cols] = gate_rows
            ups[layer, :, cols] = up_rows
            acts[layer, :, cols] = (gate_rows * jax.nn.sigmoid(gate_rows) * up_rows).astype(BF)
        part = flat_dot(acts[layer], w_down.all())
        give[number] = part[second].astype(BF)
        swap(number + 1, give.at[number], take.at[number])
        return part[own] + take[number].astype(F32)

    def feed_back(layer, pair, weights, grads, upstream_pair, number):
        w_gate, w_up, w_down = (Flat(w) for w in weights)
        gate_g, up_g, down_g = (Flat(w) for w in grads)
        turned = pair[...].astype(F32).T.astype(BF)
        for start in range(0, ff, BLOCK):
            cols = slice(start, start + BLOCK)
            active_grad = rows_dot(upstream_pair, w_down.rows(start, BLOCK))
            gate_rows, up_rows = gates[layer, :, cols], ups[layer, :, cols]
            sigmoid = jax.nn.sigmoid(gate_rows)
            slope = sigmoid * (1.0 + gate_rows * (1.0 - sigmoid))
            gate_grad = (active_grad * up_rows * slope).astype(BF)
            up_grad = (active_grad * gate_rows * sigmoid).astype(BF)
            dgate[:, cols] = gate_grad
            dup[:, cols] = up_grad
        for start in range(0, width, BLOCK):
            cols = slice(start, start + BLOCK)
            part = rows_dot(dgate[...], w_gate.rows(start, BLOCK)) + rows_dot(
                dup[...], w_up.rows(start, BLOCK)
            )
            give[number, :, cols] = part[second].astype(BF)
            att[:, cols] = part[own]
        copy = push(
            give.at[number], take.at[number], send.at[number], recv.at[number], sibling
        )
        copy.start()
        for start in range(0, ff, BLOCK):
            cols = slice(start, start + BLOCK)
            gate_g.put_columns(start, flat_dot(turned, dgate[:, cols]).astype(BF))
            up_g.put_columns(start, flat_dot(turned, dup[:, cols]).astype(BF))
            down_g.put_rows(
                start,
                flat_dot(acts[layer, :, cols].astype(F32).T.astype(BF), upstream_pair).astype(BF),
            )
        copy.wait()
        return att[...] + take[number].astype(F32)

    middle0 = hidden_ref[...] + conv_ref[...]
    normed, factor0 = norm(middle0, gains_ref[1:2, :])
    pair0[own] = normed.astype(BF)
    dmid_ref[...] = middle0
    for load in loads[:3]:
        load.wait()
    branch = feed(0, pair0, layer0, 0)
    passed = (mask * (dmid_ref[...] + branch)).astype(BF).astype(F32)
    if plan.late:
        gather.stage(0)
        gather.stage(1)

    normed, factor10 = norm(passed, gains_ref[2:3, :])
    inputs = normed.astype(BF)
    for load in loads[3:5]:
        load.wait()
    for copy in passes:
        copy.wait()
    mine = slice(reach * rows, span)
    q_buf[...] = flat_dot(inputs, w_proj[:width]).astype(BF)
    kv[mine, :width] = flat_dot(inputs, w_proj[width : 2 * width]).astype(BF)
    kv[mine, width:] = flat_dot(inputs, w_proj[2 * width :]).astype(BF)

    def ahead(distance):
        return push(
            kv.at[mine],
            kv.at[pl.ds((reach - distance) * rows, rows)],
            kv_send.at[distance - 1],
            kv_recv.at[distance - 1],
            (section, chip + distance),
        )

    for distance in range(1, reach + 1):

        @pl.when(chip + distance < chips)
        def _():
            ahead(distance).start()

        @pl.when(chip < distance)
        def _():
            kv[(reach - distance) * rows : (reach - distance + 1) * rows, :] = jnp.zeros(
                (rows, 2 * width), BF
            )

    if plan.late:
        gather.stage(2)
    half = plan.half
    row = lax.broadcasted_iota(jnp.int32, (rows, span), 0)
    col = lax.broadcasted_iota(jnp.int32, (rows, span), 1)
    inner = lax.rem(col, rows)
    q_place = 2 * lax.rem(row, half) + row // half
    k_place = (col // rows - reach) * rows + 2 * lax.rem(inner, half) + inner // half
    distance_rows = q_place - k_place
    allowed = (
        (k_place + chip * rows >= 0) & (distance_rows >= 0) & (distance_rows < WINDOW)
    )
    lane = lax.broadcasted_iota(jnp.int32, (rows, LANES), 1)
    low = lane < HEAD_DIM
    scale = HEAD_DIM ** (-0.5)
    zero = jnp.zeros((rows, LANES), BF)
    for distance in range(1, reach + 1):

        @pl.when(chip >= distance)
        def _():
            push(
                kv.at[mine],
                kv.at[pl.ds((reach - distance) * rows, rows)],
                kv_send.at[distance - 1],
                kv_recv.at[distance - 1],
                sibling,
            ).wait_recv()

    if plan.late:
        gather.stage(3)
    for pair in range(width // LANES):
        if plan.late and pair == 1:
            gather.stage(4)
        lanes = slice(LANES * pair, LANES * (pair + 1))
        keys, values = kv[:, lanes], kv[:, width + LANES * pair : width + LANES * (pair + 1)]
        parts = []
        for side in range(2):
            here = low if side == 0 else jnp.logical_not(low)
            queries = jnp.where(here, q_buf[:, lanes], zero)
            scores = rows_dot(queries, keys) * scale
            scores = jnp.where(allowed, scores, BIG_NEGATIVE)
            weights = jnp.exp(scores - jnp.max(scores, axis=-1, keepdims=True))
            weights = weights / jnp.sum(weights, axis=-1, keepdims=True)
            probs[2 * pair + side] = weights
            parts.append(flat_dot(weights.astype(BF), values))
        att[:, lanes] = jnp.where(low, parts[0], parts[1])
    attended = att[...].astype(BF)
    middle1 = passed + flat_dot(attended, w_out[...])

    if plan.late:
        gather.end()
    for load in loads[5:]:
        load.wait()
    normed, factor11 = norm(middle1, gains_ref[3:4, :])
    pair1[own] = normed.astype(BF)
    branch = feed(1, pair1, layer1, 2)
    out_ref[...] = (mask * (middle1 + branch)).astype(BF)
    if not plan.late:
        grads1 = (gate1_g, up1_g, down1_g)
    dnormed = feed_back(1, pair1, layer1, grads1, up_pair[...], 4)
    if plan.late:
        scatter.begin()
    dmiddle, gain11 = norm_back(middle1, factor11, gains_ref[3:4, :], dnormed)
    dmiddle = up_ref[...] + dmiddle
    gain_ref[3:4, :] = gain11

    dy = dmiddle.astype(BF)
    attn_all[...] = flat_dot(attended.astype(F32).T.astype(BF), dy).astype(BF)
    datt = rows_dot(dy, w_out[...]).astype(BF)
    for pair in range(width // LANES):
        if plan.late and 1 <= pair <= 3:
            scatter.stage(pair - 1)
        lanes = slice(LANES * pair, LANES * (pair + 1))
        value_lanes = slice(width + LANES * pair, width + LANES * (pair + 1))
        keys, values = kv[:, lanes], kv[:, value_lanes]
        dq_parts, key_grad, value_grad = [], None, None
        for side in range(2):
            here = low if side == 0 else jnp.logical_not(low)
            queries = jnp.where(here, q_buf[:, lanes], zero)
            upstream = jnp.where(here, datt[:, lanes], zero)
            weights = probs[2 * pair + side]
            grad = rows_dot(upstream, values)
            total = jnp.sum(weights * grad, axis=-1, keepdims=True)
            dscores = weights * (grad - total)
            dq_parts.append(flat_dot(dscores.astype(BF), keys))
            one = flat_dot(dscores.T.astype(BF), queries)
            two = flat_dot(weights.T.astype(BF), upstream)
            key_grad = one if key_grad is None else key_grad + one
            value_grad = two if value_grad is None else value_grad + two
        dq_buf[0, :, lanes] = (jnp.where(low, dq_parts[0], dq_parts[1]) * scale).astype(BF)
        key_grad = key_grad * scale
        back[:, lanes] = key_grad[: reach * rows].astype(BF)
        back[:, value_lanes] = value_grad[: reach * rows].astype(BF)
        dkv[:, lanes] = key_grad[reach * rows :]
        dkv[:, value_lanes] = value_grad[reach * rows :]

    def behind(distance, peer):
        return push(
            back.at[pl.ds((reach - distance) * rows, rows)],
            back_land.at[distance - 1],
            bk_send.at[distance - 1],
            bk_recv.at[distance - 1],
            (section, peer),
        )

    for distance in range(1, reach + 1):

        @pl.when(chip >= distance)
        def _():
            behind(distance, chip - distance).start()

    if plan.late:
        scatter.stage(3)
    for distance in range(1, reach + 1):

        @pl.when(chip + distance < chips)
        def _():
            behind(distance, chip).wait_recv()
            dkv[...] += back_land[distance - 1].astype(F32)

    dq_buf[1] = dkv[:, :width].astype(BF)
    dq_buf[2] = dkv[:, width:].astype(BF)
    turned = inputs.astype(F32).T.astype(BF)
    dnormed = None
    for part in range(3):
        term = rows_dot(dq_buf[part], w_proj[part * width : (part + 1) * width])
        dnormed = term if dnormed is None else dnormed + term
    dpassed, gain10 = norm_back(passed, factor10, gains_ref[2:3, :], dnormed)
    gain_ref[2:3, :] = gain10
    dpassed = (dmiddle + dpassed).astype(BF).astype(F32)

    if plan.late:
        scatter.stage(4)
    upstream0 = mask * dpassed
    give[5] = upstream0.astype(BF)
    copy = push(give.at[5], take.at[5], send.at[5], recv.at[5], sibling)
    copy.start()
    for part in range(3):
        proj_all[part * width : (part + 1) * width, :] = flat_dot(turned, dq_buf[part]).astype(BF)
    copy.wait()
    crossing = [
        push(
            whole.at[pl.ds(pl.multiple_of(size * (1 - section), 16), size), :],
            land,
            a_send.at[2 + i],
            a_recv.at[2 + i],
            sibling,
        )
        for i, (whole, land, size) in enumerate(
            ((proj_all, proj_take, split), (attn_all, attn_take, cut))
        )
    ]
    for cross in crossing:
        cross.start()
    both = jnp.concatenate([give[5], take[5]], 0)
    dnormed = feed_back(0, pair0, layer0, (gate0_g, up0_g, down0_g), both, 6)
    middle0 = dmid_ref[...]
    dmiddle, gain01 = norm_back(middle0, factor0, gains_ref[1:2, :], dnormed)
    gain_ref[1:2, :] = gain01
    dmiddle = upstream0 + dmiddle
    dmid_ref[...] = dmiddle
    g_ref[...] = dmiddle.astype(BF)
    for cross in crossing:
        cross.wait()
    for whole, land, size, out in (
        (proj_all, proj_take, split, proj_g),
        (attn_all, attn_take, cut, attn_g),
    ):
        own_part = whole[pl.ds(pl.multiple_of(size * section, 16), size), :]
        out[...] = (own_part.astype(F32) + land[...].astype(F32)).astype(BF)
    if plan.late:
        scatter.end()

    for distance in range(1, reach + 1):

        @pl.when(chip + distance < chips)
        def _():
            ahead(distance).wait_send()

        @pl.when(chip >= distance)
        def _():
            behind(distance, chip).wait_send()


def middle_call(plan, conv, hidden, gains, mask, upstream, pair, stored):
    rows, width = plan.rows, plan.width
    reach = WINDOW // rows
    ff = plan.ff // 2
    any_spec = pl.BlockSpec(memory_space=pl.ANY)
    vmem_spec = pl.BlockSpec(memory_space=pltpu.VMEM)
    dma = pltpu.SemaphoreType.DMA
    layer = [(width, ff), (width, ff), (ff, width)]
    grid = (plan.depth, plan.side, plan.side)
    chips = plan.chips
    spread = [grid + (a // chips, b) for a, b in layer]
    held = layer + [(3 * width, width), (width, width)] + (spread if plan.late else layer)
    split, cut = 3 * width // 2, width // 2
    extra = []
    if plan.late:
        extra = [pltpu.VMEM(w, BF) for w in spread]
        extra += Gather.semaphores(plan, 3) + Scatter.semaphores(plan, 3)
        extra += Scatter.scratch(plan, [w[3:] for w in spread])
    shapes = [
        ((rows, width), BF),
        ((rows, width), BF),
        ((rows, width), F32),
        ((8, width), F32),
    ]
    shapes += [(w, BF) for w in layer]
    shapes += [(w[3:], F32) for w in spread] if plan.late else [(w, BF) for w in layer]
    shapes += [((split, width), BF), ((cut, width), BF)]
    return pl.pallas_call(
        functools.partial(middle_kernel, plan),
        out_shape=[jax.ShapeDtypeStruct(s, d) for s, d in shapes],
        in_specs=[vmem_spec] * 6 + [any_spec] * 8,
        out_specs=[vmem_spec] * len(shapes),
        scratch_shapes=[pltpu.VMEM(w, BF) for w in held]
        + [
            pltpu.VMEM((2 * rows, width), BF),
            pltpu.VMEM((2 * rows, width), BF),
            pltpu.VMEM((SWAPS, rows, width), BF),
            pltpu.VMEM((SWAPS, rows, width), BF),
            pltpu.VMEM((2, 2 * rows, ff), F32),
            pltpu.VMEM((2, 2 * rows, ff), F32),
            pltpu.VMEM((2, 2 * rows, ff), BF),
            pltpu.VMEM((2 * rows, ff), BF),
            pltpu.VMEM((2 * rows, ff), BF),
            pltpu.VMEM(((reach + 1) * rows, 2 * width), BF),
            pltpu.VMEM((rows, width), BF),
            pltpu.VMEM((width // HEAD_DIM, rows, (reach + 1) * rows), F32),
            pltpu.VMEM((rows, 2 * width), F32),
            pltpu.VMEM((reach * rows, 2 * width), BF),
            pltpu.VMEM((reach, rows, 2 * width), BF),
            pltpu.VMEM((rows, width), F32),
            pltpu.VMEM((3, rows, width), BF),
            pltpu.VMEM((3 * width, width), BF),
            pltpu.VMEM((width, width), BF),
            pltpu.VMEM((split, width), BF),
            pltpu.VMEM((cut, width), BF),
            dma((8,)),
            dma((4,)),
            dma((4,)),
            dma((SWAPS,)),
            dma((SWAPS,)),
            dma((reach,)),
            dma((reach,)),
            dma((reach,)),
            dma((reach,)),
        ]
        + extra,
        compiler_params=pltpu.CompilerParams(
            collective_id=5, has_side_effects=True, vmem_limit_bytes=VMEM_LIMIT
        ),
        name="middle",
    )(conv, hidden, gains, mask, upstream, pair, *stored)


def swapped(block):
    return lax.ppermute(block, "section", [(0, 1), (1, 0)])


def norm_backward(values, factor, weights, upstream):
    weighted = upstream * weights
    gain_grad = jnp.sum(upstream * values * factor, axis=0)
    correction = jnp.mean(weighted * values, axis=-1, keepdims=True)
    return (factor * weighted - values * factor * factor * factor * correction, gain_grad)


def body(
    io_pair, lengths, filters, stu_maps, attn_proj, attn_out, norm_gains, mlp_gate, mlp_up, mlp_down
):
    chips = lax.axis_size("seq")
    section, chip = spot()
    core_zero = section == 0
    tok_rows = io_pair.shape[2]
    width = io_pair.shape[3]
    half = tok_rows // 2
    ff = mlp_gate.shape[2]
    ff_half = mlp_down.shape[1] // 2
    plan = Plan(chips, tok_rows, width, filters.shape[1], stu_maps.shape[0], ff)

    def join_phases(rows):
        return rows.reshape(2, half, width).swapaxes(0, 1).reshape(rows.shape)

    my_a = chip % plan.cols_out
    my_b = (chip // plan.cols_out) % plan.cols_in
    my_group = chip // (plan.cols_out * plan.cols_in)
    if plan.routed:
        maps = [stu_maps]
    else:
        whole = lax.all_gather(stu_maps, ("section", "seq"), axis=0, tiled=True)
        whole = lax.dynamic_slice(
            whole.reshape(-1, width, width),
            (0, my_b * plan.jb, my_a * plan.ia),
            (whole.shape[0] // width, plan.jb, plan.ia),
        )
        pair = whole[: 2 * plan.filters].reshape(2, plan.filters, plan.jb, plan.ia)
        pair = lax.dynamic_slice_in_dim(pair, my_group * plan.local, plan.local, 1)
        taps = jnp.where(my_group == 0, whole[2 * plan.filters :], 0).astype(BF)
        maps = [
            jnp.where(core_zero, pair[0], pair[1]),
            jnp.where(core_zero, pair[1], pair[0]),
            taps.reshape(-1, plan.ia),
        ]

    gate, up = mlp_gate[0], mlp_up[0]
    if not plan.pick_here:
        gate, up = (
            jnp.transpose(w.reshape(w.shape[0], chips, 2, ff_half), (2, 0, 1, 3)).reshape(
                2, w.shape[0], ff // 2
            )
            for w in (gate, up)
        )
    results = forward_call(
        plan,
        io_pair[0],
        norm_gains[0],
        filters,
        lengths,
        [gate, up, mlp_down[0], attn_proj, attn_out],
        maps,
    )
    weights = [w.reshape(-1, w.shape[-1]) for w in results[:8]]
    conv, hidden, upstream1, grad_pair, gains, mask_rows = results[8:14]
    v, pq, tapw, x_all, xs_all, filt = results[14:]
    block_out, g, middle0_grad, gain_sums, *grads = middle_call(
        plan,
        conv.reshape(tok_rows, width),
        hidden,
        gains,
        mask_rows,
        upstream1,
        grad_pair,
        weights,
    )
    mlp0_grads, half1, attn_grads = grads[:3], grads[3:6], grads[6:]
    gain01, gain10, gain11 = gain_sums[1], gain_sums[2], gain_sums[3]
    g = g.reshape(2, half, width)
    grid = (plan.depth, plan.side, plan.side)
    blocks0 = [w.reshape(grid + (w.shape[0] // chips, w.shape[1])) for w in mlp0_grads]
    blocks1 = [w.reshape(grid + (w.shape[0] // chips, w.shape[1])) for w in attn_grads]
    if plan.late:
        result, gate_out, up_out, down_out, proj_out, out_out, gain_tile, maps_out = backward_call(
            plan,
            g,
            filt,
            v,
            pq,
            tapw,
            x_all,
            xs_all,
            blocks0 + blocks1,
            [hidden, gains, mask_rows, middle0_grad, block_out, gain_sums, *half1],
        )
        cols = width // chips
        gain_out = lax.dynamic_slice(
            gain_tile, (2 * section, (chip % (LANES // cols)) * cols), (2, cols)
        )
        return (
            result[None],
            maps_out.astype(F32),
            proj_out,
            out_out,
            gain_out[None],
            gate_out[None],
            up_out[None],
            down_out[None],
        )
    results = backward_call(plan, g, filt, v, pq, tapw, x_all, xs_all, blocks0)
    half0, results = results[:3], results[3:]
    attn_sums = [
        lax.psum_scatter(
            w.reshape((chips,) + w.shape[3:]), "seq", scatter_dimension=0, tiled=False
        )
        for w in blocks1
    ]
    half1 = [
        lax.psum_scatter(
            w.reshape(chips, -1, w.shape[-1]), "seq", scatter_dimension=0, tiled=False
        )
        for w in half1
    ]
    signal_grad = results[0].reshape(tok_rows, width)
    piece, tap_piece = (r.astype(F32) for r in results[1:])
    full = jnp.zeros((2, plan.filters, width, width), F32)
    full = lax.dynamic_update_slice(
        full,
        piece[None],
        (section, my_group * plan.local, my_b * plan.jb, my_a * plan.ia),
    )
    tap_piece = jnp.where(core_zero & (my_group == 0), tap_piece, 0.0)
    tap_full = lax.dynamic_update_slice(
        jnp.zeros((ORDER, width, width), F32),
        tap_piece.reshape(ORDER, plan.jb, plan.ia),
        (0, my_b * plan.jb, my_a * plan.ia),
    )
    full = jnp.concatenate([full.reshape(-1, width), tap_full.reshape(-1, width)], 0)
    maps_grad = lax.psum_scatter(full, ("section", "seq"), scatter_dimension=0, tiled=True)
    spectral_factor = lax.rsqrt(jnp.mean(hidden * hidden, axis=-1, keepdims=True) + EPSILON)
    hidden_grad, gain00 = norm_backward(hidden, spectral_factor, gains[0], signal_grad)
    inputs_grad = (mask_rows * (middle0_grad + hidden_grad)).astype(BF)

    proj_out, out_out = (w.astype(F32) for w in attn_sums)
    outs = []
    for index in range(3):
        zero, one = half0[index].astype(BF), half1[index].astype(BF)
        keep = jnp.where(core_zero, zero, one)
        take = swapped(jnp.where(core_zero, one, zero))
        low = jnp.where(core_zero, keep, take).astype(F32)
        high = jnp.where(core_zero, take, keep).astype(F32)
        if index < 2:
            rows = low.shape[0]
            joined = jnp.stack(
                [low.reshape(rows, chips, ff_half), high.reshape(rows, chips, ff_half)], 2
            ).reshape(rows, ff)
        else:
            joined = jnp.concatenate([low, high], 0)
        outs.append(joined[None])

    gain_parts = jnp.stack([jnp.stack([gain00, gain01]), jnp.stack([gain10, gain11])])
    gain_cols = width // chips
    tiles = jnp.transpose(gain_parts.reshape(2, 2, chips, gain_cols), (0, 2, 1, 3))
    tiles = jnp.pad(
        tiles.reshape(2 * chips, 2, gain_cols), ((0, 0), (0, 6), (0, LANES - gain_cols))
    )
    done_in, done_out = join_phases(inputs_grad), join_phases(block_out)
    taken, landed = exit_call(chips, jnp.where(core_zero, done_out, done_in), tiles)
    first = jnp.where(core_zero, done_in, taken)
    second = jnp.where(core_zero, taken, done_out)
    result_pair = jnp.stack([first, second])[None]
    gain_out = jnp.sum(landed, axis=0)[None, :2, :gain_cols]
    return (result_pair, maps_grad, proj_out, out_out, gain_out, outs[0], outs[1], outs[2])


def solution(mesh):
    placed = (
        P("section", None, "seq", None),
        P(),
        P("seq", None),
        P(("section", "seq"), None),
        P(("section", "seq"), None),
        P(("section", "seq"), None),
        P("section", None, "seq"),
        P("section", "seq", None),
        P("section", "seq", None),
        P("section", "seq", None),
    )
    return jax.shard_map(
        body,
        mesh=mesh,
        in_specs=placed,
        out_specs=(
            P("section", None, "seq", None),
            P(("section", "seq"), None),
            P(("section", "seq"), None),
            P(("section", "seq"), None),
            P("section", None, "seq"),
            P("section", "seq", None),
            P("section", "seq", None),
            P("section", "seq", None),
        ),
        check_vma=False,
    )
```

```python
import functools
import math

import jax
import jax.numpy as jnp
from jax import lax
from jax.experimental import pallas as pl
from jax.experimental.pallas import tpu as pltpu
from jax.sharding import PartitionSpec as P

ORDER = 3
HEAD_DIM = 64
WINDOW = 512
EPSILON = 1e-05
BIG_NEGATIVE = -1e30
MESH = pl.DeviceIdType.MESH
BF = jnp.bfloat16
F32 = jnp.float32
LANES = 128
BLOCK = 256
PIECE = 16
VMEM_LIMIT = 63 * 1024 * 1024


class Plan:
    def __init__(self, chips, tok_rows, width, filter_count, map_rows, ff):
        self.chips = chips
        self.rows = tok_rows
        self.half = tok_rows // 2
        self.width = width
        self.filters = filter_count
        self.cols_in = 4
        self.cols_out = max(1, math.isqrt(chips // 4))
        self.groups = chips // (self.cols_in * self.cols_out)
        self.local = filter_count // self.groups
        self.length = chips * self.half
        self.blocks = self.length // BLOCK
        self.jb = width // self.cols_in
        self.ia = width // self.cols_out
        self.map_rows = map_rows
        self.routed = map_rows % PIECE == 0
        self.pieces = map_rows // PIECE
        self.f_rows = -(-self.local // 16) * 16
        self.batch = 4 if self.local % 4 == 0 else 2
        self.ff = ff
        self.pick_here = ff // chips == LANES
        self.late = self.pick_here and self.routed
        self.routed = self.late
        self.side = max(1, math.isqrt(chips // 4))
        self.depth = chips // (self.side * self.side)
        self.layer = self.side * self.side
        self.layered = self.layer * tok_rows == WINDOW

    def place(self, chip):
        return (
            chip // (self.side * self.side),
            lax.rem(chip // self.side, self.side),
            lax.rem(chip, self.side),
        )

    def a_of(self, chip):
        return lax.rem(chip // self.cols_in, self.cols_out)

    def b_of(self, chip):
        return lax.rem(chip, self.cols_in)

    def part_at(self, a, b, c):
        return b + self.cols_in * (a + self.cols_out * c)

    def chip_at(self, z, y, x):
        return (z * self.side + y) * self.side + x

    def routes(self, rows, index=0):
        if rows % (2 * PIECE) == 0:
            return [(0, rows // 2, True), (rows // 2, rows // 2, False)]
        return [(0, rows, index % 2 == 0)]


def spot():
    return lax.axis_index("section"), lax.axis_index("seq")


def greet_everyone(chips):
    section, chip = spot()
    me = section * chips + chip
    barrier = pltpu.get_barrier_semaphore()

    def one(step, carry):
        peer = lax.rem(me + step, 2 * chips)
        pl.semaphore_signal(
            barrier, inc=1, device_id=(peer // chips, lax.rem(peer, chips)), device_id_type=MESH
        )
        return carry

    lax.fori_loop(1, 2 * chips, one, 0)

    def wait():
        pl.semaphore_wait(barrier, 2 * chips - 1)

    return wait


def push(src, dst, send, recv, target):
    return pltpu.make_async_remote_copy(
        src_ref=src,
        dst_ref=dst,
        send_sem=send,
        recv_sem=recv,
        device_id=target,
        device_id_type=MESH,
    )


def bytes_of(ref, sem):
    pltpu.make_async_copy(ref, ref, sem).wait()


def rows_dot(left, right):
    return lax.dot_general(left, right, (((1,), (1,)), ((), ())), preferred_element_type=F32)


def cols_dot(left, right):
    return lax.dot_general(left, right, (((0,), (0,)), ((), ())), preferred_element_type=F32)


def flat_dot(left, right):
    return jnp.dot(left, right, preferred_element_type=F32)


class Flat:
    def __init__(self, ref):
        self.ref = ref
        self.split = len(ref.shape) == 5
        if self.split:
            depth, side, _, rows, _ = ref.shape
            self.plane = side * side * rows

    def columns(self, start, count):
        sl = slice(start, start + count)
        if self.split:
            return self.ref[:, :, :, :, sl].reshape(-1, count)
        return self.ref[:, sl]

    def rows(self, start, count):
        if self.split:
            sl = slice(start // self.plane, (start + count) // self.plane)
            return self.ref[sl].reshape(count, self.ref.shape[4])
        return self.ref[start : start + count, :]

    def all(self):
        return self.ref[...].reshape(-1, self.ref.shape[-1])

    def put_columns(self, start, value):
        sl = slice(start, start + value.shape[1])
        if self.split:
            shape = self.ref.shape[:4] + (value.shape[1],)
            self.ref[:, :, :, :, sl] = value.reshape(shape)
        else:
            self.ref[:, sl] = value

    def put_rows(self, start, value):
        count = value.shape[0]
        if self.split:
            sl = slice(start // self.plane, (start + count) // self.plane)
            self.ref[sl] = value.reshape((count // self.plane,) + self.ref.shape[1:])
        else:
            self.ref[start : start + count, :] = value


class Gather:
    def __init__(self, plan, shards, outs, send, recv):
        self.plan, self.shards, self.outs = plan, shards, outs
        self.send, self.recv = send, recv
        self.section, chip = spot()
        self.z, self.y, self.x = plan.place(chip)

    @staticmethod
    def semaphores(plan, count):
        return [
            pltpu.SemaphoreType.DMA((count, 5)),
            pltpu.SemaphoreType.DMA((count, 5 * plan.depth)),
        ]

    def to(self, z, y, x):
        return self.section, self.plan.chip_at(z, y, x)

    def across(self, step, along_x):
        side = self.plan.side
        if along_x:
            return self.to(self.z, self.y, lax.rem(self.x + step, side))
        return self.to(self.z, lax.rem(self.y + step, side), self.x)

    def routes(self, i):
        for number, (start, rows, x_first) in enumerate(self.plan.routes(self.outs[i].shape[3], i)):
            yield number, x_first, self.outs[i], pl.ds(start, rows)

    def level(self, t):
        return lax.rem(self.z - t + self.plan.depth, self.plan.depth)

    def begin(self):
        plan = self.plan
        for i, shard in enumerate(self.shards):
            home = self.outs[i].at[self.z, self.y, self.x]
            for step in range(1, plan.depth):
                z = lax.rem(self.z + step, plan.depth)
                push(
                    shard, home, self.send.at[i, 0], self.recv.at[i, step], self.to(z, self.y, self.x)
                ).start()
            pltpu.make_async_copy(shard, home, self.recv.at[i, 0]).start()
        self.second(0)

    def second(self, t):
        plan = self.plan
        for i, shard in enumerate(self.shards):
            z = self.level(t)
            if t > 0:
                bytes_of(self.outs[i].at[z, self.y, self.x], self.recv.at[i, t])
            for number, x_first, out, sl in self.routes(i):
                dst = out.at[z, self.y, self.x, sl]
                src = shard.at[sl] if t == 0 else dst
                for step in range(1, plan.side):
                    push(
                        src,
                        dst,
                        self.send.at[i, 1 + number],
                        self.recv.at[i, (1 + number) * plan.depth + t],
                        self.across(step, x_first),
                    ).start()

    def hand_over(self):
        plan, side = self.plan, self.plan.side
        for i, shard in enumerate(self.shards):
            pltpu.make_async_copy(
                shard, self.outs[i].at[self.z, self.y, self.x], self.recv.at[i, 0]
            ).wait()
            bytes_of(self.outs[i].at[pl.ds(0, plan.depth - 1), 0, 0], self.send.at[i, 0])
            for number, x_first, out, sl in self.routes(i):
                for t in range(plan.depth):
                    bytes_of(
                        out.at[0, 0, pl.ds(0, side - 1), sl],
                        self.recv.at[i, (1 + number) * plan.depth + t],
                    )
                bytes_of(out.at[:, 0, pl.ds(0, side - 1), sl], self.send.at[i, 1 + number])

    def held_parts(self, whole):
        for i, source in enumerate(whole):
            for number, x_first, out, sl in self.routes(i):
                if x_first:
                    yield source.at[:, self.y, :, sl], out.at[:, self.y, :, sl]
                else:
                    yield source.at[:, :, self.x, sl], out.at[:, :, self.x, sl]

    def last_only(self):
        plan, side = self.plan, self.plan.side
        for t in range(plan.depth):
            z = self.level(t)
            for i in range(len(self.shards)):
                for number, x_first, out, sl in self.routes(i):
                    src = out.at[z, self.y, :, sl] if x_first else out.at[z, :, self.x, sl]
                    for step in range(1, side):
                        push(
                            src,
                            src,
                            self.send.at[i, 3 + number],
                            self.recv.at[i, (3 + number) * plan.depth + t],
                            self.across(step, not x_first),
                        ).start()

    def third(self, t):
        plan, side = self.plan, self.plan.side
        for i, shard in enumerate(self.shards):
            z = self.level(t)
            if t == 0:
                pltpu.make_async_copy(
                    shard, self.outs[i].at[z, self.y, self.x], self.recv.at[i, 0]
                ).wait()
            for number, x_first, out, sl in self.routes(i):
                sem = self.recv.at[i, (1 + number) * plan.depth + t]
                if x_first:
                    bytes_of(out.at[z, self.y, pl.ds(0, side - 1), sl], sem)
                    src = out.at[z, self.y, :, sl]
                else:
                    bytes_of(out.at[z, pl.ds(0, side - 1), self.x, sl], sem)
                    src = out.at[z, :, self.x, sl]
                for step in range(1, side):
                    push(
                        src,
                        src,
                        self.send.at[i, 3 + number],
                        self.recv.at[i, (3 + number) * plan.depth + t],
                        self.across(step, not x_first),
                    ).start()

    def end(self, last_only=False):
        plan, side = self.plan, self.plan.side
        for i in range(len(self.shards)):
            if not last_only:
                bytes_of(self.outs[i].at[pl.ds(0, plan.depth - 1), 0, 0], self.send.at[i, 0])
            for number, x_first, out, sl in self.routes(i):
                if not last_only:
                    bytes_of(out.at[:, 0, pl.ds(0, side - 1), sl], self.send.at[i, 1 + number])
                for t in range(plan.depth):
                    bytes_of(
                        out.at[0, :, pl.ds(0, side - 1), sl],
                        self.recv.at[i, (3 + number) * plan.depth + t],
                    )
                bytes_of(out.at[:, :, pl.ds(0, side - 1), sl], self.send.at[i, 3 + number])

    def stage(self, number):
        if number > 0:
            self.third(number - 1)
        if 0 <= number < self.plan.depth - 1:
            self.second(number + 1)


class Scatter:
    @staticmethod
    def scratch(plan, shapes):
        refs = []
        for index, (rows, cols) in enumerate(shapes):
            for _, part, _ in plan.routes(rows, index):
                for lead in (
                    (plan.depth, plan.side - 1, plan.side),
                    (plan.depth, plan.side),
                    (plan.depth, plan.side - 1),
                    (plan.depth,),
                    (plan.depth - 1,),
                ):
                    refs.append(pltpu.VMEM(lead + (part, cols), BF))
        return refs

    @staticmethod
    def semaphores(plan, count):
        return [
            pltpu.SemaphoreType.DMA((count, 6)),
            pltpu.SemaphoreType.DMA((count, 4 * plan.depth + 2)),
        ]

    def __init__(self, plan, grads, outs, buffers, send, recv, lines_only=False):
        self.plan, self.grads, self.outs = plan, grads, outs
        self.lines_only = lines_only
        self.send, self.recv = send, recv
        self.section, chip = spot()
        self.z, self.y, self.x = plan.place(chip)
        self.work = []
        buffers = list(buffers)
        for i, grad in enumerate(grads):
            for number, (start, rows, x_first) in enumerate(plan.routes(grad.shape[3], i)):
                self.work.append((i, number, start, rows, x_first, buffers[:5]))
                buffers = buffers[5:]

    def to(self, z, y, x):
        return self.section, self.plan.chip_at(z, y, x)

    def level(self, t):
        return lax.rem(self.z + 1 + t, self.plan.depth)

    def begin(self):
        plan, side = self.plan, self.plan.side
        for t in range(plan.depth):
            z = self.level(t)
            for i, number, start, rows, x_first, (land, *_) in self.work:
                grad, sl = self.grads[i], pl.ds(start, rows)
                for step in range(1, side):
                    if x_first:
                        y = lax.rem(self.y + step, side)
                        src, peer = grad.at[z, y, :, sl], self.to(self.z, y, self.x)
                    else:
                        x = lax.rem(self.x + step, side)
                        src, peer = grad.at[z, :, x, sl], self.to(self.z, self.y, x)
                    push(
                        src,
                        land.at[t, step - 1],
                        self.send.at[i, number],
                        self.recv.at[i, number * plan.depth + t],
                        peer,
                    ).start()

    def second(self, t):
        plan, side = self.plan, self.plan.side
        z = self.level(t)
        for i, number, start, rows, x_first, (land, part, land2, *_) in self.work:
            grad = self.grads[i]
            bytes_of(land.at[t], self.recv.at[i, number * plan.depth + t])
            for j in range(side):
                y, x = (self.y, j) if x_first else (j, self.x)
                total = grad[z, y, x, start : start + rows, :].astype(F32)
                for step in range(side - 1):
                    total = total + land[t, step, j].astype(F32)
                part[t, j] = total.astype(BF)
            for step in range(1, side):
                if x_first:
                    j = lax.rem(self.x + step, side)
                    peer = self.to(self.z, self.y, j)
                else:
                    j = lax.rem(self.y + step, side)
                    peer = self.to(self.z, j, self.x)
                push(
                    part.at[t, j],
                    land2.at[t, step - 1],
                    self.send.at[i, 2 + number],
                    self.recv.at[i, (2 + number) * plan.depth + t],
                    peer,
                ).start()

    def third(self, t):
        plan, side = self.plan, self.plan.side
        for i, number, start, rows, x_first, (_, part, land2, line, land3) in self.work:
            bytes_of(land2.at[t], self.recv.at[i, (2 + number) * plan.depth + t])
            mine = self.x if x_first else self.y
            total = part[t, mine].astype(F32)
            for step in range(side - 1):
                total = total + land2[t, step].astype(F32)
            line[t] = total.astype(BF)
            if t < plan.depth - 1 and not self.lines_only:
                push(
                    line.at[t],
                    land3.at[t],
                    self.send.at[i, 4 + number],
                    self.recv.at[i, 4 * plan.depth + number],
                    self.to(self.level(t), self.y, self.x),
                ).start()

    def end(self):
        plan = self.plan
        for i, number, start, rows, x_first, (land, part, land2, line, land3) in self.work:
            if self.lines_only:
                self.outs[i][:, start : start + rows, :] = line[...]
                bytes_of(land, self.send.at[i, number])
                bytes_of(land2, self.send.at[i, 2 + number])
                continue
            bytes_of(land3, self.recv.at[i, 4 * plan.depth + number])
            total = line[plan.depth - 1].astype(F32)
            for step in range(plan.depth - 1):
                total = total + land3[step].astype(F32)
            self.outs[i][start : start + rows, :] = total
            bytes_of(land, self.send.at[i, number])
            bytes_of(land2, self.send.at[i, 2 + number])
            bytes_of(land3, self.send.at[i, 4 + number])

    def stage(self, number):
        if number < self.plan.depth:
            self.second(number)
        if number > 0:
            self.third(number - 1)


def exit_kernel(chips, give, tiles, take, land, send, recv, gain_send, gain_recv):
    section, chip = spot()
    me = section * chips + chip
    greet_everyone(chips)()
    swap = push(give, take, send, recv, (1 - section, chip))
    swap.start()

    def one(step, carry):
        peer = lax.rem(me + step, 2 * chips)
        push(
            tiles.at[peer],
            land.at[me],
            gain_send,
            gain_recv,
            (peer // chips, lax.rem(peer, chips)),
        ).start()
        return carry

    lax.fori_loop(1, 2 * chips, one, 0)
    pltpu.make_async_copy(tiles.at[me], land.at[me], gain_recv).start()
    bytes_of(land, gain_recv)
    bytes_of(land.at[pl.ds(0, 2 * chips - 1)], gain_send)
    swap.wait()


def exit_call(chips, give, tiles):
    any_spec = pl.BlockSpec(memory_space=pl.ANY)
    return pl.pallas_call(
        functools.partial(exit_kernel, chips),
        out_shape=[
            jax.ShapeDtypeStruct(give.shape, give.dtype),
            jax.ShapeDtypeStruct(tiles.shape, tiles.dtype),
        ],
        in_specs=[any_spec] * 2,
        out_specs=[any_spec] * 2,
        scratch_shapes=[
            pltpu.SemaphoreType.DMA,
            pltpu.SemaphoreType.DMA,
            pltpu.SemaphoreType.DMA,
            pltpu.SemaphoreType.DMA,
        ],
        compiler_params=pltpu.CompilerParams(collective_id=4, has_side_effects=True),
        name="leave",
    )(give, tiles)


def filter_rows(plan, land, table, first_row, backward):
    lane = lax.broadcasted_iota(jnp.int32, (plan.f_rows, LANES), 1)
    low = lane < plan.half
    total = plan.length // LANES
    for m in range(total):
        if backward:
            one, two = 2 * m, 2 * m + 1
        else:
            one, two = plan.chips - 1 - 2 * m, plan.chips - 2 - 2 * m
        left = land[one, first_row : first_row + plan.f_rows, :].astype(F32)
        right = land[two, first_row : first_row + plan.f_rows, :].astype(F32)
        even = jnp.where(low, left, pltpu.roll(right, plan.half, 1))
        odd = jnp.where(low, pltpu.roll(left, plan.half, 1), right)
        at = LANES * m + (BLOCK if backward else 0)
        table[0, :, at : at + LANES] = even
        table[1, :, at : at + LANES] = odd
    blank = jnp.zeros((plan.f_rows, BLOCK), F32)
    at = 0 if backward else plan.length
    for parity in range(2):
        table[parity, :, at : at + BLOCK] = blank


def build_strips(plan, table, strip, backward):
    span = plan.length + BLOCK
    shift = span - LANES if backward else span - (LANES - 1)
    part = 32

    def one(k, carry):
        for parity in range(2):
            row = table[parity, pl.ds(k, 1), :]
            for start in range(0, LANES, part):
                spread = jnp.broadcast_to(row, (part, span))
                rolled = pltpu.roll(
                    spread, (shift + start) % span, 1, stride=1, stride_axis=0
                ).astype(BF)
                strip[parity, k, LANES + start : LANES + start + part, :] = rolled[
                    :, : plan.length
                ]
                strip[parity, k, start : start + part, :] = rolled[
                    :, LANES : LANES + plan.length
                ]
        return carry

    lax.fori_loop(0, plan.local, one, 0)


def sizes(plan):
    size = plan.jb // PIECE
    while size:
        yield size
        size //= 2


def owner_pieces(plan, act):
    section, chip = spot()
    start = plan.pieces * (section * plan.chips + chip)
    per_block = plan.jb // PIECE

    def block(j, carry):
        number = start // per_block + j
        base = number * per_block
        low = jnp.maximum(start - base, 0)
        high = jnp.minimum(start + plan.pieces - base, per_block)
        count = jnp.maximum(high - low, 0)
        which = number // plan.cols_in
        b = lax.rem(number, plan.cols_in)
        sign = which // plan.filters
        full = lax.rem(which, plan.filters)
        group = full // plan.local
        k = lax.rem(full, plan.local)
        for size in sizes(plan):
            done = count // (2 * size) * (2 * size)
            here = lax.rem(count // size, 2) == 1
            source = base + low - start + done
            target = low + done

            @pl.when(jnp.logical_and(here, sign < 2))
            def _():
                for a in range(plan.cols_out):
                    to_chip = plan.part_at(a, b, group)
                    act(source, size, False, k, target, a, sign, to_chip)

            @pl.when(jnp.logical_and(here, sign >= 2))
            def _():
                for a in range(plan.cols_out):
                    for core in range(2):
                        to_chip = plan.part_at(a, b, plan.groups - 1)
                        act(source, size, True, full, target, a, core, to_chip)

        return carry

    lax.fori_loop(0, plan.pieces // per_block + 2, block, 0)


def forward_kernel(plan, *refs):
    io_ref, gain_ref, filters_ref, lengths_ref = refs[:4]
    gate_raw, up_raw, down_raw, proj_raw, attn_raw = refs[4:9]
    if plan.routed:
        maps_ref = refs[9]
        rest = refs[10:]
    else:
        mine_ref, other_ref, taps_ref = refs[9:12]
        rest = refs[12:]
    full_weights, rest = rest[:8], rest[8:]
    (
        conv_ref,
        hidden_ref,
        upstream_ref,
        pair_ref,
        gains_ref,
        mask_ref,
        v_ref,
        pq_ref,
        tapw_ref,
        x_ref,
        xs_ref,
        filt_ref,
        io_own,
        io_sib,
        gain_tile,
        gate_half,
        gate_shard,
        up_half,
        up_shard,
        down_shard,
        u_ref,
        f_ref,
        x_buf,
        xo_buf,
        xs_buf,
        xf_buf,
        f_land,
        table,
        strip,
        mine,
        other,
        taps,
        pq,
        acc,
        joined,
        y_buf,
        land,
        reduced,
        final,
        stage,
        io_sem,
        gain_send,
        gain_recv,
        s_send,
        s_recv,
        u_send,
        x_recv,
        f_send,
        f_recv,
        m_send,
        m_recv,
        t_recv,
        o_send,
        o_recv,
        c_send,
        c_recv,
        d_send,
        r_recv,
        v_sem,
        out_sem,
        w_send,
        w_recv,
    ) = rest
    chips, half, jb, ia, rows_here = plan.chips, plan.half, plan.jb, plan.ia, plan.rows
    section, chip = spot()
    dev = section * chips + chip
    sibling = (1 - section, chip)
    my_group = chip // (plan.cols_out * plan.cols_in)
    greeted = greet_everyone(chips)

    row = lax.broadcasted_iota(jnp.int32, (rows_here, rows_here), 0)
    col = lax.broadcasted_iota(jnp.int32, (rows_here, rows_here), 1)
    order = jnp.where(col == 2 * lax.rem(row, half) + row // half, 1.0, 0.0).astype(BF)
    for i in range(2):
        io_own[i] = flat_dot(order, io_ref[i]).astype(BF)
    cols = gain_ref.shape[1]
    gain_tile[0] = jnp.zeros((8, LANES), F32)
    gain_tile[0, 0:2, 0:cols] = gain_ref[...].astype(F32)
    if plan.pick_here:
        lane = lax.broadcasted_iota(jnp.int32, (gate_raw.shape[0], LANES), 1)
        low = lane < half
        for raw, halves, shard in ((gate_raw, gate_half, gate_shard), (up_raw, up_half, up_shard)):
            for j in range(raw.shape[1] // (2 * LANES)):
                one = raw[:, 2 * LANES * j : 2 * LANES * j + LANES].astype(F32)
                two = raw[:, 2 * LANES * j + LANES : 2 * LANES * (j + 1)].astype(F32)
                zero_half = jnp.where(low, one, pltpu.roll(two, half, 1)).astype(BF)
                one_half = jnp.where(low, pltpu.roll(one, half, 1), two).astype(BF)
                at = slice(LANES * j, LANES * (j + 1))
                shard[section, :, at] = jnp.where(section == 0, zero_half, one_half)
                halves[:, at] = jnp.where(section == 0, one_half, zero_half)
    else:
        for raw, halves, shard in ((gate_raw, gate_half, gate_shard), (up_raw, up_half, up_shard)):
            shard[section] = raw[section]
            halves[...] = raw[1 - section]
    part = down_shard.shape[1]
    down_shard[section] = down_raw[pl.ds(pl.multiple_of(part * section, 16), part), :]
    greeted()
    io_swap = push(io_own, io_sib, io_sem.at[0], io_sem.at[1], sibling)
    io_swap.start()

    gain_swap = push(gain_tile.at[0], gain_tile.at[1], gain_send, gain_recv, sibling)
    gain_swap.start()
    shares = [
        push(src, dst, s_send.at[i], s_recv.at[i], sibling)
        for i, (src, dst) in enumerate(
            (
                (gate_half, gate_shard.at[section]),
                (up_half, up_shard.at[section]),
                (
                    down_raw.at[pl.ds(pl.multiple_of(part * (1 - section), 16), part), :],
                    down_shard.at[section],
                ),
            )
        )
    ]
    for share in shares:
        share.start()

    if plan.routed:

        def places(source, size, tap, k, target, a):
            rows = size * PIECE
            src = maps_ref.at[pl.ds(PIECE * source, rows), pl.ds(a * ia, ia)]
            if tap:
                return src, taps.at[pl.ds(jb * k + PIECE * target, rows), :], t_recv
            return src, mine.at[k, pl.ds(PIECE * target, rows), :], m_recv

        def start_piece(source, size, tap, k, target, a, to_section, to_chip):
            src, dst, sem = places(source, size, tap, k, target, a)
            here = to_section * chips + to_chip == dev

            @pl.when(here)
            def _():
                pltpu.make_async_copy(src, dst, sem).start()

            @pl.when(jnp.logical_not(here))
            def _():
                push(src, dst, m_send, sem, (to_section, to_chip)).start()

        def drain_piece(source, size, tap, k, target, a, to_section, to_chip):
            src, dst, sem = places(source, size, tap, k, target, a)

            @pl.when(to_section * chips + to_chip != dev)
            def _():
                push(src, dst, m_send, sem, (to_section, to_chip)).wait_send()

        owner_pieces(plan, start_piece)

    lag = lax.broadcasted_iota(jnp.int32, (rows_here, LANES), 0)
    lane = lax.broadcasted_iota(jnp.int32, (rows_here, LANES), 1)
    stretch = lax.rem(lane, half)
    backwards = jnp.where(lag == 2 * (half - 1 - stretch) + lane // half, 1.0, 0.0).astype(BF)
    plain = jnp.where(lag == 2 * stretch + lane // half, 1.0, 0.0).astype(BF)
    gain_swap.wait_recv()
    core_zero = section == 0
    own_gain, sib_gain = gain_tile[0], gain_tile[1]
    gain_rows = jnp.concatenate(
        [jnp.where(core_zero, own_gain, sib_gain), jnp.where(core_zero, sib_gain, own_gain)], 0
    ).astype(BF)
    for group in range(plan.groups):
        source = lax.broadcasted_iota(jnp.int32, (plan.filters, plan.f_rows), 0)
        target = lax.broadcasted_iota(jnp.int32, (plan.filters, plan.f_rows), 1)
        chosen = jnp.where(
            (source == group * plan.local + target) & (target < plan.local), 1.0, 0.0
        ).astype(BF)
        some = flat_dot(filters_ref[...], chosen).astype(BF)
        f_ref[group, : plan.f_rows, :] = cols_dot(some, backwards).astype(BF)
        f_ref[group, plan.f_rows : 2 * plan.f_rows, :] = cols_dot(some, plain).astype(BF)
        f_ref[group, 2 * plan.f_rows :, :] = gain_rows

    def send_f(step, carry):
        peer = lax.rem(chip + step, chips)
        group = peer // (plan.cols_out * plan.cols_in)
        push(f_ref.at[group], f_land.at[chip], f_send, f_recv, (section, peer)).start()
        return carry

    lax.fori_loop(1, chips, send_f, 0)
    pltpu.make_async_copy(f_ref.at[my_group], f_land.at[chip], f_recv).start()
    for share in shares:
        share.wait_recv()
    second_layer = (gate_shard.at[1], up_shard.at[1], down_shard.at[1])
    parts = [
        (0, (gate_shard.at[0], up_shard.at[0], down_shard.at[0])),
        (3, (proj_raw, attn_raw)),
    ]
    parts.append((5, second_layer))
    groups = []
    for first, arrays in parts:
        last = first + len(arrays)
        groups.append(
            Gather(
                plan,
                arrays,
                full_weights[first:last],
                w_send.at[pl.ds(first, len(arrays))],
                w_recv.at[pl.ds(first, len(arrays))],
            )
        )
    layer0, attention, layer1 = groups
    layer0.begin()
    position = lax.broadcasted_iota(jnp.int32, (rows_here, 1), 0)
    position = chip * rows_here + 2 * lax.rem(position, half) + position // half
    length_own = jnp.where(section == 0, lengths_ref[0], lengths_ref[1])
    length_other = jnp.where(section == 0, lengths_ref[1], lengths_ref[0])
    mask = jnp.where(position < length_own, 1.0, 0.0)
    mask_other = jnp.where(position < length_other, 1.0, 0.0)
    mask_ref[...] = mask
    io_swap.wait()
    bytes_of(f_land, f_recv)
    pick_row = lax.broadcasted_iota(jnp.int32, (LANES, plan.width), 0)
    pick_col = lax.broadcasted_iota(jnp.int32, (LANES, plan.width), 1)
    repeat = jnp.where(pick_row == lax.rem(pick_col, cols), 1.0, 0.0).astype(BF)
    tile_row = lax.broadcasted_iota(jnp.int32, (chips * 16, plan.width), 0)
    tile_col = lax.broadcasted_iota(jnp.int32, (chips * 16, plan.width), 1)
    rows_all = f_land[:, 2 * plan.f_rows :, :].reshape(chips * 16, LANES)
    spread = jnp.where(
        tile_row // 16 == tile_col // cols, flat_dot(rows_all, repeat), 0.0
    ).astype(BF)
    gain_row = lax.broadcasted_iota(jnp.int32, (16, chips * 16), 0)
    gain_col = lax.broadcasted_iota(jnp.int32, (16, chips * 16), 1)
    gather_rows = jnp.where(lax.rem(gain_col, 16) == gain_row, 1.0, 0.0).astype(BF)
    gathered = flat_dot(gather_rows, spread)
    gains_ref[0:2, :] = gathered[0:2, :]
    gains_ref[2:4, :] = gathered[8:10, :]
    gains_ref[4:8, :] = jnp.zeros((4, plan.width), F32)
    hidden = jnp.where(core_zero, io_own[0], io_sib[1]).astype(F32) * mask
    hidden_ref[...] = hidden
    factor = lax.rsqrt(jnp.mean(hidden * hidden, axis=-1, keepdims=True) + EPSILON)
    u = (hidden * factor * gains_ref[0:1, :]).astype(BF)
    for b in range(plan.cols_in):
        u_ref[b, :, :jb] = u[:half, b * jb : (b + 1) * jb]
        u_ref[b, :, jb:] = u[half:, b * jb : (b + 1) * jb]

    def send_u(step, carry):
        peer = lax.rem(chip + step, chips)
        b = plan.b_of(peer)
        push(
            u_ref.at[b],
            x_buf.at[pl.ds(half * chip, half), :],
            u_send,
            x_recv,
            (section, peer),
        ).start()
        return carry

    lax.fori_loop(1, chips, send_u, 0)
    pltpu.make_async_copy(
        u_ref.at[plan.b_of(chip)],
        x_buf.at[pl.ds(half * chip, half), :],
        x_recv,
    ).start()
    for group in groups[1:]:
        group.begin()
    cot_own = jnp.where(core_zero, io_sib[0], io_own[1]).astype(F32) * mask
    cot_other = jnp.where(core_zero, io_sib[1], io_own[0]).astype(F32) * mask_other
    upstream_ref[...] = cot_own
    pair_ref[:rows_here, :] = cot_own.astype(BF)
    pair_ref[rows_here:, :] = cot_other.astype(BF)
    layer0.stage(0)
    filter_rows(plan, f_land, table, 0, False)
    build_strips(plan, table, strip, False)
    filt_out = pltpu.make_async_copy(f_land, filt_ref, out_sem.at[0])
    filt_out.start()

    if plan.routed:
        bytes_of(mine, m_recv)
        swap = push(mine, other, o_send, o_recv, (1 - section, chip))
        swap.start()

        @pl.when(my_group == plan.groups - 1)
        def _():
            bytes_of(taps, t_recv)

        @pl.when(my_group != plan.groups - 1)
        def _():
            taps[...] = jnp.zeros_like(taps)
    else:
        for src, dst in ((mine_ref, mine), (other_ref, other), (taps_ref, taps)):
            pltpu.sync_copy(src, dst)

    layer0.stage(1)
    bytes_of(x_buf, x_recv)
    x_out = pltpu.make_async_copy(x_buf, x_ref, out_sem.at[1])
    x_out.start()
    xf_buf[0:8, :] = jnp.zeros((8, 2 * jb), F32)
    for i in range(plan.blocks):
        rows = slice(BLOCK * i, BLOCK * (i + 1))
        xf_buf[8 + BLOCK * i : 8 + BLOCK * (i + 1), :] = x_buf[rows, :].astype(F32)
    for i in range(plan.blocks):
        rows = slice(BLOCK * i, BLOCK * (i + 1))
        moved = xf_buf[7 + BLOCK * i : 7 + BLOCK * (i + 1), :].astype(BF)
        xs_buf[rows, :] = moved
        xo_buf[rows, :jb] = x_buf[rows, :jb]
        xo_buf[rows, jb:] = moved[:, jb:]
    xs_out = pltpu.make_async_copy(xs_buf, xs_ref, out_sem.at[2])
    xs_out.start()

    if plan.routed:
        swap.wait()
    turn = (1 - 2 * section).astype(F32)

    def mix(k, carry):
        first = mine[k].astype(F32)
        second = other[k].astype(F32)
        pq[k, :jb, :] = (first + second).astype(BF)
        pq[k, jb:, :] = ((first - second) * turn).astype(BF)
        return carry

    lax.fori_loop(0, plan.local, mix, 0)
    pq_out = pltpu.make_async_copy(pq, pq_ref, out_sem.at[3])
    pq_out.start()
    taps_out = pltpu.make_async_copy(taps, tapw_ref, out_sem.at[4])
    taps_out.start()

    layer0.stage(2)
    attention.stage(0)
    batch = plan.batch
    my_b, level = plan.b_of(chip), chip // plan.cols_in

    def reduce_level(i):
        bytes_of(land.at[i], r_recv.at[i])
        total = y_buf[:, pl.ds(pl.multiple_of(BLOCK * i + half * my_b, half), half), :].astype(F32)
        for step_number in range(plan.cols_in - 1):
            total = total + land[i, step_number].astype(F32)
        reduced[i] = total.astype(BF)

        @pl.when(level == i)
        def _():
            final[i] = reduced[i]

        @pl.when(level != i)
        def _():
            push(
                reduced.at[i],
                final.at[level],
                d_send,
                c_recv,
                (section, i * plan.cols_in + my_b),
            ).start()

    for i in range(plan.blocks):
        if i == 1:
            layer0.stage(3)
            attention.stage(1)
        if i == 2:
            layer0.stage(4)
            attention.stage(2)
            layer1.second(1)
        if i == 3:
            attention.stage(3)
            attention.stage(4)
            layer1.second(2)
        rows = slice(BLOCK * i, BLOCK * (i + 1))
        depth = BLOCK * (i + 1)
        offset = plan.length - depth
        x_now = x_buf[rows, :]
        s_now = xs_buf[rows, :]
        acc[:BLOCK] = flat_dot(
            jnp.concatenate([x_now[:, :jb], s_now[:, jb:]], 1), taps[: 2 * jb, :]
        ) + flat_dot(s_now[:, :jb], taps[2 * jb :, :])
        acc[BLOCK:] = flat_dot(
            jnp.concatenate([x_now[:, jb:], x_now[:, :jb]], 1), taps[: 2 * jb, :]
        ) + flat_dot(s_now[:, jb:], taps[2 * jb :, :])

        def step(t, carry, i=i, depth=depth, offset=offset):
            count = plan.local // batch * i + t
            slot = lax.rem(count, 2)
            some = pl.ds(batch * t, batch)
            v_copy = pltpu.make_async_copy(
                stage.at[slot], v_ref.at[some, :, pl.ds(BLOCK * i, BLOCK), :], v_sem.at[slot]
            )
            even = flat_dot(
                strip[0, some, :, offset:].reshape(batch * BLOCK, depth), x_buf[:depth, :]
            ).astype(BF)
            odd = flat_dot(
                strip[1, some, :, offset:].reshape(batch * BLOCK, depth), xo_buf[:depth, :]
            ).astype(BF)
            if i == 0:
                pl.when(t >= 2)(v_copy.wait)
            else:
                v_copy.wait()
            for k in range(batch):
                here = slice(BLOCK * k, BLOCK * (k + 1))
                first = jnp.concatenate([even[here, :jb], odd[here, jb:]], 1)
                second = jnp.concatenate([even[here, jb:], odd[here, :jb]], 1)
                stage[slot, k, 0] = first
                stage[slot, k, 1] = second
                lanes = slice(2 * jb * k, 2 * jb * (k + 1))
                joined[:BLOCK, lanes] = first
                joined[BLOCK:, lanes] = second
            v_copy.start()
            acc[...] += flat_dot(joined[...], pq[some].reshape(batch * 2 * jb, ia))
            return carry

        lax.fori_loop(0, plan.local // batch, step, 0)
        y_buf[0, rows, :] = acc[:BLOCK].astype(BF)
        y_buf[1, rows, :] = acc[BLOCK:].astype(BF)

        if plan.layered:
            for step_number in range(1, plan.cols_in):
                peer = lax.rem(my_b + step_number, plan.cols_in)
                push(
                    y_buf.at[:, pl.ds(BLOCK * i + half * peer, half), :],
                    land.at[i, step_number - 1],
                    c_send,
                    r_recv.at[i],
                    (section, level * plan.cols_in + peer),
                ).start()
            if i > 0:
                reduce_level(i - 1)
            continue

        def give(r, carry, i=i):
            peer = BLOCK // half * i + r
            src = y_buf.at[:, pl.ds(half * peer, half), :]

            @pl.when(peer == chip)
            def _():
                pltpu.make_async_copy(src, land.at[chip], c_recv).start()

            @pl.when(peer != chip)
            def _():
                push(src, land.at[chip], c_send, c_recv, (section, peer)).start()

            return carry

        lax.fori_loop(0, BLOCK // half, give, 0)

    layer1.second(3)
    if not plan.late:
        for number in range(plan.depth):
            layer1.third(number)
    for slot in range(2):
        pltpu.make_async_copy(
            stage.at[slot], v_ref.at[pl.ds(0, batch), :, pl.ds(0, BLOCK), :], v_sem.at[slot]
        ).wait()
    bytes_of(x_buf.at[pl.ds(0, half * (chips - 1)), :], u_send)
    bytes_of(f_land.at[pl.ds(0, chips - 1)], f_send)
    if plan.routed:
        owner_pieces(plan, drain_piece)
    for copy in (filt_out, x_out, xs_out, pq_out, taps_out):
        copy.wait()
    if plan.layered:
        reduce_level(plan.blocks - 1)
        bytes_of(final.at[pl.ds(0, plan.blocks - 1)], c_recv)
    else:
        bytes_of(land, c_recv)
    for a in range(plan.cols_out):
        total = None
        for c in range(plan.groups):
            if plan.layered:
                terms = [final[a + plan.cols_out * c]]
            else:
                terms = [land[plan.part_at(a, b, c)] for b in range(plan.cols_in)]
            for term in terms:
                term = term.astype(F32)
                total = term if total is None else total + term
        conv_ref[:, :, a * ia : (a + 1) * ia] = total
    if plan.layered:
        bytes_of(land, c_send)
        bytes_of(final.at[pl.ds(0, plan.blocks - 1)], d_send)
    else:
        bytes_of(land.at[pl.ds(0, chips - 1)], c_send)
    for group in groups[:2]:
        group.end()
    if plan.late:
        layer1.hand_over()
    else:
        layer1.end()
    gain_swap.wait_send()
    for share in shares:
        share.wait_send()


def forward_call(plan, io, gain, filters, lengths, raw, maps):
    chips, half, jb, ia, rows = plan.chips, plan.half, plan.jb, plan.ia, plan.rows
    width = plan.width
    any_spec = pl.BlockSpec(memory_space=pl.ANY)
    vmem_spec = pl.BlockSpec(memory_space=pltpu.VMEM)
    smem_spec = pl.BlockSpec(memory_space=pltpu.SMEM)
    dma = pltpu.SemaphoreType.DMA
    down, proj, attn = raw[2].shape, raw[3].shape, raw[4].shape
    share = (raw[0].shape[-2], plan.ff // 2)
    down_share = (down[0] // 2, width)
    grid = (plan.depth, plan.side, plan.side)
    layer = [share, share, down_share]
    levels = plan.blocks if plan.layered else 1
    land_shape = (
        (levels, plan.cols_in - 1, 2, half, ia) if plan.layered else (chips, 2, half, ia)
    )
    gathered = [grid + w for w in layer + [proj, attn]]
    gathered += [grid + w for w in layer]
    shapes = [(w, BF) for w in gathered] + [
        ((2, half, width), F32),
        ((rows, width), F32),
        ((rows, width), F32),
        ((2 * rows, width), BF),
        ((8, width), F32),
        ((rows, 1), F32),
        ((plan.local, 2, plan.length, 2 * jb), BF),
        ((plan.local, 2 * jb, ia), BF),
        ((ORDER * jb, ia), BF),
        ((plan.length, 2 * jb), BF),
        ((plan.length, 2 * jb), BF),
        ((chips, 2 * plan.f_rows + 16, LANES), BF),
    ]
    return pl.pallas_call(
        functools.partial(forward_kernel, plan),
        out_shape=[jax.ShapeDtypeStruct(s, d) for s, d in shapes],
        in_specs=[vmem_spec] * 3
        + [smem_spec]
        + [vmem_spec] * 3
        + [any_spec] * 2
        + [vmem_spec if plan.routed else any_spec] * len(maps),
        out_specs=[any_spec] * 8 + [vmem_spec] * 6 + [any_spec] * 6,
        scratch_shapes=[
            pltpu.VMEM((2, rows, width), BF),
            pltpu.VMEM((2, rows, width), BF),
            pltpu.VMEM((2, 8, LANES), F32),
            pltpu.VMEM(share, BF),
            pltpu.VMEM((2,) + share, BF),
            pltpu.VMEM(share, BF),
            pltpu.VMEM((2,) + share, BF),
            pltpu.VMEM((2,) + down_share, BF),
            pltpu.VMEM((plan.cols_in, half, 2 * jb), BF),
            pltpu.VMEM((plan.groups, 2 * plan.f_rows + 16, LANES), BF),
            pltpu.VMEM((plan.length, 2 * jb), BF),
            pltpu.VMEM((plan.length, 2 * jb), BF),
            pltpu.VMEM((plan.length, 2 * jb), BF),
            pltpu.VMEM((plan.length + 8, 2 * jb), F32),
            pltpu.VMEM((chips, 2 * plan.f_rows + 16, LANES), BF),
            pltpu.VMEM((2, plan.f_rows, plan.length + BLOCK), F32),
            pltpu.VMEM((2, plan.local, BLOCK, plan.length), BF),
            pltpu.VMEM((plan.local, jb, ia), BF),
            pltpu.VMEM((plan.local, jb, ia), BF),
            pltpu.VMEM((ORDER * jb, ia), BF),
            pltpu.VMEM((plan.local, 2 * jb, ia), BF),
            pltpu.VMEM((2 * BLOCK, ia), F32),
            pltpu.VMEM((2 * BLOCK, plan.batch * 2 * jb), BF),
            pltpu.VMEM((2, plan.length, ia), BF),
            pltpu.VMEM(land_shape, BF),
            pltpu.VMEM((levels, 2, half, ia), BF),
            pltpu.VMEM((levels, 2, half, ia), BF),
            pltpu.VMEM((2, plan.batch, 2, BLOCK, 2 * jb), BF),
            dma((2,)),
            dma,
            dma,
            dma((3,)),
            dma((3,)),
        ]
        + [dma] * 12
        + [dma((levels,)), dma((2,)), dma((5,)), *Gather.semaphores(plan, 8)],
        compiler_params=pltpu.CompilerParams(
            collective_id=2, has_side_effects=True, vmem_limit_bytes=VMEM_LIMIT
        ),
        name="spectral_forward",
    )(io, gain, filters, lengths, *raw, *maps)


def backward_kernel(plan, number, *refs):
    g_ref, filt_ref, v_ref, pq, tapw, x_ref, xs_ref = refs[:7]
    grads, rest = refs[7 : 7 + number], refs[7 + number :]
    if plan.late:
        hidden_ref, gains_ref, mask_ref, dmid_ref, out_ref, gain_sums_ref, *lines = rest[:9]
        res_ref, gate_ref, up_ref, down_ref, proj_ref, attn_ref, gain_out, dmaps_ref = rest[9:17]
        du_ref, gain_buf, gain_land, give_res, *half_parts = rest[17:30]
        half0, crossing, arrived = half_parts[:3], half_parts[3:6], half_parts[6:9]
        e_send, e_recv, n_send, n_recv = rest[30:34]
        half1, line_land, (l_send, l_recv) = rest[34:37], rest[37:40], rest[40:42]
        rest = rest[42:]
        sums = [*half0, proj_ref, attn_ref]
    else:
        sums, rest = rest[:number], rest[number:]
        du_ref, dmap_ref, dtap_ref = rest[:3]
        rest = rest[3:]
    count = 5 * sum(len(plan.routes(grad.shape[3])) for grad in grads)
    scatter = Scatter(plan, grads, sums, rest[:count], *rest[count : count + 2])
    rest = rest[count + 2 :]
    (
        g_buf,
        gt_buf,
        table,
        strip,
        v_buf,
        z_even,
        z_odd,
        acc_even,
        acc_odd,
        kept,
        give_m,
        take_m,
        total_m,
        kept_t,
        give_t,
        take_t,
        total_t,
        du_buf,
        land,
        g_send,
        g_recv,
        v_sem,
        m_send,
        m_recv,
        t_send,
        t_recv,
        w_send,
        w_recv,
        d_send,
        d_recv,
        x_sem,
        z_send,
        z_recv,
    ) = rest
    chips, half, jb, ia = plan.chips, plan.half, plan.jb, plan.ia
    section, chip = spot()
    dev = section * chips + chip
    my_a, my_b = plan.a_of(chip), plan.b_of(chip)
    my_group = chip // (plan.cols_out * plan.cols_in)
    sibling = (1 - section, chip)
    greet_everyone(chips)()

    def send_g(step, carry):
        peer = lax.rem(chip + step, chips)
        a = plan.a_of(peer)
        push(
            g_ref.at[:, :, pl.ds(pl.multiple_of(a * ia, ia), ia)],
            g_buf.at[:, pl.ds(half * chip, half), :],
            g_send,
            g_recv,
            (section, peer),
        ).start()
        return carry

    own_g = g_ref.at[:, :, pl.ds(pl.multiple_of(my_a * ia, ia), ia)]
    level, levels = chip // plan.cols_in, chips // plan.cols_in

    def g_rows(t):
        source = lax.rem(level - t + levels, levels) * plan.cols_in + my_b
        return g_buf.at[:, pl.ds(pl.multiple_of(half * source, half), half), :]

    def spread_g(t):
        if t > 0:
            bytes_of(g_rows(t), z_recv.at[t])
        for step_number in range(1, plan.cols_in):
            peer = lax.rem(my_b + step_number, plan.cols_in)
            push(
                own_g if t == 0 else g_rows(t),
                g_rows(t),
                g_send,
                g_recv,
                (section, level * plan.cols_in + peer),
            ).start()

    if plan.layered:
        for t in range(1, levels):
            to_level = lax.rem(level + t, levels)
            to_a = lax.rem(to_level, plan.cols_out)
            push(
                g_ref.at[:, :, pl.ds(pl.multiple_of(to_a * ia, ia), ia)],
                g_rows(0),
                z_send,
                z_recv.at[t],
                (section, to_level * plan.cols_in + my_b),
            ).start()
        spread_g(0)
        pltpu.make_async_copy(own_g, g_rows(0), z_recv.at[0]).start()
    else:
        lax.fori_loop(1, chips, send_g, 0)
        pltpu.make_async_copy(
            own_g, g_buf.at[:, pl.ds(half * chip, half), :], g_recv
        ).start()
    v_copy = [pltpu.make_async_copy(v_ref.at[k], v_buf.at[k], v_sem.at[k]) for k in range(2)]
    for copy in v_copy:
        copy.start()
    x_copy = [
        pltpu.make_async_copy(src, dst, x_sem.at[i])
        for i, (src, dst) in enumerate(((x_ref, z_even), (xs_ref, z_odd)))
    ]
    for copy in x_copy:
        copy.start()
    filter_rows(plan, filt_ref, table, plan.f_rows, True)
    build_strips(plan, table, strip, True)
    if plan.layered:
        for t in range(1, levels):
            spread_g(t)
    acc_even[...] = jnp.zeros_like(acc_even)
    acc_odd[...] = jnp.zeros_like(acc_odd)
    if plan.layered:
        pltpu.make_async_copy(own_g, g_rows(0), z_recv.at[0]).wait()
        bytes_of(g_buf.at[:, pl.ds(0, half * levels * (plan.cols_in - 1)), :], g_recv)
    else:
        bytes_of(g_buf, g_recv)
    scatter.begin()
    if plan.late:
        z, y, x = plan.place(chip)
        for i in range(3):
            for t in range(plan.depth - 1):
                to = (section, plan.chip_at(lax.rem(z + 1 + t, plan.depth), y, x))
                push(
                    lines[i].at[t], line_land[i].at[t], l_send.at[i], l_recv.at[i], to
                ).start()
    for phase in range(2):
        for i in range(plan.blocks):
            rows = slice(BLOCK * i, BLOCK * (i + 1))
            gt_buf[phase, :, rows] = g_buf[phase, rows, :].astype(F32).T.astype(BF)
    turn = (1 - 2 * section).astype(F32)
    half_ways = (((1,), (1,)), ((), ()))

    def piece_copies(k, tap, begin):
        per_block = jb // PIECE
        which = 2 * plan.filters + k if tap else section * plan.filters + my_group * plan.local + k
        start = (which * plan.cols_in + my_b) * per_block
        owner, row = start // plan.pieces, lax.rem(start, plan.pieces)
        first = jnp.minimum(plan.pieces - row, per_block)
        for to, at, base, count in ((owner, row, 0, first), (owner + 1, 0, first, per_block - first)):
            for size in sizes(plan):
                done = count // (2 * size) * (2 * size)
                rows = size * PIECE
                here = lax.rem(count // size, 2) == 1
                source = PIECE * (base + done)
                src = (
                    total_t.at[pl.ds(jb * k + source, rows), :]
                    if tap
                    else total_m.at[k, pl.ds(source, rows), :]
                )
                dst = dmaps_ref.at[
                    pl.ds(PIECE * (at + done), rows), pl.ds(pl.multiple_of(my_a * ia, ia), ia)
                ]
                if begin:

                    @pl.when(jnp.logical_and(here, to == dev))
                    def _():
                        pltpu.make_async_copy(src, dst, w_recv).start()

                @pl.when(jnp.logical_and(here, to != dev))
                def _():
                    copy = push(src, dst, w_send, w_recv, (to // chips, lax.rem(to, chips)))
                    if begin:
                        copy.start()
                    else:
                        copy.wait_send()

    def exchange(k):
        return push(give_m.at[k], take_m.at[k], m_send.at[k], m_recv.at[k], (1 - section, chip))

    def finish(k):
        exchange(k).wait()
        total_m[k] = (kept[k] + take_m[k].astype(F32)).astype(BF)
        if plan.routed:
            piece_copies(k, False, True)

    for copy in x_copy:
        copy.wait()
    x_even, x_odd = z_even[:, :jb], z_even[:, jb:]
    s_even, s_odd = z_odd[:, :jb], z_odd[:, jb:]
    for tap, (on_even, on_odd) in enumerate(((x_even, x_odd), (s_odd, x_even), (s_even, s_odd))):
        tap_grad = jnp.dot(gt_buf[0], on_even, preferred_element_type=F32) + jnp.dot(
            gt_buf[1], on_odd, preferred_element_type=F32
        )
        tap_grad = tap_grad.T
        kept_t[tap * jb : (tap + 1) * jb, :] = tap_grad
        give_t[tap * jb : (tap + 1) * jb, :] = tap_grad.astype(BF)
    tap_swap = push(give_t, take_t, t_send, t_recv, (1 - section, chip))
    tap_swap.start()
    for i in range(plan.blocks):
        rows = slice(BLOCK * i, BLOCK * (i + 1))
        from_even = lax.dot_general(
            g_buf[0, rows, :], tapw[...], half_ways, preferred_element_type=F32
        )
        from_odd = lax.dot_general(
            g_buf[1, rows, :], tapw[...], half_ways, preferred_element_type=F32
        )
        acc_even[rows, :jb] = from_even[:, :jb] + from_odd[:, jb : 2 * jb]
        acc_even[rows, jb : 2 * jb] = from_odd[:, :jb]
        acc_odd[rows, :jb] = from_even[:, 2 * jb :]
        acc_odd[rows, jb : 2 * jb] = from_even[:, jb : 2 * jb] + from_odd[:, 2 * jb :]

    def step(k, carry):
        slot = lax.rem(k, 2)
        from_even = rows_dot(g_buf[0], pq[k]).astype(BF)
        from_odd = rows_dot(g_buf[1], pq[k]).astype(BF)
        z_even[:, :jb] = from_even[:, :jb]
        z_even[:, jb:] = from_odd[:, :jb]
        z_odd[:, :jb] = from_odd[:, jb:]
        z_odd[:, jb:] = from_even[:, jb:]
        pltpu.make_async_copy(v_ref.at[k], v_buf.at[slot], v_sem.at[slot]).wait()
        grad = jnp.dot(gt_buf[0], v_buf[slot, 0], preferred_element_type=F32) + jnp.dot(
            gt_buf[1], v_buf[slot, 1], preferred_element_type=F32
        )
        grad = grad.T
        plus, minus = grad[:jb, :], grad[jb:, :] * turn
        kept[k] = plus + minus
        give_m[k] = (plus - minus).astype(BF)
        exchange(k).start()

        @pl.when(k + 2 < plan.local)
        def _():
            pltpu.make_async_copy(v_ref.at[k + 2], v_buf.at[slot], v_sem.at[slot]).start()

        for j in range(plan.blocks):
            rows = slice(BLOCK * j, BLOCK * (j + 1))
            depth = plan.length - BLOCK * j
            acc_even[rows, :] += jnp.dot(
                strip[0, k, :, :depth], z_even[BLOCK * j :, :], preferred_element_type=F32
            )
            out = jnp.dot(
                strip[1, k, :, :depth], z_odd[BLOCK * j :, :], preferred_element_type=F32
            )
            acc_even[rows, :jb] += out[:, :jb]
            acc_odd[rows, jb:] += out[:, jb:]

        @pl.when(k >= 1)
        def _():
            finish(k - 1)

        for turn_number in range(plan.depth + 1):
            at = 1 + (turn_number * (plan.local - 2)) // plan.depth
            pl.when(k == at)(functools.partial(scatter.stage, turn_number))
        return carry

    lax.fori_loop(0, plan.local, step, 0)
    for i in range(plan.blocks):
        rows = slice(BLOCK * i, BLOCK * (i + 1))
        moved = acc_odd[BLOCK * i + 1 : BLOCK * (i + 1) + 1, :]
        both = (acc_even[rows, :] + moved).astype(BF)
        du_buf[0, rows, :] = both[:, :jb]
        du_buf[1, rows, :] = both[:, jb:]

        def give(r, carry, i=i):
            peer = BLOCK // half * i + r
            src = du_buf.at[:, pl.ds(half * peer, half), :]

            @pl.when(peer == chip)
            def _():
                pltpu.make_async_copy(src, land.at[chip], d_recv).start()

            @pl.when(peer != chip)
            def _():
                push(src, land.at[chip], d_send, d_recv, (section, peer)).start()

            return carry

        lax.fori_loop(0, BLOCK // half, give, 0)
    finish(plan.local - 1)
    tap_swap.wait()
    total_t[...] = (kept_t[...] + take_t[...].astype(F32)).astype(BF)
    if plan.routed:

        @pl.when(jnp.logical_and(section == 0, my_group == plan.groups - 1))
        def _():
            for tap in range(ORDER):
                piece_copies(tap, True, True)
    else:
        pltpu.sync_copy(total_m, dmap_ref)
        pltpu.sync_copy(total_t, dtap_ref)
    if plan.layered:
        bytes_of(g_buf.at[:, pl.ds(0, half * levels * (plan.cols_in - 1)), :], g_send)
        bytes_of(g_buf.at[:, pl.ds(0, half * (levels - 1)), :], z_send)
    else:
        bytes_of(g_buf.at[:, pl.ds(0, half * (chips - 1)), :], g_send)
    bytes_of(land, d_recv)
    for b in range(plan.cols_in):
        total = None
        for c in range(plan.groups):
            for a in range(plan.cols_out):
                term = land[plan.part_at(a, b, c)].astype(F32)
                total = term if total is None else total + term
        du_ref[:, :, b * jb : (b + 1) * jb] = total
    bytes_of(land.at[pl.ds(0, chips - 1)], d_send)
    scatter.end()
    if plan.late:
        core_zero = section == 0
        for i in range(3):
            bytes_of(line_land[i], l_recv.at[i])
            total = lines[i][plan.depth - 1].astype(F32)
            for t in range(plan.depth - 1):
                total = total + line_land[i][t].astype(F32)
            half1[i][...] = total
            bytes_of(line_land[i], l_send.at[i])
            crossing[i][...] = jnp.where(core_zero, half1[i][...], half0[i][...])
            push(crossing[i], arrived[i], e_send.at[i], e_recv.at[i], sibling).start()
        hidden = hidden_ref[...]
        factor = lax.rsqrt(jnp.mean(hidden * hidden, axis=-1, keepdims=True) + EPSILON)
        signal_grad = du_ref[...].reshape(plan.rows, plan.width)
        weighted = signal_grad * gains_ref[0:1, :]
        correction = jnp.mean(weighted * hidden, axis=-1, keepdims=True)
        hidden_grad = factor * weighted - hidden * factor * factor * factor * correction
        gain_buf[...] = gain_sums_ref[...]
        gain_buf[0:1, :] = jnp.sum(signal_grad * hidden * factor, axis=0, keepdims=True)
        per_tile = LANES * chips // plan.width

        def send_gain(step, carry):
            peer = lax.rem(dev + step, 2 * chips)
            tile = lax.rem(peer, chips) // per_tile
            push(
                gain_buf.at[:, pl.ds(pl.multiple_of(LANES * tile, LANES), LANES)],
                gain_land.at[dev],
                n_send,
                n_recv,
                (peer // chips, lax.rem(peer, chips)),
            ).start()
            return carry

        lax.fori_loop(1, 2 * chips, send_gain, 0)
        pltpu.make_async_copy(
            gain_buf.at[:, pl.ds(pl.multiple_of(LANES * (chip // per_tile), LANES), LANES)],
            gain_land.at[dev],
            n_recv,
        ).start()
        done_in = (mask_ref[...] * (dmid_ref[...] + hidden_grad)).astype(BF)
        row = lax.broadcasted_iota(jnp.int32, (plan.rows, plan.rows), 0)
        col = lax.broadcasted_iota(jnp.int32, (plan.rows, plan.rows), 1)
        order = jnp.where(col == 2 * lax.rem(row, half) + row // half, 1.0, 0.0).astype(BF)
        done_in = cols_dot(order, done_in).astype(BF)
        done_out = cols_dot(order, out_ref[...]).astype(BF)
        give_res[...] = jnp.where(core_zero, done_out, done_in)
        swap_res = push(give_res, res_ref.at[section], e_send.at[3], e_recv.at[3], sibling)
        swap_res.start()
        res_ref[section] = jnp.where(core_zero, done_in, done_out)
        for i in range(3):
            push(crossing[i], arrived[i], e_send.at[i], e_recv.at[i], sibling).wait()
        lane = lax.broadcasted_iota(jnp.int32, (gate_ref.shape[0], LANES), 1)
        low = lane < half
        kept_half = [jnp.where(core_zero, half0[i][...], half1[i][...]) for i in range(3)]
        for i, out in ((0, gate_ref), (1, up_ref)):
            came = arrived[i][...]
            first = jnp.where(core_zero, kept_half[i], came)
            second = jnp.where(core_zero, came, kept_half[i])
            for j in range(out.shape[1] // (2 * LANES)):
                one, two = (w[:, LANES * j : LANES * (j + 1)] for w in (first, second))
                at = 2 * LANES * j
                out[:, at : at + LANES] = jnp.where(low, one, pltpu.roll(two, half, 1))
                out[:, at + LANES : at + 2 * LANES] = jnp.where(
                    low, pltpu.roll(one, half, 1), two
                )
        part = half0[2].shape[0]
        came = arrived[2][...]
        down_ref[:part, :] = jnp.where(core_zero, kept_half[2], came)
        down_ref[part:, :] = jnp.where(core_zero, came, kept_half[2])
        swap_res.wait()
        bytes_of(gain_land, n_recv)
        gain_out[...] = jnp.sum(gain_land[...], axis=0)
        bytes_of(gain_land.at[pl.ds(0, 2 * chips - 1)], n_send)
    if plan.routed:

        def drain(k, carry):
            piece_copies(k, False, False)
            return carry

        lax.fori_loop(0, plan.local, drain, 0)

        @pl.when(jnp.logical_and(section == 0, my_group == plan.groups - 1))
        def _():
            for tap in range(ORDER):
                piece_copies(tap, True, False)

        bytes_of(dmaps_ref, w_recv)


def backward_call(plan, g, filt, v, pq, tapw, x, xs, grads, rest=()):
    chips, half, jb, ia = plan.chips, plan.half, plan.jb, plan.ia
    any_spec = pl.BlockSpec(memory_space=pl.ANY)
    vmem_spec = pl.BlockSpec(memory_space=pltpu.VMEM)
    dma = pltpu.SemaphoreType.DMA
    shapes = [g_part.shape[3:] for g_part in grads]
    rows, width = plan.rows, plan.width
    finish = []
    if plan.late:
        out_shape = [jax.ShapeDtypeStruct((2, rows, width), BF)]
        out_shape += [
            jax.ShapeDtypeStruct(shape, F32)
            for shape in (
                (shapes[0][0], plan.ff),
                (shapes[1][0], plan.ff),
                (2 * shapes[2][0], width),
                *shapes[3:],
                (8, LANES),
            )
        ]
        in_vmem = len(out_shape)
        out_shape.append(jax.ShapeDtypeStruct((plan.map_rows, width), BF))
        finish = [
            pltpu.VMEM((2, half, width), F32),
            pltpu.VMEM((8, width), F32),
            pltpu.VMEM((2 * chips, 8, LANES), F32),
            pltpu.VMEM((rows, width), BF),
        ]
        finish += [pltpu.VMEM(shape, F32) for shape in shapes[:3]] * 3
        finish += [dma((4,)), dma((4,)), dma, dma]
        finish += [pltpu.VMEM(shape, F32) for shape in shapes[:3]]
        finish += [pltpu.VMEM((plan.depth - 1,) + shape, BF) for shape in shapes[:3]]
        finish += [dma((3,)), dma((3,))]
    else:
        out_shape = [jax.ShapeDtypeStruct(shape, F32) for shape in shapes]
        out_shape.append(jax.ShapeDtypeStruct((2, half, width), F32))
        in_vmem = len(out_shape)
        out_shape.append(jax.ShapeDtypeStruct((plan.local, jb, ia), BF))
        out_shape.append(jax.ShapeDtypeStruct((ORDER * jb, ia), BF))
    return pl.pallas_call(
        functools.partial(backward_kernel, plan, len(grads)),
        out_shape=out_shape,
        in_specs=[vmem_spec, vmem_spec, any_spec, vmem_spec, vmem_spec, any_spec, any_spec]
        + [vmem_spec] * (len(grads) + len(rest)),
        out_specs=[vmem_spec] * in_vmem + [any_spec] * (len(out_shape) - in_vmem),
        scratch_shapes=finish
        + Scatter.scratch(plan, shapes)
        + Scatter.semaphores(plan, len(grads))
        + [
            pltpu.VMEM((2, plan.length, ia), BF),
            pltpu.VMEM((2, ia, plan.length), BF),
            pltpu.VMEM((2, plan.f_rows, plan.length + BLOCK), F32),
            pltpu.VMEM((2, plan.local, BLOCK, plan.length), BF),
            pltpu.VMEM((2, 2, plan.length, 2 * jb), BF),
            pltpu.VMEM((plan.length, 2 * jb), BF),
            pltpu.VMEM((plan.length, 2 * jb), BF),
            pltpu.VMEM((plan.length, 2 * jb), F32),
            pltpu.VMEM((plan.length + 8, 2 * jb), F32),
            pltpu.VMEM((plan.local, jb, ia), F32),
            pltpu.VMEM((plan.local, jb, ia), BF),
            pltpu.VMEM((plan.local, jb, ia), BF),
            pltpu.VMEM((plan.local, jb, ia), BF),
            pltpu.VMEM((ORDER * jb, ia), F32),
            pltpu.VMEM((ORDER * jb, ia), BF),
            pltpu.VMEM((ORDER * jb, ia), BF),
            pltpu.VMEM((ORDER * jb, ia), BF),
            pltpu.VMEM((2, plan.length, jb), BF),
            pltpu.VMEM((chips, 2, half, jb), BF),
            dma,
            dma,
            dma((2,)),
            dma((plan.local,)),
            dma((plan.local,)),
            dma,
            dma,
            dma,
            dma,
            dma,
            dma,
            dma((2,)),
            dma,
            dma((plan.depth,)),
        ],
        compiler_params=pltpu.CompilerParams(
            collective_id=3, has_side_effects=True, vmem_limit_bytes=VMEM_LIMIT
        ),
        name="spectral_backward",
    )(g, filt, v, pq, tapw, x, xs, *grads, *rest)

SWAPS = 7


def middle_kernel(plan, *refs):
    (
        conv_ref,
        hidden_ref,
        gains_ref,
        mask_ref,
        up_ref,
        up_pair,
        *stored,
    ) = refs[:14]
    (
        out_ref,
        g_ref,
        dmid_ref,
        gain_ref,
        gate0_g,
        up0_g,
        down0_g,
        gate1_g,
        up1_g,
        down1_g,
        proj_g,
        attn_g,
    ) = refs[14:26]
    held = refs[26:34]
    (
        pair0,
        pair1,
        give,
        take,
        gates,
        ups,
        acts,
        dgate,
        dup,
        kv,
        q_buf,
        probs,
        dkv,
        back,
        back_land,
        down_land,
        att,
        dq_buf,
        proj_all,
        attn_all,
        proj_take,
        attn_take,
        load_sem,
        a_send,
        a_recv,
        send,
        recv,
        kv_send,
        kv_recv,
        bk_send,
        bk_recv,
        *extra,
    ) = refs[34:]
    chips, rows, width = plan.chips, plan.rows, plan.width
    section, chip = spot()
    sibling = (1 - section, chip)
    reach = WINDOW // rows
    span = (reach + 1) * rows
    layer0, (w_proj, w_out), layer1 = held[:3], held[3:5], held[5:]
    split, cut = 3 * plan.width // 2, plan.width // 2
    own_rows = [
        w_proj.at[pl.ds(pl.multiple_of(split * section, 16), split), :],
        w_out.at[pl.ds(pl.multiple_of(cut * section, 16), cut), :],
    ]
    homes = list(layer0) + own_rows + ([] if plan.late else list(layer1))
    loads = [
        pltpu.make_async_copy(a, b, load_sem.at[i]) for i, (a, b) in enumerate(zip(stored, homes))
    ]
    if plan.late:
        grads1, gather_send, gather_recv, scatter_send, scatter_recv = extra[:3], *extra[3:7]
        gather = Gather(plan, layer1, layer1, gather_send, gather_recv)
        held_loads = [
            pltpu.make_async_copy(src, dst, gather_recv.at[i // 2, i % 2])
            for i, (src, dst) in enumerate(gather.held_parts(stored[5:]))
        ]
        for load in held_loads:
            load.start()
    for load in loads:
        load.start()
    greet_everyone(chips)()
    passes = [
        push(stored[3 + i], own_rows[i], a_send.at[i], a_recv.at[i], sibling) for i in range(2)
    ]
    for copy in passes:
        copy.start()
    if plan.late:
        scatter = Scatter(
            plan, grads1, (gate1_g, up1_g, down1_g), extra[7:], scatter_send, scatter_recv, True
        )
        for load in held_loads:
            load.wait()
        gather.last_only()
    ff = plan.ff // 2
    own = slice(0, rows)
    second = slice(rows, 2 * rows)
    mask = mask_ref[...]

    def swap(number, src, dst):
        copy = push(src, dst, send.at[number], recv.at[number], sibling)
        copy.start()
        copy.wait()

    def norm(values, gain):
        factor = lax.rsqrt(jnp.mean(values * values, axis=-1, keepdims=True) + EPSILON)
        return values * factor * gain, factor

    def norm_back(values, factor, gain, upstream):
        weighted = upstream * gain
        gain_grad = jnp.sum(upstream * values * factor, axis=0, keepdims=True)
        correction = jnp.mean(weighted * values, axis=-1, keepdims=True)
        return factor * weighted - values * factor * factor * factor * correction, gain_grad

    def feed(layer, pair, weights, number):
        w_gate, w_up, w_down = (Flat(w) for w in weights)
        swap(number, pair.at[own], pair.at[second])
        for start in range(0, ff, BLOCK):
            cols = slice(start, start + BLOCK)
            gate_rows = flat_dot(pair[...], w_gate.columns(start, BLOCK))
            up_rows = flat_dot(pair[...], w_up.columns(start, BLOCK))
            gates[layer, :, cols] = gate_rows
            ups[layer, :, cols] = up_rows
            acts[layer, :, cols] = (gate_rows * jax.nn.sigmoid(gate_rows) * up_rows).astype(BF)
        part = flat_dot(acts[layer], w_down.all())
        give[number] = part[second].astype(BF)
        swap(number + 1, give.at[number], take.at[number])
        return part[own] + take[number].astype(F32)

    def feed_back(layer, pair, weights, grads, upstream_pair, number):
        w_gate, w_up, w_down = (Flat(w) for w in weights)
        gate_g, up_g, down_g = (Flat(w) for w in grads)
        turned = pair[...].astype(F32).T.astype(BF)
        for start in range(0, ff, BLOCK):
            cols = slice(start, start + BLOCK)
            active_grad = rows_dot(upstream_pair, w_down.rows(start, BLOCK))
            gate_rows, up_rows = gates[layer, :, cols], ups[layer, :, cols]
            sigmoid = jax.nn.sigmoid(gate_rows)
            slope = sigmoid * (1.0 + gate_rows * (1.0 - sigmoid))
            gate_grad = (active_grad * up_rows * slope).astype(BF)
            up_grad = (active_grad * gate_rows * sigmoid).astype(BF)
            dgate[:, cols] = gate_grad
            dup[:, cols] = up_grad
        for start in range(0, width, BLOCK):
            cols = slice(start, start + BLOCK)
            part = rows_dot(dgate[...], w_gate.rows(start, BLOCK)) + rows_dot(
                dup[...], w_up.rows(start, BLOCK)
            )
            give[number, :, cols] = part[second].astype(BF)
            att[:, cols] = part[own]
        copy = push(
            give.at[number], take.at[number], send.at[number], recv.at[number], sibling
        )
        copy.start()
        for start in range(0, ff, BLOCK):
            cols = slice(start, start + BLOCK)
            gate_g.put_columns(start, flat_dot(turned, dgate[:, cols]).astype(BF))
            up_g.put_columns(start, flat_dot(turned, dup[:, cols]).astype(BF))
            down_g.put_rows(
                start,
                flat_dot(acts[layer, :, cols].astype(F32).T.astype(BF), upstream_pair).astype(BF),
            )
        copy.wait()
        return att[...] + take[number].astype(F32)

    middle0 = hidden_ref[...] + conv_ref[...]
    normed, factor0 = norm(middle0, gains_ref[1:2, :])
    pair0[own] = normed.astype(BF)
    dmid_ref[...] = middle0
    for load in loads[:3]:
        load.wait()
    branch = feed(0, pair0, layer0, 0)
    passed = (mask * (dmid_ref[...] + branch)).astype(BF).astype(F32)

    normed, factor10 = norm(passed, gains_ref[2:3, :])
    inputs = normed.astype(BF)
    for load in loads[3:5]:
        load.wait()
    for copy in passes:
        copy.wait()
    mine = slice(reach * rows, span)
    q_buf[...] = flat_dot(inputs, w_proj[:width]).astype(BF)
    kv[mine, :width] = flat_dot(inputs, w_proj[width : 2 * width]).astype(BF)
    kv[mine, width:] = flat_dot(inputs, w_proj[2 * width :]).astype(BF)

    layer, level = plan.layer, chip // plan.layer
    within = lax.rem(chip, layer)

    def slot(distance):
        return kv.at[pl.ds((reach - distance) * rows, rows)]

    def ahead(distance):
        return push(
            kv.at[mine],
            slot(distance),
            kv_send.at[distance - 1],
            kv_recv.at[distance - 1],
            (section, chip + distance),
        )

    def pass_on(place):
        distance = reach - (within - place)
        return push(
            slot(reach),
            slot(distance),
            kv_send.at[reach + place],
            kv_recv.at[distance - 1],
            (section, level * layer + place),
        )

    def goes_ahead(distance):
        if plan.layered and distance < reach:
            return within + distance < layer
        return chip + distance < chips

    def comes(distance):
        return chip >= distance

    for distance in range(reach, 0, -1):

        @pl.when(goes_ahead(distance))
        def _():
            ahead(distance).start()

        @pl.when(chip < distance)
        def _():
            kv[(reach - distance) * rows : (reach - distance + 1) * rows, :] = jnp.zeros(
                (rows, 2 * width), BF
            )

    half = plan.half
    row = lax.broadcasted_iota(jnp.int32, (rows, span), 0)
    col = lax.broadcasted_iota(jnp.int32, (rows, span), 1)
    inner = lax.rem(col, rows)
    q_place = 2 * lax.rem(row, half) + row // half
    k_place = (col // rows - reach) * rows + 2 * lax.rem(inner, half) + inner // half
    distance_rows = q_place - k_place
    allowed = (
        (k_place + chip * rows >= 0) & (distance_rows >= 0) & (distance_rows < WINDOW)
    )
    lane = lax.broadcasted_iota(jnp.int32, (rows, LANES), 1)
    low = lane < HEAD_DIM
    scale = HEAD_DIM ** (-0.5)
    zero = jnp.zeros((rows, LANES), BF)
    def arrived(distance):
        push(
            kv.at[mine],
            slot(distance),
            kv_send.at[distance - 1],
            kv_recv.at[distance - 1],
            sibling,
        ).wait_recv()

    pl.when(comes(reach))(functools.partial(arrived, reach))
    if plan.layered:
        for place in range(layer - 1):

            @pl.when(jnp.logical_and(level > 0, place < within))
            def _():
                pass_on(place).start()

    for distance in range(1, reach):
        pl.when(comes(distance))(functools.partial(arrived, distance))

    for pair in range(width // LANES):
        lanes = slice(LANES * pair, LANES * (pair + 1))
        keys, values = kv[:, lanes], kv[:, width + LANES * pair : width + LANES * (pair + 1)]
        parts = []
        for side in range(2):
            here = low if side == 0 else jnp.logical_not(low)
            queries = jnp.where(here, q_buf[:, lanes], zero)
            scores = rows_dot(queries, keys) * scale
            scores = jnp.where(allowed, scores, BIG_NEGATIVE)
            weights = jnp.exp(scores - jnp.max(scores, axis=-1, keepdims=True))
            weights = weights / jnp.sum(weights, axis=-1, keepdims=True)
            probs[2 * pair + side] = weights
            parts.append(flat_dot(weights.astype(BF), values))
        att[:, lanes] = jnp.where(low, parts[0], parts[1])
    attended = att[...].astype(BF)
    middle1 = passed + flat_dot(attended, w_out[...])

    if plan.late:
        gather.end(True)
    for load in loads[5:]:
        load.wait()
    normed, factor11 = norm(middle1, gains_ref[3:4, :])
    pair1[own] = normed.astype(BF)
    branch = feed(1, pair1, layer1, 2)
    out_ref[...] = (mask * (middle1 + branch)).astype(BF)
    if not plan.late:
        grads1 = (gate1_g, up1_g, down1_g)
    dnormed = feed_back(1, pair1, layer1, grads1, up_pair[...], 4)
    dmiddle, gain11 = norm_back(middle1, factor11, gains_ref[3:4, :], dnormed)
    dmiddle = up_ref[...] + dmiddle
    gain_ref[3:4, :] = gain11

    dy = dmiddle.astype(BF)
    attn_all[...] = flat_dot(attended.astype(F32).T.astype(BF), dy).astype(BF)
    datt = rows_dot(dy, w_out[...]).astype(BF)
    for pair in range(width // LANES):
        lanes = slice(LANES * pair, LANES * (pair + 1))
        value_lanes = slice(width + LANES * pair, width + LANES * (pair + 1))
        keys, values = kv[:, lanes], kv[:, value_lanes]
        dq_parts, key_grad, value_grad = [], None, None
        for side in range(2):
            here = low if side == 0 else jnp.logical_not(low)
            queries = jnp.where(here, q_buf[:, lanes], zero)
            upstream = jnp.where(here, datt[:, lanes], zero)
            weights = probs[2 * pair + side]
            grad = rows_dot(upstream, values)
            total = jnp.sum(weights * grad, axis=-1, keepdims=True)
            dscores = weights * (grad - total)
            dq_parts.append(flat_dot(dscores.astype(BF), keys))
            one = flat_dot(dscores.T.astype(BF), queries)
            two = flat_dot(weights.T.astype(BF), upstream)
            key_grad = one if key_grad is None else key_grad + one
            value_grad = two if value_grad is None else value_grad + two
        dq_buf[0, :, lanes] = (jnp.where(low, dq_parts[0], dq_parts[1]) * scale).astype(BF)
        key_grad = key_grad * scale
        back[:, lanes] = key_grad[: reach * rows].astype(BF)
        back[:, value_lanes] = value_grad[: reach * rows].astype(BF)
        dkv[:, lanes] = key_grad[reach * rows :]
        dkv[:, value_lanes] = value_grad[reach * rows :]

    def behind(distance, peer):
        return push(
            back.at[pl.ds((reach - distance) * rows, rows)],
            back_land.at[distance - 1],
            bk_send.at[distance - 1],
            bk_recv.at[distance - 1],
            (section, peer),
        )

    def to_place(place):
        distance = lax.rem(within - place + layer, layer)
        return push(
            back.at[pl.ds((reach - distance) * rows, rows)],
            back_land.at[within],
            bk_send.at[place],
            bk_recv.at[within],
            (section, level * layer + place),
        )

    def came_from(place):
        push(
            back_land.at[place],
            back_land.at[place],
            bk_send.at[place],
            bk_recv.at[place],
            sibling,
        ).wait_recv()

    def down():
        return push(
            back.at[pl.ds(0, rows)],
            down_land,
            bk_send.at[reach],
            bk_recv.at[reach],
            (section, chip - layer),
        )

    if plan.layered:
        for place in range(layer - 1, -1, -1):

            @pl.when(jnp.logical_and(place > within, level > 0))
            def _():
                to_place(place).start()

        for place in range(layer):

            @pl.when(place < within)
            def _():
                to_place(place).start()

    else:
        for distance in range(1, reach + 1):

            @pl.when(chip >= distance)
            def _():
                behind(distance, chip - distance).start()

    if plan.late:
        scatter.begin()
    if plan.layered:
        for place in range(layer - 1):

            @pl.when(jnp.logical_and(place < within, level > 0))
            def _():
                came_from(place)
                below = back[:rows, :].astype(F32) + back_land[place].astype(F32)
                back[:rows, :] = below.astype(BF)

        @pl.when(level > 0)
        def _():
            down().start()

        for place in range(1, layer):

            @pl.when(place > within)
            def _():
                came_from(place)
                dkv[...] += back_land[place].astype(F32)

        @pl.when(level < plan.depth - 1)
        def _():
            down().wait_recv()
            dkv[...] += down_land[...].astype(F32)

    else:
        for distance in range(1, reach + 1):

            @pl.when(chip + distance < chips)
            def _():
                behind(distance, chip).wait_recv()
                dkv[...] += back_land[distance - 1].astype(F32)

    dq_buf[1] = dkv[:, :width].astype(BF)
    dq_buf[2] = dkv[:, width:].astype(BF)
    turned = inputs.astype(F32).T.astype(BF)
    dnormed = None
    for part in range(3):
        term = rows_dot(dq_buf[part], w_proj[part * width : (part + 1) * width])
        dnormed = term if dnormed is None else dnormed + term
    dpassed, gain10 = norm_back(passed, factor10, gains_ref[2:3, :], dnormed)
    gain_ref[2:3, :] = gain10
    dpassed = (dmiddle + dpassed).astype(BF).astype(F32)

    if plan.late:
        scatter.stage(0)
    upstream0 = mask * dpassed
    give[5] = upstream0.astype(BF)
    copy = push(give.at[5], take.at[5], send.at[5], recv.at[5], sibling)
    copy.start()
    for part in range(3):
        proj_all[part * width : (part + 1) * width, :] = flat_dot(turned, dq_buf[part]).astype(BF)
    copy.wait()
    crossing = [
        push(
            whole.at[pl.ds(pl.multiple_of(size * (1 - section), 16), size), :],
            land,
            a_send.at[2 + i],
            a_recv.at[2 + i],
            sibling,
        )
        for i, (whole, land, size) in enumerate(
            ((proj_all, proj_take, split), (attn_all, attn_take, cut))
        )
    ]
    for cross in crossing:
        cross.start()
    if plan.late:
        scatter.stage(1)
    both = jnp.concatenate([give[5], take[5]], 0)
    dnormed = feed_back(0, pair0, layer0, (gate0_g, up0_g, down0_g), both, 6)
    if plan.late:
        for number in range(2, plan.depth + 1):
            scatter.stage(number)
    middle0 = dmid_ref[...]
    dmiddle, gain01 = norm_back(middle0, factor0, gains_ref[1:2, :], dnormed)
    gain_ref[1:2, :] = gain01
    dmiddle = upstream0 + dmiddle
    dmid_ref[...] = dmiddle
    g_ref[...] = dmiddle.astype(BF)
    for cross in crossing:
        cross.wait()
    for whole, land, size, out in (
        (proj_all, proj_take, split, proj_g),
        (attn_all, attn_take, cut, attn_g),
    ):
        own_part = whole[pl.ds(pl.multiple_of(size * section, 16), size), :]
        out[...] = (own_part.astype(F32) + land[...].astype(F32)).astype(BF)
    if plan.late:
        scatter.end()

    for distance in range(1, reach + 1):

        @pl.when(goes_ahead(distance))
        def _():
            ahead(distance).wait_send()

    if plan.layered:
        for place in range(layer):

            @pl.when(jnp.logical_and(level > 0, place < within))
            def _():
                pass_on(place).wait_send()

            @pl.when((place < within) | ((place > within) & (level > 0)))
            def _():
                to_place(place).wait_send()

        @pl.when(level > 0)
        def _():
            down().wait_send()

    else:
        for distance in range(1, reach + 1):

            @pl.when(chip >= distance)
            def _():
                behind(distance, chip).wait_send()


def middle_call(plan, conv, hidden, gains, mask, upstream, pair, stored):
    rows, width = plan.rows, plan.width
    reach = WINDOW // rows
    ff = plan.ff // 2
    any_spec = pl.BlockSpec(memory_space=pl.ANY)
    vmem_spec = pl.BlockSpec(memory_space=pltpu.VMEM)
    dma = pltpu.SemaphoreType.DMA
    layer = [(width, ff), (width, ff), (ff, width)]
    grid = (plan.depth, plan.side, plan.side)
    chips = plan.chips
    spread = [grid + (a // chips, b) for a, b in layer]
    held = layer + [(3 * width, width), (width, width)] + (spread if plan.late else layer)
    split, cut = 3 * width // 2, width // 2
    extra = []
    if plan.late:
        extra = [pltpu.VMEM(w, BF) for w in spread]
        extra += Gather.semaphores(plan, 3) + Scatter.semaphores(plan, 3)
        extra += Scatter.scratch(plan, [w[3:] for w in spread])
    shapes = [
        ((rows, width), BF),
        ((rows, width), BF),
        ((rows, width), F32),
        ((8, width), F32),
    ]
    shapes += [(w, BF) for w in layer]
    shapes += [((plan.depth,) + w[3:] if plan.late else v, BF) for v, w in zip(layer, spread)]
    shapes += [((split, width), BF), ((cut, width), BF)]
    return pl.pallas_call(
        functools.partial(middle_kernel, plan),
        out_shape=[jax.ShapeDtypeStruct(s, d) for s, d in shapes],
        in_specs=[vmem_spec] * 6 + [any_spec] * 8,
        out_specs=[vmem_spec] * len(shapes),
        scratch_shapes=[pltpu.VMEM(w, BF) for w in held]
        + [
            pltpu.VMEM((2 * rows, width), BF),
            pltpu.VMEM((2 * rows, width), BF),
            pltpu.VMEM((SWAPS, rows, width), BF),
            pltpu.VMEM((SWAPS, rows, width), BF),
            pltpu.VMEM((2, 2 * rows, ff), F32),
            pltpu.VMEM((2, 2 * rows, ff), F32),
            pltpu.VMEM((2, 2 * rows, ff), BF),
            pltpu.VMEM((2 * rows, ff), BF),
            pltpu.VMEM((2 * rows, ff), BF),
            pltpu.VMEM(((reach + 1) * rows, 2 * width), BF),
            pltpu.VMEM((rows, width), BF),
            pltpu.VMEM((width // HEAD_DIM, rows, (reach + 1) * rows), F32),
            pltpu.VMEM((rows, 2 * width), F32),
            pltpu.VMEM((reach * rows, 2 * width), BF),
            pltpu.VMEM((reach, rows, 2 * width), BF),
            pltpu.VMEM((rows, 2 * width), BF),
            pltpu.VMEM((rows, width), F32),
            pltpu.VMEM((3, rows, width), BF),
            pltpu.VMEM((3 * width, width), BF),
            pltpu.VMEM((width, width), BF),
            pltpu.VMEM((split, width), BF),
            pltpu.VMEM((cut, width), BF),
            dma((8,)),
            dma((4,)),
            dma((4,)),
            dma((SWAPS,)),
            dma((SWAPS,)),
            dma((2 * reach,)),
            dma((reach,)),
            dma((reach + 1,)),
            dma((reach + 1,)),
        ]
        + extra,
        compiler_params=pltpu.CompilerParams(
            collective_id=5, has_side_effects=True, vmem_limit_bytes=VMEM_LIMIT
        ),
        name="middle",
    )(conv, hidden, gains, mask, upstream, pair, *stored)


def swapped(block):
    return lax.ppermute(block, "section", [(0, 1), (1, 0)])


def norm_backward(values, factor, weights, upstream):
    weighted = upstream * weights
    gain_grad = jnp.sum(upstream * values * factor, axis=0)
    correction = jnp.mean(weighted * values, axis=-1, keepdims=True)
    return (factor * weighted - values * factor * factor * factor * correction, gain_grad)


def body(
    io_pair, lengths, filters, stu_maps, attn_proj, attn_out, norm_gains, mlp_gate, mlp_up, mlp_down
):
    chips = lax.axis_size("seq")
    section, chip = spot()
    core_zero = section == 0
    tok_rows = io_pair.shape[2]
    width = io_pair.shape[3]
    half = tok_rows // 2
    ff = mlp_gate.shape[2]
    ff_half = mlp_down.shape[1] // 2
    plan = Plan(chips, tok_rows, width, filters.shape[1], stu_maps.shape[0], ff)

    def join_phases(rows):
        return rows.reshape(2, half, width).swapaxes(0, 1).reshape(rows.shape)

    my_a, my_b = plan.a_of(chip), plan.b_of(chip)
    my_group = chip // (plan.cols_out * plan.cols_in)
    if plan.routed:
        maps = [stu_maps]
    else:
        whole = lax.all_gather(stu_maps, ("section", "seq"), axis=0, tiled=True)
        whole = lax.dynamic_slice(
            whole.reshape(-1, width, width),
            (0, my_b * plan.jb, my_a * plan.ia),
            (whole.shape[0] // width, plan.jb, plan.ia),
        )
        pair = whole[: 2 * plan.filters].reshape(2, plan.filters, plan.jb, plan.ia)
        pair = lax.dynamic_slice_in_dim(pair, my_group * plan.local, plan.local, 1)
        taps = jnp.where(my_group == 0, whole[2 * plan.filters :], 0).astype(BF)
        maps = [
            jnp.where(core_zero, pair[0], pair[1]),
            jnp.where(core_zero, pair[1], pair[0]),
            taps.reshape(-1, plan.ia),
        ]

    gate, up = mlp_gate[0], mlp_up[0]
    if not plan.pick_here:
        gate, up = (
            jnp.transpose(w.reshape(w.shape[0], chips, 2, ff_half), (2, 0, 1, 3)).reshape(
                2, w.shape[0], ff // 2
            )
            for w in (gate, up)
        )
    results = forward_call(
        plan,
        io_pair[0],
        norm_gains[0],
        filters,
        lengths,
        [gate, up, mlp_down[0], attn_proj, attn_out],
        maps,
    )
    flat = 5 if plan.late else 8
    weights = [w.reshape(-1, w.shape[-1]) for w in results[:flat]] + list(results[flat:8])
    conv, hidden, upstream1, grad_pair, gains, mask_rows = results[8:14]
    v, pq, tapw, x_all, xs_all, filt = results[14:]
    block_out, g, middle0_grad, gain_sums, *grads = middle_call(
        plan,
        conv.reshape(tok_rows, width),
        hidden,
        gains,
        mask_rows,
        upstream1,
        grad_pair,
        weights,
    )
    mlp0_grads, half1, attn_grads = grads[:3], grads[3:6], grads[6:]
    gain01, gain10, gain11 = gain_sums[1], gain_sums[2], gain_sums[3]
    g = g.reshape(2, half, width)
    grid = (plan.depth, plan.side, plan.side)
    blocks0 = [w.reshape(grid + (w.shape[0] // chips, w.shape[1])) for w in mlp0_grads]
    blocks1 = [w.reshape(grid + (w.shape[0] // chips, w.shape[1])) for w in attn_grads]
    if plan.late:
        result, gate_out, up_out, down_out, proj_out, out_out, gain_tile, maps_out = backward_call(
            plan,
            g,
            filt,
            v,
            pq,
            tapw,
            x_all,
            xs_all,
            blocks0 + blocks1,
            [hidden, gains, mask_rows, middle0_grad, block_out, gain_sums, *half1],
        )
        cols = width // chips
        gain_out = lax.dynamic_slice(
            gain_tile, (2 * section, (chip % (LANES // cols)) * cols), (2, cols)
        )
        return (
            result[None],
            maps_out.astype(F32),
            proj_out,
            out_out,
            gain_out[None],
            gate_out[None],
            up_out[None],
            down_out[None],
        )
    results = backward_call(plan, g, filt, v, pq, tapw, x_all, xs_all, blocks0)
    half0, results = results[:3], results[3:]
    attn_sums = [
        lax.psum_scatter(
            w.reshape((chips,) + w.shape[3:]), "seq", scatter_dimension=0, tiled=False
        )
        for w in blocks1
    ]
    half1 = [
        lax.psum_scatter(
            w.reshape(chips, -1, w.shape[-1]), "seq", scatter_dimension=0, tiled=False
        )
        for w in half1
    ]
    signal_grad = results[0].reshape(tok_rows, width)
    piece, tap_piece = (r.astype(F32) for r in results[1:])
    full = jnp.zeros((2, plan.filters, width, width), F32)
    full = lax.dynamic_update_slice(
        full,
        piece[None],
        (section, my_group * plan.local, my_b * plan.jb, my_a * plan.ia),
    )
    tap_piece = jnp.where(core_zero & (my_group == 0), tap_piece, 0.0)
    tap_full = lax.dynamic_update_slice(
        jnp.zeros((ORDER, width, width), F32),
        tap_piece.reshape(ORDER, plan.jb, plan.ia),
        (0, my_b * plan.jb, my_a * plan.ia),
    )
    full = jnp.concatenate([full.reshape(-1, width), tap_full.reshape(-1, width)], 0)
    maps_grad = lax.psum_scatter(full, ("section", "seq"), scatter_dimension=0, tiled=True)
    spectral_factor = lax.rsqrt(jnp.mean(hidden * hidden, axis=-1, keepdims=True) + EPSILON)
    hidden_grad, gain00 = norm_backward(hidden, spectral_factor, gains[0], signal_grad)
    inputs_grad = (mask_rows * (middle0_grad + hidden_grad)).astype(BF)

    proj_out, out_out = (w.astype(F32) for w in attn_sums)
    outs = []
    for index in range(3):
        zero, one = half0[index].astype(BF), half1[index].astype(BF)
        keep = jnp.where(core_zero, zero, one)
        take = swapped(jnp.where(core_zero, one, zero))
        low = jnp.where(core_zero, keep, take).astype(F32)
        high = jnp.where(core_zero, take, keep).astype(F32)
        if index < 2:
            rows = low.shape[0]
            joined = jnp.stack(
                [low.reshape(rows, chips, ff_half), high.reshape(rows, chips, ff_half)], 2
            ).reshape(rows, ff)
        else:
            joined = jnp.concatenate([low, high], 0)
        outs.append(joined[None])

    gain_parts = jnp.stack([jnp.stack([gain00, gain01]), jnp.stack([gain10, gain11])])
    gain_cols = width // chips
    tiles = jnp.transpose(gain_parts.reshape(2, 2, chips, gain_cols), (0, 2, 1, 3))
    tiles = jnp.pad(
        tiles.reshape(2 * chips, 2, gain_cols), ((0, 0), (0, 6), (0, LANES - gain_cols))
    )
    done_in, done_out = join_phases(inputs_grad), join_phases(block_out)
    taken, landed = exit_call(chips, jnp.where(core_zero, done_out, done_in), tiles)
    first = jnp.where(core_zero, done_in, taken)
    second = jnp.where(core_zero, taken, done_out)
    result_pair = jnp.stack([first, second])[None]
    gain_out = jnp.sum(landed, axis=0)[None, :2, :gain_cols]
    return (result_pair, maps_grad, proj_out, out_out, gain_out, outs[0], outs[1], outs[2])


def solution(mesh):
    placed = (
        P("section", None, "seq", None),
        P(),
        P("seq", None),
        P(("section", "seq"), None),
        P(("section", "seq"), None),
        P(("section", "seq"), None),
        P("section", None, "seq"),
        P("section", "seq", None),
        P("section", "seq", None),
        P("section", "seq", None),
    )
    return jax.shard_map(
        body,
        mesh=mesh,
        in_specs=placed,
        out_specs=(
            P("section", None, "seq", None),
            P(("section", "seq"), None),
            P(("section", "seq"), None),
            P(("section", "seq"), None),
            P("section", None, "seq"),
            P("section", "seq", None),
            P("section", "seq", None),
            P("section", "seq", None),
        ),
        check_vma=False,
    )
```

```python
import functools
import math

import jax
import jax.numpy as jnp
from jax import lax
from jax.experimental import pallas as pl
from jax.experimental.pallas import tpu as pltpu
from jax.sharding import PartitionSpec as P

ORDER = 3
HEAD_DIM = 64
WINDOW = 512
EPSILON = 1e-05
BIG_NEGATIVE = -1e30
MESH = pl.DeviceIdType.MESH
BF = jnp.bfloat16
F32 = jnp.float32
LANES = 128
BLOCK = 256
PIECE = 16
VMEM_LIMIT = 63 * 1024 * 1024


class Plan:
    def __init__(self, chips, tok_rows, width, filter_count, map_rows, ff):
        self.chips = chips
        self.rows = tok_rows
        self.half = tok_rows // 2
        self.width = width
        self.filters = filter_count
        self.cols_in = 4
        self.cols_out = max(1, math.isqrt(chips // 4))
        self.groups = chips // (self.cols_in * self.cols_out)
        self.local = filter_count // self.groups
        self.length = chips * self.half
        self.blocks = self.length // BLOCK
        self.jb = width // self.cols_in
        self.ia = width // self.cols_out
        self.map_rows = map_rows
        self.routed = map_rows % PIECE == 0
        self.pieces = map_rows // PIECE
        self.f_rows = -(-self.local // 16) * 16
        self.batch = 4 if self.local % 4 == 0 else 2
        self.ff = ff
        self.pick_here = ff // chips == LANES
        self.late = self.pick_here and self.routed
        self.routed = self.late
        self.side = max(1, math.isqrt(chips // 4))
        self.depth = chips // (self.side * self.side)
        self.layer = self.side * self.side
        self.layered = self.layer * tok_rows == WINDOW

    def place(self, chip):
        return (
            chip // (self.side * self.side),
            lax.rem(chip // self.side, self.side),
            lax.rem(chip, self.side),
        )

    def a_of(self, chip):
        return lax.rem(chip // self.cols_in, self.cols_out)

    def b_of(self, chip):
        return lax.rem(chip, self.cols_in)

    def part_at(self, a, b, c):
        return b + self.cols_in * (a + self.cols_out * c)

    def chip_at(self, z, y, x):
        return (z * self.side + y) * self.side + x

    def routes(self, rows, index=0):
        if rows % (2 * PIECE) == 0:
            return [(0, rows // 2, True), (rows // 2, rows // 2, False)]
        return [(0, rows, index % 2 == 0)]


def spot():
    return lax.axis_index("section"), lax.axis_index("seq")


def greet_everyone(chips):
    section, chip = spot()
    me = section * chips + chip
    barrier = pltpu.get_barrier_semaphore()

    def one(step, carry):
        peer = lax.rem(me + step, 2 * chips)
        pl.semaphore_signal(
            barrier, inc=1, device_id=(peer // chips, lax.rem(peer, chips)), device_id_type=MESH
        )
        return carry

    lax.fori_loop(1, 2 * chips, one, 0)

    def wait():
        pl.semaphore_wait(barrier, 2 * chips - 1)

    return wait


def push(src, dst, send, recv, target):
    return pltpu.make_async_remote_copy(
        src_ref=src,
        dst_ref=dst,
        send_sem=send,
        recv_sem=recv,
        device_id=target,
        device_id_type=MESH,
    )


def bytes_of(ref, sem):
    pltpu.make_async_copy(ref, ref, sem).wait()


def rows_dot(left, right):
    return lax.dot_general(left, right, (((1,), (1,)), ((), ())), preferred_element_type=F32)


def cols_dot(left, right):
    return lax.dot_general(left, right, (((0,), (0,)), ((), ())), preferred_element_type=F32)


def flat_dot(left, right):
    return jnp.dot(left, right, preferred_element_type=F32)


class Flat:
    def __init__(self, ref):
        self.ref = ref
        self.split = len(ref.shape) == 5
        if self.split:
            depth, side, _, rows, _ = ref.shape
            self.plane = side * side * rows

    def columns(self, start, count):
        sl = slice(start, start + count)
        if self.split:
            return self.ref[:, :, :, :, sl].reshape(-1, count)
        return self.ref[:, sl]

    def rows(self, start, count):
        if self.split:
            sl = slice(start // self.plane, (start + count) // self.plane)
            return self.ref[sl].reshape(count, self.ref.shape[4])
        return self.ref[start : start + count, :]

    def all(self):
        return self.ref[...].reshape(-1, self.ref.shape[-1])

    def put_columns(self, start, value):
        sl = slice(start, start + value.shape[1])
        if self.split:
            shape = self.ref.shape[:4] + (value.shape[1],)
            self.ref[:, :, :, :, sl] = value.reshape(shape)
        else:
            self.ref[:, sl] = value

    def put_rows(self, start, value):
        count = value.shape[0]
        if self.split:
            sl = slice(start // self.plane, (start + count) // self.plane)
            self.ref[sl] = value.reshape((count // self.plane,) + self.ref.shape[1:])
        else:
            self.ref[start : start + count, :] = value


class Gather:
    def __init__(self, plan, shards, outs, send, recv):
        self.plan, self.shards, self.outs = plan, shards, outs
        self.send, self.recv = send, recv
        self.section, chip = spot()
        self.z, self.y, self.x = plan.place(chip)

    @staticmethod
    def semaphores(plan, count):
        return [
            pltpu.SemaphoreType.DMA((count, 5)),
            pltpu.SemaphoreType.DMA((count, 5 * plan.depth)),
        ]

    def to(self, z, y, x):
        return self.section, self.plan.chip_at(z, y, x)

    def across(self, step, along_x):
        side = self.plan.side
        if along_x:
            return self.to(self.z, self.y, lax.rem(self.x + step, side))
        return self.to(self.z, lax.rem(self.y + step, side), self.x)

    def routes(self, i):
        for number, (start, rows, x_first) in enumerate(self.plan.routes(self.outs[i].shape[3], i)):
            yield number, x_first, self.outs[i], pl.ds(start, rows)

    def level(self, t):
        return lax.rem(self.z - t + self.plan.depth, self.plan.depth)

    def begin(self):
        plan = self.plan
        for i, shard in enumerate(self.shards):
            home = self.outs[i].at[self.z, self.y, self.x]
            for step in range(1, plan.depth):
                z = lax.rem(self.z + step, plan.depth)
                push(
                    shard, home, self.send.at[i, 0], self.recv.at[i, step], self.to(z, self.y, self.x)
                ).start()
            pltpu.make_async_copy(shard, home, self.recv.at[i, 0]).start()
        self.second(0)

    def second(self, t):
        plan = self.plan
        for i, shard in enumerate(self.shards):
            z = self.level(t)
            if t > 0:
                bytes_of(self.outs[i].at[z, self.y, self.x], self.recv.at[i, t])
            for number, x_first, out, sl in self.routes(i):
                dst = out.at[z, self.y, self.x, sl]
                src = shard.at[sl] if t == 0 else dst
                for step in range(1, plan.side):
                    push(
                        src,
                        dst,
                        self.send.at[i, 1 + number],
                        self.recv.at[i, (1 + number) * plan.depth + t],
                        self.across(step, x_first),
                    ).start()

    def hand_over(self):
        plan, side = self.plan, self.plan.side
        for i, shard in enumerate(self.shards):
            pltpu.make_async_copy(
                shard, self.outs[i].at[self.z, self.y, self.x], self.recv.at[i, 0]
            ).wait()
            bytes_of(self.outs[i].at[pl.ds(0, plan.depth - 1), 0, 0], self.send.at[i, 0])
            for number, x_first, out, sl in self.routes(i):
                for t in range(plan.depth):
                    bytes_of(
                        out.at[0, 0, pl.ds(0, side - 1), sl],
                        self.recv.at[i, (1 + number) * plan.depth + t],
                    )
                bytes_of(out.at[:, 0, pl.ds(0, side - 1), sl], self.send.at[i, 1 + number])

    def held_parts(self, whole):
        for i, source in enumerate(whole):
            for number, x_first, out, sl in self.routes(i):
                if x_first:
                    yield source.at[:, self.y, :, sl], out.at[:, self.y, :, sl]
                else:
                    yield source.at[:, :, self.x, sl], out.at[:, :, self.x, sl]

    def last_only(self):
        plan, side = self.plan, self.plan.side
        for t in range(plan.depth):
            z = self.level(t)
            for i in range(len(self.shards)):
                for number, x_first, out, sl in self.routes(i):
                    src = out.at[z, self.y, :, sl] if x_first else out.at[z, :, self.x, sl]
                    for step in range(1, side):
                        push(
                            src,
                            src,
                            self.send.at[i, 3 + number],
                            self.recv.at[i, (3 + number) * plan.depth + t],
                            self.across(step, not x_first),
                        ).start()

    def third(self, t):
        plan, side = self.plan, self.plan.side
        for i, shard in enumerate(self.shards):
            z = self.level(t)
            if t == 0:
                pltpu.make_async_copy(
                    shard, self.outs[i].at[z, self.y, self.x], self.recv.at[i, 0]
                ).wait()
            for number, x_first, out, sl in self.routes(i):
                sem = self.recv.at[i, (1 + number) * plan.depth + t]
                if x_first:
                    bytes_of(out.at[z, self.y, pl.ds(0, side - 1), sl], sem)
                    src = out.at[z, self.y, :, sl]
                else:
                    bytes_of(out.at[z, pl.ds(0, side - 1), self.x, sl], sem)
                    src = out.at[z, :, self.x, sl]
                for step in range(1, side):
                    push(
                        src,
                        src,
                        self.send.at[i, 3 + number],
                        self.recv.at[i, (3 + number) * plan.depth + t],
                        self.across(step, not x_first),
                    ).start()

    def end(self, last_only=False):
        plan, side = self.plan, self.plan.side
        for i in range(len(self.shards)):
            if not last_only:
                bytes_of(self.outs[i].at[pl.ds(0, plan.depth - 1), 0, 0], self.send.at[i, 0])
            for number, x_first, out, sl in self.routes(i):
                if not last_only:
                    bytes_of(out.at[:, 0, pl.ds(0, side - 1), sl], self.send.at[i, 1 + number])
                for t in range(plan.depth):
                    bytes_of(
                        out.at[0, :, pl.ds(0, side - 1), sl],
                        self.recv.at[i, (3 + number) * plan.depth + t],
                    )
                bytes_of(out.at[:, :, pl.ds(0, side - 1), sl], self.send.at[i, 3 + number])

    def stage(self, number):
        if number > 0:
            self.third(number - 1)
        if 0 <= number < self.plan.depth - 1:
            self.second(number + 1)


class Scatter:
    @staticmethod
    def scratch(plan, shapes):
        refs = []
        for index, (rows, cols) in enumerate(shapes):
            for _, part, _ in plan.routes(rows, index):
                for lead in (
                    (plan.depth, plan.side - 1, plan.side),
                    (plan.depth, plan.side),
                    (plan.depth, plan.side - 1),
                    (plan.depth,),
                    (plan.depth - 1,),
                ):
                    refs.append(pltpu.VMEM(lead + (part, cols), BF))
        return refs

    @staticmethod
    def semaphores(plan, count):
        return [
            pltpu.SemaphoreType.DMA((count, 6)),
            pltpu.SemaphoreType.DMA((count, 4 * plan.depth + 2)),
        ]

    def __init__(self, plan, grads, outs, buffers, send, recv, lines_only=False):
        self.plan, self.grads, self.outs = plan, grads, outs
        self.lines_only = lines_only
        self.send, self.recv = send, recv
        self.section, chip = spot()
        self.z, self.y, self.x = plan.place(chip)
        self.work = []
        buffers = list(buffers)
        for i, grad in enumerate(grads):
            for number, (start, rows, x_first) in enumerate(plan.routes(grad.shape[3], i)):
                self.work.append((i, number, start, rows, x_first, buffers[:5]))
                buffers = buffers[5:]

    def to(self, z, y, x):
        return self.section, self.plan.chip_at(z, y, x)

    def level(self, t):
        return lax.rem(self.z + 1 + t, self.plan.depth)

    def begin(self, first=0, last=None):
        plan, side = self.plan, self.plan.side
        for t in range(first, plan.depth if last is None else last):
            z = self.level(t)
            for i, number, start, rows, x_first, (land, *_) in self.work:
                grad, sl = self.grads[i], pl.ds(start, rows)
                for step in range(1, side):
                    if x_first:
                        y = lax.rem(self.y + step, side)
                        src, peer = grad.at[z, y, :, sl], self.to(self.z, y, self.x)
                    else:
                        x = lax.rem(self.x + step, side)
                        src, peer = grad.at[z, :, x, sl], self.to(self.z, self.y, x)
                    push(
                        src,
                        land.at[t, step - 1],
                        self.send.at[i, number],
                        self.recv.at[i, number * plan.depth + t],
                        peer,
                    ).start()

    def second(self, t):
        plan, side = self.plan, self.plan.side
        z = self.level(t)
        for i, number, start, rows, x_first, (land, part, land2, *_) in self.work:
            grad = self.grads[i]
            bytes_of(land.at[t], self.recv.at[i, number * plan.depth + t])
            for j in range(side):
                y, x = (self.y, j) if x_first else (j, self.x)
                total = grad[z, y, x, start : start + rows, :].astype(F32)
                for step in range(side - 1):
                    total = total + land[t, step, j].astype(F32)
                part[t, j] = total.astype(BF)
            for step in range(1, side):
                if x_first:
                    j = lax.rem(self.x + step, side)
                    peer = self.to(self.z, self.y, j)
                else:
                    j = lax.rem(self.y + step, side)
                    peer = self.to(self.z, j, self.x)
                push(
                    part.at[t, j],
                    land2.at[t, step - 1],
                    self.send.at[i, 2 + number],
                    self.recv.at[i, (2 + number) * plan.depth + t],
                    peer,
                ).start()

    def third(self, t):
        plan, side = self.plan, self.plan.side
        for i, number, start, rows, x_first, (_, part, land2, line, land3) in self.work:
            bytes_of(land2.at[t], self.recv.at[i, (2 + number) * plan.depth + t])
            mine = self.x if x_first else self.y
            total = part[t, mine].astype(F32)
            for step in range(side - 1):
                total = total + land2[t, step].astype(F32)
            line[t] = total.astype(BF)
            if t < plan.depth - 1 and not self.lines_only:
                push(
                    line.at[t],
                    land3.at[t],
                    self.send.at[i, 4 + number],
                    self.recv.at[i, 4 * plan.depth + number],
                    self.to(self.level(t), self.y, self.x),
                ).start()

    def end(self):
        plan = self.plan
        for i, number, start, rows, x_first, (land, part, land2, line, land3) in self.work:
            if self.lines_only:
                self.outs[i][:, start : start + rows, :] = line[...]
                bytes_of(land, self.send.at[i, number])
                bytes_of(land2, self.send.at[i, 2 + number])
                continue
            bytes_of(land3, self.recv.at[i, 4 * plan.depth + number])
            total = line[plan.depth - 1].astype(F32)
            for step in range(plan.depth - 1):
                total = total + land3[step].astype(F32)
            self.outs[i][start : start + rows, :] = total
            bytes_of(land, self.send.at[i, number])
            bytes_of(land2, self.send.at[i, 2 + number])
            bytes_of(land3, self.send.at[i, 4 + number])

    def stage(self, number):
        if number < self.plan.depth:
            self.second(number)
        if number > 0:
            self.third(number - 1)


def exit_kernel(chips, give, tiles, take, land, send, recv, gain_send, gain_recv):
    section, chip = spot()
    me = section * chips + chip
    greet_everyone(chips)()
    swap = push(give, take, send, recv, (1 - section, chip))
    swap.start()

    def one(step, carry):
        peer = lax.rem(me + step, 2 * chips)
        push(
            tiles.at[peer],
            land.at[me],
            gain_send,
            gain_recv,
            (peer // chips, lax.rem(peer, chips)),
        ).start()
        return carry

    lax.fori_loop(1, 2 * chips, one, 0)
    pltpu.make_async_copy(tiles.at[me], land.at[me], gain_recv).start()
    bytes_of(land, gain_recv)
    bytes_of(land.at[pl.ds(0, 2 * chips - 1)], gain_send)
    swap.wait()


def exit_call(chips, give, tiles):
    any_spec = pl.BlockSpec(memory_space=pl.ANY)
    return pl.pallas_call(
        functools.partial(exit_kernel, chips),
        out_shape=[
            jax.ShapeDtypeStruct(give.shape, give.dtype),
            jax.ShapeDtypeStruct(tiles.shape, tiles.dtype),
        ],
        in_specs=[any_spec] * 2,
        out_specs=[any_spec] * 2,
        scratch_shapes=[
            pltpu.SemaphoreType.DMA,
            pltpu.SemaphoreType.DMA,
            pltpu.SemaphoreType.DMA,
            pltpu.SemaphoreType.DMA,
        ],
        compiler_params=pltpu.CompilerParams(collective_id=4, has_side_effects=True),
        name="leave",
    )(give, tiles)


def filter_rows(plan, land, table, first_row, backward):
    lane = lax.broadcasted_iota(jnp.int32, (plan.f_rows, LANES), 1)
    low = lane < plan.half
    total = plan.length // LANES
    for m in range(total):
        if backward:
            one, two = 2 * m, 2 * m + 1
        else:
            one, two = plan.chips - 1 - 2 * m, plan.chips - 2 - 2 * m
        left = land[one, first_row : first_row + plan.f_rows, :].astype(F32)
        right = land[two, first_row : first_row + plan.f_rows, :].astype(F32)
        even = jnp.where(low, left, pltpu.roll(right, plan.half, 1))
        odd = jnp.where(low, pltpu.roll(left, plan.half, 1), right)
        at = LANES * m + (BLOCK if backward else 0)
        table[0, :, at : at + LANES] = even
        table[1, :, at : at + LANES] = odd
    blank = jnp.zeros((plan.f_rows, BLOCK), F32)
    at = 0 if backward else plan.length
    for parity in range(2):
        table[parity, :, at : at + BLOCK] = blank


def build_strips(plan, table, strip, backward):
    span = plan.length + BLOCK
    shift = span - LANES if backward else span - (LANES - 1)
    part = 32

    def one(k, carry):
        for parity in range(2):
            row = table[parity, pl.ds(k, 1), :]
            for start in range(0, LANES, part):
                spread = jnp.broadcast_to(row, (part, span))
                rolled = pltpu.roll(
                    spread, (shift + start) % span, 1, stride=1, stride_axis=0
                ).astype(BF)
                strip[parity, k, LANES + start : LANES + start + part, :] = rolled[
                    :, : plan.length
                ]
                strip[parity, k, start : start + part, :] = rolled[
                    :, LANES : LANES + plan.length
                ]
        return carry

    lax.fori_loop(0, plan.local, one, 0)


def sizes(plan):
    size = plan.jb // PIECE
    while size:
        yield size
        size //= 2


def owner_pieces(plan, act):
    section, chip = spot()
    start = plan.pieces * (section * plan.chips + chip)
    per_block = plan.jb // PIECE

    def block(j, carry):
        number = start // per_block + j
        base = number * per_block
        low = jnp.maximum(start - base, 0)
        high = jnp.minimum(start + plan.pieces - base, per_block)
        count = jnp.maximum(high - low, 0)
        which = number // plan.cols_in
        b = lax.rem(number, plan.cols_in)
        sign = which // plan.filters
        full = lax.rem(which, plan.filters)
        group = full // plan.local
        k = lax.rem(full, plan.local)
        for size in sizes(plan):
            done = count // (2 * size) * (2 * size)
            here = lax.rem(count // size, 2) == 1
            source = base + low - start + done
            target = low + done

            @pl.when(jnp.logical_and(here, sign < 2))
            def _():
                for a in range(plan.cols_out):
                    to_chip = plan.part_at(a, b, group)
                    act(source, size, False, k, target, a, sign, to_chip)

            @pl.when(jnp.logical_and(here, sign >= 2))
            def _():
                for a in range(plan.cols_out):
                    for core in range(2):
                        to_chip = plan.part_at(a, b, plan.groups - 1)
                        act(source, size, True, full, target, a, core, to_chip)

        return carry

    lax.fori_loop(0, plan.pieces // per_block + 2, block, 0)


def forward_kernel(plan, *refs):
    io_ref, gain_ref, filters_ref, lengths_ref = refs[:4]
    gate_raw, up_raw, down_raw, proj_raw, attn_raw = refs[4:9]
    if plan.routed:
        maps_ref = refs[9]
        rest = refs[10:]
    else:
        mine_ref, other_ref, taps_ref = refs[9:12]
        rest = refs[12:]
    full_weights, rest = rest[:8], rest[8:]
    (
        conv_ref,
        hidden_ref,
        upstream_ref,
        pair_ref,
        gains_ref,
        mask_ref,
        v_ref,
        pq_ref,
        tapw_ref,
        x_ref,
        xs_ref,
        filt_ref,
        io_own,
        io_sib,
        gain_tile,
        gate_half,
        gate_shard,
        up_half,
        up_shard,
        down_shard,
        u_ref,
        f_ref,
        x_buf,
        xo_buf,
        xs_buf,
        xf_buf,
        f_land,
        table,
        strip,
        mine,
        other,
        taps,
        pq,
        acc,
        joined,
        y_buf,
        land,
        reduced,
        final,
        stage,
        io_sem,
        gain_send,
        gain_recv,
        s_send,
        s_recv,
        u_send,
        x_recv,
        f_send,
        f_recv,
        m_send,
        m_recv,
        t_recv,
        o_send,
        o_recv,
        c_send,
        c_recv,
        d_send,
        r_recv,
        v_sem,
        out_sem,
        w_send,
        w_recv,
    ) = rest
    chips, half, jb, ia, rows_here = plan.chips, plan.half, plan.jb, plan.ia, plan.rows
    section, chip = spot()
    dev = section * chips + chip
    sibling = (1 - section, chip)
    my_group = chip // (plan.cols_out * plan.cols_in)
    greeted = greet_everyone(chips)

    row = lax.broadcasted_iota(jnp.int32, (rows_here, rows_here), 0)
    col = lax.broadcasted_iota(jnp.int32, (rows_here, rows_here), 1)
    order = jnp.where(col == 2 * lax.rem(row, half) + row // half, 1.0, 0.0).astype(BF)
    for i in range(2):
        io_own[i] = flat_dot(order, io_ref[i]).astype(BF)
    cols = gain_ref.shape[1]
    gain_tile[0] = jnp.zeros((8, LANES), F32)
    gain_tile[0, 0:2, 0:cols] = gain_ref[...].astype(F32)
    if plan.pick_here:
        lane = lax.broadcasted_iota(jnp.int32, (gate_raw.shape[0], LANES), 1)
        low = lane < half
        for raw, halves, shard in ((gate_raw, gate_half, gate_shard), (up_raw, up_half, up_shard)):
            for j in range(raw.shape[1] // (2 * LANES)):
                one = raw[:, 2 * LANES * j : 2 * LANES * j + LANES].astype(F32)
                two = raw[:, 2 * LANES * j + LANES : 2 * LANES * (j + 1)].astype(F32)
                zero_half = jnp.where(low, one, pltpu.roll(two, half, 1)).astype(BF)
                one_half = jnp.where(low, pltpu.roll(one, half, 1), two).astype(BF)
                at = slice(LANES * j, LANES * (j + 1))
                shard[section, :, at] = jnp.where(section == 0, zero_half, one_half)
                halves[:, at] = jnp.where(section == 0, one_half, zero_half)
    else:
        for raw, halves, shard in ((gate_raw, gate_half, gate_shard), (up_raw, up_half, up_shard)):
            shard[section] = raw[section]
            halves[...] = raw[1 - section]
    part = down_shard.shape[1]
    down_shard[section] = down_raw[pl.ds(pl.multiple_of(part * section, 16), part), :]
    greeted()
    io_swap = push(io_own, io_sib, io_sem.at[0], io_sem.at[1], sibling)
    io_swap.start()

    gain_swap = push(gain_tile.at[0], gain_tile.at[1], gain_send, gain_recv, sibling)
    gain_swap.start()
    shares = [
        push(src, dst, s_send.at[i], s_recv.at[i], sibling)
        for i, (src, dst) in enumerate(
            (
                (gate_half, gate_shard.at[section]),
                (up_half, up_shard.at[section]),
                (
                    down_raw.at[pl.ds(pl.multiple_of(part * (1 - section), 16), part), :],
                    down_shard.at[section],
                ),
            )
        )
    ]
    for share in shares:
        share.start()

    if plan.routed:

        def places(source, size, tap, k, target, a):
            rows = size * PIECE
            src = maps_ref.at[pl.ds(PIECE * source, rows), pl.ds(a * ia, ia)]
            if tap:
                return src, taps.at[pl.ds(jb * k + PIECE * target, rows), :], t_recv
            return src, mine.at[k, pl.ds(PIECE * target, rows), :], m_recv

        def start_piece(source, size, tap, k, target, a, to_section, to_chip):
            src, dst, sem = places(source, size, tap, k, target, a)
            here = to_section * chips + to_chip == dev

            @pl.when(here)
            def _():
                pltpu.make_async_copy(src, dst, sem).start()

            @pl.when(jnp.logical_not(here))
            def _():
                push(src, dst, m_send, sem, (to_section, to_chip)).start()

        def drain_piece(source, size, tap, k, target, a, to_section, to_chip):
            src, dst, sem = places(source, size, tap, k, target, a)

            @pl.when(to_section * chips + to_chip != dev)
            def _():
                push(src, dst, m_send, sem, (to_section, to_chip)).wait_send()

        owner_pieces(plan, start_piece)

    lag = lax.broadcasted_iota(jnp.int32, (rows_here, LANES), 0)
    lane = lax.broadcasted_iota(jnp.int32, (rows_here, LANES), 1)
    stretch = lax.rem(lane, half)
    backwards = jnp.where(lag == 2 * (half - 1 - stretch) + lane // half, 1.0, 0.0).astype(BF)
    plain = jnp.where(lag == 2 * stretch + lane // half, 1.0, 0.0).astype(BF)
    gain_swap.wait_recv()
    core_zero = section == 0
    own_gain, sib_gain = gain_tile[0], gain_tile[1]
    gain_rows = jnp.concatenate(
        [jnp.where(core_zero, own_gain, sib_gain), jnp.where(core_zero, sib_gain, own_gain)], 0
    ).astype(BF)
    for group in range(plan.groups):
        source = lax.broadcasted_iota(jnp.int32, (plan.filters, plan.f_rows), 0)
        target = lax.broadcasted_iota(jnp.int32, (plan.filters, plan.f_rows), 1)
        chosen = jnp.where(
            (source == group * plan.local + target) & (target < plan.local), 1.0, 0.0
        ).astype(BF)
        some = flat_dot(filters_ref[...], chosen).astype(BF)
        f_ref[group, : plan.f_rows, :] = cols_dot(some, backwards).astype(BF)
        f_ref[group, plan.f_rows : 2 * plan.f_rows, :] = cols_dot(some, plain).astype(BF)
        f_ref[group, 2 * plan.f_rows :, :] = gain_rows

    def send_f(step, carry):
        peer = lax.rem(chip + step, chips)
        group = peer // (plan.cols_out * plan.cols_in)
        push(f_ref.at[group], f_land.at[chip], f_send, f_recv, (section, peer)).start()
        return carry

    lax.fori_loop(1, chips, send_f, 0)
    pltpu.make_async_copy(f_ref.at[my_group], f_land.at[chip], f_recv).start()
    for share in shares:
        share.wait_recv()
    second_layer = (gate_shard.at[1], up_shard.at[1], down_shard.at[1])
    parts = [
        (0, (gate_shard.at[0], up_shard.at[0], down_shard.at[0])),
        (3, (proj_raw, attn_raw)),
    ]
    parts.append((5, second_layer))
    groups = []
    for first, arrays in parts:
        last = first + len(arrays)
        groups.append(
            Gather(
                plan,
                arrays,
                full_weights[first:last],
                w_send.at[pl.ds(first, len(arrays))],
                w_recv.at[pl.ds(first, len(arrays))],
            )
        )
    layer0, attention, layer1 = groups
    layer0.begin()
    position = lax.broadcasted_iota(jnp.int32, (rows_here, 1), 0)
    position = chip * rows_here + 2 * lax.rem(position, half) + position // half
    length_own = jnp.where(section == 0, lengths_ref[0], lengths_ref[1])
    length_other = jnp.where(section == 0, lengths_ref[1], lengths_ref[0])
    mask = jnp.where(position < length_own, 1.0, 0.0)
    mask_other = jnp.where(position < length_other, 1.0, 0.0)
    mask_ref[...] = mask
    io_swap.wait()
    bytes_of(f_land, f_recv)
    pick_row = lax.broadcasted_iota(jnp.int32, (LANES, plan.width), 0)
    pick_col = lax.broadcasted_iota(jnp.int32, (LANES, plan.width), 1)
    repeat = jnp.where(pick_row == lax.rem(pick_col, cols), 1.0, 0.0).astype(BF)
    tile_row = lax.broadcasted_iota(jnp.int32, (chips * 16, plan.width), 0)
    tile_col = lax.broadcasted_iota(jnp.int32, (chips * 16, plan.width), 1)
    rows_all = f_land[:, 2 * plan.f_rows :, :].reshape(chips * 16, LANES)
    spread = jnp.where(
        tile_row // 16 == tile_col // cols, flat_dot(rows_all, repeat), 0.0
    ).astype(BF)
    gain_row = lax.broadcasted_iota(jnp.int32, (16, chips * 16), 0)
    gain_col = lax.broadcasted_iota(jnp.int32, (16, chips * 16), 1)
    gather_rows = jnp.where(lax.rem(gain_col, 16) == gain_row, 1.0, 0.0).astype(BF)
    gathered = flat_dot(gather_rows, spread)
    gains_ref[0:2, :] = gathered[0:2, :]
    gains_ref[2:4, :] = gathered[8:10, :]
    gains_ref[4:8, :] = jnp.zeros((4, plan.width), F32)
    hidden = jnp.where(core_zero, io_own[0], io_sib[1]).astype(F32) * mask
    hidden_ref[...] = hidden
    factor = lax.rsqrt(jnp.mean(hidden * hidden, axis=-1, keepdims=True) + EPSILON)
    u = (hidden * factor * gains_ref[0:1, :]).astype(BF)
    for b in range(plan.cols_in):
        u_ref[b, :, :jb] = u[:half, b * jb : (b + 1) * jb]
        u_ref[b, :, jb:] = u[half:, b * jb : (b + 1) * jb]

    def send_u(step, carry):
        peer = lax.rem(chip + step, chips)
        b = plan.b_of(peer)
        push(
            u_ref.at[b],
            x_buf.at[pl.ds(half * chip, half), :],
            u_send,
            x_recv,
            (section, peer),
        ).start()
        return carry

    lax.fori_loop(1, chips, send_u, 0)
    pltpu.make_async_copy(
        u_ref.at[plan.b_of(chip)],
        x_buf.at[pl.ds(half * chip, half), :],
        x_recv,
    ).start()
    for group in groups[1:]:
        group.begin()
    cot_own = jnp.where(core_zero, io_sib[0], io_own[1]).astype(F32) * mask
    cot_other = jnp.where(core_zero, io_sib[1], io_own[0]).astype(F32) * mask_other
    upstream_ref[...] = cot_own
    pair_ref[:rows_here, :] = cot_own.astype(BF)
    pair_ref[rows_here:, :] = cot_other.astype(BF)
    layer0.stage(0)
    filter_rows(plan, f_land, table, 0, False)
    build_strips(plan, table, strip, False)
    filt_out = pltpu.make_async_copy(f_land, filt_ref, out_sem.at[0])
    filt_out.start()

    if plan.routed:
        bytes_of(mine, m_recv)
        swap = push(mine, other, o_send, o_recv, (1 - section, chip))
        swap.start()

        @pl.when(my_group == plan.groups - 1)
        def _():
            bytes_of(taps, t_recv)

        @pl.when(my_group != plan.groups - 1)
        def _():
            taps[...] = jnp.zeros_like(taps)
    else:
        for src, dst in ((mine_ref, mine), (other_ref, other), (taps_ref, taps)):
            pltpu.sync_copy(src, dst)

    layer0.stage(1)
    bytes_of(x_buf, x_recv)
    x_out = pltpu.make_async_copy(x_buf, x_ref, out_sem.at[1])
    x_out.start()
    xf_buf[0:8, :] = jnp.zeros((8, 2 * jb), F32)
    for i in range(plan.blocks):
        rows = slice(BLOCK * i, BLOCK * (i + 1))
        xf_buf[8 + BLOCK * i : 8 + BLOCK * (i + 1), :] = x_buf[rows, :].astype(F32)
    for i in range(plan.blocks):
        rows = slice(BLOCK * i, BLOCK * (i + 1))
        moved = xf_buf[7 + BLOCK * i : 7 + BLOCK * (i + 1), :].astype(BF)
        xs_buf[rows, :] = moved
        xo_buf[rows, :jb] = x_buf[rows, :jb]
        xo_buf[rows, jb:] = moved[:, jb:]
    xs_out = pltpu.make_async_copy(xs_buf, xs_ref, out_sem.at[2])
    xs_out.start()

    if plan.routed:
        swap.wait()
    turn = (1 - 2 * section).astype(F32)

    def mix(k, carry):
        first = mine[k].astype(F32)
        second = other[k].astype(F32)
        pq[k, :jb, :] = (first + second).astype(BF)
        pq[k, jb:, :] = ((first - second) * turn).astype(BF)
        return carry

    lax.fori_loop(0, plan.local, mix, 0)
    pq_out = pltpu.make_async_copy(pq, pq_ref, out_sem.at[3])
    pq_out.start()
    taps_out = pltpu.make_async_copy(taps, tapw_ref, out_sem.at[4])
    taps_out.start()

    layer0.stage(2)
    attention.stage(0)
    batch = plan.batch
    my_b, level = plan.b_of(chip), chip // plan.cols_in

    def reduce_level(i):
        bytes_of(land.at[i], r_recv.at[i])
        total = y_buf[:, pl.ds(pl.multiple_of(BLOCK * i + half * my_b, half), half), :].astype(F32)
        for step_number in range(plan.cols_in - 1):
            total = total + land[i, step_number].astype(F32)
        reduced[i] = total.astype(BF)

        @pl.when(level == i)
        def _():
            final[i] = reduced[i]

        @pl.when(level != i)
        def _():
            push(
                reduced.at[i],
                final.at[level],
                d_send,
                c_recv,
                (section, i * plan.cols_in + my_b),
            ).start()

    for i in range(plan.blocks):
        if i == 1:
            layer0.stage(3)
            attention.stage(1)
        if i == 2:
            layer0.stage(4)
            attention.stage(2)
            layer1.second(1)
        if i == 3:
            attention.stage(3)
            attention.stage(4)
            layer1.second(2)
        rows = slice(BLOCK * i, BLOCK * (i + 1))
        depth = BLOCK * (i + 1)
        offset = plan.length - depth
        x_now = x_buf[rows, :]
        s_now = xs_buf[rows, :]
        acc[:BLOCK] = flat_dot(
            jnp.concatenate([x_now[:, :jb], s_now[:, jb:]], 1), taps[: 2 * jb, :]
        ) + flat_dot(s_now[:, :jb], taps[2 * jb :, :])
        acc[BLOCK:] = flat_dot(
            jnp.concatenate([x_now[:, jb:], x_now[:, :jb]], 1), taps[: 2 * jb, :]
        ) + flat_dot(s_now[:, jb:], taps[2 * jb :, :])

        def step(t, carry, i=i, depth=depth, offset=offset):
            count = plan.local // batch * i + t
            slot = lax.rem(count, 2)
            some = pl.ds(batch * t, batch)
            v_copy = pltpu.make_async_copy(
                stage.at[slot], v_ref.at[some, :, pl.ds(BLOCK * i, BLOCK), :], v_sem.at[slot]
            )
            even = flat_dot(
                strip[0, some, :, offset:].reshape(batch * BLOCK, depth), x_buf[:depth, :]
            ).astype(BF)
            odd = flat_dot(
                strip[1, some, :, offset:].reshape(batch * BLOCK, depth), xo_buf[:depth, :]
            ).astype(BF)
            if i == 0:
                pl.when(t >= 2)(v_copy.wait)
            else:
                v_copy.wait()
            for k in range(batch):
                here = slice(BLOCK * k, BLOCK * (k + 1))
                first = jnp.concatenate([even[here, :jb], odd[here, jb:]], 1)
                second = jnp.concatenate([even[here, jb:], odd[here, :jb]], 1)
                stage[slot, k, 0] = first
                stage[slot, k, 1] = second
                lanes = slice(2 * jb * k, 2 * jb * (k + 1))
                joined[:BLOCK, lanes] = first
                joined[BLOCK:, lanes] = second
            v_copy.start()
            acc[...] += flat_dot(joined[...], pq[some].reshape(batch * 2 * jb, ia))
            return carry

        lax.fori_loop(0, plan.local // batch, step, 0)
        y_buf[0, rows, :] = acc[:BLOCK].astype(BF)
        y_buf[1, rows, :] = acc[BLOCK:].astype(BF)

        if plan.layered:
            for step_number in range(1, plan.cols_in):
                peer = lax.rem(my_b + step_number, plan.cols_in)
                push(
                    y_buf.at[:, pl.ds(BLOCK * i + half * peer, half), :],
                    land.at[i, step_number - 1],
                    c_send,
                    r_recv.at[i],
                    (section, level * plan.cols_in + peer),
                ).start()
            if i > 0:
                reduce_level(i - 1)
            continue

        def give(r, carry, i=i):
            peer = BLOCK // half * i + r
            src = y_buf.at[:, pl.ds(half * peer, half), :]

            @pl.when(peer == chip)
            def _():
                pltpu.make_async_copy(src, land.at[chip], c_recv).start()

            @pl.when(peer != chip)
            def _():
                push(src, land.at[chip], c_send, c_recv, (section, peer)).start()

            return carry

        lax.fori_loop(0, BLOCK // half, give, 0)

    layer1.second(3)
    if not plan.late:
        for number in range(plan.depth):
            layer1.third(number)
    for slot in range(2):
        pltpu.make_async_copy(
            stage.at[slot], v_ref.at[pl.ds(0, batch), :, pl.ds(0, BLOCK), :], v_sem.at[slot]
        ).wait()
    bytes_of(x_buf.at[pl.ds(0, half * (chips - 1)), :], u_send)
    bytes_of(f_land.at[pl.ds(0, chips - 1)], f_send)
    if plan.routed:
        owner_pieces(plan, drain_piece)
    for copy in (filt_out, x_out, xs_out, pq_out, taps_out):
        copy.wait()
    if plan.layered:
        reduce_level(plan.blocks - 1)
        bytes_of(final.at[pl.ds(0, plan.blocks - 1)], c_recv)
    else:
        bytes_of(land, c_recv)
    for a in range(plan.cols_out):
        total = None
        for c in range(plan.groups):
            if plan.layered:
                terms = [final[a + plan.cols_out * c]]
            else:
                terms = [land[plan.part_at(a, b, c)] for b in range(plan.cols_in)]
            for term in terms:
                term = term.astype(F32)
                total = term if total is None else total + term
        conv_ref[:, :, a * ia : (a + 1) * ia] = total
    if plan.layered:
        bytes_of(land, c_send)
        bytes_of(final.at[pl.ds(0, plan.blocks - 1)], d_send)
    else:
        bytes_of(land.at[pl.ds(0, chips - 1)], c_send)
    for group in groups[:2]:
        group.end()
    if plan.late:
        layer1.hand_over()
    else:
        layer1.end()
    gain_swap.wait_send()
    for share in shares:
        share.wait_send()


def forward_call(plan, io, gain, filters, lengths, raw, maps):
    chips, half, jb, ia, rows = plan.chips, plan.half, plan.jb, plan.ia, plan.rows
    width = plan.width
    any_spec = pl.BlockSpec(memory_space=pl.ANY)
    vmem_spec = pl.BlockSpec(memory_space=pltpu.VMEM)
    smem_spec = pl.BlockSpec(memory_space=pltpu.SMEM)
    dma = pltpu.SemaphoreType.DMA
    down, proj, attn = raw[2].shape, raw[3].shape, raw[4].shape
    share = (raw[0].shape[-2], plan.ff // 2)
    down_share = (down[0] // 2, width)
    grid = (plan.depth, plan.side, plan.side)
    layer = [share, share, down_share]
    levels = plan.blocks if plan.layered else 1
    land_shape = (
        (levels, plan.cols_in - 1, 2, half, ia) if plan.layered else (chips, 2, half, ia)
    )
    gathered = [grid + w for w in layer + [proj, attn]]
    gathered += [grid + w for w in layer]
    shapes = [(w, BF) for w in gathered] + [
        ((2, half, width), F32),
        ((rows, width), F32),
        ((rows, width), F32),
        ((2 * rows, width), BF),
        ((8, width), F32),
        ((rows, 1), F32),
        ((plan.local, 2, plan.length, 2 * jb), BF),
        ((plan.local, 2 * jb, ia), BF),
        ((ORDER * jb, ia), BF),
        ((plan.length, 2 * jb), BF),
        ((plan.length, 2 * jb), BF),
        ((chips, 2 * plan.f_rows + 16, LANES), BF),
    ]
    return pl.pallas_call(
        functools.partial(forward_kernel, plan),
        out_shape=[jax.ShapeDtypeStruct(s, d) for s, d in shapes],
        in_specs=[vmem_spec] * 3
        + [smem_spec]
        + [vmem_spec] * 3
        + [any_spec] * 2
        + [vmem_spec if plan.routed else any_spec] * len(maps),
        out_specs=[any_spec] * 8 + [vmem_spec] * 6 + [any_spec] * 6,
        scratch_shapes=[
            pltpu.VMEM((2, rows, width), BF),
            pltpu.VMEM((2, rows, width), BF),
            pltpu.VMEM((2, 8, LANES), F32),
            pltpu.VMEM(share, BF),
            pltpu.VMEM((2,) + share, BF),
            pltpu.VMEM(share, BF),
            pltpu.VMEM((2,) + share, BF),
            pltpu.VMEM((2,) + down_share, BF),
            pltpu.VMEM((plan.cols_in, half, 2 * jb), BF),
            pltpu.VMEM((plan.groups, 2 * plan.f_rows + 16, LANES), BF),
            pltpu.VMEM((plan.length, 2 * jb), BF),
            pltpu.VMEM((plan.length, 2 * jb), BF),
            pltpu.VMEM((plan.length, 2 * jb), BF),
            pltpu.VMEM((plan.length + 8, 2 * jb), F32),
            pltpu.VMEM((chips, 2 * plan.f_rows + 16, LANES), BF),
            pltpu.VMEM((2, plan.f_rows, plan.length + BLOCK), F32),
            pltpu.VMEM((2, plan.local, BLOCK, plan.length), BF),
            pltpu.VMEM((plan.local, jb, ia), BF),
            pltpu.VMEM((plan.local, jb, ia), BF),
            pltpu.VMEM((ORDER * jb, ia), BF),
            pltpu.VMEM((plan.local, 2 * jb, ia), BF),
            pltpu.VMEM((2 * BLOCK, ia), F32),
            pltpu.VMEM((2 * BLOCK, plan.batch * 2 * jb), BF),
            pltpu.VMEM((2, plan.length, ia), BF),
            pltpu.VMEM(land_shape, BF),
            pltpu.VMEM((levels, 2, half, ia), BF),
            pltpu.VMEM((levels, 2, half, ia), BF),
            pltpu.VMEM((2, plan.batch, 2, BLOCK, 2 * jb), BF),
            dma((2,)),
            dma,
            dma,
            dma((3,)),
            dma((3,)),
        ]
        + [dma] * 12
        + [dma((levels,)), dma((2,)), dma((5,)), *Gather.semaphores(plan, 8)],
        compiler_params=pltpu.CompilerParams(
            collective_id=2, has_side_effects=True, vmem_limit_bytes=VMEM_LIMIT
        ),
        name="spectral_forward",
    )(io, gain, filters, lengths, *raw, *maps)


def backward_kernel(plan, number, *refs):
    g_ref, filt_ref, v_ref, pq, tapw, x_ref, xs_ref = refs[:7]
    grads, rest = refs[7 : 7 + number], refs[7 + number :]
    if plan.late:
        hidden_ref, gains_ref, mask_ref, dmid_ref, out_ref, gain_sums_ref, *lines = rest[:9]
        res_ref, gate_ref, up_ref, down_ref, proj_ref, attn_ref, gain_out, dmaps_ref = rest[9:17]
        du_ref, gain_buf, gain_land, give_res, *half_parts = rest[17:30]
        half0, crossing, arrived = half_parts[:3], half_parts[3:6], half_parts[6:9]
        e_send, e_recv, n_send, n_recv = rest[30:34]
        half1, line_land, (l_send, l_recv) = rest[34:37], rest[37:40], rest[40:42]
        rest = rest[42:]
        sums = [*half0, proj_ref, attn_ref]
    else:
        sums, rest = rest[:number], rest[number:]
        du_ref, dmap_ref, dtap_ref = rest[:3]
        rest = rest[3:]
    count = 5 * sum(len(plan.routes(grad.shape[3])) for grad in grads)
    scatter = Scatter(plan, grads, sums, rest[:count], *rest[count : count + 2])
    rest = rest[count + 2 :]
    (
        g_buf,
        gt_buf,
        table,
        strip,
        v_buf,
        z_even,
        z_odd,
        acc_even,
        acc_odd,
        kept,
        give_m,
        take_m,
        total_m,
        kept_t,
        give_t,
        take_t,
        total_t,
        du_buf,
        land,
        g_send,
        g_recv,
        v_sem,
        m_send,
        m_recv,
        t_send,
        t_recv,
        w_send,
        w_recv,
        d_send,
        d_recv,
        x_sem,
        z_send,
        z_recv,
    ) = rest
    chips, half, jb, ia = plan.chips, plan.half, plan.jb, plan.ia
    section, chip = spot()
    dev = section * chips + chip
    my_a, my_b = plan.a_of(chip), plan.b_of(chip)
    my_group = chip // (plan.cols_out * plan.cols_in)
    sibling = (1 - section, chip)
    greet_everyone(chips)()

    def send_g(step, carry):
        peer = lax.rem(chip + step, chips)
        a = plan.a_of(peer)
        push(
            g_ref.at[:, :, pl.ds(pl.multiple_of(a * ia, ia), ia)],
            g_buf.at[:, pl.ds(half * chip, half), :],
            g_send,
            g_recv,
            (section, peer),
        ).start()
        return carry

    own_g = g_ref.at[:, :, pl.ds(pl.multiple_of(my_a * ia, ia), ia)]
    level, levels = chip // plan.cols_in, chips // plan.cols_in

    def g_rows(t):
        source = lax.rem(level - t + levels, levels) * plan.cols_in + my_b
        return g_buf.at[:, pl.ds(pl.multiple_of(half * source, half), half), :]

    def spread_g(t):
        if t > 0:
            bytes_of(g_rows(t), z_recv.at[t])
        for step_number in range(1, plan.cols_in):
            peer = lax.rem(my_b + step_number, plan.cols_in)
            push(
                own_g if t == 0 else g_rows(t),
                g_rows(t),
                g_send,
                g_recv,
                (section, level * plan.cols_in + peer),
            ).start()

    if plan.layered:
        for t in range(1, levels):
            to_level = lax.rem(level + t, levels)
            to_a = lax.rem(to_level, plan.cols_out)
            push(
                g_ref.at[:, :, pl.ds(pl.multiple_of(to_a * ia, ia), ia)],
                g_rows(0),
                z_send,
                z_recv.at[t],
                (section, to_level * plan.cols_in + my_b),
            ).start()
        spread_g(0)
        pltpu.make_async_copy(own_g, g_rows(0), z_recv.at[0]).start()
    else:
        lax.fori_loop(1, chips, send_g, 0)
        pltpu.make_async_copy(
            own_g, g_buf.at[:, pl.ds(half * chip, half), :], g_recv
        ).start()
    v_copy = [pltpu.make_async_copy(v_ref.at[k], v_buf.at[k], v_sem.at[k]) for k in range(2)]
    for copy in v_copy:
        copy.start()
    x_copy = [
        pltpu.make_async_copy(src, dst, x_sem.at[i])
        for i, (src, dst) in enumerate(((x_ref, z_even), (xs_ref, z_odd)))
    ]
    for copy in x_copy:
        copy.start()
    if plan.late:
        z, y, x = plan.place(chip)
        for i in range(3):
            for t in range(plan.depth - 1):
                to = (section, plan.chip_at(lax.rem(z + 1 + t, plan.depth), y, x))
                push(
                    lines[i].at[t], line_land[i].at[t], l_send.at[i], l_recv.at[i], to
                ).start()
    scatter.begin(0, EARLY)
    filter_rows(plan, filt_ref, table, plan.f_rows, True)
    build_strips(plan, table, strip, True)
    if plan.layered:
        for t in range(1, levels):
            spread_g(t)
    acc_even[...] = jnp.zeros_like(acc_even)
    acc_odd[...] = jnp.zeros_like(acc_odd)
    if plan.layered:
        pltpu.make_async_copy(own_g, g_rows(0), z_recv.at[0]).wait()
        bytes_of(g_buf.at[:, pl.ds(0, half * levels * (plan.cols_in - 1)), :], g_recv)
    else:
        bytes_of(g_buf, g_recv)
    scatter.begin(EARLY)
    for phase in range(2):
        for i in range(plan.blocks):
            rows = slice(BLOCK * i, BLOCK * (i + 1))
            gt_buf[phase, :, rows] = g_buf[phase, rows, :].astype(F32).T.astype(BF)
    turn = (1 - 2 * section).astype(F32)
    half_ways = (((1,), (1,)), ((), ()))

    def piece_copies(k, tap, begin):
        per_block = jb // PIECE
        which = 2 * plan.filters + k if tap else section * plan.filters + my_group * plan.local + k
        start = (which * plan.cols_in + my_b) * per_block
        owner, row = start // plan.pieces, lax.rem(start, plan.pieces)
        first = jnp.minimum(plan.pieces - row, per_block)
        for to, at, base, count in ((owner, row, 0, first), (owner + 1, 0, first, per_block - first)):
            for size in sizes(plan):
                done = count // (2 * size) * (2 * size)
                rows = size * PIECE
                here = lax.rem(count // size, 2) == 1
                source = PIECE * (base + done)
                src = (
                    total_t.at[pl.ds(jb * k + source, rows), :]
                    if tap
                    else total_m.at[k, pl.ds(source, rows), :]
                )
                dst = dmaps_ref.at[
                    pl.ds(PIECE * (at + done), rows), pl.ds(pl.multiple_of(my_a * ia, ia), ia)
                ]
                if begin:

                    @pl.when(jnp.logical_and(here, to == dev))
                    def _():
                        pltpu.make_async_copy(src, dst, w_recv).start()

                @pl.when(jnp.logical_and(here, to != dev))
                def _():
                    copy = push(src, dst, w_send, w_recv, (to // chips, lax.rem(to, chips)))
                    if begin:
                        copy.start()
                    else:
                        copy.wait_send()

    def exchange(k):
        return push(give_m.at[k], take_m.at[k], m_send.at[k], m_recv.at[k], (1 - section, chip))

    def finish(k):
        exchange(k).wait()
        total_m[k] = (kept[k] + take_m[k].astype(F32)).astype(BF)
        if plan.routed:
            piece_copies(k, False, True)

    for copy in x_copy:
        copy.wait()
    x_even, x_odd = z_even[:, :jb], z_even[:, jb:]
    s_even, s_odd = z_odd[:, :jb], z_odd[:, jb:]
    for tap, (on_even, on_odd) in enumerate(((x_even, x_odd), (s_odd, x_even), (s_even, s_odd))):
        tap_grad = jnp.dot(gt_buf[0], on_even, preferred_element_type=F32) + jnp.dot(
            gt_buf[1], on_odd, preferred_element_type=F32
        )
        tap_grad = tap_grad.T
        kept_t[tap * jb : (tap + 1) * jb, :] = tap_grad
        give_t[tap * jb : (tap + 1) * jb, :] = tap_grad.astype(BF)
    tap_swap = push(give_t, take_t, t_send, t_recv, (1 - section, chip))
    tap_swap.start()
    for i in range(plan.blocks):
        rows = slice(BLOCK * i, BLOCK * (i + 1))
        from_even = lax.dot_general(
            g_buf[0, rows, :], tapw[...], half_ways, preferred_element_type=F32
        )
        from_odd = lax.dot_general(
            g_buf[1, rows, :], tapw[...], half_ways, preferred_element_type=F32
        )
        acc_even[rows, :jb] = from_even[:, :jb] + from_odd[:, jb : 2 * jb]
        acc_even[rows, jb : 2 * jb] = from_odd[:, :jb]
        acc_odd[rows, :jb] = from_even[:, 2 * jb :]
        acc_odd[rows, jb : 2 * jb] = from_even[:, jb : 2 * jb] + from_odd[:, 2 * jb :]

    def step(k, carry):
        slot = lax.rem(k, 2)
        from_even = rows_dot(g_buf[0], pq[k]).astype(BF)
        from_odd = rows_dot(g_buf[1], pq[k]).astype(BF)
        z_even[:, :jb] = from_even[:, :jb]
        z_even[:, jb:] = from_odd[:, :jb]
        z_odd[:, :jb] = from_odd[:, jb:]
        z_odd[:, jb:] = from_even[:, jb:]
        pltpu.make_async_copy(v_ref.at[k], v_buf.at[slot], v_sem.at[slot]).wait()
        grad = jnp.dot(gt_buf[0], v_buf[slot, 0], preferred_element_type=F32) + jnp.dot(
            gt_buf[1], v_buf[slot, 1], preferred_element_type=F32
        )
        grad = grad.T
        plus, minus = grad[:jb, :], grad[jb:, :] * turn
        kept[k] = plus + minus
        give_m[k] = (plus - minus).astype(BF)
        exchange(k).start()

        @pl.when(k + 2 < plan.local)
        def _():
            pltpu.make_async_copy(v_ref.at[k + 2], v_buf.at[slot], v_sem.at[slot]).start()

        for j in range(plan.blocks):
            rows = slice(BLOCK * j, BLOCK * (j + 1))
            depth = plan.length - BLOCK * j
            acc_even[rows, :] += jnp.dot(
                strip[0, k, :, :depth], z_even[BLOCK * j :, :], preferred_element_type=F32
            )
            out = jnp.dot(
                strip[1, k, :, :depth], z_odd[BLOCK * j :, :], preferred_element_type=F32
            )
            acc_even[rows, :jb] += out[:, :jb]
            acc_odd[rows, jb:] += out[:, jb:]

        @pl.when(k >= 1)
        def _():
            finish(k - 1)

        for turn_number in range(plan.depth + 1):
            at = 1 + (turn_number * (plan.local - 2)) // plan.depth
            pl.when(k == at)(functools.partial(scatter.stage, turn_number))
        return carry

    lax.fori_loop(0, plan.local, step, 0)
    for i in range(plan.blocks):
        rows = slice(BLOCK * i, BLOCK * (i + 1))
        moved = acc_odd[BLOCK * i + 1 : BLOCK * (i + 1) + 1, :]
        both = (acc_even[rows, :] + moved).astype(BF)
        du_buf[0, rows, :] = both[:, :jb]
        du_buf[1, rows, :] = both[:, jb:]

        def give(r, carry, i=i):
            peer = BLOCK // half * i + r
            src = du_buf.at[:, pl.ds(half * peer, half), :]

            @pl.when(peer == chip)
            def _():
                pltpu.make_async_copy(src, land.at[chip], d_recv).start()

            @pl.when(peer != chip)
            def _():
                push(src, land.at[chip], d_send, d_recv, (section, peer)).start()

            return carry

        lax.fori_loop(0, BLOCK // half, give, 0)
    finish(plan.local - 1)
    tap_swap.wait()
    total_t[...] = (kept_t[...] + take_t[...].astype(F32)).astype(BF)
    if plan.routed:

        @pl.when(jnp.logical_and(section == 0, my_group == plan.groups - 1))
        def _():
            for tap in range(ORDER):
                piece_copies(tap, True, True)
    else:
        pltpu.sync_copy(total_m, dmap_ref)
        pltpu.sync_copy(total_t, dtap_ref)
    if plan.layered:
        bytes_of(g_buf.at[:, pl.ds(0, half * levels * (plan.cols_in - 1)), :], g_send)
        bytes_of(g_buf.at[:, pl.ds(0, half * (levels - 1)), :], z_send)
    else:
        bytes_of(g_buf.at[:, pl.ds(0, half * (chips - 1)), :], g_send)
    bytes_of(land, d_recv)
    for b in range(plan.cols_in):
        total = None
        for c in range(plan.groups):
            for a in range(plan.cols_out):
                term = land[plan.part_at(a, b, c)].astype(F32)
                total = term if total is None else total + term
        du_ref[:, :, b * jb : (b + 1) * jb] = total
    bytes_of(land.at[pl.ds(0, chips - 1)], d_send)
    scatter.end()
    if plan.late:
        core_zero = section == 0
        for i in range(3):
            bytes_of(line_land[i], l_recv.at[i])
            total = lines[i][plan.depth - 1].astype(F32)
            for t in range(plan.depth - 1):
                total = total + line_land[i][t].astype(F32)
            half1[i][...] = total
            bytes_of(line_land[i], l_send.at[i])
            crossing[i][...] = jnp.where(core_zero, half1[i][...], half0[i][...])
            push(crossing[i], arrived[i], e_send.at[i], e_recv.at[i], sibling).start()
        hidden = hidden_ref[...]
        factor = lax.rsqrt(jnp.mean(hidden * hidden, axis=-1, keepdims=True) + EPSILON)
        signal_grad = du_ref[...].reshape(plan.rows, plan.width)
        weighted = signal_grad * gains_ref[0:1, :]
        correction = jnp.mean(weighted * hidden, axis=-1, keepdims=True)
        hidden_grad = factor * weighted - hidden * factor * factor * factor * correction
        gain_buf[...] = gain_sums_ref[...]
        gain_buf[0:1, :] = jnp.sum(signal_grad * hidden * factor, axis=0, keepdims=True)
        per_tile = LANES * chips // plan.width

        def send_gain(step, carry):
            peer = lax.rem(dev + step, 2 * chips)
            tile = lax.rem(peer, chips) // per_tile
            push(
                gain_buf.at[:, pl.ds(pl.multiple_of(LANES * tile, LANES), LANES)],
                gain_land.at[dev],
                n_send,
                n_recv,
                (peer // chips, lax.rem(peer, chips)),
            ).start()
            return carry

        lax.fori_loop(1, 2 * chips, send_gain, 0)
        pltpu.make_async_copy(
            gain_buf.at[:, pl.ds(pl.multiple_of(LANES * (chip // per_tile), LANES), LANES)],
            gain_land.at[dev],
            n_recv,
        ).start()
        done_in = (mask_ref[...] * (dmid_ref[...] + hidden_grad)).astype(BF)
        row = lax.broadcasted_iota(jnp.int32, (plan.rows, plan.rows), 0)
        col = lax.broadcasted_iota(jnp.int32, (plan.rows, plan.rows), 1)
        order = jnp.where(col == 2 * lax.rem(row, half) + row // half, 1.0, 0.0).astype(BF)
        done_in = cols_dot(order, done_in).astype(BF)
        done_out = cols_dot(order, out_ref[...]).astype(BF)
        give_res[...] = jnp.where(core_zero, done_out, done_in)
        swap_res = push(give_res, res_ref.at[section], e_send.at[3], e_recv.at[3], sibling)
        swap_res.start()
        res_ref[section] = jnp.where(core_zero, done_in, done_out)
        for i in range(3):
            push(crossing[i], arrived[i], e_send.at[i], e_recv.at[i], sibling).wait()
        lane = lax.broadcasted_iota(jnp.int32, (gate_ref.shape[0], LANES), 1)
        low = lane < half
        kept_half = [jnp.where(core_zero, half0[i][...], half1[i][...]) for i in range(3)]
        for i, out in ((0, gate_ref), (1, up_ref)):
            came = arrived[i][...]
            first = jnp.where(core_zero, kept_half[i], came)
            second = jnp.where(core_zero, came, kept_half[i])
            for j in range(out.shape[1] // (2 * LANES)):
                one, two = (w[:, LANES * j : LANES * (j + 1)] for w in (first, second))
                at = 2 * LANES * j
                out[:, at : at + LANES] = jnp.where(low, one, pltpu.roll(two, half, 1))
                out[:, at + LANES : at + 2 * LANES] = jnp.where(
                    low, pltpu.roll(one, half, 1), two
                )
        part = half0[2].shape[0]
        came = arrived[2][...]
        down_ref[:part, :] = jnp.where(core_zero, kept_half[2], came)
        down_ref[part:, :] = jnp.where(core_zero, came, kept_half[2])
        swap_res.wait()
        bytes_of(gain_land, n_recv)
        gain_out[...] = jnp.sum(gain_land[...], axis=0)
        bytes_of(gain_land.at[pl.ds(0, 2 * chips - 1)], n_send)
    if plan.routed:

        def drain(k, carry):
            piece_copies(k, False, False)
            return carry

        lax.fori_loop(0, plan.local, drain, 0)

        @pl.when(jnp.logical_and(section == 0, my_group == plan.groups - 1))
        def _():
            for tap in range(ORDER):
                piece_copies(tap, True, False)

        bytes_of(dmaps_ref, w_recv)


def backward_call(plan, g, filt, v, pq, tapw, x, xs, grads, rest=()):
    chips, half, jb, ia = plan.chips, plan.half, plan.jb, plan.ia
    any_spec = pl.BlockSpec(memory_space=pl.ANY)
    vmem_spec = pl.BlockSpec(memory_space=pltpu.VMEM)
    dma = pltpu.SemaphoreType.DMA
    shapes = [g_part.shape[3:] for g_part in grads]
    rows, width = plan.rows, plan.width
    finish = []
    if plan.late:
        out_shape = [jax.ShapeDtypeStruct((2, rows, width), BF)]
        out_shape += [
            jax.ShapeDtypeStruct(shape, F32)
            for shape in (
                (shapes[0][0], plan.ff),
                (shapes[1][0], plan.ff),
                (2 * shapes[2][0], width),
                *shapes[3:],
                (8, LANES),
            )
        ]
        in_vmem = len(out_shape)
        out_shape.append(jax.ShapeDtypeStruct((plan.map_rows, width), BF))
        finish = [
            pltpu.VMEM((2, half, width), F32),
            pltpu.VMEM((8, width), F32),
            pltpu.VMEM((2 * chips, 8, LANES), F32),
            pltpu.VMEM((rows, width), BF),
        ]
        finish += [pltpu.VMEM(shape, F32) for shape in shapes[:3]] * 3
        finish += [dma((4,)), dma((4,)), dma, dma]
        finish += [pltpu.VMEM(shape, F32) for shape in shapes[:3]]
        finish += [pltpu.VMEM((plan.depth - 1,) + shape, BF) for shape in shapes[:3]]
        finish += [dma((3,)), dma((3,))]
    else:
        out_shape = [jax.ShapeDtypeStruct(shape, F32) for shape in shapes]
        out_shape.append(jax.ShapeDtypeStruct((2, half, width), F32))
        in_vmem = len(out_shape)
        out_shape.append(jax.ShapeDtypeStruct((plan.local, jb, ia), BF))
        out_shape.append(jax.ShapeDtypeStruct((ORDER * jb, ia), BF))
    return pl.pallas_call(
        functools.partial(backward_kernel, plan, len(grads)),
        out_shape=out_shape,
        in_specs=[vmem_spec, vmem_spec, any_spec, vmem_spec, vmem_spec, any_spec, any_spec]
        + [vmem_spec] * (len(grads) + len(rest)),
        out_specs=[vmem_spec] * in_vmem + [any_spec] * (len(out_shape) - in_vmem),
        scratch_shapes=finish
        + Scatter.scratch(plan, shapes)
        + Scatter.semaphores(plan, len(grads))
        + [
            pltpu.VMEM((2, plan.length, ia), BF),
            pltpu.VMEM((2, ia, plan.length), BF),
            pltpu.VMEM((2, plan.f_rows, plan.length + BLOCK), F32),
            pltpu.VMEM((2, plan.local, BLOCK, plan.length), BF),
            pltpu.VMEM((2, 2, plan.length, 2 * jb), BF),
            pltpu.VMEM((plan.length, 2 * jb), BF),
            pltpu.VMEM((plan.length, 2 * jb), BF),
            pltpu.VMEM((plan.length, 2 * jb), F32),
            pltpu.VMEM((plan.length + 8, 2 * jb), F32),
            pltpu.VMEM((plan.local, jb, ia), F32),
            pltpu.VMEM((plan.local, jb, ia), BF),
            pltpu.VMEM((plan.local, jb, ia), BF),
            pltpu.VMEM((plan.local, jb, ia), BF),
            pltpu.VMEM((ORDER * jb, ia), F32),
            pltpu.VMEM((ORDER * jb, ia), BF),
            pltpu.VMEM((ORDER * jb, ia), BF),
            pltpu.VMEM((ORDER * jb, ia), BF),
            pltpu.VMEM((2, plan.length, jb), BF),
            pltpu.VMEM((chips, 2, half, jb), BF),
            dma,
            dma,
            dma((2,)),
            dma((plan.local,)),
            dma((plan.local,)),
            dma,
            dma,
            dma,
            dma,
            dma,
            dma,
            dma((2,)),
            dma,
            dma((plan.depth,)),
        ],
        compiler_params=pltpu.CompilerParams(
            collective_id=3, has_side_effects=True, vmem_limit_bytes=VMEM_LIMIT
        ),
        name="spectral_backward",
    )(g, filt, v, pq, tapw, x, xs, *grads, *rest)

SWAPS = 7
EARLY = 1


def middle_kernel(plan, *refs):
    (
        conv_ref,
        hidden_ref,
        gains_ref,
        mask_ref,
        up_ref,
        up_pair,
        *stored,
    ) = refs[:14]
    (
        out_ref,
        g_ref,
        dmid_ref,
        gain_ref,
        gate0_g,
        up0_g,
        down0_g,
        gate1_g,
        up1_g,
        down1_g,
        proj_g,
        attn_g,
    ) = refs[14:26]
    held = refs[26:34]
    (
        pair0,
        pair1,
        give,
        take,
        gates,
        ups,
        acts,
        dgate,
        dup,
        window,
        kv,
        q_buf,
        probs,
        dkv,
        dn,
        back,
        back_land,
        down_land,
        att,
        dq_buf,
        proj_all,
        attn_all,
        proj_take,
        attn_take,
        load_sem,
        a_send,
        a_recv,
        send,
        recv,
        kv_send,
        kv_recv,
        bk_send,
        bk_recv,
        *extra,
    ) = refs[34:]
    chips, rows, width = plan.chips, plan.rows, plan.width
    section, chip = spot()
    sibling = (1 - section, chip)
    reach = WINDOW // rows
    span = (reach + 1) * rows
    layer0, (w_proj, w_out), layer1 = held[:3], held[3:5], held[5:]
    split, cut = 3 * plan.width // 2, plan.width // 2
    own_rows = [
        w_proj.at[pl.ds(pl.multiple_of(split * section, 16), split), :],
        w_out.at[pl.ds(pl.multiple_of(cut * section, 16), cut), :],
    ]
    homes = list(layer0) + own_rows + ([] if plan.late else list(layer1))
    loads = [
        pltpu.make_async_copy(a, b, load_sem.at[i]) for i, (a, b) in enumerate(zip(stored, homes))
    ]
    if plan.late:
        grads1, gather_send, gather_recv, scatter_send, scatter_recv = extra[:3], *extra[3:7]
        gather = Gather(plan, layer1, layer1, gather_send, gather_recv)
        held_loads = [
            pltpu.make_async_copy(src, dst, gather_recv.at[i // 2, i % 2])
            for i, (src, dst) in enumerate(gather.held_parts(stored[5:]))
        ]
        for load in held_loads:
            load.start()
    for load in loads:
        load.start()
    greet_everyone(chips)()
    passes = [
        push(stored[3 + i], own_rows[i], a_send.at[i], a_recv.at[i], sibling) for i in range(2)
    ]
    for copy in passes:
        copy.start()
    if plan.late:
        scatter = Scatter(
            plan, grads1, (gate1_g, up1_g, down1_g), extra[7:], scatter_send, scatter_recv, True
        )
        for load in held_loads:
            load.wait()
        gather.last_only()
    ff = plan.ff // 2
    own = slice(0, rows)
    second = slice(rows, 2 * rows)
    mask = mask_ref[...]

    def swap(number, src, dst):
        copy = push(src, dst, send.at[number], recv.at[number], sibling)
        copy.start()
        copy.wait()

    def norm(values, gain):
        factor = lax.rsqrt(jnp.mean(values * values, axis=-1, keepdims=True) + EPSILON)
        return values * factor * gain, factor

    def norm_back(values, factor, gain, upstream):
        weighted = upstream * gain
        gain_grad = jnp.sum(upstream * values * factor, axis=0, keepdims=True)
        correction = jnp.mean(weighted * values, axis=-1, keepdims=True)
        return factor * weighted - values * factor * factor * factor * correction, gain_grad

    def feed(layer, pair, weights, number):
        w_gate, w_up, w_down = (Flat(w) for w in weights)
        swap(number, pair.at[own], pair.at[second])
        for start in range(0, ff, BLOCK):
            cols = slice(start, start + BLOCK)
            gate_rows = flat_dot(pair[...], w_gate.columns(start, BLOCK))
            up_rows = flat_dot(pair[...], w_up.columns(start, BLOCK))
            gates[layer, :, cols] = gate_rows
            ups[layer, :, cols] = up_rows
            acts[layer, :, cols] = (gate_rows * jax.nn.sigmoid(gate_rows) * up_rows).astype(BF)
        part = flat_dot(acts[layer], w_down.all())
        give[number] = part[second].astype(BF)
        swap(number + 1, give.at[number], take.at[number])
        return part[own] + take[number].astype(F32)

    def feed_back(layer, pair, weights, grads, upstream_pair, number):
        w_gate, w_up, w_down = (Flat(w) for w in weights)
        gate_g, up_g, down_g = (Flat(w) for w in grads)
        turned = pair[...].astype(F32).T.astype(BF)
        for start in range(0, ff, BLOCK):
            cols = slice(start, start + BLOCK)
            active_grad = rows_dot(upstream_pair, w_down.rows(start, BLOCK))
            gate_rows, up_rows = gates[layer, :, cols], ups[layer, :, cols]
            sigmoid = jax.nn.sigmoid(gate_rows)
            slope = sigmoid * (1.0 + gate_rows * (1.0 - sigmoid))
            gate_grad = (active_grad * up_rows * slope).astype(BF)
            up_grad = (active_grad * gate_rows * sigmoid).astype(BF)
            dgate[:, cols] = gate_grad
            dup[:, cols] = up_grad
        for start in range(0, width, BLOCK):
            cols = slice(start, start + BLOCK)
            part = rows_dot(dgate[...], w_gate.rows(start, BLOCK)) + rows_dot(
                dup[...], w_up.rows(start, BLOCK)
            )
            give[number, :, cols] = part[second].astype(BF)
            att[:, cols] = part[own]
        copy = push(
            give.at[number], take.at[number], send.at[number], recv.at[number], sibling
        )
        copy.start()
        for start in range(0, ff, BLOCK):
            cols = slice(start, start + BLOCK)
            gate_g.put_columns(start, flat_dot(turned, dgate[:, cols]).astype(BF))
            up_g.put_columns(start, flat_dot(turned, dup[:, cols]).astype(BF))
            down_g.put_rows(
                start,
                flat_dot(acts[layer, :, cols].astype(F32).T.astype(BF), upstream_pair).astype(BF),
            )
        copy.wait()
        return att[...] + take[number].astype(F32)

    middle0 = hidden_ref[...] + conv_ref[...]
    normed, factor0 = norm(middle0, gains_ref[1:2, :])
    pair0[own] = normed.astype(BF)
    dmid_ref[...] = middle0
    for load in loads[:3]:
        load.wait()
    branch = feed(0, pair0, layer0, 0)
    passed = (mask * (dmid_ref[...] + branch)).astype(BF).astype(F32)

    normed, factor10 = norm(passed, gains_ref[2:3, :])
    inputs = normed.astype(BF)
    mine = slice(reach * rows, span)
    window[mine, :] = inputs

    layer, level = plan.layer, chip // plan.layer
    within = lax.rem(chip, layer)

    def slot(distance):
        return window.at[pl.ds((reach - distance) * rows, rows)]

    def ahead(distance):
        return push(
            window.at[mine],
            slot(distance),
            kv_send.at[distance - 1],
            kv_recv.at[distance - 1],
            (section, chip + distance),
        )

    def pass_on(place):
        distance = reach - (within - place)
        return push(
            slot(reach),
            slot(distance),
            kv_send.at[reach + place],
            kv_recv.at[distance - 1],
            (section, level * layer + place),
        )

    def goes_ahead(distance):
        if plan.layered and distance < reach:
            return within + distance < layer
        return chip + distance < chips

    def comes(distance):
        return chip >= distance

    for distance in range(reach, 0, -1):

        @pl.when(goes_ahead(distance))
        def _():
            ahead(distance).start()

        @pl.when(chip < distance)
        def _():
            window[(reach - distance) * rows : (reach - distance + 1) * rows, :] = jnp.zeros(
                (rows, width), BF
            )

    half = plan.half
    row = lax.broadcasted_iota(jnp.int32, (rows, span), 0)
    col = lax.broadcasted_iota(jnp.int32, (rows, span), 1)
    inner = lax.rem(col, rows)
    q_place = 2 * lax.rem(row, half) + row // half
    k_place = (col // rows - reach) * rows + 2 * lax.rem(inner, half) + inner // half
    distance_rows = q_place - k_place
    allowed = (
        (k_place + chip * rows >= 0) & (distance_rows >= 0) & (distance_rows < WINDOW)
    )
    lane = lax.broadcasted_iota(jnp.int32, (rows, LANES), 1)
    low = lane < HEAD_DIM
    scale = HEAD_DIM ** (-0.5)
    zero = jnp.zeros((rows, LANES), BF)
    for load in loads[3:5]:
        load.wait()
    for copy in passes:
        copy.wait()
    w_query, w_key, w_value = (w_proj.at[pl.ds(part * width, width)] for part in range(3))
    q_buf[...] = flat_dot(inputs, w_query[...]).astype(BF)
    kv[mine, :width] = flat_dot(inputs, w_key[...]).astype(BF)
    kv[mine, width:] = flat_dot(inputs, w_value[...]).astype(BF)

    def arrived(distance):
        push(
            window.at[mine],
            slot(distance),
            kv_send.at[distance - 1],
            kv_recv.at[distance - 1],
            sibling,
        ).wait_recv()

    pl.when(comes(reach))(functools.partial(arrived, reach))
    if plan.layered:
        for place in range(layer - 1):

            @pl.when(jnp.logical_and(level > 0, place < within))
            def _():
                pass_on(place).start()

    for distance in range(1, reach):
        pl.when(comes(distance))(functools.partial(arrived, distance))
    earlier = slice(0, reach * rows)
    kv[earlier, :width] = flat_dot(window[earlier, :], w_key[...]).astype(BF)
    kv[earlier, width:] = flat_dot(window[earlier, :], w_value[...]).astype(BF)

    for pair in range(width // LANES):
        lanes = slice(LANES * pair, LANES * (pair + 1))
        keys, values = kv[:, lanes], kv[:, width + LANES * pair : width + LANES * (pair + 1)]
        parts = []
        for side in range(2):
            here = low if side == 0 else jnp.logical_not(low)
            queries = jnp.where(here, q_buf[:, lanes], zero)
            scores = rows_dot(queries, keys) * scale
            scores = jnp.where(allowed, scores, BIG_NEGATIVE)
            weights = jnp.exp(scores - jnp.max(scores, axis=-1, keepdims=True))
            weights = weights / jnp.sum(weights, axis=-1, keepdims=True)
            probs[2 * pair + side] = weights
            parts.append(flat_dot(weights.astype(BF), values))
        att[:, lanes] = jnp.where(low, parts[0], parts[1])
    attended = att[...].astype(BF)
    middle1 = passed + flat_dot(attended, w_out[...])

    if plan.late:
        gather.end(True)
    for load in loads[5:]:
        load.wait()
    normed, factor11 = norm(middle1, gains_ref[3:4, :])
    pair1[own] = normed.astype(BF)
    branch = feed(1, pair1, layer1, 2)
    out_ref[...] = (mask * (middle1 + branch)).astype(BF)
    if not plan.late:
        grads1 = (gate1_g, up1_g, down1_g)
    dnormed = feed_back(1, pair1, layer1, grads1, up_pair[...], 4)
    dmiddle, gain11 = norm_back(middle1, factor11, gains_ref[3:4, :], dnormed)
    dmiddle = up_ref[...] + dmiddle
    gain_ref[3:4, :] = gain11

    dy = dmiddle.astype(BF)
    attn_all[...] = flat_dot(attended.astype(F32).T.astype(BF), dy).astype(BF)
    datt = rows_dot(dy, w_out[...]).astype(BF)
    for pair in range(width // LANES):
        lanes = slice(LANES * pair, LANES * (pair + 1))
        value_lanes = slice(width + LANES * pair, width + LANES * (pair + 1))
        keys, values = kv[:, lanes], kv[:, value_lanes]
        dq_parts, key_grad, value_grad = [], None, None
        for side in range(2):
            here = low if side == 0 else jnp.logical_not(low)
            queries = jnp.where(here, q_buf[:, lanes], zero)
            upstream = jnp.where(here, datt[:, lanes], zero)
            weights = probs[2 * pair + side]
            grad = rows_dot(upstream, values)
            total = jnp.sum(weights * grad, axis=-1, keepdims=True)
            dscores = weights * (grad - total)
            dq_parts.append(flat_dot(dscores.astype(BF), keys))
            one = flat_dot(dscores.T.astype(BF), queries)
            two = flat_dot(weights.T.astype(BF), upstream)
            key_grad = one if key_grad is None else key_grad + one
            value_grad = two if value_grad is None else value_grad + two
        dq_buf[:, lanes] = (jnp.where(low, dq_parts[0], dq_parts[1]) * scale).astype(BF)
        dkv[:, lanes] = (key_grad * scale).astype(BF)
        dkv[:, value_lanes] = value_grad.astype(BF)
    back[...] = (
        rows_dot(dkv[earlier, :width], w_key[...]) + rows_dot(dkv[earlier, width:], w_value[...])
    ).astype(BF)

    def behind(distance, peer):
        return push(
            back.at[pl.ds((reach - distance) * rows, rows)],
            back_land.at[distance - 1],
            bk_send.at[distance - 1],
            bk_recv.at[distance - 1],
            (section, peer),
        )

    def to_place(place):
        distance = lax.rem(within - place + layer, layer)
        return push(
            back.at[pl.ds((reach - distance) * rows, rows)],
            back_land.at[within],
            bk_send.at[place],
            bk_recv.at[within],
            (section, level * layer + place),
        )

    def came_from(place):
        push(
            back_land.at[place],
            back_land.at[place],
            bk_send.at[place],
            bk_recv.at[place],
            sibling,
        ).wait_recv()

    def down():
        return push(
            back.at[pl.ds(0, rows)],
            down_land,
            bk_send.at[reach],
            bk_recv.at[reach],
            (section, chip - layer),
        )

    if plan.layered:
        for place in range(layer - 1, -1, -1):

            @pl.when(jnp.logical_and(place > within, level > 0))
            def _():
                to_place(place).start()

        for place in range(layer):

            @pl.when(place < within)
            def _():
                to_place(place).start()

    else:
        for distance in range(1, reach + 1):

            @pl.when(chip >= distance)
            def _():
                behind(distance, chip - distance).start()

    if plan.late:
        scatter.begin()
    dn[...] = (
        rows_dot(dq_buf[...], w_query[...])
        + rows_dot(dkv[mine, :width], w_key[...])
        + rows_dot(dkv[mine, width:], w_value[...])
    )
    if plan.layered:
        for place in range(layer - 1):

            @pl.when(jnp.logical_and(place < within, level > 0))
            def _():
                came_from(place)
                below = back[:rows, :].astype(F32) + back_land[place].astype(F32)
                back[:rows, :] = below.astype(BF)

        @pl.when(level > 0)
        def _():
            down().start()

        for place in range(1, layer):

            @pl.when(place > within)
            def _():
                came_from(place)
                dn[...] += back_land[place].astype(F32)

        @pl.when(level < plan.depth - 1)
        def _():
            down().wait_recv()
            dn[...] += down_land[...].astype(F32)

    else:
        for distance in range(1, reach + 1):

            @pl.when(chip + distance < chips)
            def _():
                behind(distance, chip).wait_recv()
                dn[...] += back_land[distance - 1].astype(F32)

    dnormed = dn[...]
    dpassed, gain10 = norm_back(passed, factor10, gains_ref[2:3, :], dnormed)
    gain_ref[2:3, :] = gain10
    dpassed = (dmiddle + dpassed).astype(BF).astype(F32)

    if plan.late:
        scatter.stage(0)
    upstream0 = mask * dpassed
    give[5] = upstream0.astype(BF)
    copy = push(give.at[5], take.at[5], send.at[5], recv.at[5], sibling)
    copy.start()
    turned = window[...].astype(F32).T.astype(BF)
    proj_all[:width, :] = flat_dot(turned[:, reach * rows :], dq_buf[...]).astype(BF)
    proj_all[width : 2 * width, :] = flat_dot(turned, dkv[:, :width]).astype(BF)
    proj_all[2 * width :, :] = flat_dot(turned, dkv[:, width:]).astype(BF)
    copy.wait()
    crossing = [
        push(
            whole.at[pl.ds(pl.multiple_of(size * (1 - section), 16), size), :],
            land,
            a_send.at[2 + i],
            a_recv.at[2 + i],
            sibling,
        )
        for i, (whole, land, size) in enumerate(
            ((proj_all, proj_take, split), (attn_all, attn_take, cut))
        )
    ]
    for cross in crossing:
        cross.start()
    if plan.late:
        scatter.stage(1)
    both = jnp.concatenate([give[5], take[5]], 0)
    dnormed = feed_back(0, pair0, layer0, (gate0_g, up0_g, down0_g), both, 6)
    if plan.late:
        for number in range(2, plan.depth + 1):
            scatter.stage(number)
    middle0 = dmid_ref[...]
    dmiddle, gain01 = norm_back(middle0, factor0, gains_ref[1:2, :], dnormed)
    gain_ref[1:2, :] = gain01
    dmiddle = upstream0 + dmiddle
    dmid_ref[...] = dmiddle
    g_ref[...] = dmiddle.astype(BF)
    for cross in crossing:
        cross.wait()
    for whole, land, size, out in (
        (proj_all, proj_take, split, proj_g),
        (attn_all, attn_take, cut, attn_g),
    ):
        own_part = whole[pl.ds(pl.multiple_of(size * section, 16), size), :]
        out[...] = (own_part.astype(F32) + land[...].astype(F32)).astype(BF)
    if plan.late:
        scatter.end()

    for distance in range(1, reach + 1):

        @pl.when(goes_ahead(distance))
        def _():
            ahead(distance).wait_send()

    if plan.layered:
        for place in range(layer):

            @pl.when(jnp.logical_and(level > 0, place < within))
            def _():
                pass_on(place).wait_send()

            @pl.when((place < within) | ((place > within) & (level > 0)))
            def _():
                to_place(place).wait_send()

        @pl.when(level > 0)
        def _():
            down().wait_send()

    else:
        for distance in range(1, reach + 1):

            @pl.when(chip >= distance)
            def _():
                behind(distance, chip).wait_send()


def middle_call(plan, conv, hidden, gains, mask, upstream, pair, stored):
    rows, width = plan.rows, plan.width
    reach = WINDOW // rows
    ff = plan.ff // 2
    any_spec = pl.BlockSpec(memory_space=pl.ANY)
    vmem_spec = pl.BlockSpec(memory_space=pltpu.VMEM)
    dma = pltpu.SemaphoreType.DMA
    layer = [(width, ff), (width, ff), (ff, width)]
    grid = (plan.depth, plan.side, plan.side)
    chips = plan.chips
    spread = [grid + (a // chips, b) for a, b in layer]
    held = layer + [(3 * width, width), (width, width)] + (spread if plan.late else layer)
    split, cut = 3 * width // 2, width // 2
    extra = []
    if plan.late:
        extra = [pltpu.VMEM(w, BF) for w in spread]
        extra += Gather.semaphores(plan, 3) + Scatter.semaphores(plan, 3)
        extra += Scatter.scratch(plan, [w[3:] for w in spread])
    shapes = [
        ((rows, width), BF),
        ((rows, width), BF),
        ((rows, width), F32),
        ((8, width), F32),
    ]
    shapes += [(w, BF) for w in layer]
    shapes += [((plan.depth,) + w[3:] if plan.late else v, BF) for v, w in zip(layer, spread)]
    shapes += [((split, width), BF), ((cut, width), BF)]
    return pl.pallas_call(
        functools.partial(middle_kernel, plan),
        out_shape=[jax.ShapeDtypeStruct(s, d) for s, d in shapes],
        in_specs=[vmem_spec] * 6 + [any_spec] * 8,
        out_specs=[vmem_spec] * len(shapes),
        scratch_shapes=[pltpu.VMEM(w, BF) for w in held]
        + [
            pltpu.VMEM((2 * rows, width), BF),
            pltpu.VMEM((2 * rows, width), BF),
            pltpu.VMEM((SWAPS, rows, width), BF),
            pltpu.VMEM((SWAPS, rows, width), BF),
            pltpu.VMEM((2, 2 * rows, ff), F32),
            pltpu.VMEM((2, 2 * rows, ff), F32),
            pltpu.VMEM((2, 2 * rows, ff), BF),
            pltpu.VMEM((2 * rows, ff), BF),
            pltpu.VMEM((2 * rows, ff), BF),
            pltpu.VMEM(((reach + 1) * rows, width), BF),
            pltpu.VMEM(((reach + 1) * rows, 2 * width), BF),
            pltpu.VMEM((rows, width), BF),
            pltpu.VMEM((width // HEAD_DIM, rows, (reach + 1) * rows), F32),
            pltpu.VMEM(((reach + 1) * rows, 2 * width), BF),
            pltpu.VMEM((rows, width), F32),
            pltpu.VMEM((reach * rows, width), BF),
            pltpu.VMEM((reach, rows, width), BF),
            pltpu.VMEM((rows, width), BF),
            pltpu.VMEM((rows, width), F32),
            pltpu.VMEM((rows, width), BF),
            pltpu.VMEM((3 * width, width), BF),
            pltpu.VMEM((width, width), BF),
            pltpu.VMEM((split, width), BF),
            pltpu.VMEM((cut, width), BF),
            dma((8,)),
            dma((4,)),
            dma((4,)),
            dma((SWAPS,)),
            dma((SWAPS,)),
            dma((2 * reach,)),
            dma((reach,)),
            dma((reach + 1,)),
            dma((reach + 1,)),
        ]
        + extra,
        compiler_params=pltpu.CompilerParams(
            collective_id=5, has_side_effects=True, vmem_limit_bytes=VMEM_LIMIT
        ),
        name="middle",
    )(conv, hidden, gains, mask, upstream, pair, *stored)


def swapped(block):
    return lax.ppermute(block, "section", [(0, 1), (1, 0)])


def norm_backward(values, factor, weights, upstream):
    weighted = upstream * weights
    gain_grad = jnp.sum(upstream * values * factor, axis=0)
    correction = jnp.mean(weighted * values, axis=-1, keepdims=True)
    return (factor * weighted - values * factor * factor * factor * correction, gain_grad)


def body(
    io_pair, lengths, filters, stu_maps, attn_proj, attn_out, norm_gains, mlp_gate, mlp_up, mlp_down
):
    chips = lax.axis_size("seq")
    section, chip = spot()
    core_zero = section == 0
    tok_rows = io_pair.shape[2]
    width = io_pair.shape[3]
    half = tok_rows // 2
    ff = mlp_gate.shape[2]
    ff_half = mlp_down.shape[1] // 2
    plan = Plan(chips, tok_rows, width, filters.shape[1], stu_maps.shape[0], ff)

    def join_phases(rows):
        return rows.reshape(2, half, width).swapaxes(0, 1).reshape(rows.shape)

    my_a, my_b = plan.a_of(chip), plan.b_of(chip)
    my_group = chip // (plan.cols_out * plan.cols_in)
    if plan.routed:
        maps = [stu_maps]
    else:
        whole = lax.all_gather(stu_maps, ("section", "seq"), axis=0, tiled=True)
        whole = lax.dynamic_slice(
            whole.reshape(-1, width, width),
            (0, my_b * plan.jb, my_a * plan.ia),
            (whole.shape[0] // width, plan.jb, plan.ia),
        )
        pair = whole[: 2 * plan.filters].reshape(2, plan.filters, plan.jb, plan.ia)
        pair = lax.dynamic_slice_in_dim(pair, my_group * plan.local, plan.local, 1)
        taps = jnp.where(my_group == 0, whole[2 * plan.filters :], 0).astype(BF)
        maps = [
            jnp.where(core_zero, pair[0], pair[1]),
            jnp.where(core_zero, pair[1], pair[0]),
            taps.reshape(-1, plan.ia),
        ]

    gate, up = mlp_gate[0], mlp_up[0]
    if not plan.pick_here:
        gate, up = (
            jnp.transpose(w.reshape(w.shape[0], chips, 2, ff_half), (2, 0, 1, 3)).reshape(
                2, w.shape[0], ff // 2
            )
            for w in (gate, up)
        )
    results = forward_call(
        plan,
        io_pair[0],
        norm_gains[0],
        filters,
        lengths,
        [gate, up, mlp_down[0], attn_proj, attn_out],
        maps,
    )
    flat = 5 if plan.late else 8
    weights = [w.reshape(-1, w.shape[-1]) for w in results[:flat]] + list(results[flat:8])
    conv, hidden, upstream1, grad_pair, gains, mask_rows = results[8:14]
    v, pq, tapw, x_all, xs_all, filt = results[14:]
    block_out, g, middle0_grad, gain_sums, *grads = middle_call(
        plan,
        conv.reshape(tok_rows, width),
        hidden,
        gains,
        mask_rows,
        upstream1,
        grad_pair,
        weights,
    )
    mlp0_grads, half1, attn_grads = grads[:3], grads[3:6], grads[6:]
    gain01, gain10, gain11 = gain_sums[1], gain_sums[2], gain_sums[3]
    g = g.reshape(2, half, width)
    grid = (plan.depth, plan.side, plan.side)
    blocks0 = [w.reshape(grid + (w.shape[0] // chips, w.shape[1])) for w in mlp0_grads]
    blocks1 = [w.reshape(grid + (w.shape[0] // chips, w.shape[1])) for w in attn_grads]
    if plan.late:
        result, gate_out, up_out, down_out, proj_out, out_out, gain_tile, maps_out = backward_call(
            plan,
            g,
            filt,
            v,
            pq,
            tapw,
            x_all,
            xs_all,
            blocks0 + blocks1,
            [hidden, gains, mask_rows, middle0_grad, block_out, gain_sums, *half1],
        )
        cols = width // chips
        gain_out = lax.dynamic_slice(
            gain_tile, (2 * section, (chip % (LANES // cols)) * cols), (2, cols)
        )
        return (
            result[None],
            maps_out.astype(F32),
            proj_out,
            out_out,
            gain_out[None],
            gate_out[None],
            up_out[None],
            down_out[None],
        )
    results = backward_call(plan, g, filt, v, pq, tapw, x_all, xs_all, blocks0)
    half0, results = results[:3], results[3:]
    attn_sums = [
        lax.psum_scatter(
            w.reshape((chips,) + w.shape[3:]), "seq", scatter_dimension=0, tiled=False
        )
        for w in blocks1
    ]
    half1 = [
        lax.psum_scatter(
            w.reshape(chips, -1, w.shape[-1]), "seq", scatter_dimension=0, tiled=False
        )
        for w in half1
    ]
    signal_grad = results[0].reshape(tok_rows, width)
    piece, tap_piece = (r.astype(F32) for r in results[1:])
    full = jnp.zeros((2, plan.filters, width, width), F32)
    full = lax.dynamic_update_slice(
        full,
        piece[None],
        (section, my_group * plan.local, my_b * plan.jb, my_a * plan.ia),
    )
    tap_piece = jnp.where(core_zero & (my_group == 0), tap_piece, 0.0)
    tap_full = lax.dynamic_update_slice(
        jnp.zeros((ORDER, width, width), F32),
        tap_piece.reshape(ORDER, plan.jb, plan.ia),
        (0, my_b * plan.jb, my_a * plan.ia),
    )
    full = jnp.concatenate([full.reshape(-1, width), tap_full.reshape(-1, width)], 0)
    maps_grad = lax.psum_scatter(full, ("section", "seq"), scatter_dimension=0, tiled=True)
    spectral_factor = lax.rsqrt(jnp.mean(hidden * hidden, axis=-1, keepdims=True) + EPSILON)
    hidden_grad, gain00 = norm_backward(hidden, spectral_factor, gains[0], signal_grad)
    inputs_grad = (mask_rows * (middle0_grad + hidden_grad)).astype(BF)

    proj_out, out_out = (w.astype(F32) for w in attn_sums)
    outs = []
    for index in range(3):
        zero, one = half0[index].astype(BF), half1[index].astype(BF)
        keep = jnp.where(core_zero, zero, one)
        take = swapped(jnp.where(core_zero, one, zero))
        low = jnp.where(core_zero, keep, take).astype(F32)
        high = jnp.where(core_zero, take, keep).astype(F32)
        if index < 2:
            rows = low.shape[0]
            joined = jnp.stack(
                [low.reshape(rows, chips, ff_half), high.reshape(rows, chips, ff_half)], 2
            ).reshape(rows, ff)
        else:
            joined = jnp.concatenate([low, high], 0)
        outs.append(joined[None])

    gain_parts = jnp.stack([jnp.stack([gain00, gain01]), jnp.stack([gain10, gain11])])
    gain_cols = width // chips
    tiles = jnp.transpose(gain_parts.reshape(2, 2, chips, gain_cols), (0, 2, 1, 3))
    tiles = jnp.pad(
        tiles.reshape(2 * chips, 2, gain_cols), ((0, 0), (0, 6), (0, LANES - gain_cols))
    )
    done_in, done_out = join_phases(inputs_grad), join_phases(block_out)
    taken, landed = exit_call(chips, jnp.where(core_zero, done_out, done_in), tiles)
    first = jnp.where(core_zero, done_in, taken)
    second = jnp.where(core_zero, taken, done_out)
    result_pair = jnp.stack([first, second])[None]
    gain_out = jnp.sum(landed, axis=0)[None, :2, :gain_cols]
    return (result_pair, maps_grad, proj_out, out_out, gain_out, outs[0], outs[1], outs[2])


def solution(mesh):
    placed = (
        P("section", None, "seq", None),
        P(),
        P("seq", None),
        P(("section", "seq"), None),
        P(("section", "seq"), None),
        P(("section", "seq"), None),
        P("section", None, "seq"),
        P("section", "seq", None),
        P("section", "seq", None),
        P("section", "seq", None),
    )
    return jax.shard_map(
        body,
        mesh=mesh,
        in_specs=placed,
        out_specs=(
            P("section", None, "seq", None),
            P(("section", "seq"), None),
            P(("section", "seq"), None),
            P(("section", "seq"), None),
            P("section", None, "seq"),
            P("section", "seq", None),
            P("section", "seq", None),
            P("section", "seq", None),
        ),
        check_vma=False,
    )
```

```python
import functools
import math

import jax
import jax.numpy as jnp
from jax import lax
from jax.experimental import pallas as pl
from jax.experimental.pallas import tpu as pltpu
from jax.sharding import PartitionSpec as P

ORDER = 3
HEAD_DIM = 64
WINDOW = 512
EPSILON = 1e-05
BIG_NEGATIVE = -1e30
MESH = pl.DeviceIdType.MESH
BF = jnp.bfloat16
F32 = jnp.float32
LANES = 128
BLOCK = 256
PIECE = 16
VMEM_LIMIT = 63 * 1024 * 1024


class Plan:
    def __init__(self, chips, tok_rows, width, filter_count, map_rows, ff):
        self.chips = chips
        self.rows = tok_rows
        self.half = tok_rows // 2
        self.width = width
        self.filters = filter_count
        self.cols_in = 4
        self.cols_out = max(1, math.isqrt(chips // 4))
        self.groups = chips // (self.cols_in * self.cols_out)
        self.local = filter_count // self.groups
        self.length = chips * self.half
        self.blocks = self.length // BLOCK
        self.jb = width // self.cols_in
        self.ia = width // self.cols_out
        self.map_rows = map_rows
        self.routed = map_rows % PIECE == 0
        self.pieces = map_rows // PIECE
        self.f_rows = -(-self.local // 16) * 16
        self.batch = 4 if self.local % 4 == 0 else 2
        self.ff = ff
        self.pick_here = ff // chips == LANES
        self.late = self.pick_here and self.routed
        self.routed = self.late
        self.side = max(1, math.isqrt(chips // 4))
        self.depth = chips // (self.side * self.side)
        self.layer = self.side * self.side
        self.layered = self.layer * tok_rows == WINDOW

    def place(self, chip):
        return (
            chip // (self.side * self.side),
            lax.rem(chip // self.side, self.side),
            lax.rem(chip, self.side),
        )

    def a_of(self, chip):
        return lax.rem(chip // self.cols_in, self.cols_out)

    def b_of(self, chip):
        return lax.rem(chip, self.cols_in)

    def part_at(self, a, b, c):
        return b + self.cols_in * (a + self.cols_out * c)

    def chip_at(self, z, y, x):
        return (z * self.side + y) * self.side + x

    def routes(self, rows, index=0):
        if rows % (2 * PIECE) == 0:
            return [(0, rows // 2, True), (rows // 2, rows // 2, False)]
        return [(0, rows, index % 2 == 0)]


def spot():
    return lax.axis_index("section"), lax.axis_index("seq")


def greet_everyone(chips):
    section, chip = spot()
    me = section * chips + chip
    barrier = pltpu.get_barrier_semaphore()

    def one(step, carry):
        peer = lax.rem(me + step, 2 * chips)
        pl.semaphore_signal(
            barrier, inc=1, device_id=(peer // chips, lax.rem(peer, chips)), device_id_type=MESH
        )
        return carry

    lax.fori_loop(1, 2 * chips, one, 0)

    def wait():
        pl.semaphore_wait(barrier, 2 * chips - 1)

    return wait


def push(src, dst, send, recv, target):
    return pltpu.make_async_remote_copy(
        src_ref=src,
        dst_ref=dst,
        send_sem=send,
        recv_sem=recv,
        device_id=target,
        device_id_type=MESH,
    )


def bytes_of(ref, sem):
    pltpu.make_async_copy(ref, ref, sem).wait()


def rows_dot(left, right):
    return lax.dot_general(left, right, (((1,), (1,)), ((), ())), preferred_element_type=F32)


def cols_dot(left, right):
    return lax.dot_general(left, right, (((0,), (0,)), ((), ())), preferred_element_type=F32)


def flat_dot(left, right):
    return jnp.dot(left, right, preferred_element_type=F32)


class Flat:
    def __init__(self, ref):
        self.ref = ref
        self.split = len(ref.shape) == 5
        if self.split:
            depth, side, _, rows, _ = ref.shape
            self.plane = side * side * rows

    def columns(self, start, count):
        sl = slice(start, start + count)
        if self.split:
            return self.ref[:, :, :, :, sl].reshape(-1, count)
        return self.ref[:, sl]

    def rows(self, start, count):
        if self.split:
            sl = slice(start // self.plane, (start + count) // self.plane)
            return self.ref[sl].reshape(count, self.ref.shape[4])
        return self.ref[start : start + count, :]

    def all(self):
        return self.ref[...].reshape(-1, self.ref.shape[-1])

    def put_columns(self, start, value):
        sl = slice(start, start + value.shape[1])
        if self.split:
            shape = self.ref.shape[:4] + (value.shape[1],)
            self.ref[:, :, :, :, sl] = value.reshape(shape)
        else:
            self.ref[:, sl] = value

    def put_rows(self, start, value):
        count = value.shape[0]
        if self.split:
            sl = slice(start // self.plane, (start + count) // self.plane)
            self.ref[sl] = value.reshape((count // self.plane,) + self.ref.shape[1:])
        else:
            self.ref[start : start + count, :] = value


class Gather:
    def __init__(self, plan, shards, outs, send, recv):
        self.plan, self.shards, self.outs = plan, shards, outs
        self.send, self.recv = send, recv
        self.section, chip = spot()
        self.z, self.y, self.x = plan.place(chip)

    @staticmethod
    def semaphores(plan, count):
        return [
            pltpu.SemaphoreType.DMA((count, 5)),
            pltpu.SemaphoreType.DMA((count, 5 * plan.depth)),
        ]

    def to(self, z, y, x):
        return self.section, self.plan.chip_at(z, y, x)

    def across(self, step, along_x):
        side = self.plan.side
        if along_x:
            return self.to(self.z, self.y, lax.rem(self.x + step, side))
        return self.to(self.z, lax.rem(self.y + step, side), self.x)

    def routes(self, i):
        for number, (start, rows, x_first) in enumerate(self.plan.routes(self.outs[i].shape[3], i)):
            yield number, x_first, self.outs[i], pl.ds(start, rows)

    def level(self, t):
        return lax.rem(self.z - t + self.plan.depth, self.plan.depth)

    def begin(self):
        plan = self.plan
        for i, shard in enumerate(self.shards):
            home = self.outs[i].at[self.z, self.y, self.x]
            for step in range(1, plan.depth):
                z = lax.rem(self.z + step, plan.depth)
                push(
                    shard, home, self.send.at[i, 0], self.recv.at[i, step], self.to(z, self.y, self.x)
                ).start()
            pltpu.make_async_copy(shard, home, self.recv.at[i, 0]).start()
        self.second(0)

    def second(self, t):
        plan = self.plan
        for i, shard in enumerate(self.shards):
            z = self.level(t)
            if t > 0:
                bytes_of(self.outs[i].at[z, self.y, self.x], self.recv.at[i, t])
            for number, x_first, out, sl in self.routes(i):
                dst = out.at[z, self.y, self.x, sl]
                src = shard.at[sl] if t == 0 else dst
                for step in range(1, plan.side):
                    push(
                        src,
                        dst,
                        self.send.at[i, 1 + number],
                        self.recv.at[i, (1 + number) * plan.depth + t],
                        self.across(step, x_first),
                    ).start()

    def hand_over(self):
        plan, side = self.plan, self.plan.side
        for i, shard in enumerate(self.shards):
            pltpu.make_async_copy(
                shard, self.outs[i].at[self.z, self.y, self.x], self.recv.at[i, 0]
            ).wait()
            bytes_of(self.outs[i].at[pl.ds(0, plan.depth - 1), 0, 0], self.send.at[i, 0])
            for number, x_first, out, sl in self.routes(i):
                for t in range(plan.depth):
                    bytes_of(
                        out.at[0, 0, pl.ds(0, side - 1), sl],
                        self.recv.at[i, (1 + number) * plan.depth + t],
                    )
                bytes_of(out.at[:, 0, pl.ds(0, side - 1), sl], self.send.at[i, 1 + number])

    def held_parts(self, whole):
        for i, source in enumerate(whole):
            for number, x_first, out, sl in self.routes(i):
                if x_first:
                    yield source.at[:, self.y, :, sl], out.at[:, self.y, :, sl]
                else:
                    yield source.at[:, :, self.x, sl], out.at[:, :, self.x, sl]

    def last_only(self):
        plan, side = self.plan, self.plan.side
        for t in range(plan.depth):
            z = self.level(t)
            for i in range(len(self.shards)):
                for number, x_first, out, sl in self.routes(i):
                    src = out.at[z, self.y, :, sl] if x_first else out.at[z, :, self.x, sl]
                    for step in range(1, side):
                        push(
                            src,
                            src,
                            self.send.at[i, 3 + number],
                            self.recv.at[i, (3 + number) * plan.depth + t],
                            self.across(step, not x_first),
                        ).start()

    def third(self, t):
        plan, side = self.plan, self.plan.side
        for i, shard in enumerate(self.shards):
            z = self.level(t)
            if t == 0:
                pltpu.make_async_copy(
                    shard, self.outs[i].at[z, self.y, self.x], self.recv.at[i, 0]
                ).wait()
            for number, x_first, out, sl in self.routes(i):
                sem = self.recv.at[i, (1 + number) * plan.depth + t]
                if x_first:
                    bytes_of(out.at[z, self.y, pl.ds(0, side - 1), sl], sem)
                    src = out.at[z, self.y, :, sl]
                else:
                    bytes_of(out.at[z, pl.ds(0, side - 1), self.x, sl], sem)
                    src = out.at[z, :, self.x, sl]
                for step in range(1, side):
                    push(
                        src,
                        src,
                        self.send.at[i, 3 + number],
                        self.recv.at[i, (3 + number) * plan.depth + t],
                        self.across(step, not x_first),
                    ).start()

    def end(self, last_only=False):
        plan, side = self.plan, self.plan.side
        for i in range(len(self.shards)):
            if not last_only:
                bytes_of(self.outs[i].at[pl.ds(0, plan.depth - 1), 0, 0], self.send.at[i, 0])
            for number, x_first, out, sl in self.routes(i):
                if not last_only:
                    bytes_of(out.at[:, 0, pl.ds(0, side - 1), sl], self.send.at[i, 1 + number])
                for t in range(plan.depth):
                    bytes_of(
                        out.at[0, :, pl.ds(0, side - 1), sl],
                        self.recv.at[i, (3 + number) * plan.depth + t],
                    )
                bytes_of(out.at[:, :, pl.ds(0, side - 1), sl], self.send.at[i, 3 + number])

    def stage(self, number):
        if number > 0:
            self.third(number - 1)
        if 0 <= number < self.plan.depth - 1:
            self.second(number + 1)


class Scatter:
    @staticmethod
    def scratch(plan, shapes):
        refs = []
        for index, (rows, cols) in enumerate(shapes):
            for _, part, _ in plan.routes(rows, index):
                for lead in (
                    (plan.depth, plan.side - 1, plan.side),
                    (plan.depth, plan.side),
                    (plan.depth, plan.side - 1),
                    (plan.depth,),
                    (plan.depth - 1,),
                ):
                    refs.append(pltpu.VMEM(lead + (part, cols), BF))
        return refs

    @staticmethod
    def semaphores(plan, count):
        return [
            pltpu.SemaphoreType.DMA((count, 6)),
            pltpu.SemaphoreType.DMA((count, 4 * plan.depth + 2)),
        ]

    def __init__(self, plan, grads, outs, buffers, send, recv, lines_only=False):
        self.plan, self.grads, self.outs = plan, grads, outs
        self.lines_only = lines_only
        self.send, self.recv = send, recv
        self.section, chip = spot()
        self.z, self.y, self.x = plan.place(chip)
        self.work = []
        buffers = list(buffers)
        for i, grad in enumerate(grads):
            for number, (start, rows, x_first) in enumerate(plan.routes(grad.shape[3], i)):
                self.work.append((i, number, start, rows, x_first, buffers[:5]))
                buffers = buffers[5:]

    def to(self, z, y, x):
        return self.section, self.plan.chip_at(z, y, x)

    def level(self, t):
        return lax.rem(self.z + 1 + t, self.plan.depth)

    def begin(self, first=0, last=None):
        plan, side = self.plan, self.plan.side
        for t in range(first, plan.depth if last is None else last):
            z = self.level(t)
            for i, number, start, rows, x_first, (land, *_) in self.work:
                grad, sl = self.grads[i], pl.ds(start, rows)
                for step in range(1, side):
                    if x_first:
                        y = lax.rem(self.y + step, side)
                        src, peer = grad.at[z, y, :, sl], self.to(self.z, y, self.x)
                    else:
                        x = lax.rem(self.x + step, side)
                        src, peer = grad.at[z, :, x, sl], self.to(self.z, self.y, x)
                    push(
                        src,
                        land.at[t, step - 1],
                        self.send.at[i, number],
                        self.recv.at[i, number * plan.depth + t],
                        peer,
                    ).start()

    def second(self, t):
        plan, side = self.plan, self.plan.side
        z = self.level(t)
        for i, number, start, rows, x_first, (land, part, land2, *_) in self.work:
            grad = self.grads[i]
            bytes_of(land.at[t], self.recv.at[i, number * plan.depth + t])
            for j in range(side):
                y, x = (self.y, j) if x_first else (j, self.x)
                total = grad[z, y, x, start : start + rows, :].astype(F32)
                for step in range(side - 1):
                    total = total + land[t, step, j].astype(F32)
                part[t, j] = total.astype(BF)
            for step in range(1, side):
                if x_first:
                    j = lax.rem(self.x + step, side)
                    peer = self.to(self.z, self.y, j)
                else:
                    j = lax.rem(self.y + step, side)
                    peer = self.to(self.z, j, self.x)
                push(
                    part.at[t, j],
                    land2.at[t, step - 1],
                    self.send.at[i, 2 + number],
                    self.recv.at[i, (2 + number) * plan.depth + t],
                    peer,
                ).start()

    def third(self, t):
        plan, side = self.plan, self.plan.side
        for i, number, start, rows, x_first, (_, part, land2, line, land3) in self.work:
            bytes_of(land2.at[t], self.recv.at[i, (2 + number) * plan.depth + t])
            mine = self.x if x_first else self.y
            total = part[t, mine].astype(F32)
            for step in range(side - 1):
                total = total + land2[t, step].astype(F32)
            line[t] = total.astype(BF)
            if t < plan.depth - 1 and not self.lines_only:
                push(
                    line.at[t],
                    land3.at[t],
                    self.send.at[i, 4 + number],
                    self.recv.at[i, 4 * plan.depth + number],
                    self.to(self.level(t), self.y, self.x),
                ).start()

    def end(self):
        plan = self.plan
        for i, number, start, rows, x_first, (land, part, land2, line, land3) in self.work:
            if self.lines_only:
                self.outs[i][:, start : start + rows, :] = line[...]
                bytes_of(land, self.send.at[i, number])
                bytes_of(land2, self.send.at[i, 2 + number])
                continue
            bytes_of(land3, self.recv.at[i, 4 * plan.depth + number])
            total = line[plan.depth - 1].astype(F32)
            for step in range(plan.depth - 1):
                total = total + land3[step].astype(F32)
            self.outs[i][start : start + rows, :] = total
            bytes_of(land, self.send.at[i, number])
            bytes_of(land2, self.send.at[i, 2 + number])
            bytes_of(land3, self.send.at[i, 4 + number])

    def stage(self, number):
        if number < self.plan.depth:
            self.second(number)
        if number > 0:
            self.third(number - 1)


def exit_kernel(chips, give, tiles, take, land, send, recv, gain_send, gain_recv):
    section, chip = spot()
    me = section * chips + chip
    greet_everyone(chips)()
    swap = push(give, take, send, recv, (1 - section, chip))
    swap.start()

    def one(step, carry):
        peer = lax.rem(me + step, 2 * chips)
        push(
            tiles.at[peer],
            land.at[me],
            gain_send,
            gain_recv,
            (peer // chips, lax.rem(peer, chips)),
        ).start()
        return carry

    lax.fori_loop(1, 2 * chips, one, 0)
    pltpu.make_async_copy(tiles.at[me], land.at[me], gain_recv).start()
    bytes_of(land, gain_recv)
    bytes_of(land.at[pl.ds(0, 2 * chips - 1)], gain_send)
    swap.wait()


def exit_call(chips, give, tiles):
    any_spec = pl.BlockSpec(memory_space=pl.ANY)
    return pl.pallas_call(
        functools.partial(exit_kernel, chips),
        out_shape=[
            jax.ShapeDtypeStruct(give.shape, give.dtype),
            jax.ShapeDtypeStruct(tiles.shape, tiles.dtype),
        ],
        in_specs=[any_spec] * 2,
        out_specs=[any_spec] * 2,
        scratch_shapes=[
            pltpu.SemaphoreType.DMA,
            pltpu.SemaphoreType.DMA,
            pltpu.SemaphoreType.DMA,
            pltpu.SemaphoreType.DMA,
        ],
        compiler_params=pltpu.CompilerParams(collective_id=4, has_side_effects=True),
        name="leave",
    )(give, tiles)


def filter_rows(plan, land, table, first_row, backward):
    lane = lax.broadcasted_iota(jnp.int32, (plan.f_rows, LANES), 1)
    low = lane < plan.half
    total = plan.length // LANES
    for m in range(total):
        if backward:
            one, two = 2 * m, 2 * m + 1
        else:
            one, two = plan.chips - 1 - 2 * m, plan.chips - 2 - 2 * m
        left = land[one, first_row : first_row + plan.f_rows, :].astype(F32)
        right = land[two, first_row : first_row + plan.f_rows, :].astype(F32)
        even = jnp.where(low, left, pltpu.roll(right, plan.half, 1))
        odd = jnp.where(low, pltpu.roll(left, plan.half, 1), right)
        at = LANES * m + (BLOCK if backward else 0)
        table[0, :, at : at + LANES] = even
        table[1, :, at : at + LANES] = odd
    blank = jnp.zeros((plan.f_rows, BLOCK), F32)
    at = 0 if backward else plan.length
    for parity in range(2):
        table[parity, :, at : at + BLOCK] = blank


def build_strips(plan, table, strip, backward):
    span = plan.length + BLOCK
    shift = span - LANES if backward else span - (LANES - 1)
    part = 32

    def one(k, carry):
        for parity in range(2):
            row = table[parity, pl.ds(k, 1), :]
            for start in range(0, LANES, part):
                spread = jnp.broadcast_to(row, (part, span))
                rolled = pltpu.roll(
                    spread, (shift + start) % span, 1, stride=1, stride_axis=0
                ).astype(BF)
                strip[parity, k, LANES + start : LANES + start + part, :] = rolled[
                    :, : plan.length
                ]
                strip[parity, k, start : start + part, :] = rolled[
                    :, LANES : LANES + plan.length
                ]
        return carry

    lax.fori_loop(0, plan.local, one, 0)


def sizes(plan):
    size = plan.jb // PIECE
    while size:
        yield size
        size //= 2


def owner_pieces(plan, act):
    section, chip = spot()
    start = plan.pieces * (section * plan.chips + chip)
    per_block = plan.jb // PIECE

    def block(j, carry):
        number = start // per_block + j
        base = number * per_block
        low = jnp.maximum(start - base, 0)
        high = jnp.minimum(start + plan.pieces - base, per_block)
        count = jnp.maximum(high - low, 0)
        which = number // plan.cols_in
        b = lax.rem(number, plan.cols_in)
        sign = which // plan.filters
        full = lax.rem(which, plan.filters)
        group = full // plan.local
        k = lax.rem(full, plan.local)
        for size in sizes(plan):
            done = count // (2 * size) * (2 * size)
            here = lax.rem(count // size, 2) == 1
            source = base + low - start + done
            target = low + done

            @pl.when(jnp.logical_and(here, sign < 2))
            def _():
                for a in range(plan.cols_out):
                    to_chip = plan.part_at(a, b, group)
                    act(source, size, False, k, target, a, sign, to_chip)

            @pl.when(jnp.logical_and(here, sign >= 2))
            def _():
                for a in range(plan.cols_out):
                    for core in range(2):
                        to_chip = plan.part_at(a, b, plan.groups - 1)
                        act(source, size, True, full, target, a, core, to_chip)

        return carry

    lax.fori_loop(0, plan.pieces // per_block + 2, block, 0)


def forward_kernel(plan, *refs):
    io_ref, gain_ref, filters_ref, lengths_ref = refs[:4]
    gate_raw, up_raw, down_raw, proj_raw, attn_raw = refs[4:9]
    if plan.routed:
        maps_ref = refs[9]
        rest = refs[10:]
    else:
        mine_ref, other_ref, taps_ref = refs[9:12]
        rest = refs[12:]
    full_weights, rest = rest[:8], rest[8:]
    (
        conv_ref,
        hidden_ref,
        upstream_ref,
        pair_ref,
        gains_ref,
        mask_ref,
        v_ref,
        pq_ref,
        tapw_ref,
        x_ref,
        xs_ref,
        filt_ref,
        io_own,
        io_sib,
        gain_tile,
        gate_half,
        gate_shard,
        up_half,
        up_shard,
        down_shard,
        u_ref,
        f_ref,
        x_buf,
        xo_buf,
        xs_buf,
        xf_buf,
        f_land,
        table,
        strip,
        mine,
        other,
        taps,
        pq,
        acc,
        joined,
        y_buf,
        land,
        reduced,
        final,
        stage,
        io_sem,
        gain_send,
        gain_recv,
        s_send,
        s_recv,
        u_send,
        x_recv,
        f_send,
        f_recv,
        m_send,
        m_recv,
        t_recv,
        o_send,
        o_recv,
        c_send,
        c_recv,
        d_send,
        r_recv,
        v_sem,
        out_sem,
        w_send,
        w_recv,
    ) = rest
    chips, half, jb, ia, rows_here = plan.chips, plan.half, plan.jb, plan.ia, plan.rows
    section, chip = spot()
    dev = section * chips + chip
    sibling = (1 - section, chip)
    my_group = chip // (plan.cols_out * plan.cols_in)
    greeted = greet_everyone(chips)

    row = lax.broadcasted_iota(jnp.int32, (rows_here, rows_here), 0)
    col = lax.broadcasted_iota(jnp.int32, (rows_here, rows_here), 1)
    order = jnp.where(col == 2 * lax.rem(row, half) + row // half, 1.0, 0.0).astype(BF)
    for i in range(2):
        io_own[i] = flat_dot(order, io_ref[i]).astype(BF)
    cols = gain_ref.shape[1]
    gain_tile[0] = jnp.zeros((8, LANES), F32)
    gain_tile[0, 0:2, 0:cols] = gain_ref[...].astype(F32)
    if plan.pick_here:
        lane = lax.broadcasted_iota(jnp.int32, (gate_raw.shape[0], LANES), 1)
        low = lane < half
        for raw, halves, shard in ((gate_raw, gate_half, gate_shard), (up_raw, up_half, up_shard)):
            for j in range(raw.shape[1] // (2 * LANES)):
                one = raw[:, 2 * LANES * j : 2 * LANES * j + LANES].astype(F32)
                two = raw[:, 2 * LANES * j + LANES : 2 * LANES * (j + 1)].astype(F32)
                zero_half = jnp.where(low, one, pltpu.roll(two, half, 1)).astype(BF)
                one_half = jnp.where(low, pltpu.roll(one, half, 1), two).astype(BF)
                at = slice(LANES * j, LANES * (j + 1))
                shard[section, :, at] = jnp.where(section == 0, zero_half, one_half)
                halves[:, at] = jnp.where(section == 0, one_half, zero_half)
    else:
        for raw, halves, shard in ((gate_raw, gate_half, gate_shard), (up_raw, up_half, up_shard)):
            shard[section] = raw[section]
            halves[...] = raw[1 - section]
    part = down_shard.shape[1]
    down_shard[section] = down_raw[pl.ds(pl.multiple_of(part * section, 16), part), :]
    greeted()
    io_swap = push(io_own, io_sib, io_sem.at[0], io_sem.at[1], sibling)
    io_swap.start()

    gain_swap = push(gain_tile.at[0], gain_tile.at[1], gain_send, gain_recv, sibling)
    gain_swap.start()
    shares = [
        push(src, dst, s_send.at[i], s_recv.at[i], sibling)
        for i, (src, dst) in enumerate(
            (
                (gate_half, gate_shard.at[section]),
                (up_half, up_shard.at[section]),
                (
                    down_raw.at[pl.ds(pl.multiple_of(part * (1 - section), 16), part), :],
                    down_shard.at[section],
                ),
            )
        )
    ]
    for share in shares:
        share.start()

    if plan.routed:

        def places(source, size, tap, k, target, a):
            rows = size * PIECE
            src = maps_ref.at[pl.ds(PIECE * source, rows), pl.ds(a * ia, ia)]
            if tap:
                return src, taps.at[pl.ds(jb * k + PIECE * target, rows), :], t_recv
            return src, mine.at[k, pl.ds(PIECE * target, rows), :], m_recv

        def start_piece(source, size, tap, k, target, a, to_section, to_chip):
            src, dst, sem = places(source, size, tap, k, target, a)
            here = to_section * chips + to_chip == dev

            @pl.when(here)
            def _():
                pltpu.make_async_copy(src, dst, sem).start()

            @pl.when(jnp.logical_not(here))
            def _():
                push(src, dst, m_send, sem, (to_section, to_chip)).start()

        def drain_piece(source, size, tap, k, target, a, to_section, to_chip):
            src, dst, sem = places(source, size, tap, k, target, a)

            @pl.when(to_section * chips + to_chip != dev)
            def _():
                push(src, dst, m_send, sem, (to_section, to_chip)).wait_send()

        owner_pieces(plan, start_piece)

    lag = lax.broadcasted_iota(jnp.int32, (rows_here, LANES), 0)
    lane = lax.broadcasted_iota(jnp.int32, (rows_here, LANES), 1)
    stretch = lax.rem(lane, half)
    backwards = jnp.where(lag == 2 * (half - 1 - stretch) + lane // half, 1.0, 0.0).astype(BF)
    plain = jnp.where(lag == 2 * stretch + lane // half, 1.0, 0.0).astype(BF)
    gain_swap.wait_recv()
    core_zero = section == 0
    own_gain, sib_gain = gain_tile[0], gain_tile[1]
    gain_rows = jnp.concatenate(
        [jnp.where(core_zero, own_gain, sib_gain), jnp.where(core_zero, sib_gain, own_gain)], 0
    ).astype(BF)
    for group in range(plan.groups):
        source = lax.broadcasted_iota(jnp.int32, (plan.filters, plan.f_rows), 0)
        target = lax.broadcasted_iota(jnp.int32, (plan.filters, plan.f_rows), 1)
        chosen = jnp.where(
            (source == group * plan.local + target) & (target < plan.local), 1.0, 0.0
        ).astype(BF)
        some = flat_dot(filters_ref[...], chosen).astype(BF)
        f_ref[group, : plan.f_rows, :] = cols_dot(some, backwards).astype(BF)
        f_ref[group, plan.f_rows : 2 * plan.f_rows, :] = cols_dot(some, plain).astype(BF)
        f_ref[group, 2 * plan.f_rows :, :] = gain_rows

    def send_f(step, carry):
        peer = lax.rem(chip + step, chips)
        group = peer // (plan.cols_out * plan.cols_in)
        push(f_ref.at[group], f_land.at[chip], f_send, f_recv, (section, peer)).start()
        return carry

    lax.fori_loop(1, chips, send_f, 0)
    pltpu.make_async_copy(f_ref.at[my_group], f_land.at[chip], f_recv).start()
    for share in shares:
        share.wait_recv()
    second_layer = (gate_shard.at[1], up_shard.at[1], down_shard.at[1])
    parts = [
        (0, (gate_shard.at[0], up_shard.at[0], down_shard.at[0])),
        (3, (proj_raw, attn_raw)),
    ]
    parts.append((5, second_layer))
    groups = []
    for first, arrays in parts:
        last = first + len(arrays)
        groups.append(
            Gather(
                plan,
                arrays,
                full_weights[first:last],
                w_send.at[pl.ds(first, len(arrays))],
                w_recv.at[pl.ds(first, len(arrays))],
            )
        )
    layer0, attention, layer1 = groups
    layer0.begin()
    position = lax.broadcasted_iota(jnp.int32, (rows_here, 1), 0)
    position = chip * rows_here + 2 * lax.rem(position, half) + position // half
    length_own = jnp.where(section == 0, lengths_ref[0], lengths_ref[1])
    length_other = jnp.where(section == 0, lengths_ref[1], lengths_ref[0])
    mask = jnp.where(position < length_own, 1.0, 0.0)
    mask_other = jnp.where(position < length_other, 1.0, 0.0)
    mask_ref[...] = mask
    io_swap.wait()
    bytes_of(f_land, f_recv)
    pick_row = lax.broadcasted_iota(jnp.int32, (LANES, plan.width), 0)
    pick_col = lax.broadcasted_iota(jnp.int32, (LANES, plan.width), 1)
    repeat = jnp.where(pick_row == lax.rem(pick_col, cols), 1.0, 0.0).astype(BF)
    tile_row = lax.broadcasted_iota(jnp.int32, (chips * 16, plan.width), 0)
    tile_col = lax.broadcasted_iota(jnp.int32, (chips * 16, plan.width), 1)
    rows_all = f_land[:, 2 * plan.f_rows :, :].reshape(chips * 16, LANES)
    spread = jnp.where(
        tile_row // 16 == tile_col // cols, flat_dot(rows_all, repeat), 0.0
    ).astype(BF)
    gain_row = lax.broadcasted_iota(jnp.int32, (16, chips * 16), 0)
    gain_col = lax.broadcasted_iota(jnp.int32, (16, chips * 16), 1)
    gather_rows = jnp.where(lax.rem(gain_col, 16) == gain_row, 1.0, 0.0).astype(BF)
    gathered = flat_dot(gather_rows, spread)
    gains_ref[0:2, :] = gathered[0:2, :]
    gains_ref[2:4, :] = gathered[8:10, :]
    gains_ref[4:8, :] = jnp.zeros((4, plan.width), F32)
    hidden = jnp.where(core_zero, io_own[0], io_sib[1]).astype(F32) * mask
    hidden_ref[...] = hidden
    factor = lax.rsqrt(jnp.mean(hidden * hidden, axis=-1, keepdims=True) + EPSILON)
    u = (hidden * factor * gains_ref[0:1, :]).astype(BF)
    for b in range(plan.cols_in):
        u_ref[b, :, :jb] = u[:half, b * jb : (b + 1) * jb]
        u_ref[b, :, jb:] = u[half:, b * jb : (b + 1) * jb]

    def send_u(step, carry):
        peer = lax.rem(chip + step, chips)
        b = plan.b_of(peer)
        push(
            u_ref.at[b],
            x_buf.at[pl.ds(half * chip, half), :],
            u_send,
            x_recv,
            (section, peer),
        ).start()
        return carry

    lax.fori_loop(1, chips, send_u, 0)
    pltpu.make_async_copy(
        u_ref.at[plan.b_of(chip)],
        x_buf.at[pl.ds(half * chip, half), :],
        x_recv,
    ).start()
    for group in groups[1:]:
        group.begin()
    cot_own = jnp.where(core_zero, io_sib[0], io_own[1]).astype(F32) * mask
    cot_other = jnp.where(core_zero, io_sib[1], io_own[0]).astype(F32) * mask_other
    upstream_ref[...] = cot_own
    pair_ref[:rows_here, :] = cot_own.astype(BF)
    pair_ref[rows_here:, :] = cot_other.astype(BF)
    layer0.stage(0)
    filter_rows(plan, f_land, table, 0, False)
    build_strips(plan, table, strip, False)
    filt_out = pltpu.make_async_copy(f_land, filt_ref, out_sem.at[0])
    filt_out.start()

    if plan.routed:
        bytes_of(mine, m_recv)
        swap = push(mine, other, o_send, o_recv, (1 - section, chip))
        swap.start()

        @pl.when(my_group == plan.groups - 1)
        def _():
            bytes_of(taps, t_recv)

        @pl.when(my_group != plan.groups - 1)
        def _():
            taps[...] = jnp.zeros_like(taps)
    else:
        for src, dst in ((mine_ref, mine), (other_ref, other), (taps_ref, taps)):
            pltpu.sync_copy(src, dst)

    layer0.stage(1)
    bytes_of(x_buf, x_recv)
    x_out = pltpu.make_async_copy(x_buf, x_ref, out_sem.at[1])
    x_out.start()
    xf_buf[0:8, :] = jnp.zeros((8, 2 * jb), F32)
    for i in range(plan.blocks):
        rows = slice(BLOCK * i, BLOCK * (i + 1))
        xf_buf[8 + BLOCK * i : 8 + BLOCK * (i + 1), :] = x_buf[rows, :].astype(F32)
    for i in range(plan.blocks):
        rows = slice(BLOCK * i, BLOCK * (i + 1))
        moved = xf_buf[7 + BLOCK * i : 7 + BLOCK * (i + 1), :].astype(BF)
        xs_buf[rows, :] = moved
        xo_buf[rows, :jb] = x_buf[rows, :jb]
        xo_buf[rows, jb:] = moved[:, jb:]
    xs_out = pltpu.make_async_copy(xs_buf, xs_ref, out_sem.at[2])
    xs_out.start()

    if plan.routed:
        swap.wait()
    turn = (1 - 2 * section).astype(F32)

    def mix(k, carry):
        first = mine[k].astype(F32)
        second = other[k].astype(F32)
        pq[k, :jb, :] = (first + second).astype(BF)
        pq[k, jb:, :] = ((first - second) * turn).astype(BF)
        return carry

    lax.fori_loop(0, plan.local, mix, 0)
    pq_out = pltpu.make_async_copy(pq, pq_ref, out_sem.at[3])
    pq_out.start()
    taps_out = pltpu.make_async_copy(taps, tapw_ref, out_sem.at[4])
    taps_out.start()

    layer0.stage(2)
    attention.stage(0)
    batch = plan.batch
    my_b, level = plan.b_of(chip), chip // plan.cols_in

    def reduce_level(i):
        bytes_of(land.at[i], r_recv.at[i])
        total = y_buf[:, pl.ds(pl.multiple_of(BLOCK * i + half * my_b, half), half), :].astype(F32)
        for step_number in range(plan.cols_in - 1):
            total = total + land[i, step_number].astype(F32)
        reduced[i] = total.astype(BF)

        @pl.when(level == i)
        def _():
            final[i] = reduced[i]

        @pl.when(level != i)
        def _():
            push(
                reduced.at[i],
                final.at[level],
                d_send,
                c_recv,
                (section, i * plan.cols_in + my_b),
            ).start()

    for i in range(plan.blocks):
        if i == 1:
            layer0.stage(3)
            attention.stage(1)
        if i == 2:
            layer0.stage(4)
            attention.stage(2)
            layer1.second(1)
        if i == 3:
            attention.stage(3)
            attention.stage(4)
            layer1.second(2)
        rows = slice(BLOCK * i, BLOCK * (i + 1))
        depth = BLOCK * (i + 1)
        offset = plan.length - depth
        x_now = x_buf[rows, :]
        s_now = xs_buf[rows, :]
        acc[:BLOCK] = flat_dot(
            jnp.concatenate([x_now[:, :jb], s_now[:, jb:]], 1), taps[: 2 * jb, :]
        ) + flat_dot(s_now[:, :jb], taps[2 * jb :, :])
        acc[BLOCK:] = flat_dot(
            jnp.concatenate([x_now[:, jb:], x_now[:, :jb]], 1), taps[: 2 * jb, :]
        ) + flat_dot(s_now[:, jb:], taps[2 * jb :, :])

        def step(t, carry, i=i, depth=depth, offset=offset):
            count = plan.local // batch * i + t
            slot = lax.rem(count, 2)
            some = pl.ds(batch * t, batch)
            v_copy = pltpu.make_async_copy(
                stage.at[slot], v_ref.at[some, :, pl.ds(BLOCK * i, BLOCK), :], v_sem.at[slot]
            )
            even = flat_dot(
                strip[0, some, :, offset:].reshape(batch * BLOCK, depth), x_buf[:depth, :]
            ).astype(BF)
            odd = flat_dot(
                strip[1, some, :, offset:].reshape(batch * BLOCK, depth), xo_buf[:depth, :]
            ).astype(BF)
            if i == 0:
                pl.when(t >= 2)(v_copy.wait)
            else:
                v_copy.wait()
            for k in range(batch):
                here = slice(BLOCK * k, BLOCK * (k + 1))
                first = jnp.concatenate([even[here, :jb], odd[here, jb:]], 1)
                second = jnp.concatenate([even[here, jb:], odd[here, :jb]], 1)
                stage[slot, k, 0] = first
                stage[slot, k, 1] = second
                lanes = slice(2 * jb * k, 2 * jb * (k + 1))
                joined[:BLOCK, lanes] = first
                joined[BLOCK:, lanes] = second
            v_copy.start()
            acc[...] += flat_dot(joined[...], pq[some].reshape(batch * 2 * jb, ia))
            return carry

        lax.fori_loop(0, plan.local // batch, step, 0)
        y_buf[0, rows, :] = acc[:BLOCK].astype(BF)
        y_buf[1, rows, :] = acc[BLOCK:].astype(BF)

        if plan.layered:
            for step_number in range(1, plan.cols_in):
                peer = lax.rem(my_b + step_number, plan.cols_in)
                push(
                    y_buf.at[:, pl.ds(BLOCK * i + half * peer, half), :],
                    land.at[i, step_number - 1],
                    c_send,
                    r_recv.at[i],
                    (section, level * plan.cols_in + peer),
                ).start()
            if i > 0:
                reduce_level(i - 1)
            continue

        def give(r, carry, i=i):
            peer = BLOCK // half * i + r
            src = y_buf.at[:, pl.ds(half * peer, half), :]

            @pl.when(peer == chip)
            def _():
                pltpu.make_async_copy(src, land.at[chip], c_recv).start()

            @pl.when(peer != chip)
            def _():
                push(src, land.at[chip], c_send, c_recv, (section, peer)).start()

            return carry

        lax.fori_loop(0, BLOCK // half, give, 0)

    layer1.second(3)
    if not plan.late:
        for number in range(plan.depth):
            layer1.third(number)
    for slot in range(2):
        pltpu.make_async_copy(
            stage.at[slot], v_ref.at[pl.ds(0, batch), :, pl.ds(0, BLOCK), :], v_sem.at[slot]
        ).wait()
    bytes_of(x_buf.at[pl.ds(0, half * (chips - 1)), :], u_send)
    bytes_of(f_land.at[pl.ds(0, chips - 1)], f_send)
    if plan.routed:
        owner_pieces(plan, drain_piece)
    for copy in (filt_out, x_out, xs_out, pq_out, taps_out):
        copy.wait()
    if plan.layered:
        reduce_level(plan.blocks - 1)
        bytes_of(final.at[pl.ds(0, plan.blocks - 1)], c_recv)
    else:
        bytes_of(land, c_recv)
    for a in range(plan.cols_out):
        total = None
        for c in range(plan.groups):
            if plan.layered:
                terms = [final[a + plan.cols_out * c]]
            else:
                terms = [land[plan.part_at(a, b, c)] for b in range(plan.cols_in)]
            for term in terms:
                term = term.astype(F32)
                total = term if total is None else total + term
        conv_ref[:, :, a * ia : (a + 1) * ia] = total
    if plan.layered:
        bytes_of(land, c_send)
        bytes_of(final.at[pl.ds(0, plan.blocks - 1)], d_send)
    else:
        bytes_of(land.at[pl.ds(0, chips - 1)], c_send)
    for group in groups[:2]:
        group.end()
    if plan.late:
        layer1.hand_over()
    else:
        layer1.end()
    gain_swap.wait_send()
    for share in shares:
        share.wait_send()


def forward_call(plan, io, gain, filters, lengths, raw, maps):
    chips, half, jb, ia, rows = plan.chips, plan.half, plan.jb, plan.ia, plan.rows
    width = plan.width
    any_spec = pl.BlockSpec(memory_space=pl.ANY)
    vmem_spec = pl.BlockSpec(memory_space=pltpu.VMEM)
    smem_spec = pl.BlockSpec(memory_space=pltpu.SMEM)
    dma = pltpu.SemaphoreType.DMA
    down, proj, attn = raw[2].shape, raw[3].shape, raw[4].shape
    share = (raw[0].shape[-2], plan.ff // 2)
    down_share = (down[0] // 2, width)
    grid = (plan.depth, plan.side, plan.side)
    layer = [share, share, down_share]
    levels = plan.blocks if plan.layered else 1
    land_shape = (
        (levels, plan.cols_in - 1, 2, half, ia) if plan.layered else (chips, 2, half, ia)
    )
    gathered = [grid + w for w in layer + [proj, attn]]
    gathered += [grid + w for w in layer]
    shapes = [(w, BF) for w in gathered] + [
        ((2, half, width), F32),
        ((rows, width), F32),
        ((rows, width), F32),
        ((2 * rows, width), BF),
        ((8, width), F32),
        ((rows, 1), F32),
        ((plan.local, 2, plan.length, 2 * jb), BF),
        ((plan.local, 2 * jb, ia), BF),
        ((ORDER * jb, ia), BF),
        ((plan.length, 2 * jb), BF),
        ((plan.length, 2 * jb), BF),
        ((chips, 2 * plan.f_rows + 16, LANES), BF),
    ]
    return pl.pallas_call(
        functools.partial(forward_kernel, plan),
        out_shape=[jax.ShapeDtypeStruct(s, d) for s, d in shapes],
        in_specs=[vmem_spec] * 3
        + [smem_spec]
        + [vmem_spec] * 3
        + [any_spec] * 2
        + [vmem_spec if plan.routed else any_spec] * len(maps),
        out_specs=[any_spec] * 8 + [vmem_spec] * 6 + [any_spec] * 6,
        scratch_shapes=[
            pltpu.VMEM((2, rows, width), BF),
            pltpu.VMEM((2, rows, width), BF),
            pltpu.VMEM((2, 8, LANES), F32),
            pltpu.VMEM(share, BF),
            pltpu.VMEM((2,) + share, BF),
            pltpu.VMEM(share, BF),
            pltpu.VMEM((2,) + share, BF),
            pltpu.VMEM((2,) + down_share, BF),
            pltpu.VMEM((plan.cols_in, half, 2 * jb), BF),
            pltpu.VMEM((plan.groups, 2 * plan.f_rows + 16, LANES), BF),
            pltpu.VMEM((plan.length, 2 * jb), BF),
            pltpu.VMEM((plan.length, 2 * jb), BF),
            pltpu.VMEM((plan.length, 2 * jb), BF),
            pltpu.VMEM((plan.length + 8, 2 * jb), F32),
            pltpu.VMEM((chips, 2 * plan.f_rows + 16, LANES), BF),
            pltpu.VMEM((2, plan.f_rows, plan.length + BLOCK), F32),
            pltpu.VMEM((2, plan.local, BLOCK, plan.length), BF),
            pltpu.VMEM((plan.local, jb, ia), BF),
            pltpu.VMEM((plan.local, jb, ia), BF),
            pltpu.VMEM((ORDER * jb, ia), BF),
            pltpu.VMEM((plan.local, 2 * jb, ia), BF),
            pltpu.VMEM((2 * BLOCK, ia), F32),
            pltpu.VMEM((2 * BLOCK, plan.batch * 2 * jb), BF),
            pltpu.VMEM((2, plan.length, ia), BF),
            pltpu.VMEM(land_shape, BF),
            pltpu.VMEM((levels, 2, half, ia), BF),
            pltpu.VMEM((levels, 2, half, ia), BF),
            pltpu.VMEM((2, plan.batch, 2, BLOCK, 2 * jb), BF),
            dma((2,)),
            dma,
            dma,
            dma((3,)),
            dma((3,)),
        ]
        + [dma] * 12
        + [dma((levels,)), dma((2,)), dma((5,)), *Gather.semaphores(plan, 8)],
        compiler_params=pltpu.CompilerParams(
            collective_id=2, has_side_effects=True, vmem_limit_bytes=VMEM_LIMIT
        ),
        name="spectral_forward",
    )(io, gain, filters, lengths, *raw, *maps)


def backward_kernel(plan, number, *refs):
    g_ref, filt_ref, v_ref, pq, tapw, x_ref, xs_ref = refs[:7]
    grads, rest = refs[7 : 7 + number], refs[7 + number :]
    if plan.late:
        hidden_ref, gains_ref, mask_ref, dmid_ref, out_ref, gain_sums_ref, *lines = rest[:9]
        res_ref, gate_ref, up_ref, down_ref, proj_ref, attn_ref, gain_out, dmaps_ref = rest[9:17]
        du_ref, gain_buf, gain_land, give_res, *half_parts = rest[17:30]
        half0, crossing, arrived = half_parts[:3], half_parts[3:6], half_parts[6:9]
        e_send, e_recv, n_send, n_recv = rest[30:34]
        half1, line_land, (l_send, l_recv) = rest[34:37], rest[37:40], rest[40:42]
        rest = rest[42:]
        sums = [*half0, proj_ref, attn_ref]
    else:
        sums, rest = rest[:number], rest[number:]
        du_ref, dmap_ref, dtap_ref = rest[:3]
        rest = rest[3:]
    count = 5 * sum(len(plan.routes(grad.shape[3])) for grad in grads)
    scatter = Scatter(plan, grads, sums, rest[:count], *rest[count : count + 2])
    rest = rest[count + 2 :]
    (
        g_buf,
        gt_buf,
        table,
        strip,
        v_buf,
        z_even,
        z_odd,
        acc_even,
        acc_odd,
        kept,
        give_m,
        take_m,
        total_m,
        kept_t,
        give_t,
        take_t,
        total_t,
        du_buf,
        land,
        g_send,
        g_recv,
        v_sem,
        m_send,
        m_recv,
        t_send,
        t_recv,
        w_send,
        w_recv,
        d_send,
        d_recv,
        x_sem,
        z_send,
        z_recv,
    ) = rest
    chips, half, jb, ia = plan.chips, plan.half, plan.jb, plan.ia
    section, chip = spot()
    dev = section * chips + chip
    my_a, my_b = plan.a_of(chip), plan.b_of(chip)
    my_group = chip // (plan.cols_out * plan.cols_in)
    sibling = (1 - section, chip)
    greet_everyone(chips)()

    def send_g(step, carry):
        peer = lax.rem(chip + step, chips)
        a = plan.a_of(peer)
        push(
            g_ref.at[:, :, pl.ds(pl.multiple_of(a * ia, ia), ia)],
            g_buf.at[:, pl.ds(half * chip, half), :],
            g_send,
            g_recv,
            (section, peer),
        ).start()
        return carry

    own_g = g_ref.at[:, :, pl.ds(pl.multiple_of(my_a * ia, ia), ia)]
    level, levels = chip // plan.cols_in, chips // plan.cols_in

    def g_rows(t):
        source = lax.rem(level - t + levels, levels) * plan.cols_in + my_b
        return g_buf.at[:, pl.ds(pl.multiple_of(half * source, half), half), :]

    def spread_g(t):
        if t > 0:
            bytes_of(g_rows(t), z_recv.at[t])
        for step_number in range(1, plan.cols_in):
            peer = lax.rem(my_b + step_number, plan.cols_in)
            push(
                own_g if t == 0 else g_rows(t),
                g_rows(t),
                g_send,
                g_recv,
                (section, level * plan.cols_in + peer),
            ).start()

    if plan.layered:
        for t in range(1, levels):
            to_level = lax.rem(level + t, levels)
            to_a = lax.rem(to_level, plan.cols_out)
            push(
                g_ref.at[:, :, pl.ds(pl.multiple_of(to_a * ia, ia), ia)],
                g_rows(0),
                z_send,
                z_recv.at[t],
                (section, to_level * plan.cols_in + my_b),
            ).start()
        spread_g(0)
        pltpu.make_async_copy(own_g, g_rows(0), z_recv.at[0]).start()
    else:
        lax.fori_loop(1, chips, send_g, 0)
        pltpu.make_async_copy(
            own_g, g_buf.at[:, pl.ds(half * chip, half), :], g_recv
        ).start()
    v_copy = [pltpu.make_async_copy(v_ref.at[k], v_buf.at[k], v_sem.at[k]) for k in range(2)]
    for copy in v_copy:
        copy.start()
    x_copy = [
        pltpu.make_async_copy(src, dst, x_sem.at[i])
        for i, (src, dst) in enumerate(((x_ref, z_even), (xs_ref, z_odd)))
    ]
    for copy in x_copy:
        copy.start()
    if plan.late:
        z, y, x = plan.place(chip)
        for i in range(3):
            for t in range(plan.depth - 1):
                to = (section, plan.chip_at(lax.rem(z + 1 + t, plan.depth), y, x))
                push(
                    lines[i].at[t], line_land[i].at[t], l_send.at[i], l_recv.at[i], to
                ).start()
    scatter.begin(0, EARLY)
    filter_rows(plan, filt_ref, table, plan.f_rows, True)
    build_strips(plan, table, strip, True)
    if plan.layered:
        for t in range(1, levels):
            spread_g(t)
    acc_even[...] = jnp.zeros_like(acc_even)
    acc_odd[...] = jnp.zeros_like(acc_odd)
    if plan.layered:
        pltpu.make_async_copy(own_g, g_rows(0), z_recv.at[0]).wait()
        bytes_of(g_buf.at[:, pl.ds(0, half * levels * (plan.cols_in - 1)), :], g_recv)
    else:
        bytes_of(g_buf, g_recv)
    scatter.begin(EARLY)
    for phase in range(2):
        for i in range(plan.blocks):
            rows = slice(BLOCK * i, BLOCK * (i + 1))
            gt_buf[phase, :, rows] = g_buf[phase, rows, :].astype(F32).T.astype(BF)
    turn = (1 - 2 * section).astype(F32)
    half_ways = (((1,), (1,)), ((), ()))

    def piece_copies(k, tap, begin):
        per_block = jb // PIECE
        which = 2 * plan.filters + k if tap else section * plan.filters + my_group * plan.local + k
        start = (which * plan.cols_in + my_b) * per_block
        owner, row = start // plan.pieces, lax.rem(start, plan.pieces)
        first = jnp.minimum(plan.pieces - row, per_block)
        for to, at, base, count in ((owner, row, 0, first), (owner + 1, 0, first, per_block - first)):
            for size in sizes(plan):
                done = count // (2 * size) * (2 * size)
                rows = size * PIECE
                here = lax.rem(count // size, 2) == 1
                source = PIECE * (base + done)
                src = (
                    total_t.at[pl.ds(jb * k + source, rows), :]
                    if tap
                    else total_m.at[k, pl.ds(source, rows), :]
                )
                dst = dmaps_ref.at[
                    pl.ds(PIECE * (at + done), rows), pl.ds(pl.multiple_of(my_a * ia, ia), ia)
                ]
                if begin:

                    @pl.when(jnp.logical_and(here, to == dev))
                    def _():
                        pltpu.make_async_copy(src, dst, w_recv).start()

                @pl.when(jnp.logical_and(here, to != dev))
                def _():
                    copy = push(src, dst, w_send, w_recv, (to // chips, lax.rem(to, chips)))
                    if begin:
                        copy.start()
                    else:
                        copy.wait_send()

    def exchange(k):
        return push(give_m.at[k], take_m.at[k], m_send.at[k], m_recv.at[k], (1 - section, chip))

    def finish(k):
        exchange(k).wait()
        total_m[k] = (kept[k] + take_m[k].astype(F32)).astype(BF)
        if plan.routed:
            piece_copies(k, False, True)

    for copy in x_copy:
        copy.wait()
    x_even, x_odd = z_even[:, :jb], z_even[:, jb:]
    s_even, s_odd = z_odd[:, :jb], z_odd[:, jb:]
    for tap, (on_even, on_odd) in enumerate(((x_even, x_odd), (s_odd, x_even), (s_even, s_odd))):
        tap_grad = jnp.dot(gt_buf[0], on_even, preferred_element_type=F32) + jnp.dot(
            gt_buf[1], on_odd, preferred_element_type=F32
        )
        tap_grad = tap_grad.T
        kept_t[tap * jb : (tap + 1) * jb, :] = tap_grad
        give_t[tap * jb : (tap + 1) * jb, :] = tap_grad.astype(BF)
    tap_swap = push(give_t, take_t, t_send, t_recv, (1 - section, chip))
    tap_swap.start()
    for i in range(plan.blocks):
        rows = slice(BLOCK * i, BLOCK * (i + 1))
        from_even = lax.dot_general(
            g_buf[0, rows, :], tapw[...], half_ways, preferred_element_type=F32
        )
        from_odd = lax.dot_general(
            g_buf[1, rows, :], tapw[...], half_ways, preferred_element_type=F32
        )
        acc_even[rows, :jb] = from_even[:, :jb] + from_odd[:, jb : 2 * jb]
        acc_even[rows, jb : 2 * jb] = from_odd[:, :jb]
        acc_odd[rows, :jb] = from_even[:, 2 * jb :]
        acc_odd[rows, jb : 2 * jb] = from_even[:, jb : 2 * jb] + from_odd[:, 2 * jb :]

    def step(k, carry):
        slot = lax.rem(k, 2)
        from_even = rows_dot(g_buf[0], pq[k]).astype(BF)
        from_odd = rows_dot(g_buf[1], pq[k]).astype(BF)
        z_even[:, :jb] = from_even[:, :jb]
        z_even[:, jb:] = from_odd[:, :jb]
        z_odd[:, :jb] = from_odd[:, jb:]
        z_odd[:, jb:] = from_even[:, jb:]
        pltpu.make_async_copy(v_ref.at[k], v_buf.at[slot], v_sem.at[slot]).wait()
        grad = jnp.dot(gt_buf[0], v_buf[slot, 0], preferred_element_type=F32) + jnp.dot(
            gt_buf[1], v_buf[slot, 1], preferred_element_type=F32
        )
        grad = grad.T
        plus, minus = grad[:jb, :], grad[jb:, :] * turn
        kept[k] = plus + minus
        give_m[k] = (plus - minus).astype(BF)
        exchange(k).start()

        @pl.when(k + 2 < plan.local)
        def _():
            pltpu.make_async_copy(v_ref.at[k + 2], v_buf.at[slot], v_sem.at[slot]).start()

        for j in range(plan.blocks):
            rows = slice(BLOCK * j, BLOCK * (j + 1))
            depth = plan.length - BLOCK * j
            acc_even[rows, :] += jnp.dot(
                strip[0, k, :, :depth], z_even[BLOCK * j :, :], preferred_element_type=F32
            )
            out = jnp.dot(
                strip[1, k, :, :depth], z_odd[BLOCK * j :, :], preferred_element_type=F32
            )
            acc_even[rows, :jb] += out[:, :jb]
            acc_odd[rows, jb:] += out[:, jb:]

        @pl.when(k >= 1)
        def _():
            finish(k - 1)

        for turn_number in range(plan.depth + 1):
            at = plan.local // 2 - 1 + 3 * turn_number
            if at < plan.local:
                pl.when(k == at)(functools.partial(scatter.stage, turn_number))
        return carry

    lax.fori_loop(0, plan.local, step, 0)
    for i in range(plan.blocks):
        rows = slice(BLOCK * i, BLOCK * (i + 1))
        moved = acc_odd[BLOCK * i + 1 : BLOCK * (i + 1) + 1, :]
        both = (acc_even[rows, :] + moved).astype(BF)
        du_buf[0, rows, :] = both[:, :jb]
        du_buf[1, rows, :] = both[:, jb:]

        def give(r, carry, i=i):
            peer = BLOCK // half * i + r
            src = du_buf.at[:, pl.ds(half * peer, half), :]

            @pl.when(peer == chip)
            def _():
                pltpu.make_async_copy(src, land.at[chip], d_recv).start()

            @pl.when(peer != chip)
            def _():
                push(src, land.at[chip], d_send, d_recv, (section, peer)).start()

            return carry

        lax.fori_loop(0, BLOCK // half, give, 0)
    for turn_number in range(plan.depth + 1):
        if plan.local // 2 - 1 + 3 * turn_number >= plan.local:
            scatter.stage(turn_number)
    finish(plan.local - 1)
    tap_swap.wait()
    total_t[...] = (kept_t[...] + take_t[...].astype(F32)).astype(BF)
    if plan.routed:

        @pl.when(jnp.logical_and(section == 0, my_group == plan.groups - 1))
        def _():
            for tap in range(ORDER):
                piece_copies(tap, True, True)
    else:
        pltpu.sync_copy(total_m, dmap_ref)
        pltpu.sync_copy(total_t, dtap_ref)
    if plan.layered:
        bytes_of(g_buf.at[:, pl.ds(0, half * levels * (plan.cols_in - 1)), :], g_send)
        bytes_of(g_buf.at[:, pl.ds(0, half * (levels - 1)), :], z_send)
    else:
        bytes_of(g_buf.at[:, pl.ds(0, half * (chips - 1)), :], g_send)
    bytes_of(land, d_recv)
    for b in range(plan.cols_in):
        total = None
        for c in range(plan.groups):
            for a in range(plan.cols_out):
                term = land[plan.part_at(a, b, c)].astype(F32)
                total = term if total is None else total + term
        du_ref[:, :, b * jb : (b + 1) * jb] = total
    bytes_of(land.at[pl.ds(0, chips - 1)], d_send)
    scatter.end()
    if plan.late:
        core_zero = section == 0
        for i in range(3):
            bytes_of(line_land[i], l_recv.at[i])
            total = lines[i][plan.depth - 1].astype(F32)
            for t in range(plan.depth - 1):
                total = total + line_land[i][t].astype(F32)
            half1[i][...] = total
            bytes_of(line_land[i], l_send.at[i])
            crossing[i][...] = jnp.where(core_zero, half1[i][...], half0[i][...])
            push(crossing[i], arrived[i], e_send.at[i], e_recv.at[i], sibling).start()
        hidden = hidden_ref[...]
        factor = lax.rsqrt(jnp.mean(hidden * hidden, axis=-1, keepdims=True) + EPSILON)
        signal_grad = du_ref[...].reshape(plan.rows, plan.width)
        weighted = signal_grad * gains_ref[0:1, :]
        correction = jnp.mean(weighted * hidden, axis=-1, keepdims=True)
        hidden_grad = factor * weighted - hidden * factor * factor * factor * correction
        gain_buf[...] = gain_sums_ref[...]
        gain_buf[0:1, :] = jnp.sum(signal_grad * hidden * factor, axis=0, keepdims=True)
        per_tile = LANES * chips // plan.width

        def send_gain(step, carry):
            peer = lax.rem(dev + step, 2 * chips)
            tile = lax.rem(peer, chips) // per_tile
            push(
                gain_buf.at[:, pl.ds(pl.multiple_of(LANES * tile, LANES), LANES)],
                gain_land.at[dev],
                n_send,
                n_recv,
                (peer // chips, lax.rem(peer, chips)),
            ).start()
            return carry

        lax.fori_loop(1, 2 * chips, send_gain, 0)
        pltpu.make_async_copy(
            gain_buf.at[:, pl.ds(pl.multiple_of(LANES * (chip // per_tile), LANES), LANES)],
            gain_land.at[dev],
            n_recv,
        ).start()
        done_in = (mask_ref[...] * (dmid_ref[...] + hidden_grad)).astype(BF)
        row = lax.broadcasted_iota(jnp.int32, (plan.rows, plan.rows), 0)
        col = lax.broadcasted_iota(jnp.int32, (plan.rows, plan.rows), 1)
        order = jnp.where(col == 2 * lax.rem(row, half) + row // half, 1.0, 0.0).astype(BF)
        done_in = cols_dot(order, done_in).astype(BF)
        done_out = cols_dot(order, out_ref[...]).astype(BF)
        give_res[...] = jnp.where(core_zero, done_out, done_in)
        swap_res = push(give_res, res_ref.at[section], e_send.at[3], e_recv.at[3], sibling)
        swap_res.start()
        res_ref[section] = jnp.where(core_zero, done_in, done_out)
        for i in range(3):
            push(crossing[i], arrived[i], e_send.at[i], e_recv.at[i], sibling).wait()
        lane = lax.broadcasted_iota(jnp.int32, (gate_ref.shape[0], LANES), 1)
        low = lane < half
        kept_half = [jnp.where(core_zero, half0[i][...], half1[i][...]) for i in range(3)]
        for i, out in ((0, gate_ref), (1, up_ref)):
            came = arrived[i][...]
            first = jnp.where(core_zero, kept_half[i], came)
            second = jnp.where(core_zero, came, kept_half[i])
            for j in range(out.shape[1] // (2 * LANES)):
                one, two = (w[:, LANES * j : LANES * (j + 1)] for w in (first, second))
                at = 2 * LANES * j
                out[:, at : at + LANES] = jnp.where(low, one, pltpu.roll(two, half, 1))
                out[:, at + LANES : at + 2 * LANES] = jnp.where(
                    low, pltpu.roll(one, half, 1), two
                )
        part = half0[2].shape[0]
        came = arrived[2][...]
        down_ref[:part, :] = jnp.where(core_zero, kept_half[2], came)
        down_ref[part:, :] = jnp.where(core_zero, came, kept_half[2])
        swap_res.wait()
        bytes_of(gain_land, n_recv)
        gain_out[...] = jnp.sum(gain_land[...], axis=0)
        bytes_of(gain_land.at[pl.ds(0, 2 * chips - 1)], n_send)
    if plan.routed:

        def drain(k, carry):
            piece_copies(k, False, False)
            return carry

        lax.fori_loop(0, plan.local, drain, 0)

        @pl.when(jnp.logical_and(section == 0, my_group == plan.groups - 1))
        def _():
            for tap in range(ORDER):
                piece_copies(tap, True, False)

        bytes_of(dmaps_ref, w_recv)


def backward_call(plan, g, filt, v, pq, tapw, x, xs, grads, rest=()):
    chips, half, jb, ia = plan.chips, plan.half, plan.jb, plan.ia
    any_spec = pl.BlockSpec(memory_space=pl.ANY)
    vmem_spec = pl.BlockSpec(memory_space=pltpu.VMEM)
    dma = pltpu.SemaphoreType.DMA
    shapes = [g_part.shape[3:] for g_part in grads]
    rows, width = plan.rows, plan.width
    finish = []
    if plan.late:
        out_shape = [jax.ShapeDtypeStruct((2, rows, width), BF)]
        out_shape += [
            jax.ShapeDtypeStruct(shape, F32)
            for shape in (
                (shapes[0][0], plan.ff),
                (shapes[1][0], plan.ff),
                (2 * shapes[2][0], width),
                *shapes[3:],
                (8, LANES),
            )
        ]
        in_vmem = len(out_shape)
        out_shape.append(jax.ShapeDtypeStruct((plan.map_rows, width), BF))
        finish = [
            pltpu.VMEM((2, half, width), F32),
            pltpu.VMEM((8, width), F32),
            pltpu.VMEM((2 * chips, 8, LANES), F32),
            pltpu.VMEM((rows, width), BF),
        ]
        finish += [pltpu.VMEM(shape, F32) for shape in shapes[:3]] * 3
        finish += [dma((4,)), dma((4,)), dma, dma]
        finish += [pltpu.VMEM(shape, F32) for shape in shapes[:3]]
        finish += [pltpu.VMEM((plan.depth - 1,) + shape, BF) for shape in shapes[:3]]
        finish += [dma((3,)), dma((3,))]
    else:
        out_shape = [jax.ShapeDtypeStruct(shape, F32) for shape in shapes]
        out_shape.append(jax.ShapeDtypeStruct((2, half, width), F32))
        in_vmem = len(out_shape)
        out_shape.append(jax.ShapeDtypeStruct((plan.local, jb, ia), BF))
        out_shape.append(jax.ShapeDtypeStruct((ORDER * jb, ia), BF))
    return pl.pallas_call(
        functools.partial(backward_kernel, plan, len(grads)),
        out_shape=out_shape,
        in_specs=[vmem_spec, vmem_spec, any_spec, vmem_spec, vmem_spec, any_spec, any_spec]
        + [vmem_spec] * (len(grads) + len(rest)),
        out_specs=[vmem_spec] * in_vmem + [any_spec] * (len(out_shape) - in_vmem),
        scratch_shapes=finish
        + Scatter.scratch(plan, shapes)
        + Scatter.semaphores(plan, len(grads))
        + [
            pltpu.VMEM((2, plan.length, ia), BF),
            pltpu.VMEM((2, ia, plan.length), BF),
            pltpu.VMEM((2, plan.f_rows, plan.length + BLOCK), F32),
            pltpu.VMEM((2, plan.local, BLOCK, plan.length), BF),
            pltpu.VMEM((2, 2, plan.length, 2 * jb), BF),
            pltpu.VMEM((plan.length, 2 * jb), BF),
            pltpu.VMEM((plan.length, 2 * jb), BF),
            pltpu.VMEM((plan.length, 2 * jb), F32),
            pltpu.VMEM((plan.length + 8, 2 * jb), F32),
            pltpu.VMEM((plan.local, jb, ia), F32),
            pltpu.VMEM((plan.local, jb, ia), BF),
            pltpu.VMEM((plan.local, jb, ia), BF),
            pltpu.VMEM((plan.local, jb, ia), BF),
            pltpu.VMEM((ORDER * jb, ia), F32),
            pltpu.VMEM((ORDER * jb, ia), BF),
            pltpu.VMEM((ORDER * jb, ia), BF),
            pltpu.VMEM((ORDER * jb, ia), BF),
            pltpu.VMEM((2, plan.length, jb), BF),
            pltpu.VMEM((chips, 2, half, jb), BF),
            dma,
            dma,
            dma((2,)),
            dma((plan.local,)),
            dma((plan.local,)),
            dma,
            dma,
            dma,
            dma,
            dma,
            dma,
            dma((2,)),
            dma,
            dma((plan.depth,)),
        ],
        compiler_params=pltpu.CompilerParams(
            collective_id=3, has_side_effects=True, vmem_limit_bytes=VMEM_LIMIT
        ),
        name="spectral_backward",
    )(g, filt, v, pq, tapw, x, xs, *grads, *rest)

SWAPS = 7
EARLY = 1


def middle_kernel(plan, *refs):
    (
        conv_ref,
        hidden_ref,
        gains_ref,
        mask_ref,
        up_ref,
        up_pair,
        *stored,
    ) = refs[:14]
    (
        out_ref,
        g_ref,
        dmid_ref,
        gain_ref,
        gate0_g,
        up0_g,
        down0_g,
        gate1_g,
        up1_g,
        down1_g,
        proj_g,
        attn_g,
    ) = refs[14:26]
    held = refs[26:34]
    (
        pair0,
        pair1,
        give,
        take,
        gates,
        ups,
        acts,
        dgate,
        dup,
        window,
        kv,
        q_buf,
        probs,
        dkv,
        dn,
        back,
        back_land,
        down_land,
        att,
        dq_buf,
        proj_all,
        attn_all,
        proj_take,
        attn_take,
        load_sem,
        a_send,
        a_recv,
        send,
        recv,
        kv_send,
        kv_recv,
        bk_send,
        bk_recv,
        *extra,
    ) = refs[34:]
    chips, rows, width = plan.chips, plan.rows, plan.width
    section, chip = spot()
    sibling = (1 - section, chip)
    reach = WINDOW // rows
    span = (reach + 1) * rows
    layer0, (w_proj, w_out), layer1 = held[:3], held[3:5], held[5:]
    split, cut = 3 * plan.width // 2, plan.width // 2
    own_rows = [
        w_proj.at[pl.ds(pl.multiple_of(split * section, 16), split), :],
        w_out.at[pl.ds(pl.multiple_of(cut * section, 16), cut), :],
    ]
    homes = list(layer0) + own_rows + ([] if plan.late else list(layer1))
    loads = [
        pltpu.make_async_copy(a, b, load_sem.at[i]) for i, (a, b) in enumerate(zip(stored, homes))
    ]
    if plan.late:
        grads1, gather_send, gather_recv, scatter_send, scatter_recv = extra[:3], *extra[3:7]
        gather = Gather(plan, layer1, layer1, gather_send, gather_recv)
        held_loads = [
            pltpu.make_async_copy(src, dst, gather_recv.at[i // 2, i % 2])
            for i, (src, dst) in enumerate(gather.held_parts(stored[5:]))
        ]
        for load in held_loads:
            load.start()
    for load in loads:
        load.start()
    greet_everyone(chips)()
    passes = [
        push(stored[3 + i], own_rows[i], a_send.at[i], a_recv.at[i], sibling) for i in range(2)
    ]
    for copy in passes:
        copy.start()
    if plan.late:
        scatter = Scatter(
            plan, grads1, (gate1_g, up1_g, down1_g), extra[7:], scatter_send, scatter_recv, True
        )
        for load in held_loads:
            load.wait()
        gather.last_only()
    ff = plan.ff // 2
    own = slice(0, rows)
    second = slice(rows, 2 * rows)
    mask = mask_ref[...]

    def swap(number, src, dst):
        copy = push(src, dst, send.at[number], recv.at[number], sibling)
        copy.start()
        copy.wait()

    def norm(values, gain):
        factor = lax.rsqrt(jnp.mean(values * values, axis=-1, keepdims=True) + EPSILON)
        return values * factor * gain, factor

    def norm_back(values, factor, gain, upstream):
        weighted = upstream * gain
        gain_grad = jnp.sum(upstream * values * factor, axis=0, keepdims=True)
        correction = jnp.mean(weighted * values, axis=-1, keepdims=True)
        return factor * weighted - values * factor * factor * factor * correction, gain_grad

    def feed(layer, pair, weights, number):
        w_gate, w_up, w_down = (Flat(w) for w in weights)
        swap(number, pair.at[own], pair.at[second])
        for start in range(0, ff, BLOCK):
            cols = slice(start, start + BLOCK)
            gate_rows = flat_dot(pair[...], w_gate.columns(start, BLOCK))
            up_rows = flat_dot(pair[...], w_up.columns(start, BLOCK))
            gates[layer, :, cols] = gate_rows
            ups[layer, :, cols] = up_rows
            acts[layer, :, cols] = (gate_rows * jax.nn.sigmoid(gate_rows) * up_rows).astype(BF)
        part = flat_dot(acts[layer], w_down.all())
        give[number] = part[second].astype(BF)
        swap(number + 1, give.at[number], take.at[number])
        return part[own] + take[number].astype(F32)

    def feed_back(layer, pair, weights, grads, upstream_pair, number):
        w_gate, w_up, w_down = (Flat(w) for w in weights)
        gate_g, up_g, down_g = (Flat(w) for w in grads)
        turned = pair[...].astype(F32).T.astype(BF)
        for start in range(0, ff, BLOCK):
            cols = slice(start, start + BLOCK)
            active_grad = rows_dot(upstream_pair, w_down.rows(start, BLOCK))
            gate_rows, up_rows = gates[layer, :, cols], ups[layer, :, cols]
            sigmoid = jax.nn.sigmoid(gate_rows)
            slope = sigmoid * (1.0 + gate_rows * (1.0 - sigmoid))
            gate_grad = (active_grad * up_rows * slope).astype(BF)
            up_grad = (active_grad * gate_rows * sigmoid).astype(BF)
            dgate[:, cols] = gate_grad
            dup[:, cols] = up_grad
        for start in range(0, width, BLOCK):
            cols = slice(start, start + BLOCK)
            part = rows_dot(dgate[...], w_gate.rows(start, BLOCK)) + rows_dot(
                dup[...], w_up.rows(start, BLOCK)
            )
            give[number, :, cols] = part[second].astype(BF)
            att[:, cols] = part[own]
        copy = push(
            give.at[number], take.at[number], send.at[number], recv.at[number], sibling
        )
        copy.start()
        for start in range(0, ff, BLOCK):
            cols = slice(start, start + BLOCK)
            gate_g.put_columns(start, flat_dot(turned, dgate[:, cols]).astype(BF))
            up_g.put_columns(start, flat_dot(turned, dup[:, cols]).astype(BF))
            down_g.put_rows(
                start,
                flat_dot(acts[layer, :, cols].astype(F32).T.astype(BF), upstream_pair).astype(BF),
            )
        copy.wait()
        return att[...] + take[number].astype(F32)

    middle0 = hidden_ref[...] + conv_ref[...]
    normed, factor0 = norm(middle0, gains_ref[1:2, :])
    pair0[own] = normed.astype(BF)
    dmid_ref[...] = middle0
    for load in loads[:3]:
        load.wait()
    branch = feed(0, pair0, layer0, 0)
    passed = (mask * (dmid_ref[...] + branch)).astype(BF).astype(F32)

    normed, factor10 = norm(passed, gains_ref[2:3, :])
    inputs = normed.astype(BF)
    mine = slice(reach * rows, span)
    window[mine, :] = inputs

    layer, level = plan.layer, chip // plan.layer
    within = lax.rem(chip, layer)

    def slot(distance):
        return window.at[pl.ds((reach - distance) * rows, rows)]

    def ahead(distance):
        return push(
            window.at[mine],
            slot(distance),
            kv_send.at[distance - 1],
            kv_recv.at[distance - 1],
            (section, chip + distance),
        )

    def pass_on(place):
        distance = reach - (within - place)
        return push(
            slot(reach),
            slot(distance),
            kv_send.at[reach + place],
            kv_recv.at[distance - 1],
            (section, level * layer + place),
        )

    def goes_ahead(distance):
        if plan.layered and distance < reach:
            return within + distance < layer
        return chip + distance < chips

    def comes(distance):
        return chip >= distance

    for distance in range(reach, 0, -1):

        @pl.when(goes_ahead(distance))
        def _():
            ahead(distance).start()

        @pl.when(chip < distance)
        def _():
            window[(reach - distance) * rows : (reach - distance + 1) * rows, :] = jnp.zeros(
                (rows, width), BF
            )

    half = plan.half
    row = lax.broadcasted_iota(jnp.int32, (rows, span), 0)
    col = lax.broadcasted_iota(jnp.int32, (rows, span), 1)
    inner = lax.rem(col, rows)
    q_place = 2 * lax.rem(row, half) + row // half
    k_place = (col // rows - reach) * rows + 2 * lax.rem(inner, half) + inner // half
    distance_rows = q_place - k_place
    allowed = (
        (k_place + chip * rows >= 0) & (distance_rows >= 0) & (distance_rows < WINDOW)
    )
    lane = lax.broadcasted_iota(jnp.int32, (rows, LANES), 1)
    low = lane < HEAD_DIM
    scale = HEAD_DIM ** (-0.5)
    zero = jnp.zeros((rows, LANES), BF)
    for load in loads[3:5]:
        load.wait()
    for copy in passes:
        copy.wait()
    w_query, w_key, w_value = (w_proj.at[pl.ds(part * width, width)] for part in range(3))
    q_buf[...] = flat_dot(inputs, w_query[...]).astype(BF)
    kv[mine, :width] = flat_dot(inputs, w_key[...]).astype(BF)
    kv[mine, width:] = flat_dot(inputs, w_value[...]).astype(BF)

    def arrived(distance):
        push(
            window.at[mine],
            slot(distance),
            kv_send.at[distance - 1],
            kv_recv.at[distance - 1],
            sibling,
        ).wait_recv()

    pl.when(comes(reach))(functools.partial(arrived, reach))
    if plan.layered:
        for place in range(layer - 1):

            @pl.when(jnp.logical_and(level > 0, place < within))
            def _():
                pass_on(place).start()

    for distance in range(1, reach):
        pl.when(comes(distance))(functools.partial(arrived, distance))
    earlier = slice(0, reach * rows)
    kv[earlier, :width] = flat_dot(window[earlier, :], w_key[...]).astype(BF)
    kv[earlier, width:] = flat_dot(window[earlier, :], w_value[...]).astype(BF)

    for pair in range(width // LANES):
        lanes = slice(LANES * pair, LANES * (pair + 1))
        keys, values = kv[:, lanes], kv[:, width + LANES * pair : width + LANES * (pair + 1)]
        parts = []
        for side in range(2):
            here = low if side == 0 else jnp.logical_not(low)
            queries = jnp.where(here, q_buf[:, lanes], zero)
            scores = rows_dot(queries, keys) * scale
            scores = jnp.where(allowed, scores, BIG_NEGATIVE)
            weights = jnp.exp(scores - jnp.max(scores, axis=-1, keepdims=True))
            weights = weights / jnp.sum(weights, axis=-1, keepdims=True)
            probs[2 * pair + side] = weights
            parts.append(flat_dot(weights.astype(BF), values))
        att[:, lanes] = jnp.where(low, parts[0], parts[1])
    attended = att[...].astype(BF)
    middle1 = passed + flat_dot(attended, w_out[...])

    if plan.late:
        gather.end(True)
    for load in loads[5:]:
        load.wait()
    normed, factor11 = norm(middle1, gains_ref[3:4, :])
    pair1[own] = normed.astype(BF)
    branch = feed(1, pair1, layer1, 2)
    out_ref[...] = (mask * (middle1 + branch)).astype(BF)
    if not plan.late:
        grads1 = (gate1_g, up1_g, down1_g)
    dnormed = feed_back(1, pair1, layer1, grads1, up_pair[...], 4)
    if plan.late:
        scatter.begin(0, plan.depth // 2)
    dmiddle, gain11 = norm_back(middle1, factor11, gains_ref[3:4, :], dnormed)
    dmiddle = up_ref[...] + dmiddle
    gain_ref[3:4, :] = gain11

    dy = dmiddle.astype(BF)
    attn_all[...] = flat_dot(attended.astype(F32).T.astype(BF), dy).astype(BF)
    datt = rows_dot(dy, w_out[...]).astype(BF)
    for pair in range(width // LANES):
        lanes = slice(LANES * pair, LANES * (pair + 1))
        value_lanes = slice(width + LANES * pair, width + LANES * (pair + 1))
        keys, values = kv[:, lanes], kv[:, value_lanes]
        dq_parts, key_grad, value_grad = [], None, None
        for side in range(2):
            here = low if side == 0 else jnp.logical_not(low)
            queries = jnp.where(here, q_buf[:, lanes], zero)
            upstream = jnp.where(here, datt[:, lanes], zero)
            weights = probs[2 * pair + side]
            grad = rows_dot(upstream, values)
            total = jnp.sum(weights * grad, axis=-1, keepdims=True)
            dscores = weights * (grad - total)
            dq_parts.append(flat_dot(dscores.astype(BF), keys))
            one = flat_dot(dscores.T.astype(BF), queries)
            two = flat_dot(weights.T.astype(BF), upstream)
            key_grad = one if key_grad is None else key_grad + one
            value_grad = two if value_grad is None else value_grad + two
        dq_buf[:, lanes] = (jnp.where(low, dq_parts[0], dq_parts[1]) * scale).astype(BF)
        dkv[:, lanes] = (key_grad * scale).astype(BF)
        dkv[:, value_lanes] = value_grad.astype(BF)
    back[...] = (
        rows_dot(dkv[earlier, :width], w_key[...]) + rows_dot(dkv[earlier, width:], w_value[...])
    ).astype(BF)

    def behind(distance, peer):
        return push(
            back.at[pl.ds((reach - distance) * rows, rows)],
            back_land.at[distance - 1],
            bk_send.at[distance - 1],
            bk_recv.at[distance - 1],
            (section, peer),
        )

    def to_place(place):
        distance = lax.rem(within - place + layer, layer)
        return push(
            back.at[pl.ds((reach - distance) * rows, rows)],
            back_land.at[within],
            bk_send.at[place],
            bk_recv.at[within],
            (section, level * layer + place),
        )

    def came_from(place):
        push(
            back_land.at[place],
            back_land.at[place],
            bk_send.at[place],
            bk_recv.at[place],
            sibling,
        ).wait_recv()

    def down():
        return push(
            back.at[pl.ds(0, rows)],
            down_land,
            bk_send.at[reach],
            bk_recv.at[reach],
            (section, chip - layer),
        )

    if plan.layered:
        for place in range(layer - 1, -1, -1):

            @pl.when(jnp.logical_and(place > within, level > 0))
            def _():
                to_place(place).start()

        for place in range(layer):

            @pl.when(place < within)
            def _():
                to_place(place).start()

    else:
        for distance in range(1, reach + 1):

            @pl.when(chip >= distance)
            def _():
                behind(distance, chip - distance).start()

    if plan.late:
        scatter.begin(plan.depth // 2)
    dn[...] = (
        rows_dot(dq_buf[...], w_query[...])
        + rows_dot(dkv[mine, :width], w_key[...])
        + rows_dot(dkv[mine, width:], w_value[...])
    )
    if plan.layered:
        for place in range(layer - 1):

            @pl.when(jnp.logical_and(place < within, level > 0))
            def _():
                came_from(place)
                below = back[:rows, :].astype(F32) + back_land[place].astype(F32)
                back[:rows, :] = below.astype(BF)

        @pl.when(level > 0)
        def _():
            down().start()

        for place in range(1, layer):

            @pl.when(place > within)
            def _():
                came_from(place)
                dn[...] += back_land[place].astype(F32)

        @pl.when(level < plan.depth - 1)
        def _():
            down().wait_recv()
            dn[...] += down_land[...].astype(F32)

    else:
        for distance in range(1, reach + 1):

            @pl.when(chip + distance < chips)
            def _():
                behind(distance, chip).wait_recv()
                dn[...] += back_land[distance - 1].astype(F32)

    dnormed = dn[...]
    dpassed, gain10 = norm_back(passed, factor10, gains_ref[2:3, :], dnormed)
    gain_ref[2:3, :] = gain10
    dpassed = (dmiddle + dpassed).astype(BF).astype(F32)

    upstream0 = mask * dpassed
    give[5] = upstream0.astype(BF)
    copy = push(give.at[5], take.at[5], send.at[5], recv.at[5], sibling)
    copy.start()
    turned = window[...].astype(F32).T.astype(BF)
    proj_all[:width, :] = flat_dot(turned[:, reach * rows :], dq_buf[...]).astype(BF)
    proj_all[width : 2 * width, :] = flat_dot(turned, dkv[:, :width]).astype(BF)
    proj_all[2 * width :, :] = flat_dot(turned, dkv[:, width:]).astype(BF)
    copy.wait()
    crossing = [
        push(
            whole.at[pl.ds(pl.multiple_of(size * (1 - section), 16), size), :],
            land,
            a_send.at[2 + i],
            a_recv.at[2 + i],
            sibling,
        )
        for i, (whole, land, size) in enumerate(
            ((proj_all, proj_take, split), (attn_all, attn_take, cut))
        )
    ]
    for cross in crossing:
        cross.start()
    if plan.late:
        scatter.stage(0)
    both = jnp.concatenate([give[5], take[5]], 0)
    dnormed = feed_back(0, pair0, layer0, (gate0_g, up0_g, down0_g), both, 6)
    if plan.late:
        for number in range(1, plan.depth + 1):
            scatter.stage(number)
    middle0 = dmid_ref[...]
    dmiddle, gain01 = norm_back(middle0, factor0, gains_ref[1:2, :], dnormed)
    gain_ref[1:2, :] = gain01
    dmiddle = upstream0 + dmiddle
    dmid_ref[...] = dmiddle
    g_ref[...] = dmiddle.astype(BF)
    for cross in crossing:
        cross.wait()
    for whole, land, size, out in (
        (proj_all, proj_take, split, proj_g),
        (attn_all, attn_take, cut, attn_g),
    ):
        own_part = whole[pl.ds(pl.multiple_of(size * section, 16), size), :]
        out[...] = (own_part.astype(F32) + land[...].astype(F32)).astype(BF)
    if plan.late:
        scatter.end()

    for distance in range(1, reach + 1):

        @pl.when(goes_ahead(distance))
        def _():
            ahead(distance).wait_send()

    if plan.layered:
        for place in range(layer):

            @pl.when(jnp.logical_and(level > 0, place < within))
            def _():
                pass_on(place).wait_send()

            @pl.when((place < within) | ((place > within) & (level > 0)))
            def _():
                to_place(place).wait_send()

        @pl.when(level > 0)
        def _():
            down().wait_send()

    else:
        for distance in range(1, reach + 1):

            @pl.when(chip >= distance)
            def _():
                behind(distance, chip).wait_send()


def middle_call(plan, conv, hidden, gains, mask, upstream, pair, stored):
    rows, width = plan.rows, plan.width
    reach = WINDOW // rows
    ff = plan.ff // 2
    any_spec = pl.BlockSpec(memory_space=pl.ANY)
    vmem_spec = pl.BlockSpec(memory_space=pltpu.VMEM)
    dma = pltpu.SemaphoreType.DMA
    layer = [(width, ff), (width, ff), (ff, width)]
    grid = (plan.depth, plan.side, plan.side)
    chips = plan.chips
    spread = [grid + (a // chips, b) for a, b in layer]
    held = layer + [(3 * width, width), (width, width)] + (spread if plan.late else layer)
    split, cut = 3 * width // 2, width // 2
    extra = []
    if plan.late:
        extra = [pltpu.VMEM(w, BF) for w in spread]
        extra += Gather.semaphores(plan, 3) + Scatter.semaphores(plan, 3)
        extra += Scatter.scratch(plan, [w[3:] for w in spread])
    shapes = [
        ((rows, width), BF),
        ((rows, width), BF),
        ((rows, width), F32),
        ((8, width), F32),
    ]
    shapes += [(w, BF) for w in layer]
    shapes += [((plan.depth,) + w[3:] if plan.late else v, BF) for v, w in zip(layer, spread)]
    shapes += [((split, width), BF), ((cut, width), BF)]
    return pl.pallas_call(
        functools.partial(middle_kernel, plan),
        out_shape=[jax.ShapeDtypeStruct(s, d) for s, d in shapes],
        in_specs=[vmem_spec] * 6 + [any_spec] * 8,
        out_specs=[vmem_spec] * len(shapes),
        scratch_shapes=[pltpu.VMEM(w, BF) for w in held]
        + [
            pltpu.VMEM((2 * rows, width), BF),
            pltpu.VMEM((2 * rows, width), BF),
            pltpu.VMEM((SWAPS, rows, width), BF),
            pltpu.VMEM((SWAPS, rows, width), BF),
            pltpu.VMEM((2, 2 * rows, ff), F32),
            pltpu.VMEM((2, 2 * rows, ff), F32),
            pltpu.VMEM((2, 2 * rows, ff), BF),
            pltpu.VMEM((2 * rows, ff), BF),
            pltpu.VMEM((2 * rows, ff), BF),
            pltpu.VMEM(((reach + 1) * rows, width), BF),
            pltpu.VMEM(((reach + 1) * rows, 2 * width), BF),
            pltpu.VMEM((rows, width), BF),
            pltpu.VMEM((width // HEAD_DIM, rows, (reach + 1) * rows), F32),
            pltpu.VMEM(((reach + 1) * rows, 2 * width), BF),
            pltpu.VMEM((rows, width), F32),
            pltpu.VMEM((reach * rows, width), BF),
            pltpu.VMEM((reach, rows, width), BF),
            pltpu.VMEM((rows, width), BF),
            pltpu.VMEM((rows, width), F32),
            pltpu.VMEM((rows, width), BF),
            pltpu.VMEM((3 * width, width), BF),
            pltpu.VMEM((width, width), BF),
            pltpu.VMEM((split, width), BF),
            pltpu.VMEM((cut, width), BF),
            dma((8,)),
            dma((4,)),
            dma((4,)),
            dma((SWAPS,)),
            dma((SWAPS,)),
            dma((2 * reach,)),
            dma((reach,)),
            dma((reach + 1,)),
            dma((reach + 1,)),
        ]
        + extra,
        compiler_params=pltpu.CompilerParams(
            collective_id=5, has_side_effects=True, vmem_limit_bytes=VMEM_LIMIT
        ),
        name="middle",
    )(conv, hidden, gains, mask, upstream, pair, *stored)


def swapped(block):
    return lax.ppermute(block, "section", [(0, 1), (1, 0)])


def norm_backward(values, factor, weights, upstream):
    weighted = upstream * weights
    gain_grad = jnp.sum(upstream * values * factor, axis=0)
    correction = jnp.mean(weighted * values, axis=-1, keepdims=True)
    return (factor * weighted - values * factor * factor * factor * correction, gain_grad)


def body(
    io_pair, lengths, filters, stu_maps, attn_proj, attn_out, norm_gains, mlp_gate, mlp_up, mlp_down
):
    chips = lax.axis_size("seq")
    section, chip = spot()
    core_zero = section == 0
    tok_rows = io_pair.shape[2]
    width = io_pair.shape[3]
    half = tok_rows // 2
    ff = mlp_gate.shape[2]
    ff_half = mlp_down.shape[1] // 2
    plan = Plan(chips, tok_rows, width, filters.shape[1], stu_maps.shape[0], ff)

    def join_phases(rows):
        return rows.reshape(2, half, width).swapaxes(0, 1).reshape(rows.shape)

    my_a, my_b = plan.a_of(chip), plan.b_of(chip)
    my_group = chip // (plan.cols_out * plan.cols_in)
    if plan.routed:
        maps = [stu_maps]
    else:
        whole = lax.all_gather(stu_maps, ("section", "seq"), axis=0, tiled=True)
        whole = lax.dynamic_slice(
            whole.reshape(-1, width, width),
            (0, my_b * plan.jb, my_a * plan.ia),
            (whole.shape[0] // width, plan.jb, plan.ia),
        )
        pair = whole[: 2 * plan.filters].reshape(2, plan.filters, plan.jb, plan.ia)
        pair = lax.dynamic_slice_in_dim(pair, my_group * plan.local, plan.local, 1)
        taps = jnp.where(my_group == 0, whole[2 * plan.filters :], 0).astype(BF)
        maps = [
            jnp.where(core_zero, pair[0], pair[1]),
            jnp.where(core_zero, pair[1], pair[0]),
            taps.reshape(-1, plan.ia),
        ]

    gate, up = mlp_gate[0], mlp_up[0]
    if not plan.pick_here:
        gate, up = (
            jnp.transpose(w.reshape(w.shape[0], chips, 2, ff_half), (2, 0, 1, 3)).reshape(
                2, w.shape[0], ff // 2
            )
            for w in (gate, up)
        )
    results = forward_call(
        plan,
        io_pair[0],
        norm_gains[0],
        filters,
        lengths,
        [gate, up, mlp_down[0], attn_proj, attn_out],
        maps,
    )
    flat = 5 if plan.late else 8
    weights = [w.reshape(-1, w.shape[-1]) for w in results[:flat]] + list(results[flat:8])
    conv, hidden, upstream1, grad_pair, gains, mask_rows = results[8:14]
    v, pq, tapw, x_all, xs_all, filt = results[14:]
    block_out, g, middle0_grad, gain_sums, *grads = middle_call(
        plan,
        conv.reshape(tok_rows, width),
        hidden,
        gains,
        mask_rows,
        upstream1,
        grad_pair,
        weights,
    )
    mlp0_grads, half1, attn_grads = grads[:3], grads[3:6], grads[6:]
    gain01, gain10, gain11 = gain_sums[1], gain_sums[2], gain_sums[3]
    g = g.reshape(2, half, width)
    grid = (plan.depth, plan.side, plan.side)
    blocks0 = [w.reshape(grid + (w.shape[0] // chips, w.shape[1])) for w in mlp0_grads]
    blocks1 = [w.reshape(grid + (w.shape[0] // chips, w.shape[1])) for w in attn_grads]
    if plan.late:
        result, gate_out, up_out, down_out, proj_out, out_out, gain_tile, maps_out = backward_call(
            plan,
            g,
            filt,
            v,
            pq,
            tapw,
            x_all,
            xs_all,
            blocks0 + blocks1,
            [hidden, gains, mask_rows, middle0_grad, block_out, gain_sums, *half1],
        )
        cols = width // chips
        gain_out = lax.dynamic_slice(
            gain_tile, (2 * section, (chip % (LANES // cols)) * cols), (2, cols)
        )
        return (
            result[None],
            maps_out.astype(F32),
            proj_out,
            out_out,
            gain_out[None],
            gate_out[None],
            up_out[None],
            down_out[None],
        )
    results = backward_call(plan, g, filt, v, pq, tapw, x_all, xs_all, blocks0)
    half0, results = results[:3], results[3:]
    attn_sums = [
        lax.psum_scatter(
            w.reshape((chips,) + w.shape[3:]), "seq", scatter_dimension=0, tiled=False
        )
        for w in blocks1
    ]
    half1 = [
        lax.psum_scatter(
            w.reshape(chips, -1, w.shape[-1]), "seq", scatter_dimension=0, tiled=False
        )
        for w in half1
    ]
    signal_grad = results[0].reshape(tok_rows, width)
    piece, tap_piece = (r.astype(F32) for r in results[1:])
    full = jnp.zeros((2, plan.filters, width, width), F32)
    full = lax.dynamic_update_slice(
        full,
        piece[None],
        (section, my_group * plan.local, my_b * plan.jb, my_a * plan.ia),
    )
    tap_piece = jnp.where(core_zero & (my_group == 0), tap_piece, 0.0)
    tap_full = lax.dynamic_update_slice(
        jnp.zeros((ORDER, width, width), F32),
        tap_piece.reshape(ORDER, plan.jb, plan.ia),
        (0, my_b * plan.jb, my_a * plan.ia),
    )
    full = jnp.concatenate([full.reshape(-1, width), tap_full.reshape(-1, width)], 0)
    maps_grad = lax.psum_scatter(full, ("section", "seq"), scatter_dimension=0, tiled=True)
    spectral_factor = lax.rsqrt(jnp.mean(hidden * hidden, axis=-1, keepdims=True) + EPSILON)
    hidden_grad, gain00 = norm_backward(hidden, spectral_factor, gains[0], signal_grad)
    inputs_grad = (mask_rows * (middle0_grad + hidden_grad)).astype(BF)

    proj_out, out_out = (w.astype(F32) for w in attn_sums)
    outs = []
    for index in range(3):
        zero, one = half0[index].astype(BF), half1[index].astype(BF)
        keep = jnp.where(core_zero, zero, one)
        take = swapped(jnp.where(core_zero, one, zero))
        low = jnp.where(core_zero, keep, take).astype(F32)
        high = jnp.where(core_zero, take, keep).astype(F32)
        if index < 2:
            rows = low.shape[0]
            joined = jnp.stack(
                [low.reshape(rows, chips, ff_half), high.reshape(rows, chips, ff_half)], 2
            ).reshape(rows, ff)
        else:
            joined = jnp.concatenate([low, high], 0)
        outs.append(joined[None])

    gain_parts = jnp.stack([jnp.stack([gain00, gain01]), jnp.stack([gain10, gain11])])
    gain_cols = width // chips
    tiles = jnp.transpose(gain_parts.reshape(2, 2, chips, gain_cols), (0, 2, 1, 3))
    tiles = jnp.pad(
        tiles.reshape(2 * chips, 2, gain_cols), ((0, 0), (0, 6), (0, LANES - gain_cols))
    )
    done_in, done_out = join_phases(inputs_grad), join_phases(block_out)
    taken, landed = exit_call(chips, jnp.where(core_zero, done_out, done_in), tiles)
    first = jnp.where(core_zero, done_in, taken)
    second = jnp.where(core_zero, taken, done_out)
    result_pair = jnp.stack([first, second])[None]
    gain_out = jnp.sum(landed, axis=0)[None, :2, :gain_cols]
    return (result_pair, maps_grad, proj_out, out_out, gain_out, outs[0], outs[1], outs[2])


def solution(mesh):
    placed = (
        P("section", None, "seq", None),
        P(),
        P("seq", None),
        P(("section", "seq"), None),
        P(("section", "seq"), None),
        P(("section", "seq"), None),
        P("section", None, "seq"),
        P("section", "seq", None),
        P("section", "seq", None),
        P("section", "seq", None),
    )
    return jax.shard_map(
        body,
        mesh=mesh,
        in_specs=placed,
        out_specs=(
            P("section", None, "seq", None),
            P(("section", "seq"), None),
            P(("section", "seq"), None),
            P(("section", "seq"), None),
            P("section", None, "seq"),
            P("section", "seq", None),
            P("section", "seq", None),
            P("section", "seq", None),
        ),
        check_vma=False,
    )
```

```python
import functools
import math

import jax
import jax.numpy as jnp
from jax import lax
from jax.experimental import pallas as pl
from jax.experimental.pallas import tpu as pltpu
from jax.sharding import PartitionSpec as P

ORDER = 3
HEAD_DIM = 64
WINDOW = 512
EPSILON = 1e-05
BIG_NEGATIVE = -1e30
MESH = pl.DeviceIdType.MESH
BF = jnp.bfloat16
F32 = jnp.float32
LANES = 128
BLOCK = 256
PIECE = 16
VMEM_LIMIT = 63 * 1024 * 1024


class Plan:
    def __init__(self, chips, tok_rows, width, filter_count, map_rows, ff):
        self.chips = chips
        self.rows = tok_rows
        self.half = tok_rows // 2
        self.width = width
        self.filters = filter_count
        self.cols_in = 4
        self.cols_out = max(1, math.isqrt(chips // 4))
        self.groups = chips // (self.cols_in * self.cols_out)
        self.local = filter_count // self.groups
        self.length = chips * self.half
        self.blocks = self.length // BLOCK
        self.jb = width // self.cols_in
        self.ia = width // self.cols_out
        self.map_rows = map_rows
        self.routed = map_rows % PIECE == 0
        self.pieces = map_rows // PIECE
        self.f_rows = -(-self.local // 16) * 16
        self.batch = 4 if self.local % 4 == 0 else 2
        self.ff = ff
        self.pick_here = ff // chips == LANES
        self.late = self.pick_here and self.routed
        self.routed = self.late
        self.side = max(1, math.isqrt(chips // 4))
        self.depth = chips // (self.side * self.side)
        self.layer = self.side * self.side
        self.layered = self.layer * tok_rows == WINDOW

    def place(self, chip):
        return (
            chip // (self.side * self.side),
            lax.rem(chip // self.side, self.side),
            lax.rem(chip, self.side),
        )

    def a_of(self, chip):
        return lax.rem(chip // self.cols_in, self.cols_out)

    def b_of(self, chip):
        return lax.rem(chip, self.cols_in)

    def part_at(self, a, b, c):
        return b + self.cols_in * (a + self.cols_out * c)

    def chip_at(self, z, y, x):
        return (z * self.side + y) * self.side + x

    def routes(self, rows, index=0):
        if rows % (2 * PIECE) == 0:
            return [(0, rows // 2, True), (rows // 2, rows // 2, False)]
        return [(0, rows, index % 2 == 0)]


def spot():
    return lax.axis_index("section"), lax.axis_index("seq")


def greet_everyone(chips):
    section, chip = spot()
    me = section * chips + chip
    barrier = pltpu.get_barrier_semaphore()

    def one(step, carry):
        peer = lax.rem(me + step, 2 * chips)
        pl.semaphore_signal(
            barrier, inc=1, device_id=(peer // chips, lax.rem(peer, chips)), device_id_type=MESH
        )
        return carry

    lax.fori_loop(1, 2 * chips, one, 0)

    def wait():
        pl.semaphore_wait(barrier, 2 * chips - 1)

    return wait


def push(src, dst, send, recv, target):
    return pltpu.make_async_remote_copy(
        src_ref=src,
        dst_ref=dst,
        send_sem=send,
        recv_sem=recv,
        device_id=target,
        device_id_type=MESH,
    )


def bytes_of(ref, sem):
    pltpu.make_async_copy(ref, ref, sem).wait()


def rows_dot(left, right):
    return lax.dot_general(left, right, (((1,), (1,)), ((), ())), preferred_element_type=F32)


def cols_dot(left, right):
    return lax.dot_general(left, right, (((0,), (0,)), ((), ())), preferred_element_type=F32)


def flat_dot(left, right):
    return jnp.dot(left, right, preferred_element_type=F32)


class Flat:
    def __init__(self, ref):
        self.ref = ref
        self.split = len(ref.shape) == 5
        if self.split:
            depth, side, _, rows, _ = ref.shape
            self.plane = side * side * rows

    def columns(self, start, count):
        sl = slice(start, start + count)
        if self.split:
            return self.ref[:, :, :, :, sl].reshape(-1, count)
        return self.ref[:, sl]

    def rows(self, start, count):
        if self.split:
            sl = slice(start // self.plane, (start + count) // self.plane)
            return self.ref[sl].reshape(count, self.ref.shape[4])
        return self.ref[start : start + count, :]

    def all(self):
        return self.ref[...].reshape(-1, self.ref.shape[-1])

    def put_columns(self, start, value):
        sl = slice(start, start + value.shape[1])
        if self.split:
            shape = self.ref.shape[:4] + (value.shape[1],)
            self.ref[:, :, :, :, sl] = value.reshape(shape)
        else:
            self.ref[:, sl] = value

    def put_rows(self, start, value):
        count = value.shape[0]
        if self.split:
            sl = slice(start // self.plane, (start + count) // self.plane)
            self.ref[sl] = value.reshape((count // self.plane,) + self.ref.shape[1:])
        else:
            self.ref[start : start + count, :] = value


class Gather:
    def __init__(self, plan, shards, outs, send, recv):
        self.plan, self.shards, self.outs = plan, shards, outs
        self.send, self.recv = send, recv
        self.section, chip = spot()
        self.z, self.y, self.x = plan.place(chip)

    @staticmethod
    def semaphores(plan, count):
        return [
            pltpu.SemaphoreType.DMA((count, 5)),
            pltpu.SemaphoreType.DMA((count, 5 * plan.depth)),
        ]

    def to(self, z, y, x):
        return self.section, self.plan.chip_at(z, y, x)

    def across(self, step, along_x):
        side = self.plan.side
        if along_x:
            return self.to(self.z, self.y, lax.rem(self.x + step, side))
        return self.to(self.z, lax.rem(self.y + step, side), self.x)

    def routes(self, i):
        for number, (start, rows, x_first) in enumerate(self.plan.routes(self.outs[i].shape[3], i)):
            yield number, x_first, self.outs[i], pl.ds(start, rows)

    def level(self, t):
        return lax.rem(self.z - t + self.plan.depth, self.plan.depth)

    def begin(self):
        plan = self.plan
        for i, shard in enumerate(self.shards):
            home = self.outs[i].at[self.z, self.y, self.x]
            for step in range(1, plan.depth):
                z = lax.rem(self.z + step, plan.depth)
                push(
                    shard, home, self.send.at[i, 0], self.recv.at[i, step], self.to(z, self.y, self.x)
                ).start()
            pltpu.make_async_copy(shard, home, self.recv.at[i, 0]).start()
        self.second(0)

    def second(self, t):
        plan = self.plan
        for i, shard in enumerate(self.shards):
            z = self.level(t)
            if t > 0:
                bytes_of(self.outs[i].at[z, self.y, self.x], self.recv.at[i, t])
            for number, x_first, out, sl in self.routes(i):
                dst = out.at[z, self.y, self.x, sl]
                src = shard.at[sl] if t == 0 else dst
                for step in range(1, plan.side):
                    push(
                        src,
                        dst,
                        self.send.at[i, 1 + number],
                        self.recv.at[i, (1 + number) * plan.depth + t],
                        self.across(step, x_first),
                    ).start()

    def hand_over(self):
        plan, side = self.plan, self.plan.side
        for i, shard in enumerate(self.shards):
            pltpu.make_async_copy(
                shard, self.outs[i].at[self.z, self.y, self.x], self.recv.at[i, 0]
            ).wait()
            bytes_of(self.outs[i].at[pl.ds(0, plan.depth - 1), 0, 0], self.send.at[i, 0])
            for number, x_first, out, sl in self.routes(i):
                for t in range(plan.depth):
                    bytes_of(
                        out.at[0, 0, pl.ds(0, side - 1), sl],
                        self.recv.at[i, (1 + number) * plan.depth + t],
                    )
                bytes_of(out.at[:, 0, pl.ds(0, side - 1), sl], self.send.at[i, 1 + number])

    def held_parts(self, whole):
        for i, source in enumerate(whole):
            for number, x_first, out, sl in self.routes(i):
                if x_first:
                    yield source.at[:, self.y, :, sl], out.at[:, self.y, :, sl]
                else:
                    yield source.at[:, :, self.x, sl], out.at[:, :, self.x, sl]

    def last_only(self):
        plan, side = self.plan, self.plan.side
        for t in range(plan.depth):
            z = self.level(t)
            for i in range(len(self.shards)):
                for number, x_first, out, sl in self.routes(i):
                    src = out.at[z, self.y, :, sl] if x_first else out.at[z, :, self.x, sl]
                    for step in range(1, side):
                        push(
                            src,
                            src,
                            self.send.at[i, 3 + number],
                            self.recv.at[i, (3 + number) * plan.depth + t],
                            self.across(step, not x_first),
                        ).start()

    def third(self, t):
        plan, side = self.plan, self.plan.side
        for i, shard in enumerate(self.shards):
            z = self.level(t)
            if t == 0:
                pltpu.make_async_copy(
                    shard, self.outs[i].at[z, self.y, self.x], self.recv.at[i, 0]
                ).wait()
            for number, x_first, out, sl in self.routes(i):
                sem = self.recv.at[i, (1 + number) * plan.depth + t]
                if x_first:
                    bytes_of(out.at[z, self.y, pl.ds(0, side - 1), sl], sem)
                    src = out.at[z, self.y, :, sl]
                else:
                    bytes_of(out.at[z, pl.ds(0, side - 1), self.x, sl], sem)
                    src = out.at[z, :, self.x, sl]
                for step in range(1, side):
                    push(
                        src,
                        src,
                        self.send.at[i, 3 + number],
                        self.recv.at[i, (3 + number) * plan.depth + t],
                        self.across(step, not x_first),
                    ).start()

    def end(self, last_only=False):
        plan, side = self.plan, self.plan.side
        for i in range(len(self.shards)):
            if not last_only:
                bytes_of(self.outs[i].at[pl.ds(0, plan.depth - 1), 0, 0], self.send.at[i, 0])
            for number, x_first, out, sl in self.routes(i):
                if not last_only:
                    bytes_of(out.at[:, 0, pl.ds(0, side - 1), sl], self.send.at[i, 1 + number])
                for t in range(plan.depth):
                    bytes_of(
                        out.at[0, :, pl.ds(0, side - 1), sl],
                        self.recv.at[i, (3 + number) * plan.depth + t],
                    )
                bytes_of(out.at[:, :, pl.ds(0, side - 1), sl], self.send.at[i, 3 + number])

    def stage(self, number):
        if number > 0:
            self.third(number - 1)
        if 0 <= number < self.plan.depth - 1:
            self.second(number + 1)


class Scatter:
    @staticmethod
    def scratch(plan, shapes):
        refs = []
        for index, (rows, cols) in enumerate(shapes):
            for _, part, _ in plan.routes(rows, index):
                for lead in (
                    (plan.depth, plan.side - 1, plan.side),
                    (plan.depth, plan.side),
                    (plan.depth, plan.side - 1),
                    (plan.depth,),
                    (plan.depth - 1,),
                ):
                    refs.append(pltpu.VMEM(lead + (part, cols), BF))
        return refs

    @staticmethod
    def semaphores(plan, count):
        return [
            pltpu.SemaphoreType.DMA((count, 6)),
            pltpu.SemaphoreType.DMA((count, 4 * plan.depth + 2)),
        ]

    def __init__(self, plan, grads, outs, buffers, send, recv, lines_only=False):
        self.plan, self.grads, self.outs = plan, grads, outs
        self.lines_only = lines_only
        self.send, self.recv = send, recv
        self.section, chip = spot()
        self.z, self.y, self.x = plan.place(chip)
        self.work = []
        buffers = list(buffers)
        for i, grad in enumerate(grads):
            for number, (start, rows, x_first) in enumerate(plan.routes(grad.shape[3], i)):
                self.work.append((i, number, start, rows, x_first, buffers[:5]))
                buffers = buffers[5:]

    def to(self, z, y, x):
        return self.section, self.plan.chip_at(z, y, x)

    def level(self, t):
        return lax.rem(self.z + 1 + t, self.plan.depth)

    def begin(self, first=0, last=None):
        plan, side = self.plan, self.plan.side
        for t in range(first, plan.depth if last is None else last):
            z = self.level(t)
            for i, number, start, rows, x_first, (land, *_) in self.work:
                grad, sl = self.grads[i], pl.ds(start, rows)
                for step in range(1, side):
                    if x_first:
                        y = lax.rem(self.y + step, side)
                        src, peer = grad.at[z, y, :, sl], self.to(self.z, y, self.x)
                    else:
                        x = lax.rem(self.x + step, side)
                        src, peer = grad.at[z, :, x, sl], self.to(self.z, self.y, x)
                    push(
                        src,
                        land.at[t, step - 1],
                        self.send.at[i, number],
                        self.recv.at[i, number * plan.depth + t],
                        peer,
                    ).start()

    def second(self, t):
        plan, side = self.plan, self.plan.side
        z = self.level(t)
        for i, number, start, rows, x_first, (land, part, land2, *_) in self.work:
            grad = self.grads[i]
            bytes_of(land.at[t], self.recv.at[i, number * plan.depth + t])
            for j in range(side):
                y, x = (self.y, j) if x_first else (j, self.x)
                total = grad[z, y, x, start : start + rows, :].astype(F32)
                for step in range(side - 1):
                    total = total + land[t, step, j].astype(F32)
                part[t, j] = total.astype(BF)
            for step in range(1, side):
                if x_first:
                    j = lax.rem(self.x + step, side)
                    peer = self.to(self.z, self.y, j)
                else:
                    j = lax.rem(self.y + step, side)
                    peer = self.to(self.z, j, self.x)
                push(
                    part.at[t, j],
                    land2.at[t, step - 1],
                    self.send.at[i, 2 + number],
                    self.recv.at[i, (2 + number) * plan.depth + t],
                    peer,
                ).start()

    def third(self, t):
        plan, side = self.plan, self.plan.side
        for i, number, start, rows, x_first, (_, part, land2, line, land3) in self.work:
            bytes_of(land2.at[t], self.recv.at[i, (2 + number) * plan.depth + t])
            mine = self.x if x_first else self.y
            total = part[t, mine].astype(F32)
            for step in range(side - 1):
                total = total + land2[t, step].astype(F32)
            line[t] = total.astype(BF)
            if t < plan.depth - 1 and not self.lines_only:
                push(
                    line.at[t],
                    land3.at[t],
                    self.send.at[i, 4 + number],
                    self.recv.at[i, 4 * plan.depth + number],
                    self.to(self.level(t), self.y, self.x),
                ).start()

    def end(self):
        plan = self.plan
        for i, number, start, rows, x_first, (land, part, land2, line, land3) in self.work:
            if self.lines_only:
                self.outs[i][:, start : start + rows, :] = line[...]
                bytes_of(land, self.send.at[i, number])
                bytes_of(land2, self.send.at[i, 2 + number])
                continue
            bytes_of(land3, self.recv.at[i, 4 * plan.depth + number])
            total = line[plan.depth - 1].astype(F32)
            for step in range(plan.depth - 1):
                total = total + land3[step].astype(F32)
            self.outs[i][start : start + rows, :] = total
            bytes_of(land, self.send.at[i, number])
            bytes_of(land2, self.send.at[i, 2 + number])
            bytes_of(land3, self.send.at[i, 4 + number])

    def stage(self, number):
        if number < self.plan.depth:
            self.second(number)
        if number > 0:
            self.third(number - 1)


def exit_kernel(chips, give, tiles, take, land, send, recv, gain_send, gain_recv):
    section, chip = spot()
    me = section * chips + chip
    greet_everyone(chips)()
    swap = push(give, take, send, recv, (1 - section, chip))
    swap.start()

    def one(step, carry):
        peer = lax.rem(me + step, 2 * chips)
        push(
            tiles.at[peer],
            land.at[me],
            gain_send,
            gain_recv,
            (peer // chips, lax.rem(peer, chips)),
        ).start()
        return carry

    lax.fori_loop(1, 2 * chips, one, 0)
    pltpu.make_async_copy(tiles.at[me], land.at[me], gain_recv).start()
    bytes_of(land, gain_recv)
    bytes_of(land.at[pl.ds(0, 2 * chips - 1)], gain_send)
    swap.wait()


def exit_call(chips, give, tiles):
    any_spec = pl.BlockSpec(memory_space=pl.ANY)
    return pl.pallas_call(
        functools.partial(exit_kernel, chips),
        out_shape=[
            jax.ShapeDtypeStruct(give.shape, give.dtype),
            jax.ShapeDtypeStruct(tiles.shape, tiles.dtype),
        ],
        in_specs=[any_spec] * 2,
        out_specs=[any_spec] * 2,
        scratch_shapes=[
            pltpu.SemaphoreType.DMA,
            pltpu.SemaphoreType.DMA,
            pltpu.SemaphoreType.DMA,
            pltpu.SemaphoreType.DMA,
        ],
        compiler_params=pltpu.CompilerParams(collective_id=4, has_side_effects=True),
        name="leave",
    )(give, tiles)


def filter_rows(plan, land, table, first_row, backward):
    lane = lax.broadcasted_iota(jnp.int32, (plan.f_rows, LANES), 1)
    low = lane < plan.half
    total = plan.length // LANES
    for m in range(total):
        if backward:
            one, two = 2 * m, 2 * m + 1
        else:
            one, two = plan.chips - 1 - 2 * m, plan.chips - 2 - 2 * m
        left = land[one, first_row : first_row + plan.f_rows, :].astype(F32)
        right = land[two, first_row : first_row + plan.f_rows, :].astype(F32)
        even = jnp.where(low, left, pltpu.roll(right, plan.half, 1))
        odd = jnp.where(low, pltpu.roll(left, plan.half, 1), right)
        at = LANES * m + (BLOCK if backward else 0)
        table[0, :, at : at + LANES] = even
        table[1, :, at : at + LANES] = odd
    blank = jnp.zeros((plan.f_rows, BLOCK), F32)
    at = 0 if backward else plan.length
    for parity in range(2):
        table[parity, :, at : at + BLOCK] = blank


def build_strips(plan, table, strip, backward):
    span = plan.length + BLOCK
    shift = span - LANES if backward else span - (LANES - 1)
    part = 32

    def one(k, carry):
        for parity in range(2):
            row = table[parity, pl.ds(k, 1), :]
            for start in range(0, LANES, part):
                spread = jnp.broadcast_to(row, (part, span))
                rolled = pltpu.roll(
                    spread, (shift + start) % span, 1, stride=1, stride_axis=0
                ).astype(BF)
                strip[parity, k, LANES + start : LANES + start + part, :] = rolled[
                    :, : plan.length
                ]
                strip[parity, k, start : start + part, :] = rolled[
                    :, LANES : LANES + plan.length
                ]
        return carry

    lax.fori_loop(0, plan.local, one, 0)


def sizes(plan):
    size = plan.jb // PIECE
    while size:
        yield size
        size //= 2


def owner_pieces(plan, act):
    section, chip = spot()
    start = plan.pieces * (section * plan.chips + chip)
    per_block = plan.jb // PIECE

    def block(j, carry):
        number = start // per_block + j
        base = number * per_block
        low = jnp.maximum(start - base, 0)
        high = jnp.minimum(start + plan.pieces - base, per_block)
        count = jnp.maximum(high - low, 0)
        which = number // plan.cols_in
        b = lax.rem(number, plan.cols_in)
        sign = which // plan.filters
        full = lax.rem(which, plan.filters)
        group = full // plan.local
        k = lax.rem(full, plan.local)
        for size in sizes(plan):
            done = count // (2 * size) * (2 * size)
            here = lax.rem(count // size, 2) == 1
            source = base + low - start + done
            target = low + done

            @pl.when(jnp.logical_and(here, sign < 2))
            def _():
                for a in range(plan.cols_out):
                    to_chip = plan.part_at(a, b, group)
                    act(source, size, False, k, target, a, sign, to_chip)

            @pl.when(jnp.logical_and(here, sign >= 2))
            def _():
                for a in range(plan.cols_out):
                    for core in range(2):
                        to_chip = plan.part_at(a, b, plan.groups - 1)
                        act(source, size, True, full, target, a, core, to_chip)

        return carry

    lax.fori_loop(0, plan.pieces // per_block + 2, block, 0)


def forward_kernel(plan, *refs):
    io_ref, gain_ref, filters_ref, lengths_ref = refs[:4]
    gate_raw, up_raw, down_raw, proj_raw, attn_raw = refs[4:9]
    if plan.routed:
        maps_ref = refs[9]
        rest = refs[10:]
    else:
        mine_ref, other_ref, taps_ref = refs[9:12]
        rest = refs[12:]
    full_weights, rest = rest[:8], rest[8:]
    (
        conv_ref,
        hidden_ref,
        upstream_ref,
        pair_ref,
        gains_ref,
        mask_ref,
        v_ref,
        pq_ref,
        tapw_ref,
        x_ref,
        xs_ref,
        filt_ref,
        io_own,
        io_sib,
        gain_tile,
        gate_half,
        gate_shard,
        up_half,
        up_shard,
        down_shard,
        u_ref,
        f_ref,
        x_buf,
        xo_buf,
        xs_buf,
        xf_buf,
        f_land,
        table,
        strip,
        mine,
        other,
        taps,
        pq,
        acc,
        joined,
        y_buf,
        land,
        reduced,
        final,
        stage,
        io_sem,
        gain_send,
        gain_recv,
        s_send,
        s_recv,
        u_send,
        x_recv,
        f_send,
        f_recv,
        m_send,
        m_recv,
        t_recv,
        o_send,
        o_recv,
        c_send,
        c_recv,
        d_send,
        r_recv,
        v_sem,
        out_sem,
        w_send,
        w_recv,
    ) = rest
    chips, half, jb, ia, rows_here = plan.chips, plan.half, plan.jb, plan.ia, plan.rows
    section, chip = spot()
    dev = section * chips + chip
    sibling = (1 - section, chip)
    my_group = chip // (plan.cols_out * plan.cols_in)
    greeted = greet_everyone(chips)

    row = lax.broadcasted_iota(jnp.int32, (rows_here, rows_here), 0)
    col = lax.broadcasted_iota(jnp.int32, (rows_here, rows_here), 1)
    order = jnp.where(col == 2 * lax.rem(row, half) + row // half, 1.0, 0.0).astype(BF)
    for i in range(2):
        io_own[i] = flat_dot(order, io_ref[i]).astype(BF)
    cols = gain_ref.shape[1]
    gain_tile[0] = jnp.zeros((8, LANES), F32)
    gain_tile[0, 0:2, 0:cols] = gain_ref[...].astype(F32)
    if plan.pick_here:
        lane = lax.broadcasted_iota(jnp.int32, (gate_raw.shape[0], LANES), 1)
        low = lane < half
        for raw, halves, shard in ((gate_raw, gate_half, gate_shard), (up_raw, up_half, up_shard)):
            for j in range(raw.shape[1] // (2 * LANES)):
                one = raw[:, 2 * LANES * j : 2 * LANES * j + LANES].astype(F32)
                two = raw[:, 2 * LANES * j + LANES : 2 * LANES * (j + 1)].astype(F32)
                zero_half = jnp.where(low, one, pltpu.roll(two, half, 1)).astype(BF)
                one_half = jnp.where(low, pltpu.roll(one, half, 1), two).astype(BF)
                at = slice(LANES * j, LANES * (j + 1))
                shard[section, :, at] = jnp.where(section == 0, zero_half, one_half)
                halves[:, at] = jnp.where(section == 0, one_half, zero_half)
    else:
        for raw, halves, shard in ((gate_raw, gate_half, gate_shard), (up_raw, up_half, up_shard)):
            shard[section] = raw[section]
            halves[...] = raw[1 - section]
    part = down_shard.shape[1]
    down_shard[section] = down_raw[pl.ds(pl.multiple_of(part * section, 16), part), :]
    greeted()
    io_swap = push(io_own, io_sib, io_sem.at[0], io_sem.at[1], sibling)
    io_swap.start()

    gain_swap = push(gain_tile.at[0], gain_tile.at[1], gain_send, gain_recv, sibling)
    gain_swap.start()
    shares = [
        push(src, dst, s_send.at[i], s_recv.at[i], sibling)
        for i, (src, dst) in enumerate(
            (
                (gate_half, gate_shard.at[section]),
                (up_half, up_shard.at[section]),
                (
                    down_raw.at[pl.ds(pl.multiple_of(part * (1 - section), 16), part), :],
                    down_shard.at[section],
                ),
            )
        )
    ]
    for share in shares:
        share.start()

    if plan.routed:

        def places(source, size, tap, k, target, a):
            rows = size * PIECE
            src = maps_ref.at[pl.ds(PIECE * source, rows), pl.ds(a * ia, ia)]
            if tap:
                return src, taps.at[pl.ds(jb * k + PIECE * target, rows), :], t_recv
            return src, mine.at[k, pl.ds(PIECE * target, rows), :], m_recv

        def start_piece(source, size, tap, k, target, a, to_section, to_chip):
            src, dst, sem = places(source, size, tap, k, target, a)
            here = to_section * chips + to_chip == dev

            @pl.when(here)
            def _():
                pltpu.make_async_copy(src, dst, sem).start()

            @pl.when(jnp.logical_not(here))
            def _():
                push(src, dst, m_send, sem, (to_section, to_chip)).start()

        def drain_piece(source, size, tap, k, target, a, to_section, to_chip):
            src, dst, sem = places(source, size, tap, k, target, a)

            @pl.when(to_section * chips + to_chip != dev)
            def _():
                push(src, dst, m_send, sem, (to_section, to_chip)).wait_send()

        owner_pieces(plan, start_piece)

    lag = lax.broadcasted_iota(jnp.int32, (rows_here, LANES), 0)
    lane = lax.broadcasted_iota(jnp.int32, (rows_here, LANES), 1)
    stretch = lax.rem(lane, half)
    backwards = jnp.where(lag == 2 * (half - 1 - stretch) + lane // half, 1.0, 0.0).astype(BF)
    plain = jnp.where(lag == 2 * stretch + lane // half, 1.0, 0.0).astype(BF)
    gain_swap.wait_recv()
    core_zero = section == 0
    own_gain, sib_gain = gain_tile[0], gain_tile[1]
    gain_rows = jnp.concatenate(
        [jnp.where(core_zero, own_gain, sib_gain), jnp.where(core_zero, sib_gain, own_gain)], 0
    ).astype(BF)
    for group in range(plan.groups):
        source = lax.broadcasted_iota(jnp.int32, (plan.filters, plan.f_rows), 0)
        target = lax.broadcasted_iota(jnp.int32, (plan.filters, plan.f_rows), 1)
        chosen = jnp.where(
            (source == group * plan.local + target) & (target < plan.local), 1.0, 0.0
        ).astype(BF)
        some = flat_dot(filters_ref[...], chosen).astype(BF)
        f_ref[group, : plan.f_rows, :] = cols_dot(some, backwards).astype(BF)
        f_ref[group, plan.f_rows : 2 * plan.f_rows, :] = cols_dot(some, plain).astype(BF)
        f_ref[group, 2 * plan.f_rows :, :] = gain_rows

    def send_f(step, carry):
        peer = lax.rem(chip + step, chips)
        group = peer // (plan.cols_out * plan.cols_in)
        push(f_ref.at[group], f_land.at[chip], f_send, f_recv, (section, peer)).start()
        return carry

    lax.fori_loop(1, chips, send_f, 0)
    pltpu.make_async_copy(f_ref.at[my_group], f_land.at[chip], f_recv).start()
    for share in shares:
        share.wait_recv()
    second_layer = (gate_shard.at[1], up_shard.at[1], down_shard.at[1])
    parts = [
        (0, (gate_shard.at[0], up_shard.at[0], down_shard.at[0])),
        (3, (proj_raw, attn_raw)),
    ]
    parts.append((5, second_layer))
    groups = []
    for first, arrays in parts:
        last = first + len(arrays)
        groups.append(
            Gather(
                plan,
                arrays,
                full_weights[first:last],
                w_send.at[pl.ds(first, len(arrays))],
                w_recv.at[pl.ds(first, len(arrays))],
            )
        )
    layer0, attention, layer1 = groups
    layer0.begin()
    position = lax.broadcasted_iota(jnp.int32, (rows_here, 1), 0)
    position = chip * rows_here + 2 * lax.rem(position, half) + position // half
    length_own = jnp.where(section == 0, lengths_ref[0], lengths_ref[1])
    length_other = jnp.where(section == 0, lengths_ref[1], lengths_ref[0])
    mask = jnp.where(position < length_own, 1.0, 0.0)
    mask_other = jnp.where(position < length_other, 1.0, 0.0)
    mask_ref[...] = mask
    io_swap.wait()
    bytes_of(f_land, f_recv)
    pick_row = lax.broadcasted_iota(jnp.int32, (LANES, plan.width), 0)
    pick_col = lax.broadcasted_iota(jnp.int32, (LANES, plan.width), 1)
    repeat = jnp.where(pick_row == lax.rem(pick_col, cols), 1.0, 0.0).astype(BF)
    tile_row = lax.broadcasted_iota(jnp.int32, (chips * 16, plan.width), 0)
    tile_col = lax.broadcasted_iota(jnp.int32, (chips * 16, plan.width), 1)
    rows_all = f_land[:, 2 * plan.f_rows :, :].reshape(chips * 16, LANES)
    spread = jnp.where(
        tile_row // 16 == tile_col // cols, flat_dot(rows_all, repeat), 0.0
    ).astype(BF)
    gain_row = lax.broadcasted_iota(jnp.int32, (16, chips * 16), 0)
    gain_col = lax.broadcasted_iota(jnp.int32, (16, chips * 16), 1)
    gather_rows = jnp.where(lax.rem(gain_col, 16) == gain_row, 1.0, 0.0).astype(BF)
    gathered = flat_dot(gather_rows, spread)
    gains_ref[0:2, :] = gathered[0:2, :]
    gains_ref[2:4, :] = gathered[8:10, :]
    gains_ref[4:8, :] = jnp.zeros((4, plan.width), F32)
    hidden = jnp.where(core_zero, io_own[0], io_sib[1]).astype(F32) * mask
    hidden_ref[...] = hidden
    factor = lax.rsqrt(jnp.mean(hidden * hidden, axis=-1, keepdims=True) + EPSILON)
    u = (hidden * factor * gains_ref[0:1, :]).astype(BF)
    for b in range(plan.cols_in):
        u_ref[b, :, :jb] = u[:half, b * jb : (b + 1) * jb]
        u_ref[b, :, jb:] = u[half:, b * jb : (b + 1) * jb]

    def send_u(step, carry):
        peer = lax.rem(chip + step, chips)
        b = plan.b_of(peer)
        push(
            u_ref.at[b],
            x_buf.at[pl.ds(half * chip, half), :],
            u_send,
            x_recv,
            (section, peer),
        ).start()
        return carry

    lax.fori_loop(1, chips, send_u, 0)
    pltpu.make_async_copy(
        u_ref.at[plan.b_of(chip)],
        x_buf.at[pl.ds(half * chip, half), :],
        x_recv,
    ).start()
    for group in groups[1:]:
        group.begin()
    cot_own = jnp.where(core_zero, io_sib[0], io_own[1]).astype(F32) * mask
    cot_other = jnp.where(core_zero, io_sib[1], io_own[0]).astype(F32) * mask_other
    upstream_ref[...] = cot_own
    pair_ref[:rows_here, :] = cot_own.astype(BF)
    pair_ref[rows_here:, :] = cot_other.astype(BF)
    layer0.stage(0)
    filter_rows(plan, f_land, table, 0, False)
    build_strips(plan, table, strip, False)
    filt_out = pltpu.make_async_copy(f_land, filt_ref, out_sem.at[0])
    filt_out.start()

    if plan.routed:
        bytes_of(mine, m_recv)
        swap = push(mine, other, o_send, o_recv, (1 - section, chip))
        swap.start()

        @pl.when(my_group == plan.groups - 1)
        def _():
            bytes_of(taps, t_recv)

        @pl.when(my_group != plan.groups - 1)
        def _():
            taps[...] = jnp.zeros_like(taps)
    else:
        for src, dst in ((mine_ref, mine), (other_ref, other), (taps_ref, taps)):
            pltpu.sync_copy(src, dst)

    layer0.stage(1)
    bytes_of(x_buf, x_recv)
    x_out = pltpu.make_async_copy(x_buf, x_ref, out_sem.at[1])
    x_out.start()
    xf_buf[0:8, :] = jnp.zeros((8, 2 * jb), F32)
    for i in range(plan.blocks):
        rows = slice(BLOCK * i, BLOCK * (i + 1))
        xf_buf[8 + BLOCK * i : 8 + BLOCK * (i + 1), :] = x_buf[rows, :].astype(F32)
    for i in range(plan.blocks):
        rows = slice(BLOCK * i, BLOCK * (i + 1))
        moved = xf_buf[7 + BLOCK * i : 7 + BLOCK * (i + 1), :].astype(BF)
        xs_buf[rows, :] = moved
        xo_buf[rows, :jb] = x_buf[rows, :jb]
        xo_buf[rows, jb:] = moved[:, jb:]
    xs_out = pltpu.make_async_copy(xs_buf, xs_ref, out_sem.at[2])
    xs_out.start()

    if plan.routed:
        swap.wait()
    turn = (1 - 2 * section).astype(F32)

    def mix(k, carry):
        first = mine[k].astype(F32)
        second = other[k].astype(F32)
        pq[k, :jb, :] = (first + second).astype(BF)
        pq[k, jb:, :] = ((first - second) * turn).astype(BF)
        return carry

    lax.fori_loop(0, plan.local, mix, 0)
    pq_out = pltpu.make_async_copy(pq, pq_ref, out_sem.at[3])
    pq_out.start()
    taps_out = pltpu.make_async_copy(taps, tapw_ref, out_sem.at[4])
    taps_out.start()

    layer0.stage(2)
    attention.stage(0)
    batch = plan.batch
    my_b, level = plan.b_of(chip), chip // plan.cols_in

    def reduce_level(i):
        bytes_of(land.at[i], r_recv.at[i])
        total = y_buf[:, pl.ds(pl.multiple_of(BLOCK * i + half * my_b, half), half), :].astype(F32)
        for step_number in range(plan.cols_in - 1):
            total = total + land[i, step_number].astype(F32)
        reduced[i] = total.astype(BF)

        @pl.when(level == i)
        def _():
            final[i] = reduced[i]

        @pl.when(level != i)
        def _():
            push(
                reduced.at[i],
                final.at[level],
                d_send,
                c_recv,
                (section, i * plan.cols_in + my_b),
            ).start()

    for i in range(plan.blocks):
        if i == 1:
            layer0.stage(3)
            attention.stage(1)
        if i == 2:
            layer0.stage(4)
        if i == 3:
            attention.stage(2)
        rows = slice(BLOCK * i, BLOCK * (i + 1))
        depth = BLOCK * (i + 1)
        offset = plan.length - depth
        x_now = x_buf[rows, :]
        s_now = xs_buf[rows, :]
        acc[:BLOCK] = flat_dot(
            jnp.concatenate([x_now[:, :jb], s_now[:, jb:]], 1), taps[: 2 * jb, :]
        ) + flat_dot(s_now[:, :jb], taps[2 * jb :, :])
        acc[BLOCK:] = flat_dot(
            jnp.concatenate([x_now[:, jb:], x_now[:, :jb]], 1), taps[: 2 * jb, :]
        ) + flat_dot(s_now[:, jb:], taps[2 * jb :, :])

        def step(t, carry, i=i, depth=depth, offset=offset):
            count = plan.local // batch * i + t
            slot = lax.rem(count, 2)
            some = pl.ds(batch * t, batch)
            v_copy = pltpu.make_async_copy(
                stage.at[slot], v_ref.at[some, :, pl.ds(BLOCK * i, BLOCK), :], v_sem.at[slot]
            )
            even = flat_dot(
                strip[0, some, :, offset:].reshape(batch * BLOCK, depth), x_buf[:depth, :]
            ).astype(BF)
            odd = flat_dot(
                strip[1, some, :, offset:].reshape(batch * BLOCK, depth), xo_buf[:depth, :]
            ).astype(BF)
            if i == 0:
                pl.when(t >= 2)(v_copy.wait)
            else:
                v_copy.wait()
            for k in range(batch):
                here = slice(BLOCK * k, BLOCK * (k + 1))
                first = jnp.concatenate([even[here, :jb], odd[here, jb:]], 1)
                second = jnp.concatenate([even[here, jb:], odd[here, :jb]], 1)
                stage[slot, k, 0] = first
                stage[slot, k, 1] = second
                lanes = slice(2 * jb * k, 2 * jb * (k + 1))
                joined[:BLOCK, lanes] = first
                joined[BLOCK:, lanes] = second
            v_copy.start()
            acc[...] += flat_dot(joined[...], pq[some].reshape(batch * 2 * jb, ia))
            return carry

        lax.fori_loop(0, plan.local // batch, step, 0)
        y_buf[0, rows, :] = acc[:BLOCK].astype(BF)
        y_buf[1, rows, :] = acc[BLOCK:].astype(BF)

        if plan.layered:
            for step_number in range(1, plan.cols_in):
                peer = lax.rem(my_b + step_number, plan.cols_in)
                push(
                    y_buf.at[:, pl.ds(BLOCK * i + half * peer, half), :],
                    land.at[i, step_number - 1],
                    c_send,
                    r_recv.at[i],
                    (section, level * plan.cols_in + peer),
                ).start()
            if i > 0:
                reduce_level(i - 1)
            continue

        def give(r, carry, i=i):
            peer = BLOCK // half * i + r
            src = y_buf.at[:, pl.ds(half * peer, half), :]

            @pl.when(peer == chip)
            def _():
                pltpu.make_async_copy(src, land.at[chip], c_recv).start()

            @pl.when(peer != chip)
            def _():
                push(src, land.at[chip], c_send, c_recv, (section, peer)).start()

            return carry

        lax.fori_loop(0, BLOCK // half, give, 0)

    attention.stage(3)
    attention.stage(4)
    for number in range(1, plan.depth):
        layer1.second(number)
    if not plan.late:
        for number in range(plan.depth):
            layer1.third(number)
    for slot in range(2):
        pltpu.make_async_copy(
            stage.at[slot], v_ref.at[pl.ds(0, batch), :, pl.ds(0, BLOCK), :], v_sem.at[slot]
        ).wait()
    bytes_of(x_buf.at[pl.ds(0, half * (chips - 1)), :], u_send)
    bytes_of(f_land.at[pl.ds(0, chips - 1)], f_send)
    if plan.routed:
        owner_pieces(plan, drain_piece)
    for copy in (filt_out, x_out, xs_out, pq_out, taps_out):
        copy.wait()
    if plan.layered:
        reduce_level(plan.blocks - 1)
        bytes_of(final.at[pl.ds(0, plan.blocks - 1)], c_recv)
    else:
        bytes_of(land, c_recv)
    for a in range(plan.cols_out):
        total = None
        for c in range(plan.groups):
            if plan.layered:
                terms = [final[a + plan.cols_out * c]]
            else:
                terms = [land[plan.part_at(a, b, c)] for b in range(plan.cols_in)]
            for term in terms:
                term = term.astype(F32)
                total = term if total is None else total + term
        conv_ref[:, :, a * ia : (a + 1) * ia] = total
    if plan.layered:
        bytes_of(land, c_send)
        bytes_of(final.at[pl.ds(0, plan.blocks - 1)], d_send)
    else:
        bytes_of(land.at[pl.ds(0, chips - 1)], c_send)
    for group in groups[:2]:
        group.end()
    if plan.late:
        layer1.hand_over()
    else:
        layer1.end()
    gain_swap.wait_send()
    for share in shares:
        share.wait_send()


def forward_call(plan, io, gain, filters, lengths, raw, maps):
    chips, half, jb, ia, rows = plan.chips, plan.half, plan.jb, plan.ia, plan.rows
    width = plan.width
    any_spec = pl.BlockSpec(memory_space=pl.ANY)
    vmem_spec = pl.BlockSpec(memory_space=pltpu.VMEM)
    smem_spec = pl.BlockSpec(memory_space=pltpu.SMEM)
    dma = pltpu.SemaphoreType.DMA
    down, proj, attn = raw[2].shape, raw[3].shape, raw[4].shape
    share = (raw[0].shape[-2], plan.ff // 2)
    down_share = (down[0] // 2, width)
    grid = (plan.depth, plan.side, plan.side)
    layer = [share, share, down_share]
    levels = plan.blocks if plan.layered else 1
    land_shape = (
        (levels, plan.cols_in - 1, 2, half, ia) if plan.layered else (chips, 2, half, ia)
    )
    gathered = [grid + w for w in layer + [proj, attn]]
    gathered += [grid + w for w in layer]
    shapes = [(w, BF) for w in gathered] + [
        ((2, half, width), F32),
        ((rows, width), F32),
        ((rows, width), F32),
        ((2 * rows, width), BF),
        ((8, width), F32),
        ((rows, 1), F32),
        ((plan.local, 2, plan.length, 2 * jb), BF),
        ((plan.local, 2 * jb, ia), BF),
        ((ORDER * jb, ia), BF),
        ((plan.length, 2 * jb), BF),
        ((plan.length, 2 * jb), BF),
        ((chips, 2 * plan.f_rows + 16, LANES), BF),
    ]
    return pl.pallas_call(
        functools.partial(forward_kernel, plan),
        out_shape=[jax.ShapeDtypeStruct(s, d) for s, d in shapes],
        in_specs=[vmem_spec] * 3
        + [smem_spec]
        + [vmem_spec] * 3
        + [any_spec] * 2
        + [vmem_spec if plan.routed else any_spec] * len(maps),
        out_specs=[any_spec] * 8 + [vmem_spec] * 6 + [any_spec] * 6,
        scratch_shapes=[
            pltpu.VMEM((2, rows, width), BF),
            pltpu.VMEM((2, rows, width), BF),
            pltpu.VMEM((2, 8, LANES), F32),
            pltpu.VMEM(share, BF),
            pltpu.VMEM((2,) + share, BF),
            pltpu.VMEM(share, BF),
            pltpu.VMEM((2,) + share, BF),
            pltpu.VMEM((2,) + down_share, BF),
            pltpu.VMEM((plan.cols_in, half, 2 * jb), BF),
            pltpu.VMEM((plan.groups, 2 * plan.f_rows + 16, LANES), BF),
            pltpu.VMEM((plan.length, 2 * jb), BF),
            pltpu.VMEM((plan.length, 2 * jb), BF),
            pltpu.VMEM((plan.length, 2 * jb), BF),
            pltpu.VMEM((plan.length + 8, 2 * jb), F32),
            pltpu.VMEM((chips, 2 * plan.f_rows + 16, LANES), BF),
            pltpu.VMEM((2, plan.f_rows, plan.length + BLOCK), F32),
            pltpu.VMEM((2, plan.local, BLOCK, plan.length), BF),
            pltpu.VMEM((plan.local, jb, ia), BF),
            pltpu.VMEM((plan.local, jb, ia), BF),
            pltpu.VMEM((ORDER * jb, ia), BF),
            pltpu.VMEM((plan.local, 2 * jb, ia), BF),
            pltpu.VMEM((2 * BLOCK, ia), F32),
            pltpu.VMEM((2 * BLOCK, plan.batch * 2 * jb), BF),
            pltpu.VMEM((2, plan.length, ia), BF),
            pltpu.VMEM(land_shape, BF),
            pltpu.VMEM((levels, 2, half, ia), BF),
            pltpu.VMEM((levels, 2, half, ia), BF),
            pltpu.VMEM((2, plan.batch, 2, BLOCK, 2 * jb), BF),
            dma((2,)),
            dma,
            dma,
            dma((3,)),
            dma((3,)),
        ]
        + [dma] * 12
        + [dma((levels,)), dma((2,)), dma((5,)), *Gather.semaphores(plan, 8)],
        compiler_params=pltpu.CompilerParams(
            collective_id=2, has_side_effects=True, vmem_limit_bytes=VMEM_LIMIT
        ),
        name="spectral_forward",
    )(io, gain, filters, lengths, *raw, *maps)


def backward_kernel(plan, number, *refs):
    g_ref, filt_ref, v_ref, pq, tapw, x_ref, xs_ref = refs[:7]
    grads, rest = refs[7 : 7 + number], refs[7 + number :]
    if plan.late:
        hidden_ref, gains_ref, mask_ref, dmid_ref, out_ref, gain_sums_ref, *lines = rest[:9]
        res_ref, gate_ref, up_ref, down_ref, proj_ref, attn_ref, gain_out, dmaps_ref = rest[9:17]
        du_ref, gain_buf, gain_land, give_res, *half_parts = rest[17:30]
        half0, crossing, arrived = half_parts[:3], half_parts[3:6], half_parts[6:9]
        e_send, e_recv, n_send, n_recv = rest[30:34]
        half1, line_land, (l_send, l_recv) = rest[34:37], rest[37:40], rest[40:42]
        rest = rest[42:]
        sums = [*half0, proj_ref, attn_ref]
    else:
        sums, rest = rest[:number], rest[number:]
        du_ref, dmap_ref, dtap_ref = rest[:3]
        rest = rest[3:]
    count = 5 * sum(len(plan.routes(grad.shape[3])) for grad in grads)
    scatter = Scatter(plan, grads, sums, rest[:count], *rest[count : count + 2])
    rest = rest[count + 2 :]
    (
        g_buf,
        gt_buf,
        table,
        strip,
        v_buf,
        z_even,
        z_odd,
        acc_even,
        acc_odd,
        kept,
        give_m,
        take_m,
        total_m,
        kept_t,
        give_t,
        take_t,
        total_t,
        du_buf,
        land,
        g_send,
        g_recv,
        v_sem,
        m_send,
        m_recv,
        t_send,
        t_recv,
        w_send,
        w_recv,
        d_send,
        d_recv,
        x_sem,
        z_send,
        z_recv,
    ) = rest
    chips, half, jb, ia = plan.chips, plan.half, plan.jb, plan.ia
    section, chip = spot()
    dev = section * chips + chip
    my_a, my_b = plan.a_of(chip), plan.b_of(chip)
    my_group = chip // (plan.cols_out * plan.cols_in)
    sibling = (1 - section, chip)
    greet_everyone(chips)()

    def send_g(step, carry):
        peer = lax.rem(chip + step, chips)
        a = plan.a_of(peer)
        push(
            g_ref.at[:, :, pl.ds(pl.multiple_of(a * ia, ia), ia)],
            g_buf.at[:, pl.ds(half * chip, half), :],
            g_send,
            g_recv,
            (section, peer),
        ).start()
        return carry

    own_g = g_ref.at[:, :, pl.ds(pl.multiple_of(my_a * ia, ia), ia)]
    level, levels = chip // plan.cols_in, chips // plan.cols_in

    def g_rows(t):
        source = lax.rem(level - t + levels, levels) * plan.cols_in + my_b
        return g_buf.at[:, pl.ds(pl.multiple_of(half * source, half), half), :]

    def spread_g(t):
        if t > 0:
            bytes_of(g_rows(t), z_recv.at[t])
        for step_number in range(1, plan.cols_in):
            peer = lax.rem(my_b + step_number, plan.cols_in)
            push(
                own_g if t == 0 else g_rows(t),
                g_rows(t),
                g_send,
                g_recv,
                (section, level * plan.cols_in + peer),
            ).start()

    if plan.layered:
        for t in range(1, levels):
            to_level = lax.rem(level + t, levels)
            to_a = lax.rem(to_level, plan.cols_out)
            push(
                g_ref.at[:, :, pl.ds(pl.multiple_of(to_a * ia, ia), ia)],
                g_rows(0),
                z_send,
                z_recv.at[t],
                (section, to_level * plan.cols_in + my_b),
            ).start()
        spread_g(0)
        pltpu.make_async_copy(own_g, g_rows(0), z_recv.at[0]).start()
    else:
        lax.fori_loop(1, chips, send_g, 0)
        pltpu.make_async_copy(
            own_g, g_buf.at[:, pl.ds(half * chip, half), :], g_recv
        ).start()
    v_copy = [pltpu.make_async_copy(v_ref.at[k], v_buf.at[k], v_sem.at[k]) for k in range(2)]
    for copy in v_copy:
        copy.start()
    x_copy = [
        pltpu.make_async_copy(src, dst, x_sem.at[i])
        for i, (src, dst) in enumerate(((x_ref, z_even), (xs_ref, z_odd)))
    ]
    for copy in x_copy:
        copy.start()
    if plan.late:
        z, y, x = plan.place(chip)
        for i in range(3):
            for t in range(plan.depth - 1):
                to = (section, plan.chip_at(lax.rem(z + 1 + t, plan.depth), y, x))
                push(
                    lines[i].at[t], line_land[i].at[t], l_send.at[i], l_recv.at[i], to
                ).start()
    scatter.begin(0, EARLY)
    filter_rows(plan, filt_ref, table, plan.f_rows, True)
    build_strips(plan, table, strip, True)
    if plan.layered:
        for t in range(1, levels):
            spread_g(t)
    acc_even[...] = jnp.zeros_like(acc_even)
    acc_odd[...] = jnp.zeros_like(acc_odd)
    if plan.layered:
        pltpu.make_async_copy(own_g, g_rows(0), z_recv.at[0]).wait()
        bytes_of(g_buf.at[:, pl.ds(0, half * levels * (plan.cols_in - 1)), :], g_recv)
    else:
        bytes_of(g_buf, g_recv)
    scatter.begin(EARLY)
    for phase in range(2):
        for i in range(plan.blocks):
            rows = slice(BLOCK * i, BLOCK * (i + 1))
            gt_buf[phase, :, rows] = g_buf[phase, rows, :].astype(F32).T.astype(BF)
    turn = (1 - 2 * section).astype(F32)
    half_ways = (((1,), (1,)), ((), ()))

    def piece_copies(k, tap, begin):
        per_block = jb // PIECE
        which = 2 * plan.filters + k if tap else section * plan.filters + my_group * plan.local + k
        start = (which * plan.cols_in + my_b) * per_block
        owner, row = start // plan.pieces, lax.rem(start, plan.pieces)
        first = jnp.minimum(plan.pieces - row, per_block)
        for to, at, base, count in ((owner, row, 0, first), (owner + 1, 0, first, per_block - first)):
            for size in sizes(plan):
                done = count // (2 * size) * (2 * size)
                rows = size * PIECE
                here = lax.rem(count // size, 2) == 1
                source = PIECE * (base + done)
                src = (
                    total_t.at[pl.ds(jb * k + source, rows), :]
                    if tap
                    else total_m.at[k, pl.ds(source, rows), :]
                )
                dst = dmaps_ref.at[
                    pl.ds(PIECE * (at + done), rows), pl.ds(pl.multiple_of(my_a * ia, ia), ia)
                ]
                if begin:

                    @pl.when(jnp.logical_and(here, to == dev))
                    def _():
                        pltpu.make_async_copy(src, dst, w_recv).start()

                @pl.when(jnp.logical_and(here, to != dev))
                def _():
                    copy = push(src, dst, w_send, w_recv, (to // chips, lax.rem(to, chips)))
                    if begin:
                        copy.start()
                    else:
                        copy.wait_send()

    def exchange(k):
        return push(give_m.at[k], take_m.at[k], m_send.at[k], m_recv.at[k], (1 - section, chip))

    def finish(k):
        exchange(k).wait()
        total_m[k] = (kept[k] + take_m[k].astype(F32)).astype(BF)
        if plan.routed:
            piece_copies(k, False, True)

    for copy in x_copy:
        copy.wait()
    x_even, x_odd = z_even[:, :jb], z_even[:, jb:]
    s_even, s_odd = z_odd[:, :jb], z_odd[:, jb:]
    for tap, (on_even, on_odd) in enumerate(((x_even, x_odd), (s_odd, x_even), (s_even, s_odd))):
        tap_grad = jnp.dot(gt_buf[0], on_even, preferred_element_type=F32) + jnp.dot(
            gt_buf[1], on_odd, preferred_element_type=F32
        )
        tap_grad = tap_grad.T
        kept_t[tap * jb : (tap + 1) * jb, :] = tap_grad
        give_t[tap * jb : (tap + 1) * jb, :] = tap_grad.astype(BF)
    tap_swap = push(give_t, take_t, t_send, t_recv, (1 - section, chip))
    tap_swap.start()
    for i in range(plan.blocks):
        rows = slice(BLOCK * i, BLOCK * (i + 1))
        from_even = lax.dot_general(
            g_buf[0, rows, :], tapw[...], half_ways, preferred_element_type=F32
        )
        from_odd = lax.dot_general(
            g_buf[1, rows, :], tapw[...], half_ways, preferred_element_type=F32
        )
        acc_even[rows, :jb] = from_even[:, :jb] + from_odd[:, jb : 2 * jb]
        acc_even[rows, jb : 2 * jb] = from_odd[:, :jb]
        acc_odd[rows, :jb] = from_even[:, 2 * jb :]
        acc_odd[rows, jb : 2 * jb] = from_even[:, jb : 2 * jb] + from_odd[:, 2 * jb :]

    def step(k, carry):
        slot = lax.rem(k, 2)
        from_even = rows_dot(g_buf[0], pq[k]).astype(BF)
        from_odd = rows_dot(g_buf[1], pq[k]).astype(BF)
        z_even[:, :jb] = from_even[:, :jb]
        z_even[:, jb:] = from_odd[:, :jb]
        z_odd[:, :jb] = from_odd[:, jb:]
        z_odd[:, jb:] = from_even[:, jb:]
        pltpu.make_async_copy(v_ref.at[k], v_buf.at[slot], v_sem.at[slot]).wait()
        grad = jnp.dot(gt_buf[0], v_buf[slot, 0], preferred_element_type=F32) + jnp.dot(
            gt_buf[1], v_buf[slot, 1], preferred_element_type=F32
        )
        grad = grad.T
        plus, minus = grad[:jb, :], grad[jb:, :] * turn
        kept[k] = plus + minus
        give_m[k] = (plus - minus).astype(BF)
        exchange(k).start()

        @pl.when(k + 2 < plan.local)
        def _():
            pltpu.make_async_copy(v_ref.at[k + 2], v_buf.at[slot], v_sem.at[slot]).start()

        for j in range(plan.blocks):
            rows = slice(BLOCK * j, BLOCK * (j + 1))
            depth = plan.length - BLOCK * j
            acc_even[rows, :] += jnp.dot(
                strip[0, k, :, :depth], z_even[BLOCK * j :, :], preferred_element_type=F32
            )
            out = jnp.dot(
                strip[1, k, :, :depth], z_odd[BLOCK * j :, :], preferred_element_type=F32
            )
            acc_even[rows, :jb] += out[:, :jb]
            acc_odd[rows, jb:] += out[:, jb:]

        @pl.when(k >= 1)
        def _():
            finish(k - 1)

        for turn_number in range(plan.depth + 1):
            at = plan.local // 2 - 1 + 3 * turn_number
            if at < plan.local:
                pl.when(k == at)(functools.partial(scatter.stage, turn_number))
        return carry

    lax.fori_loop(0, plan.local, step, 0)
    for i in range(plan.blocks):
        rows = slice(BLOCK * i, BLOCK * (i + 1))
        moved = acc_odd[BLOCK * i + 1 : BLOCK * (i + 1) + 1, :]
        both = (acc_even[rows, :] + moved).astype(BF)
        du_buf[0, rows, :] = both[:, :jb]
        du_buf[1, rows, :] = both[:, jb:]

        def give(r, carry, i=i):
            peer = BLOCK // half * i + r
            src = du_buf.at[:, pl.ds(half * peer, half), :]

            @pl.when(peer == chip)
            def _():
                pltpu.make_async_copy(src, land.at[chip], d_recv).start()

            @pl.when(peer != chip)
            def _():
                push(src, land.at[chip], d_send, d_recv, (section, peer)).start()

            return carry

        lax.fori_loop(0, BLOCK // half, give, 0)
    for turn_number in range(plan.depth + 1):
        if plan.local // 2 - 1 + 3 * turn_number >= plan.local:
            scatter.stage(turn_number)
    finish(plan.local - 1)
    tap_swap.wait()
    total_t[...] = (kept_t[...] + take_t[...].astype(F32)).astype(BF)
    if plan.routed:

        @pl.when(jnp.logical_and(section == 0, my_group == plan.groups - 1))
        def _():
            for tap in range(ORDER):
                piece_copies(tap, True, True)
    else:
        pltpu.sync_copy(total_m, dmap_ref)
        pltpu.sync_copy(total_t, dtap_ref)
    if plan.layered:
        bytes_of(g_buf.at[:, pl.ds(0, half * levels * (plan.cols_in - 1)), :], g_send)
        bytes_of(g_buf.at[:, pl.ds(0, half * (levels - 1)), :], z_send)
    else:
        bytes_of(g_buf.at[:, pl.ds(0, half * (chips - 1)), :], g_send)
    bytes_of(land, d_recv)
    for b in range(plan.cols_in):
        total = None
        for c in range(plan.groups):
            for a in range(plan.cols_out):
                term = land[plan.part_at(a, b, c)].astype(F32)
                total = term if total is None else total + term
        du_ref[:, :, b * jb : (b + 1) * jb] = total
    bytes_of(land.at[pl.ds(0, chips - 1)], d_send)
    scatter.end()
    if plan.late:
        core_zero = section == 0
        for i in range(3):
            bytes_of(line_land[i], l_recv.at[i])
            total = lines[i][plan.depth - 1].astype(F32)
            for t in range(plan.depth - 1):
                total = total + line_land[i][t].astype(F32)
            half1[i][...] = total
            bytes_of(line_land[i], l_send.at[i])
            crossing[i][...] = jnp.where(core_zero, half1[i][...], half0[i][...])
            push(crossing[i], arrived[i], e_send.at[i], e_recv.at[i], sibling).start()
        hidden = hidden_ref[...]
        factor = lax.rsqrt(jnp.mean(hidden * hidden, axis=-1, keepdims=True) + EPSILON)
        signal_grad = du_ref[...].reshape(plan.rows, plan.width)
        weighted = signal_grad * gains_ref[0:1, :]
        correction = jnp.mean(weighted * hidden, axis=-1, keepdims=True)
        hidden_grad = factor * weighted - hidden * factor * factor * factor * correction
        gain_buf[...] = gain_sums_ref[...]
        gain_buf[0:1, :] = jnp.sum(signal_grad * hidden * factor, axis=0, keepdims=True)
        per_tile = LANES * chips // plan.width

        def send_gain(step, carry):
            peer = lax.rem(dev + step, 2 * chips)
            tile = lax.rem(peer, chips) // per_tile
            push(
                gain_buf.at[:, pl.ds(pl.multiple_of(LANES * tile, LANES), LANES)],
                gain_land.at[dev],
                n_send,
                n_recv,
                (peer // chips, lax.rem(peer, chips)),
            ).start()
            return carry

        lax.fori_loop(1, 2 * chips, send_gain, 0)
        pltpu.make_async_copy(
            gain_buf.at[:, pl.ds(pl.multiple_of(LANES * (chip // per_tile), LANES), LANES)],
            gain_land.at[dev],
            n_recv,
        ).start()
        done_in = (mask_ref[...] * (dmid_ref[...] + hidden_grad)).astype(BF)
        row = lax.broadcasted_iota(jnp.int32, (plan.rows, plan.rows), 0)
        col = lax.broadcasted_iota(jnp.int32, (plan.rows, plan.rows), 1)
        order = jnp.where(col == 2 * lax.rem(row, half) + row // half, 1.0, 0.0).astype(BF)
        done_in = cols_dot(order, done_in).astype(BF)
        done_out = cols_dot(order, out_ref[...]).astype(BF)
        give_res[...] = jnp.where(core_zero, done_out, done_in)
        swap_res = push(give_res, res_ref.at[section], e_send.at[3], e_recv.at[3], sibling)
        swap_res.start()
        res_ref[section] = jnp.where(core_zero, done_in, done_out)
        for i in range(3):
            push(crossing[i], arrived[i], e_send.at[i], e_recv.at[i], sibling).wait()
        lane = lax.broadcasted_iota(jnp.int32, (gate_ref.shape[0], LANES), 1)
        low = lane < half
        kept_half = [jnp.where(core_zero, half0[i][...], half1[i][...]) for i in range(3)]
        for i, out in ((0, gate_ref), (1, up_ref)):
            came = arrived[i][...]
            first = jnp.where(core_zero, kept_half[i], came)
            second = jnp.where(core_zero, came, kept_half[i])
            for j in range(out.shape[1] // (2 * LANES)):
                one, two = (w[:, LANES * j : LANES * (j + 1)] for w in (first, second))
                at = 2 * LANES * j
                out[:, at : at + LANES] = jnp.where(low, one, pltpu.roll(two, half, 1))
                out[:, at + LANES : at + 2 * LANES] = jnp.where(
                    low, pltpu.roll(one, half, 1), two
                )
        part = half0[2].shape[0]
        came = arrived[2][...]
        down_ref[:part, :] = jnp.where(core_zero, kept_half[2], came)
        down_ref[part:, :] = jnp.where(core_zero, came, kept_half[2])
        swap_res.wait()
        bytes_of(gain_land, n_recv)
        gain_out[...] = jnp.sum(gain_land[...], axis=0)
        bytes_of(gain_land.at[pl.ds(0, 2 * chips - 1)], n_send)
    if plan.routed:

        def drain(k, carry):
            piece_copies(k, False, False)
            return carry

        lax.fori_loop(0, plan.local, drain, 0)

        @pl.when(jnp.logical_and(section == 0, my_group == plan.groups - 1))
        def _():
            for tap in range(ORDER):
                piece_copies(tap, True, False)

        bytes_of(dmaps_ref, w_recv)


def backward_call(plan, g, filt, v, pq, tapw, x, xs, grads, rest=()):
    chips, half, jb, ia = plan.chips, plan.half, plan.jb, plan.ia
    any_spec = pl.BlockSpec(memory_space=pl.ANY)
    vmem_spec = pl.BlockSpec(memory_space=pltpu.VMEM)
    dma = pltpu.SemaphoreType.DMA
    shapes = [g_part.shape[3:] for g_part in grads]
    rows, width = plan.rows, plan.width
    finish = []
    if plan.late:
        out_shape = [jax.ShapeDtypeStruct((2, rows, width), BF)]
        out_shape += [
            jax.ShapeDtypeStruct(shape, F32)
            for shape in (
                (shapes[0][0], plan.ff),
                (shapes[1][0], plan.ff),
                (2 * shapes[2][0], width),
                *shapes[3:],
                (8, LANES),
            )
        ]
        in_vmem = len(out_shape)
        out_shape.append(jax.ShapeDtypeStruct((plan.map_rows, width), BF))
        finish = [
            pltpu.VMEM((2, half, width), F32),
            pltpu.VMEM((8, width), F32),
            pltpu.VMEM((2 * chips, 8, LANES), F32),
            pltpu.VMEM((rows, width), BF),
        ]
        finish += [pltpu.VMEM(shape, F32) for shape in shapes[:3]] * 3
        finish += [dma((4,)), dma((4,)), dma, dma]
        finish += [pltpu.VMEM(shape, F32) for shape in shapes[:3]]
        finish += [pltpu.VMEM((plan.depth - 1,) + shape, BF) for shape in shapes[:3]]
        finish += [dma((3,)), dma((3,))]
    else:
        out_shape = [jax.ShapeDtypeStruct(shape, F32) for shape in shapes]
        out_shape.append(jax.ShapeDtypeStruct((2, half, width), F32))
        in_vmem = len(out_shape)
        out_shape.append(jax.ShapeDtypeStruct((plan.local, jb, ia), BF))
        out_shape.append(jax.ShapeDtypeStruct((ORDER * jb, ia), BF))
    return pl.pallas_call(
        functools.partial(backward_kernel, plan, len(grads)),
        out_shape=out_shape,
        in_specs=[vmem_spec, vmem_spec, any_spec, vmem_spec, vmem_spec, any_spec, any_spec]
        + [vmem_spec] * (len(grads) + len(rest)),
        out_specs=[vmem_spec] * in_vmem + [any_spec] * (len(out_shape) - in_vmem),
        scratch_shapes=finish
        + Scatter.scratch(plan, shapes)
        + Scatter.semaphores(plan, len(grads))
        + [
            pltpu.VMEM((2, plan.length, ia), BF),
            pltpu.VMEM((2, ia, plan.length), BF),
            pltpu.VMEM((2, plan.f_rows, plan.length + BLOCK), F32),
            pltpu.VMEM((2, plan.local, BLOCK, plan.length), BF),
            pltpu.VMEM((2, 2, plan.length, 2 * jb), BF),
            pltpu.VMEM((plan.length, 2 * jb), BF),
            pltpu.VMEM((plan.length, 2 * jb), BF),
            pltpu.VMEM((plan.length, 2 * jb), F32),
            pltpu.VMEM((plan.length + 8, 2 * jb), F32),
            pltpu.VMEM((plan.local, jb, ia), F32),
            pltpu.VMEM((plan.local, jb, ia), BF),
            pltpu.VMEM((plan.local, jb, ia), BF),
            pltpu.VMEM((plan.local, jb, ia), BF),
            pltpu.VMEM((ORDER * jb, ia), F32),
            pltpu.VMEM((ORDER * jb, ia), BF),
            pltpu.VMEM((ORDER * jb, ia), BF),
            pltpu.VMEM((ORDER * jb, ia), BF),
            pltpu.VMEM((2, plan.length, jb), BF),
            pltpu.VMEM((chips, 2, half, jb), BF),
            dma,
            dma,
            dma((2,)),
            dma((plan.local,)),
            dma((plan.local,)),
            dma,
            dma,
            dma,
            dma,
            dma,
            dma,
            dma((2,)),
            dma,
            dma((plan.depth,)),
        ],
        compiler_params=pltpu.CompilerParams(
            collective_id=3, has_side_effects=True, vmem_limit_bytes=VMEM_LIMIT
        ),
        name="spectral_backward",
    )(g, filt, v, pq, tapw, x, xs, *grads, *rest)

SWAPS = 7
EARLY = 1


def middle_kernel(plan, *refs):
    (
        conv_ref,
        hidden_ref,
        gains_ref,
        mask_ref,
        up_ref,
        up_pair,
        *stored,
    ) = refs[:14]
    (
        out_ref,
        g_ref,
        dmid_ref,
        gain_ref,
        gate0_g,
        up0_g,
        down0_g,
        gate1_g,
        up1_g,
        down1_g,
        proj_g,
        attn_g,
    ) = refs[14:26]
    held = refs[26:34]
    (
        pair0,
        pair1,
        give,
        take,
        gates,
        ups,
        acts,
        dgate,
        dup,
        window,
        kv,
        q_buf,
        probs,
        dkv,
        dn,
        back,
        back_land,
        down_land,
        att,
        dq_buf,
        proj_all,
        attn_all,
        proj_take,
        attn_take,
        load_sem,
        a_send,
        a_recv,
        send,
        recv,
        kv_send,
        kv_recv,
        bk_send,
        bk_recv,
        *extra,
    ) = refs[34:]
    chips, rows, width = plan.chips, plan.rows, plan.width
    section, chip = spot()
    sibling = (1 - section, chip)
    reach = WINDOW // rows
    span = (reach + 1) * rows
    layer0, (w_proj, w_out), layer1 = held[:3], held[3:5], held[5:]
    split, cut = 3 * plan.width // 2, plan.width // 2
    own_rows = [
        w_proj.at[pl.ds(pl.multiple_of(split * section, 16), split), :],
        w_out.at[pl.ds(pl.multiple_of(cut * section, 16), cut), :],
    ]
    homes = list(layer0) + own_rows + ([] if plan.late else list(layer1))
    loads = [
        pltpu.make_async_copy(a, b, load_sem.at[i]) for i, (a, b) in enumerate(zip(stored, homes))
    ]
    if plan.late:
        grads1, gather_send, gather_recv, scatter_send, scatter_recv = extra[:3], *extra[3:7]
        gather = Gather(plan, layer1, layer1, gather_send, gather_recv)
        held_loads = [
            pltpu.make_async_copy(src, dst, gather_recv.at[i // 2, i % 2])
            for i, (src, dst) in enumerate(gather.held_parts(stored[5:]))
        ]
        for load in held_loads:
            load.start()
    for load in loads:
        load.start()
    greet_everyone(chips)()
    passes = [
        push(stored[3 + i], own_rows[i], a_send.at[i], a_recv.at[i], sibling) for i in range(2)
    ]
    for copy in passes:
        copy.start()
    if plan.late:
        scatter = Scatter(
            plan, grads1, (gate1_g, up1_g, down1_g), extra[7:], scatter_send, scatter_recv, True
        )
        for load in held_loads:
            load.wait()
        gather.last_only()
    ff = plan.ff // 2
    own = slice(0, rows)
    second = slice(rows, 2 * rows)
    mask = mask_ref[...]

    def swap(number, src, dst):
        copy = push(src, dst, send.at[number], recv.at[number], sibling)
        copy.start()
        copy.wait()

    def norm(values, gain):
        factor = lax.rsqrt(jnp.mean(values * values, axis=-1, keepdims=True) + EPSILON)
        return values * factor * gain, factor

    def norm_back(values, factor, gain, upstream):
        weighted = upstream * gain
        gain_grad = jnp.sum(upstream * values * factor, axis=0, keepdims=True)
        correction = jnp.mean(weighted * values, axis=-1, keepdims=True)
        return factor * weighted - values * factor * factor * factor * correction, gain_grad

    def feed(layer, pair, weights, number):
        w_gate, w_up, w_down = (Flat(w) for w in weights)
        swap(number, pair.at[own], pair.at[second])
        for start in range(0, ff, BLOCK):
            cols = slice(start, start + BLOCK)
            gate_rows = flat_dot(pair[...], w_gate.columns(start, BLOCK))
            up_rows = flat_dot(pair[...], w_up.columns(start, BLOCK))
            gates[layer, :, cols] = gate_rows
            ups[layer, :, cols] = up_rows
            acts[layer, :, cols] = (gate_rows * jax.nn.sigmoid(gate_rows) * up_rows).astype(BF)
        part = flat_dot(acts[layer], w_down.all())
        give[number] = part[second].astype(BF)
        swap(number + 1, give.at[number], take.at[number])
        return part[own] + take[number].astype(F32)

    def feed_back(layer, pair, weights, grads, upstream_pair, number):
        w_gate, w_up, w_down = (Flat(w) for w in weights)
        gate_g, up_g, down_g = (Flat(w) for w in grads)
        turned = pair[...].astype(F32).T.astype(BF)
        for start in range(0, ff, BLOCK):
            cols = slice(start, start + BLOCK)
            active_grad = rows_dot(upstream_pair, w_down.rows(start, BLOCK))
            gate_rows, up_rows = gates[layer, :, cols], ups[layer, :, cols]
            sigmoid = jax.nn.sigmoid(gate_rows)
            slope = sigmoid * (1.0 + gate_rows * (1.0 - sigmoid))
            gate_grad = (active_grad * up_rows * slope).astype(BF)
            up_grad = (active_grad * gate_rows * sigmoid).astype(BF)
            dgate[:, cols] = gate_grad
            dup[:, cols] = up_grad
        for start in range(0, width, BLOCK):
            cols = slice(start, start + BLOCK)
            part = rows_dot(dgate[...], w_gate.rows(start, BLOCK)) + rows_dot(
                dup[...], w_up.rows(start, BLOCK)
            )
            give[number, :, cols] = part[second].astype(BF)
            att[:, cols] = part[own]
        copy = push(
            give.at[number], take.at[number], send.at[number], recv.at[number], sibling
        )
        copy.start()
        for start in range(0, ff, BLOCK):
            cols = slice(start, start + BLOCK)
            gate_g.put_columns(start, flat_dot(turned, dgate[:, cols]).astype(BF))
            up_g.put_columns(start, flat_dot(turned, dup[:, cols]).astype(BF))
            down_g.put_rows(
                start,
                flat_dot(acts[layer, :, cols].astype(F32).T.astype(BF), upstream_pair).astype(BF),
            )
        copy.wait()
        return att[...] + take[number].astype(F32)

    middle0 = hidden_ref[...] + conv_ref[...]
    normed, factor0 = norm(middle0, gains_ref[1:2, :])
    pair0[own] = normed.astype(BF)
    dmid_ref[...] = middle0
    for load in loads[:3]:
        load.wait()
    branch = feed(0, pair0, layer0, 0)
    passed = (mask * (dmid_ref[...] + branch)).astype(BF).astype(F32)

    normed, factor10 = norm(passed, gains_ref[2:3, :])
    inputs = normed.astype(BF)
    mine = slice(reach * rows, span)
    window[mine, :] = inputs

    layer, level = plan.layer, chip // plan.layer
    within = lax.rem(chip, layer)

    def slot(distance):
        return window.at[pl.ds((reach - distance) * rows, rows)]

    def ahead(distance):
        return push(
            window.at[mine],
            slot(distance),
            kv_send.at[distance - 1],
            kv_recv.at[distance - 1],
            (section, chip + distance),
        )

    def pass_on(place):
        distance = reach - (within - place)
        return push(
            slot(reach),
            slot(distance),
            kv_send.at[reach + place],
            kv_recv.at[distance - 1],
            (section, level * layer + place),
        )

    def goes_ahead(distance):
        if plan.layered and distance < reach:
            return within + distance < layer
        return chip + distance < chips

    def comes(distance):
        return chip >= distance

    for distance in range(reach, 0, -1):

        @pl.when(goes_ahead(distance))
        def _():
            ahead(distance).start()

        @pl.when(chip < distance)
        def _():
            window[(reach - distance) * rows : (reach - distance + 1) * rows, :] = jnp.zeros(
                (rows, width), BF
            )

    half = plan.half
    row = lax.broadcasted_iota(jnp.int32, (rows, span), 0)
    col = lax.broadcasted_iota(jnp.int32, (rows, span), 1)
    inner = lax.rem(col, rows)
    q_place = 2 * lax.rem(row, half) + row // half
    k_place = (col // rows - reach) * rows + 2 * lax.rem(inner, half) + inner // half
    distance_rows = q_place - k_place
    allowed = (
        (k_place + chip * rows >= 0) & (distance_rows >= 0) & (distance_rows < WINDOW)
    )
    lane = lax.broadcasted_iota(jnp.int32, (rows, LANES), 1)
    low = lane < HEAD_DIM
    scale = HEAD_DIM ** (-0.5)
    zero = jnp.zeros((rows, LANES), BF)
    for load in loads[3:5]:
        load.wait()
    for copy in passes:
        copy.wait()
    w_query, w_key, w_value = (w_proj.at[pl.ds(part * width, width)] for part in range(3))
    q_buf[...] = flat_dot(inputs, w_query[...]).astype(BF)
    kv[mine, :width] = flat_dot(inputs, w_key[...]).astype(BF)
    kv[mine, width:] = flat_dot(inputs, w_value[...]).astype(BF)

    def arrived(distance):
        push(
            window.at[mine],
            slot(distance),
            kv_send.at[distance - 1],
            kv_recv.at[distance - 1],
            sibling,
        ).wait_recv()

    pl.when(comes(reach))(functools.partial(arrived, reach))
    if plan.layered:
        for place in range(layer - 1):

            @pl.when(jnp.logical_and(level > 0, place < within))
            def _():
                pass_on(place).start()

    for distance in range(1, reach):
        pl.when(comes(distance))(functools.partial(arrived, distance))
    earlier = slice(0, reach * rows)
    kv[earlier, :width] = flat_dot(window[earlier, :], w_key[...]).astype(BF)
    kv[earlier, width:] = flat_dot(window[earlier, :], w_value[...]).astype(BF)

    for pair in range(width // LANES):
        lanes = slice(LANES * pair, LANES * (pair + 1))
        keys, values = kv[:, lanes], kv[:, width + LANES * pair : width + LANES * (pair + 1)]
        parts = []
        for side in range(2):
            here = low if side == 0 else jnp.logical_not(low)
            queries = jnp.where(here, q_buf[:, lanes], zero)
            scores = rows_dot(queries, keys) * scale
            scores = jnp.where(allowed, scores, BIG_NEGATIVE)
            weights = jnp.exp(scores - jnp.max(scores, axis=-1, keepdims=True))
            weights = weights / jnp.sum(weights, axis=-1, keepdims=True)
            probs[2 * pair + side] = weights
            parts.append(flat_dot(weights.astype(BF), values))
        att[:, lanes] = jnp.where(low, parts[0], parts[1])
    attended = att[...].astype(BF)
    middle1 = passed + flat_dot(attended, w_out[...])

    if plan.late:
        gather.end(True)
    for load in loads[5:]:
        load.wait()
    normed, factor11 = norm(middle1, gains_ref[3:4, :])
    pair1[own] = normed.astype(BF)
    branch = feed(1, pair1, layer1, 2)
    out_ref[...] = (mask * (middle1 + branch)).astype(BF)
    if not plan.late:
        grads1 = (gate1_g, up1_g, down1_g)
    dnormed = feed_back(1, pair1, layer1, grads1, up_pair[...], 4)
    if plan.late:
        scatter.begin(0, plan.depth // 2)
    dmiddle, gain11 = norm_back(middle1, factor11, gains_ref[3:4, :], dnormed)
    dmiddle = up_ref[...] + dmiddle
    gain_ref[3:4, :] = gain11

    dy = dmiddle.astype(BF)
    attn_all[...] = flat_dot(attended.astype(F32).T.astype(BF), dy).astype(BF)
    datt = rows_dot(dy, w_out[...]).astype(BF)
    for pair in range(width // LANES):
        lanes = slice(LANES * pair, LANES * (pair + 1))
        value_lanes = slice(width + LANES * pair, width + LANES * (pair + 1))
        keys, values = kv[:, lanes], kv[:, value_lanes]
        dq_parts, key_grad, value_grad = [], None, None
        for side in range(2):
            here = low if side == 0 else jnp.logical_not(low)
            queries = jnp.where(here, q_buf[:, lanes], zero)
            upstream = jnp.where(here, datt[:, lanes], zero)
            weights = probs[2 * pair + side]
            grad = rows_dot(upstream, values)
            total = jnp.sum(weights * grad, axis=-1, keepdims=True)
            dscores = weights * (grad - total)
            dq_parts.append(flat_dot(dscores.astype(BF), keys))
            one = flat_dot(dscores.T.astype(BF), queries)
            two = flat_dot(weights.T.astype(BF), upstream)
            key_grad = one if key_grad is None else key_grad + one
            value_grad = two if value_grad is None else value_grad + two
        dq_buf[:, lanes] = (jnp.where(low, dq_parts[0], dq_parts[1]) * scale).astype(BF)
        dkv[:, lanes] = (key_grad * scale).astype(BF)
        dkv[:, value_lanes] = value_grad.astype(BF)
    back[...] = (
        rows_dot(dkv[earlier, :width], w_key[...]) + rows_dot(dkv[earlier, width:], w_value[...])
    ).astype(BF)

    def behind(distance, peer):
        return push(
            back.at[pl.ds((reach - distance) * rows, rows)],
            back_land.at[distance - 1],
            bk_send.at[distance - 1],
            bk_recv.at[distance - 1],
            (section, peer),
        )

    def to_place(place):
        distance = lax.rem(within - place + layer, layer)
        return push(
            back.at[pl.ds((reach - distance) * rows, rows)],
            back_land.at[within],
            bk_send.at[place],
            bk_recv.at[within],
            (section, level * layer + place),
        )

    def came_from(place):
        push(
            back_land.at[place],
            back_land.at[place],
            bk_send.at[place],
            bk_recv.at[place],
            sibling,
        ).wait_recv()

    def down():
        return push(
            back.at[pl.ds(0, rows)],
            down_land,
            bk_send.at[reach],
            bk_recv.at[reach],
            (section, chip - layer),
        )

    if plan.layered:
        for place in range(layer - 1, -1, -1):

            @pl.when(jnp.logical_and(place > within, level > 0))
            def _():
                to_place(place).start()

        for place in range(layer):

            @pl.when(place < within)
            def _():
                to_place(place).start()

    else:
        for distance in range(1, reach + 1):

            @pl.when(chip >= distance)
            def _():
                behind(distance, chip - distance).start()

    if plan.late:
        scatter.begin(plan.depth // 2)
    dn[...] = (
        rows_dot(dq_buf[...], w_query[...])
        + rows_dot(dkv[mine, :width], w_key[...])
        + rows_dot(dkv[mine, width:], w_value[...])
    )
    if plan.layered:
        for place in range(layer - 1):

            @pl.when(jnp.logical_and(place < within, level > 0))
            def _():
                came_from(place)
                below = back[:rows, :].astype(F32) + back_land[place].astype(F32)
                back[:rows, :] = below.astype(BF)

        @pl.when(level > 0)
        def _():
            down().start()

        for place in range(1, layer):

            @pl.when(place > within)
            def _():
                came_from(place)
                dn[...] += back_land[place].astype(F32)

        @pl.when(level < plan.depth - 1)
        def _():
            down().wait_recv()
            dn[...] += down_land[...].astype(F32)

    else:
        for distance in range(1, reach + 1):

            @pl.when(chip + distance < chips)
            def _():
                behind(distance, chip).wait_recv()
                dn[...] += back_land[distance - 1].astype(F32)

    dnormed = dn[...]
    dpassed, gain10 = norm_back(passed, factor10, gains_ref[2:3, :], dnormed)
    gain_ref[2:3, :] = gain10
    dpassed = (dmiddle + dpassed).astype(BF).astype(F32)

    upstream0 = mask * dpassed
    give[5] = upstream0.astype(BF)
    copy = push(give.at[5], take.at[5], send.at[5], recv.at[5], sibling)
    copy.start()
    turned = window[...].astype(F32).T.astype(BF)
    proj_all[:width, :] = flat_dot(turned[:, reach * rows :], dq_buf[...]).astype(BF)
    proj_all[width : 2 * width, :] = flat_dot(turned, dkv[:, :width]).astype(BF)
    proj_all[2 * width :, :] = flat_dot(turned, dkv[:, width:]).astype(BF)
    copy.wait()
    crossing = [
        push(
            whole.at[pl.ds(pl.multiple_of(size * (1 - section), 16), size), :],
            land,
            a_send.at[2 + i],
            a_recv.at[2 + i],
            sibling,
        )
        for i, (whole, land, size) in enumerate(
            ((proj_all, proj_take, split), (attn_all, attn_take, cut))
        )
    ]
    for cross in crossing:
        cross.start()
    if plan.late:
        scatter.stage(0)
    both = jnp.concatenate([give[5], take[5]], 0)
    dnormed = feed_back(0, pair0, layer0, (gate0_g, up0_g, down0_g), both, 6)
    if plan.late:
        for number in range(1, plan.depth + 1):
            scatter.stage(number)
    middle0 = dmid_ref[...]
    dmiddle, gain01 = norm_back(middle0, factor0, gains_ref[1:2, :], dnormed)
    gain_ref[1:2, :] = gain01
    dmiddle = upstream0 + dmiddle
    dmid_ref[...] = dmiddle
    g_ref[...] = dmiddle.astype(BF)
    for cross in crossing:
        cross.wait()
    for whole, land, size, out in (
        (proj_all, proj_take, split, proj_g),
        (attn_all, attn_take, cut, attn_g),
    ):
        own_part = whole[pl.ds(pl.multiple_of(size * section, 16), size), :]
        out[...] = (own_part.astype(F32) + land[...].astype(F32)).astype(BF)
    if plan.late:
        scatter.end()

    for distance in range(1, reach + 1):

        @pl.when(goes_ahead(distance))
        def _():
            ahead(distance).wait_send()

    if plan.layered:
        for place in range(layer):

            @pl.when(jnp.logical_and(level > 0, place < within))
            def _():
                pass_on(place).wait_send()

            @pl.when((place < within) | ((place > within) & (level > 0)))
            def _():
                to_place(place).wait_send()

        @pl.when(level > 0)
        def _():
            down().wait_send()

    else:
        for distance in range(1, reach + 1):

            @pl.when(chip >= distance)
            def _():
                behind(distance, chip).wait_send()


def middle_call(plan, conv, hidden, gains, mask, upstream, pair, stored):
    rows, width = plan.rows, plan.width
    reach = WINDOW // rows
    ff = plan.ff // 2
    any_spec = pl.BlockSpec(memory_space=pl.ANY)
    vmem_spec = pl.BlockSpec(memory_space=pltpu.VMEM)
    dma = pltpu.SemaphoreType.DMA
    layer = [(width, ff), (width, ff), (ff, width)]
    grid = (plan.depth, plan.side, plan.side)
    chips = plan.chips
    spread = [grid + (a // chips, b) for a, b in layer]
    held = layer + [(3 * width, width), (width, width)] + (spread if plan.late else layer)
    split, cut = 3 * width // 2, width // 2
    extra = []
    if plan.late:
        extra = [pltpu.VMEM(w, BF) for w in spread]
        extra += Gather.semaphores(plan, 3) + Scatter.semaphores(plan, 3)
        extra += Scatter.scratch(plan, [w[3:] for w in spread])
    shapes = [
        ((rows, width), BF),
        ((rows, width), BF),
        ((rows, width), F32),
        ((8, width), F32),
    ]
    shapes += [(w, BF) for w in layer]
    shapes += [((plan.depth,) + w[3:] if plan.late else v, BF) for v, w in zip(layer, spread)]
    shapes += [((split, width), BF), ((cut, width), BF)]
    return pl.pallas_call(
        functools.partial(middle_kernel, plan),
        out_shape=[jax.ShapeDtypeStruct(s, d) for s, d in shapes],
        in_specs=[vmem_spec] * 6 + [any_spec] * 8,
        out_specs=[vmem_spec] * len(shapes),
        scratch_shapes=[pltpu.VMEM(w, BF) for w in held]
        + [
            pltpu.VMEM((2 * rows, width), BF),
            pltpu.VMEM((2 * rows, width), BF),
            pltpu.VMEM((SWAPS, rows, width), BF),
            pltpu.VMEM((SWAPS, rows, width), BF),
            pltpu.VMEM((2, 2 * rows, ff), F32),
            pltpu.VMEM((2, 2 * rows, ff), F32),
            pltpu.VMEM((2, 2 * rows, ff), BF),
            pltpu.VMEM((2 * rows, ff), BF),
            pltpu.VMEM((2 * rows, ff), BF),
            pltpu.VMEM(((reach + 1) * rows, width), BF),
            pltpu.VMEM(((reach + 1) * rows, 2 * width), BF),
            pltpu.VMEM((rows, width), BF),
            pltpu.VMEM((width // HEAD_DIM, rows, (reach + 1) * rows), F32),
            pltpu.VMEM(((reach + 1) * rows, 2 * width), BF),
            pltpu.VMEM((rows, width), F32),
            pltpu.VMEM((reach * rows, width), BF),
            pltpu.VMEM((reach, rows, width), BF),
            pltpu.VMEM((rows, width), BF),
            pltpu.VMEM((rows, width), F32),
            pltpu.VMEM((rows, width), BF),
            pltpu.VMEM((3 * width, width), BF),
            pltpu.VMEM((width, width), BF),
            pltpu.VMEM((split, width), BF),
            pltpu.VMEM((cut, width), BF),
            dma((8,)),
            dma((4,)),
            dma((4,)),
            dma((SWAPS,)),
            dma((SWAPS,)),
            dma((2 * reach,)),
            dma((reach,)),
            dma((reach + 1,)),
            dma((reach + 1,)),
        ]
        + extra,
        compiler_params=pltpu.CompilerParams(
            collective_id=5, has_side_effects=True, vmem_limit_bytes=VMEM_LIMIT
        ),
        name="middle",
    )(conv, hidden, gains, mask, upstream, pair, *stored)


def swapped(block):
    return lax.ppermute(block, "section", [(0, 1), (1, 0)])


def norm_backward(values, factor, weights, upstream):
    weighted = upstream * weights
    gain_grad = jnp.sum(upstream * values * factor, axis=0)
    correction = jnp.mean(weighted * values, axis=-1, keepdims=True)
    return (factor * weighted - values * factor * factor * factor * correction, gain_grad)


def body(
    io_pair, lengths, filters, stu_maps, attn_proj, attn_out, norm_gains, mlp_gate, mlp_up, mlp_down
):
    chips = lax.axis_size("seq")
    section, chip = spot()
    core_zero = section == 0
    tok_rows = io_pair.shape[2]
    width = io_pair.shape[3]
    half = tok_rows // 2
    ff = mlp_gate.shape[2]
    ff_half = mlp_down.shape[1] // 2
    plan = Plan(chips, tok_rows, width, filters.shape[1], stu_maps.shape[0], ff)

    def join_phases(rows):
        return rows.reshape(2, half, width).swapaxes(0, 1).reshape(rows.shape)

    my_a, my_b = plan.a_of(chip), plan.b_of(chip)
    my_group = chip // (plan.cols_out * plan.cols_in)
    if plan.routed:
        maps = [stu_maps]
    else:
        whole = lax.all_gather(stu_maps, ("section", "seq"), axis=0, tiled=True)
        whole = lax.dynamic_slice(
            whole.reshape(-1, width, width),
            (0, my_b * plan.jb, my_a * plan.ia),
            (whole.shape[0] // width, plan.jb, plan.ia),
        )
        pair = whole[: 2 * plan.filters].reshape(2, plan.filters, plan.jb, plan.ia)
        pair = lax.dynamic_slice_in_dim(pair, my_group * plan.local, plan.local, 1)
        taps = jnp.where(my_group == 0, whole[2 * plan.filters :], 0).astype(BF)
        maps = [
            jnp.where(core_zero, pair[0], pair[1]),
            jnp.where(core_zero, pair[1], pair[0]),
            taps.reshape(-1, plan.ia),
        ]

    gate, up = mlp_gate[0], mlp_up[0]
    if not plan.pick_here:
        gate, up = (
            jnp.transpose(w.reshape(w.shape[0], chips, 2, ff_half), (2, 0, 1, 3)).reshape(
                2, w.shape[0], ff // 2
            )
            for w in (gate, up)
        )
    results = forward_call(
        plan,
        io_pair[0],
        norm_gains[0],
        filters,
        lengths,
        [gate, up, mlp_down[0], attn_proj, attn_out],
        maps,
    )
    flat = 5 if plan.late else 8
    weights = [w.reshape(-1, w.shape[-1]) for w in results[:flat]] + list(results[flat:8])
    conv, hidden, upstream1, grad_pair, gains, mask_rows = results[8:14]
    v, pq, tapw, x_all, xs_all, filt = results[14:]
    block_out, g, middle0_grad, gain_sums, *grads = middle_call(
        plan,
        conv.reshape(tok_rows, width),
        hidden,
        gains,
        mask_rows,
        upstream1,
        grad_pair,
        weights,
    )
    mlp0_grads, half1, attn_grads = grads[:3], grads[3:6], grads[6:]
    gain01, gain10, gain11 = gain_sums[1], gain_sums[2], gain_sums[3]
    g = g.reshape(2, half, width)
    grid = (plan.depth, plan.side, plan.side)
    blocks0 = [w.reshape(grid + (w.shape[0] // chips, w.shape[1])) for w in mlp0_grads]
    blocks1 = [w.reshape(grid + (w.shape[0] // chips, w.shape[1])) for w in attn_grads]
    if plan.late:
        result, gate_out, up_out, down_out, proj_out, out_out, gain_tile, maps_out = backward_call(
            plan,
            g,
            filt,
            v,
            pq,
            tapw,
            x_all,
            xs_all,
            blocks0 + blocks1,
            [hidden, gains, mask_rows, middle0_grad, block_out, gain_sums, *half1],
        )
        cols = width // chips
        gain_out = lax.dynamic_slice(
            gain_tile, (2 * section, (chip % (LANES // cols)) * cols), (2, cols)
        )
        return (
            result[None],
            maps_out.astype(F32),
            proj_out,
            out_out,
            gain_out[None],
            gate_out[None],
            up_out[None],
            down_out[None],
        )
    results = backward_call(plan, g, filt, v, pq, tapw, x_all, xs_all, blocks0)
    half0, results = results[:3], results[3:]
    attn_sums = [
        lax.psum_scatter(
            w.reshape((chips,) + w.shape[3:]), "seq", scatter_dimension=0, tiled=False
        )
        for w in blocks1
    ]
    half1 = [
        lax.psum_scatter(
            w.reshape(chips, -1, w.shape[-1]), "seq", scatter_dimension=0, tiled=False
        )
        for w in half1
    ]
    signal_grad = results[0].reshape(tok_rows, width)
    piece, tap_piece = (r.astype(F32) for r in results[1:])
    full = jnp.zeros((2, plan.filters, width, width), F32)
    full = lax.dynamic_update_slice(
        full,
        piece[None],
        (section, my_group * plan.local, my_b * plan.jb, my_a * plan.ia),
    )
    tap_piece = jnp.where(core_zero & (my_group == 0), tap_piece, 0.0)
    tap_full = lax.dynamic_update_slice(
        jnp.zeros((ORDER, width, width), F32),
        tap_piece.reshape(ORDER, plan.jb, plan.ia),
        (0, my_b * plan.jb, my_a * plan.ia),
    )
    full = jnp.concatenate([full.reshape(-1, width), tap_full.reshape(-1, width)], 0)
    maps_grad = lax.psum_scatter(full, ("section", "seq"), scatter_dimension=0, tiled=True)
    spectral_factor = lax.rsqrt(jnp.mean(hidden * hidden, axis=-1, keepdims=True) + EPSILON)
    hidden_grad, gain00 = norm_backward(hidden, spectral_factor, gains[0], signal_grad)
    inputs_grad = (mask_rows * (middle0_grad + hidden_grad)).astype(BF)

    proj_out, out_out = (w.astype(F32) for w in attn_sums)
    outs = []
    for index in range(3):
        zero, one = half0[index].astype(BF), half1[index].astype(BF)
        keep = jnp.where(core_zero, zero, one)
        take = swapped(jnp.where(core_zero, one, zero))
        low = jnp.where(core_zero, keep, take).astype(F32)
        high = jnp.where(core_zero, take, keep).astype(F32)
        if index < 2:
            rows = low.shape[0]
            joined = jnp.stack(
                [low.reshape(rows, chips, ff_half), high.reshape(rows, chips, ff_half)], 2
            ).reshape(rows, ff)
        else:
            joined = jnp.concatenate([low, high], 0)
        outs.append(joined[None])

    gain_parts = jnp.stack([jnp.stack([gain00, gain01]), jnp.stack([gain10, gain11])])
    gain_cols = width // chips
    tiles = jnp.transpose(gain_parts.reshape(2, 2, chips, gain_cols), (0, 2, 1, 3))
    tiles = jnp.pad(
        tiles.reshape(2 * chips, 2, gain_cols), ((0, 0), (0, 6), (0, LANES - gain_cols))
    )
    done_in, done_out = join_phases(inputs_grad), join_phases(block_out)
    taken, landed = exit_call(chips, jnp.where(core_zero, done_out, done_in), tiles)
    first = jnp.where(core_zero, done_in, taken)
    second = jnp.where(core_zero, taken, done_out)
    result_pair = jnp.stack([first, second])[None]
    gain_out = jnp.sum(landed, axis=0)[None, :2, :gain_cols]
    return (result_pair, maps_grad, proj_out, out_out, gain_out, outs[0], outs[1], outs[2])


def solution(mesh):
    placed = (
        P("section", None, "seq", None),
        P(),
        P("seq", None),
        P(("section", "seq"), None),
        P(("section", "seq"), None),
        P(("section", "seq"), None),
        P("section", None, "seq"),
        P("section", "seq", None),
        P("section", "seq", None),
        P("section", "seq", None),
    )
    return jax.shard_map(
        body,
        mesh=mesh,
        in_specs=placed,
        out_specs=(
            P("section", None, "seq", None),
            P(("section", "seq"), None),
            P(("section", "seq"), None),
            P(("section", "seq"), None),
            P("section", None, "seq"),
            P("section", "seq", None),
            P("section", "seq", None),
            P("section", "seq", None),
        ),
        check_vma=False,
    )
```
